32 devices in a mesh: dp: 16 (over z, y, x), tensor: 2 (over core).
Axes of the slice: x: 2, y: 2, z: 4, core: 2. Of those that a mesh axis runs over, the one named last changes fastest.
Arguments:
- layer_input: bfloat16 [10240, 1536], P(('dp', 'tensor')), may hold values from -6 to 6
- out_cotangent: bfloat16 [10240, 1536], P(('dp', 'tensor')), may hold values from -6 to 6
- positions: int32 [10240], P('dp'), may hold values from 0 to 2559, as said below
- segment_ids: int32 [10240], replicated, may hold values from 0 to 25, as said below
- parent_ids: int32 [26], replicated, may hold values from 0 to 17, as said below
- attention_gain: bfloat16 [1536], P('dp'), may hold values from 0.25 to 1.75
- query_weight: bfloat16 [1536, 1536], P('dp', 'tensor'), may hold values from -0.21875 to 0.21875
- query_bias: bfloat16 [12, 128], P('tensor', 'dp'), may hold values from -3 to 3
- key_weight: bfloat16 [1536, 256], P('dp', 'tensor'), may hold values from -0.15625 to 0.15625
- key_bias: bfloat16 [2, 128], P('tensor', 'dp'), may hold values from -3 to 3
- value_weight: bfloat16 [1536, 256], P('dp', 'tensor'), may hold values from -0.15625 to 0.15625
- value_bias: bfloat16 [2, 128], P('tensor', 'dp'), may hold values from -3 to 3
- output_weight: bfloat16 [1536, 1536], P('tensor', 'dp'), may hold values from -1.75 to 1.75
- feedforward_gain: bfloat16 [1536], P('dp'), may hold values from 0.25 to 1.75
- gate_weight: bfloat16 [1536, 8960], P('dp', 'tensor'), may hold values from -0.15625 to 0.15625
- up_weight: bfloat16 [1536, 8960], P('dp', 'tensor'), may hold values from -0.15625 to 0.15625
- down_weight: bfloat16 [8960, 1536], P('tensor', 'dp'), may hold values from -0.125 to 0.125
Outputs:
- layer_output: bfloat16 [10240, 1536], P(('dp', 'tensor'))
- input_grad: bfloat16 [10240, 1536], P(('dp', 'tensor'))
- attention_gain_grad: float32 [1536], P('dp')
- query_weight_grad: float32 [1536, 1536], P('dp', 'tensor')
- query_bias_grad: float32 [12, 128], P('tensor', 'dp')
- key_weight_grad: float32 [1536, 256], P('dp', 'tensor')
- key_bias_grad: float32 [2, 128], P('tensor', 'dp')
- value_weight_grad: float32 [1536, 256], P('dp', 'tensor')
- value_bias_grad: float32 [2, 128], P('tensor', 'dp')
- output_weight_grad: float32 [1536, 1536], P('tensor', 'dp')
- feedforward_gain_grad: float32 [1536], P('dp')
- gate_weight_grad: float32 [1536, 8960], P('dp', 'tensor')
- up_weight_grad: float32 [1536, 8960], P('dp', 'tensor')
- down_weight_grad: float32 [8960, 1536], P('tensor', 'dp')
The draws below stay inside these ranges and needn't reach their ends.
Inputs may be any that keep to these rules, and one draw needn't show every extreme that they name: `segment_ids`: the tokens form 2 trees of 5120 consecutive tokens; tree t holds segments 13 t to 13 t + 12: its trunk of 2048 tokens comes first, then its 4 branches of 256 tokens and 8 leaves of 256 tokens in any order, each segment's tokens consecutive. `parent_ids`: A trunk is its own parent; a branch's parent is its tree's trunk; a leaf's parent is a branch of its tree, two leaves to each branch. `positions`: A trunk token's place in its trunk; 2048 plus a branch token's place in its branch; 2304 plus a leaf token's place in its leaf.
All inputs are finite; a program needn't handle non-finite values.
Results may differ from the reference program's by a relative error of at most 0.023.
Values may be sent and summed in bfloat16 or wider, within the bound.
A program may use at most 256 MiB of HBM per device.

```python
import jax
import jax.numpy as jnp
from jax import lax

D = 1536
H = 12
KV = 2
HD = 128
FF = 8960
TRUNK = 2048
BRANCH = 256
LEAF = 256
BRANCHES = 4
TREE_TOK = 5120
TOK_DEV = 640
TREES = 2
TOKENS = 10240


def tree_layout(key):
    per_tree = 1 + 3 * BRANCHES

    def one_tree(tree):
        tree_key = jax.random.fold_in(key, tree)
        order_key, leaf_key = jax.random.split(tree_key)
        order = jnp.concatenate([jnp.zeros((1,), jnp.int32), 1 + jax.random.permutation(order_key, per_tree - 1).astype(jnp.int32)])
        lengths = jnp.where(order == 0, TRUNK, jnp.where(order <= BRANCHES, BRANCH, LEAF)).astype(jnp.int32)
        starts = jnp.cumsum(lengths) - lengths
        token = jnp.arange(TREE_TOK, dtype=jnp.int32)
        slot = jnp.sum((token[:, None] >= starts[None, 1:]).astype(jnp.int32), axis=1)
        chosen = slot[:, None] == jnp.arange(per_tree, dtype=jnp.int32)[None, :]
        local = jnp.sum(jnp.where(chosen, order[None, :], 0), axis=1)
        offset = token - jnp.sum(jnp.where(chosen, starts[None, :], 0), axis=1)
        place = jnp.where(local == 0, offset, jnp.where(local <= BRANCHES, TRUNK + offset, TRUNK + BRANCH + offset))
        leaf_parents = 1 + jax.random.permutation(leaf_key, jnp.arange(2 * BRANCHES, dtype=jnp.int32) // 2)
        parents = jnp.concatenate([jnp.zeros((1 + BRANCHES,), jnp.int32), leaf_parents.astype(jnp.int32)])
        base = tree * per_tree
        return (local + base, parents + base, place)
    segs, parents, places = jax.vmap(one_tree)(jnp.arange(TREES, dtype=jnp.int32))
    return (segs.reshape(-1), parents.reshape(-1), places.reshape(-1))


def draw_segment_ids(key, part):
    return tree_layout(jax.random.fold_in(key, 11))[0]


def draw_parent_ids(key, part):
    return tree_layout(jax.random.fold_in(key, 11))[1]


def draw_positions(key, part):
    return tree_layout(jax.random.fold_in(key, 11))[2]


def level_of(key, shape, pieces, smallest, high):
    def one(axis_at, shards_of):
        draws = jax.random.uniform(jax.random.fold_in(jax.random.fold_in(key, 6), axis_at), (shards_of,), jnp.float32, smallest / len(pieces), high / len(pieces))
        return jnp.repeat(jnp.exp(draws), shape[axis_at] // shards_of).reshape((-1,) + (1,) * (len(shape) - axis_at - 1))

    factor_of = one(*pieces[0])
    for cut in pieces[1:]:
        factor_of = factor_of * one(*cut)
    return factor_of


def normal_values(rng, extent, width, bound, cuts=(), kind=jnp.bfloat16):
    array = width * jax.random.normal(rng, extent, jnp.float32)
    if cuts:
        array = array * level_of(rng, extent, cuts, -0.22, 0.18)
    return jnp.clip(array, -bound, bound).astype(kind)


def setup_inputs(seed: int = 0) -> dict:
    arg_keys = jax.random.split(jax.random.key(seed), 18)
    return {
        "layer_input": normal_values(arg_keys[0], (TOKENS, D), 1.0, 6.0, ((0, 32),)),
        "out_cotangent": normal_values(arg_keys[1], (TOKENS, D), 1.0, 6.0, ((0, 32),)),
        "positions": draw_positions(jax.random.fold_in(arg_keys[17], 71), 0),
        "segment_ids": draw_segment_ids(jax.random.fold_in(arg_keys[17], 71), 0),
        "parent_ids": draw_parent_ids(jax.random.fold_in(arg_keys[17], 71), 0),
        "attention_gain": jnp.clip(1.0 + 0.15 * jax.random.normal(arg_keys[5], (D,), jnp.float32), 0.25, 1.75).astype(jnp.bfloat16),
        "query_weight": normal_values(arg_keys[6], (D, H * HD), (D // 2) ** -0.5, 0.21875, ((0, 16), (1, 2))),
        "query_bias": normal_values(arg_keys[7], (H, HD), 0.3, 3.0, ((0, 2), (1, 16))),
        "key_weight": normal_values(arg_keys[8], (D, KV * HD), D ** -0.5, 0.15625, ((0, 16), (1, 2))),
        "key_bias": normal_values(arg_keys[9], (KV, HD), 0.3, 3.0, ((0, 2), (1, 16))),
        "value_weight": normal_values(arg_keys[10], (D, KV * HD), D ** -0.5, 0.15625, ((0, 16), (1, 2))),
        "value_bias": normal_values(arg_keys[11], (KV, HD), 0.3, 3.0, ((0, 2), (1, 16))),
        "output_weight": normal_values(arg_keys[12], (H * HD, D), (H * HD // 128) ** -0.5, 1.75, ((0, 2), (1, 16))),
        "feedforward_gain": jnp.clip(1.0 + 0.15 * jax.random.normal(arg_keys[13], (D,), jnp.float32), 0.25, 1.75).astype(jnp.bfloat16),
        "gate_weight": normal_values(arg_keys[14], (D, FF), D ** -0.5, 0.15625, ((0, 16), (1, 2))),
        "up_weight": normal_values(arg_keys[15], (D, FF), D ** -0.5, 0.15625, ((0, 16), (1, 2))),
        "down_weight": normal_values(arg_keys[16], (FF, D), (FF // 4) ** -0.5, 0.125, ((0, 2), (1, 16))),
    }


EPS = 1e-06
NEG = -1e+30
THETA = 10000.0
HIGH = lax.Precision.HIGHEST

@jax.custom_vjp
def low(v):
    return lax.optimization_barrier(v.astype(jnp.bfloat16)).astype(jnp.float32)

@jax.custom_vjp
def low_back(v):
    return v

def low_keep(v):
    return (low(v), None)

def low_pass(kept, grad):
    return (grad,)

def back_keep(v):
    return (v, None)

def back_low(kept, grad):
    return (low(grad),)
low.defvjp(low_keep, low_pass)
low_back.defvjp(back_keep, back_low)

def rms_scale(values):
    return lax.rsqrt(lax.optimization_barrier(jnp.mean(values * values, axis=1, keepdims=True)) + EPS)

def rotate(values, cosines, sines):
    midpoint = values.shape[-1] // 2
    leading = values[..., :midpoint]
    trailing = values[..., midpoint:]
    return jnp.concatenate([leading * cosines - trailing * sines, trailing * cosines + leading * sines], axis=-1)

def rope_tables(positions, head_dim):
    exponents = jnp.arange(head_dim // 2, dtype=jnp.float32) * (2.0 / head_dim)
    frequency = jnp.power(THETA, -exponents)
    angles = positions.astype(jnp.float32)[:, None] * frequency[None, :]
    return (jnp.cos(angles)[:, None, :], jnp.sin(angles)[:, None, :])

def visibility(query_segs, up_one, up_two, query_rows, key_segs, key_rows):
    above = (key_segs[None, :] == up_one[:, None]) | (key_segs[None, :] == up_two[:, None])
    above = above & (key_segs[None, :] != query_segs[:, None])
    same = (key_segs[None, :] == query_segs[:, None]) & (key_rows[None, :] <= query_rows[:, None])
    return above | same

def tree_layer(params, hidden, places, segs, parent_ids):
    attention_gain, query_weight, query_bias, key_weight, key_bias, value_weight, value_bias, output_weight, feedforward_gain, gate_weight, up_weight, down_weight = params
    count = hidden.shape[0]
    score_scale = HD ** (-0.5)
    groups = H // KV
    normed_one = low(hidden * rms_scale(hidden) * attention_gain)
    queries = low_back(jnp.dot(normed_one, query_weight, precision=HIGH) + query_bias.reshape(-1))
    keys_raw = low_back(jnp.dot(normed_one, key_weight, precision=HIGH) + key_bias.reshape(-1))
    values = low(low_back(jnp.dot(normed_one, value_weight, precision=HIGH) + value_bias.reshape(-1)))
    cosines, sines = rope_tables(places, HD)
    query_rot = low(rotate(queries.reshape(count, H, HD), cosines, sines)).reshape(count, KV, groups, HD)
    key_rot = low(rotate(keys_raw.reshape(count, KV, HD), cosines, sines))
    values = values.reshape(count, KV, HD)
    up_one = parent_ids[segs]
    up_two = parent_ids[up_one]
    rows = jnp.arange(count, dtype=jnp.int32)
    blocks = count // TOK_DEV

    def attend(block):
        query_blk, seg_blk, one_blk, two_blk, row_blk = block
        mask = visibility(seg_blk, one_blk, two_blk, row_blk, segs, rows)
        scores = low_back(jnp.einsum('icgd,jcd->cgij', query_blk, key_rot, precision=HIGH) * score_scale)
        probs = jax.nn.softmax(jnp.where(mask, scores, NEG), axis=-1)
        return low(low_back(jnp.einsum('cgij,jcd->icgd', low(probs), values, precision=HIGH)))
    attended = lax.map(jax.checkpoint(attend), (query_rot.reshape(blocks, TOK_DEV, KV, groups, HD), segs.reshape(blocks, TOK_DEV), up_one.reshape(blocks, TOK_DEV), up_two.reshape(blocks, TOK_DEV), rows.reshape(blocks, TOK_DEV)))
    attended = attended.reshape(count, H * HD)
    middle = hidden + low_back(jnp.dot(attended, output_weight, precision=HIGH))
    normed_two = low(middle * rms_scale(middle) * feedforward_gain)
    gate = low_back(jnp.dot(normed_two, gate_weight, precision=HIGH))
    upper = low_back(jnp.dot(normed_two, up_weight, precision=HIGH))
    product = low(jax.nn.silu(gate) * upper)
    return low(middle + jnp.dot(product, down_weight, precision=HIGH))

def reference(layer_input, out_cotangent, positions, segment_ids, parent_ids, attention_gain, query_weight, query_bias, key_weight, key_bias, value_weight, value_bias, output_weight, feedforward_gain, gate_weight, up_weight, down_weight):
    params = tuple((weight.astype(jnp.float32) for weight in (attention_gain, query_weight, query_bias, key_weight, key_bias, value_weight, value_bias, output_weight, feedforward_gain, gate_weight, up_weight, down_weight)))

    def one_tree(totals, items):
        hidden, cotangent, places, segs = items
        result, pullback = jax.vjp(lambda weights, values: tree_layer(weights, values, places, segs, parent_ids), params, hidden)
        grads, hidden_grad = pullback(cotangent)
        totals = jax.tree.map(jnp.add, totals, grads)
        return (totals, (result, hidden_grad))
    zeros = jax.tree.map(jnp.zeros_like, params)
    totals, (results, hidden_grads) = lax.scan(one_tree, zeros, (layer_input.astype(jnp.float32).reshape(TREES, TREE_TOK, D), out_cotangent.astype(jnp.float32).reshape(TREES, TREE_TOK, D), positions.reshape(TREES, TREE_TOK), segment_ids.reshape(TREES, TREE_TOK)))
    return (results.reshape(TOKENS, D).astype(jnp.bfloat16), hidden_grads.reshape(TOKENS, D).astype(jnp.bfloat16), totals[0], totals[1], totals[2], totals[3], totals[4], totals[5], totals[6], totals[7], totals[8], totals[9], totals[10], totals[11])
```

```python
import jax, functools
import jax.numpy as jnp
from jax import lax
from jax.experimental import pallas as pl
from jax.experimental.pallas import tpu as pltpu
from jax.sharding import PartitionSpec as P
NEG=-1e30
QB=128; KC=512; KB=256
LOG2E=1.4426950408889634

def dot_nt(a,b): return lax.dot_general(a,b,(((1,),(1,)),((),())),preferred_element_type=jnp.float32)
def dot_nn(a,b): return lax.dot_general(a,b,(((1,),(0,)),((),())),preferred_element_type=jnp.float32)

def fwd_kernel(info, q_ref, k_ref, v_ref, o_ref, l_ref, *, heads, scale):
    blk = pl.program_id(0)
    nfull = info[blk*8]
    rows = heads*QB
    q = jnp.concatenate([q_ref[:, h*128:(h+1)*128] for h in range(heads)], axis=0)
    c2 = scale*LOG2E
    def step(carry, s, v):
        m,l,acc = carry
        mt = s[:, :128]
        for j in range(1, KC//128): mt = jnp.maximum(mt, s[:, j*128:(j+1)*128])
        mn = jnp.maximum(m, jnp.max(mt, axis=1, keepdims=True))
        p = jnp.exp2((s-mn)*c2)
        ps = p[:, :128]
        for j in range(1, KC//128): ps = ps + p[:, j*128:(j+1)*128]
        a = jnp.exp2((m-mn)*c2)
        l = l*a + ps
        acc = acc*a + dot_nn(p.astype(jnp.bfloat16), v)
        return mn,l,acc
    def body(c, carry):
        k = k_ref[pl.ds(pl.multiple_of(c*KC,KC),KC),:]
        v = v_ref[pl.ds(pl.multiple_of(c*KC,KC),KC),:]
        return step(carry, dot_nt(q,k), v)
    init = (jnp.full((rows,1),NEG,jnp.float32), jnp.zeros((rows,128),jnp.float32), jnp.zeros((rows,128),jnp.float32))
    b0 = pl.multiple_of(info[blk*8+1]*KB,KB); b1 = pl.multiple_of(info[blk*8+2]*KB,KB)
    k = jnp.concatenate([k_ref[pl.ds(b0,KB),:], k_ref[pl.ds(b1,KB),:]],axis=0)
    v = jnp.concatenate([v_ref[pl.ds(b0,KB),:], v_ref[pl.ds(b1,KB),:]],axis=0)
    s = dot_nt(q,k)
    col = lax.broadcasted_iota(jnp.int32,(QB,KC),1)
    row = lax.broadcasted_iota(jnp.int32,(QB,KC),0)
    base = jnp.where(col<KB, info[blk*8+3], info[blk*8+4]-KB)
    ok = col+base <= row
    s = jnp.concatenate([jnp.where(ok, s[h*QB:(h+1)*QB], NEG) for h in range(heads)],axis=0)
    carry = step(init, s, v)
    m,l,acc = lax.fori_loop(0,nfull,body,carry)
    lsum = jnp.sum(l,axis=1,keepdims=True)
    out = (acc/lsum).astype(jnp.bfloat16)
    o_ref[...] = jnp.concatenate([out[h*QB:(h+1)*QB] for h in range(heads)],axis=1)
    lse2 = m*c2+jnp.log2(lsum)
    t = jnp.broadcast_to(lse2,(rows,128)).T
    l_ref[...] = t[:8,:].reshape(1,8,rows)

def attn_fwd(info, q, k, v, scale):
    T=q.shape[0]; heads=q.shape[1]//128; nb=T//QB; rows=heads*QB
    return pl.pallas_call(functools.partial(fwd_kernel,heads=heads,scale=scale),
        grid_spec=pltpu.PrefetchScalarGridSpec(num_scalar_prefetch=1,grid=(nb,),
            in_specs=[pl.BlockSpec((QB,heads*128),lambda i,s:(i,0)),
                      pl.BlockSpec(k.shape,lambda i,s:(0,0)),pl.BlockSpec(v.shape,lambda i,s:(0,0))],
            out_specs=[pl.BlockSpec((QB,heads*128),lambda i,s:(i,0)),pl.BlockSpec((1,8,rows),lambda i,s:(i,0,0))]),
        out_shape=[jax.ShapeDtypeStruct((T,heads*128),jnp.bfloat16),jax.ShapeDtypeStruct((nb,8,rows),jnp.float32)],
        compiler_params=pltpu.CompilerParams(vmem_limit_bytes=56<<20),
        name="attention_forward",
        cost_estimate=pl.CostEstimate(flops=4*T*heads*128*2304,bytes_accessed=6<<20,transcendentals=T*heads*2304),
    )(info,q,k,v)

def bwd_kernel(info, q_ref, do_ref, o_ref, l_ref, k_ref, v_ref, dq_ref, dk_ref, dv_ref, *, heads, scale):
    blk = pl.program_id(0)
    @pl.when(blk==0)
    def _():
        dk_ref[...] = jnp.zeros_like(dk_ref)
        dv_ref[...] = jnp.zeros_like(dv_ref)
    nfull = info[blk*8]
    rows = heads*QB
    cat = lambda ref: jnp.concatenate([ref[:, h*128:(h+1)*128] for h in range(heads)], axis=0)
    q = cat(q_ref); do = cat(do_ref); o = cat(o_ref)
    c2 = scale*LOG2E
    delta = jnp.sum((do.astype(jnp.float32)*o.astype(jnp.float32)).T, axis=0, keepdims=True)
    lse2 = l_ref[0,0:1,:]
    def tile(k, v, ok):
        s = dot_nt(k,q)
        p = jnp.exp2(s*c2-lse2)
        if ok is not None:
            p = jnp.concatenate([jnp.where(ok, p[:, h*QB:(h+1)*QB], 0.0) for h in range(heads)],axis=1)
        dp = dot_nt(v,do)
        ds = (p*(dp-delta)).astype(jnp.bfloat16)
        dv = dot_nn(p.astype(jnp.bfloat16), do)
        dk = dot_nn(ds, q)
        dq = lax.dot_general(ds,k,(((0,),(0,)),((),())),preferred_element_type=jnp.float32)
        return dq,dk,dv
    def body(c, acc):
        at = pl.ds(pl.multiple_of(c*KC,KC),KC)
        dq,dk,dv = tile(k_ref[at,:], v_ref[at,:], None)
        dk_ref[at,:] += dk
        dv_ref[at,:] += dv
        return acc+dq
    b0 = pl.multiple_of(info[blk*8+1]*KB,KB); b1 = pl.multiple_of(info[blk*8+2]*KB,KB)
    k = jnp.concatenate([k_ref[pl.ds(b0,KB),:], k_ref[pl.ds(b1,KB),:]],axis=0)
    v = jnp.concatenate([v_ref[pl.ds(b0,KB),:], v_ref[pl.ds(b1,KB),:]],axis=0)
    col = lax.broadcasted_iota(jnp.int32,(KC,QB),0)
    row = lax.broadcasted_iota(jnp.int32,(KC,QB),1)
    base = jnp.where(col<KB, info[blk*8+3], info[blk*8+4]-KB)
    dq,dk,dv = tile(k,v,col+base<=row)
    dk_ref[pl.ds(b0,KB),:] += dk[:KB]
    dv_ref[pl.ds(b0,KB),:] += dv[:KB]
    dk_ref[pl.ds(b1,KB),:] += dk[KB:]
    dv_ref[pl.ds(b1,KB),:] += dv[KB:]
    dq = lax.fori_loop(0,nfull,body,dq)
    dq = dq*scale
    dq_ref[...] = jnp.concatenate([dq[h*QB:(h+1)*QB] for h in range(heads)],axis=1)

def attn_bwd(info,q,do,o,lse,k,v,scale):
    T=q.shape[0]; heads=q.shape[1]//128; nb=T//QB; rows=heads*QB
    qspec=pl.BlockSpec((QB,heads*128),lambda i,s:(i,0))
    full=pl.BlockSpec(k.shape,lambda i,s:(0,0))
    return pl.pallas_call(functools.partial(bwd_kernel,heads=heads,scale=scale),
        grid_spec=pltpu.PrefetchScalarGridSpec(num_scalar_prefetch=1,grid=(nb,),
            in_specs=[qspec,qspec,qspec,pl.BlockSpec((1,8,rows),lambda i,s:(i,0,0)),full,full],
            out_specs=[qspec,full,full]),
        out_shape=[jax.ShapeDtypeStruct((T,heads*128),jnp.float32),jax.ShapeDtypeStruct(k.shape,jnp.float32),jax.ShapeDtypeStruct(v.shape,jnp.float32)],
        compiler_params=pltpu.CompilerParams(vmem_limit_bytes=56<<20),
        name="attention_backward",
        cost_estimate=pl.CostEstimate(flops=10*T*heads*128*2304,bytes_accessed=12<<20,transcendentals=T*heads*2304),
    )(info,q,do,o,lse,k,v)
EPS = 1e-06
THETA = 10000.0
TREE_TOK = 5120
TRUNK = 2048
PLANE = 4


def swap(block, axis, count, bits):
    return lax.ppermute(block, axis, [(i, i ^ bits) for i in range(count)])


def rms_scale(values):
    return lax.rsqrt(jnp.mean(values * values, axis=1, keepdims=True) + EPS)


def norm_back(grad, values, gain):
    scale = rms_scale(values)
    z = values * scale
    w = grad * gain
    gain_grad = jnp.sum(grad * z, axis=0)
    return scale * (w - z * jnp.mean(w * z, axis=1, keepdims=True)), gain_grad


def turn(values, cosines, sines):
    swapped = jnp.concatenate([values[..., 64:], values[..., :64]], axis=-1)
    return values * cosines + swapped * sines


def rope_tables(positions):
    exponents = jnp.arange(64, dtype=jnp.float32) * (2.0 / 128)
    frequency = jnp.power(THETA, -exponents)
    angles = positions.astype(jnp.float32)[:, None] * frequency[None, :]
    cosines, sines = jnp.cos(angles), jnp.sin(angles)
    return (
        jnp.concatenate([cosines, cosines], axis=1)[:, None, :],
        jnp.concatenate([-sines, sines], axis=1)[:, None, :],
    )


def contract_rows(left, right):
    return lax.dot_general(
        left, right, (((0,), (0,)), ((), ())), preferred_element_type=jnp.float32
    )


def contract_cols(left, right):
    return lax.dot_general(
        left, right, (((1,), (1,)), ((), ())), preferred_element_type=jnp.float32
    )


def matmul(left, right):
    return jnp.dot(left, right, preferred_element_type=jnp.float32)


def attention_plan(segment_ids, parent_ids, dp_index, local_tok):
    members = TREE_TOK // local_tok
    first = dp_index // members * TREE_TOK
    slots = lax.dynamic_slice_in_dim(segment_ids, first, TREE_TOK)[::KB]
    numbers = jnp.arange(parent_ids.shape[0], dtype=jnp.int32)
    parents = jnp.sum(jnp.where(slots[:, None] == numbers[None, :], parent_ids[None, :], 0), axis=1)
    places = jnp.arange(slots.shape[0], dtype=jnp.int32)
    holder = jnp.sum(jnp.where(parents[:, None] == slots[None, :], places[None, :], 0), axis=1)
    starts = dp_index % members * local_tok + QB * jnp.arange(local_tok // QB, dtype=jnp.int32)
    slot = starts // KB
    chosen = slot[:, None] == places[None, :]
    pick = lambda table: jnp.sum(jnp.where(chosen, table[None, :], 0), axis=1)
    in_trunk = starts < TRUNK
    is_leaf = pick(parents) != slots[0]
    chunk = jnp.minimum(starts, TRUNK) // KC
    far = jnp.int32(1 << 20)
    block0 = jnp.where(in_trunk, 2 * chunk, jnp.where(is_leaf, pick(holder), TRUNK // KB))
    block1 = jnp.where(in_trunk, 2 * chunk + 1, slot)
    shift0 = jnp.where(in_trunk, block0 * KB - starts, jnp.where(is_leaf, -far, far))
    shift1 = block1 * KB - starts
    zero = jnp.zeros_like(chunk)
    return jnp.stack([chunk, block0, block1, shift0, shift1, zero, zero, zero], axis=1).reshape(-1)


def on_device(
    dp_size,
    layer_input,
    out_cotangent,
    positions,
    segment_ids,
    parent_ids,
    attention_gain,
    query_weight,
    query_bias,
    key_weight,
    key_bias,
    value_weight,
    value_bias,
    output_weight,
    feedforward_gain,
    gate_weight,
    up_weight,
    down_weight,
):
    bf16, f32 = jnp.bfloat16, jnp.float32
    local_tok = positions.shape[0]
    half_tok = layer_input.shape[0]
    width = layer_input.shape[1]
    shard = attention_gain.shape[0]
    heads, head_dim = query_bias.shape[0], 128
    q_width = heads * head_dim
    hidden = gate_weight.shape[1]
    block = -(-hidden // (PLANE * 128)) * 128
    lines = dp_size // PLANE
    members = TREE_TOK // local_tok
    dp_index = lax.axis_index("dp")
    core = lax.axis_index("tensor")
    plane_at = dp_index % PLANE
    member = dp_index % members
    z_at = dp_index // PLANE
    scale = head_dim ** (-0.5)
    line_groups = [[j + PLANE * z for z in range(lines)] for j in range(PLANE)]

    def by_core(mine):
        other = swap(mine, "tensor", 2, 1)
        first = jnp.where(core == 0, mine, other)
        second = jnp.where(core == 0, other, mine)
        return jnp.concatenate([first, second], axis=0)

    def to_tokens(values):
        halves = values.reshape(2, half_tok, width)
        mine = lax.dynamic_index_in_dim(halves, core, 0, keepdims=False)
        theirs = lax.dynamic_index_in_dim(halves, 1 - core, 0, keepdims=False)
        return mine + swap(theirs.astype(bf16), "tensor", 2, 1).astype(f32)

    extra = jnp.zeros((shard, 128), bf16)
    extra = extra.at[:, 0].set(attention_gain).at[:, 1].set(feedforward_gain)
    biases = jnp.concatenate([query_bias.reshape(-1), key_bias.reshape(-1), value_bias.reshape(-1)])
    per = biases.shape[0]
    pad_to = -(-per // shard)
    biases = jnp.pad(biases, (0, pad_to * shard - per)).reshape(pad_to, shard)
    extra = extra.at[:, 2 : 2 + pad_to].set(biases.T)
    first_stack = jnp.concatenate([query_weight, key_weight, value_weight, extra], axis=1)
    first_all = lax.all_gather(first_stack, "dp", axis=0, tiled=True)
    out_t = lax.all_gather(output_weight.T, "dp", axis=0, tiled=True)

    def spread(weight):
        padded = jnp.pad(weight, ((0, 0), (0, PLANE * block - hidden)))
        result = jnp.zeros((PLANE * shard, block), bf16)
        for bits in range(PLANE):
            there = plane_at ^ bits
            piece = lax.dynamic_slice_in_dim(padded, there * block, block, axis=1)
            if bits:
                piece = swap(piece, "dp", dp_size, bits)
            result = lax.dynamic_update_slice_in_dim(result, piece, there * shard, axis=0)
        return lax.all_gather(result, "dp", axis=0, tiled=True, axis_index_groups=line_groups)

    gate_mat = spread(gate_weight)
    up_mat = spread(up_weight)
    down_t = spread(down_weight.T)

    input_wide = layer_input.astype(f32)
    input_all = by_core(layer_input).astype(f32)
    z_all = input_all * rms_scale(input_all)
    gain_one = first_all[:, q_width + 256].astype(f32)
    gain_two = first_all[:, q_width + 257].astype(f32)
    bias_all = first_all[:, q_width + 258 : q_width + 258 + pad_to].astype(f32)
    bias_all = bias_all.reshape(dp_size, shard, pad_to).transpose(0, 2, 1).reshape(dp_size, -1)
    per_head = query_bias.shape[1]
    bias_all = bias_all[:, :per].reshape(dp_size, heads + 2, per_head)
    bias_all = bias_all.transpose(1, 0, 2).reshape((heads + 2) * head_dim)
    normed = (z_all * gain_one).astype(bf16)
    qkv = matmul(normed, first_all[:, : q_width + 256]) + bias_all
    cosines, sines = rope_tables(positions)
    q_rot = turn(qkv[:, :q_width].reshape(local_tok, heads, head_dim), cosines, sines)
    q_rot = q_rot.astype(bf16).reshape(local_tok, q_width)
    k_rot = turn(qkv[:, None, q_width : q_width + 128], cosines, sines).astype(bf16)[:, 0]
    pair = jnp.concatenate([k_rot, qkv[:, q_width + 128 :].astype(bf16)], axis=1)
    tree = jnp.zeros((TREE_TOK, 256), bf16)
    for bits in range(members):
        piece = swap(pair, "dp", dp_size, bits) if bits else pair
        tree = lax.dynamic_update_slice_in_dim(tree, piece, (member ^ bits) * local_tok, axis=0)
    k_tree, v_tree = tree[:, :128], tree[:, 128:]
    plan = attention_plan(segment_ids, parent_ids, dp_index, local_tok)
    attended, lse = attn_fwd(plan, q_rot, k_tree, v_tree, scale)
    middle = input_wide + to_tokens(contract_cols(attended, out_t))
    normed_two = (middle * rms_scale(middle) * gain_two).astype(bf16)

    def to_plane(mine):
        parts = [mine] + [swap(mine, "dp", dp_size, bits) for bits in range(1, PLANE)]
        parts = jnp.concatenate(parts, axis=0)
        return jnp.concatenate([parts, swap(parts, "tensor", 2, 1)], axis=0)

    def from_plane(partial):
        both = partial.astype(bf16).reshape(2, PLANE * half_tok, width)
        sums = both[0].astype(f32) + swap(both[1], "tensor", 2, 1).astype(f32)
        sums = sums.reshape(PLANE, half_tok, width)
        total = sums[0]
        for bits in range(1, PLANE):
            total = total + swap(sums[bits].astype(bf16), "dp", dp_size, bits).astype(f32)
        return total

    cot = to_plane(out_cotangent)
    x = to_plane(normed_two)
    gate = matmul(x, gate_mat)
    up = matmul(x, up_mat)
    product_grad = matmul(cot, down_t)
    sig = jax.nn.sigmoid(gate)
    silu = gate * sig
    product = (silu * up).astype(bf16)
    gate_grad = (product_grad * up * sig * (1 + gate * (1 - sig))).astype(bf16)
    up_grad = (product_grad * silu).astype(bf16)
    normed_two_grad = from_plane(contract_cols(gate_grad, gate_mat) + contract_cols(up_grad, up_mat))

    def collect(grad):
        rows = PLANE * shard
        if lines == 4:
            chunks = grad.astype(bf16)
            take = lambda d: lax.dynamic_slice_in_dim(chunks, jnp.clip(d, 0, lines - 1) * rows, rows)
            total = take(z_at).astype(f32)
            for sign in (1, -1):
                carried = None
                for step in range(lines - 1):
                    place = z_at if sign == 1 else lines - 1 - z_at
                    target = lines - 1 - step + place
                    send = take(target if sign == 1 else lines - 1 - target).astype(f32)
                    if carried is not None:
                        send = send + jnp.where(place > 0, carried.astype(f32), 0)
                    route = []
                    for z in range(step + 1):
                        for j in range(PLANE):
                            a = z if sign == 1 else lines - 1 - z
                            route.append((a * PLANE + j, (a + sign) * PLANE + j))
                    carried = lax.ppermute(send.astype(bf16), "dp", route)
                total = total + jnp.where(place > 0, carried.astype(f32), 0)
        else:
            total = lax.psum_scatter(
                grad.astype(bf16), "dp", scatter_dimension=0, tiled=True, axis_index_groups=line_groups
            )
        total = total.astype(bf16)
        result = jnp.zeros((shard, PLANE * block), bf16)
        for bits in range(PLANE):
            there = plane_at ^ bits
            piece = lax.dynamic_slice_in_dim(total, there * shard, shard, axis=0)
            if bits:
                piece = swap(piece, "dp", dp_size, bits)
            result = lax.dynamic_update_slice_in_dim(result, piece, there * block, axis=1)
        return result[:, :hidden].astype(f32)

    gate_out = collect(contract_rows(x, gate_grad))
    up_out = collect(contract_rows(x, up_grad))
    down_out = collect(contract_rows(cot, product)).T
    layer_output = (middle + from_plane(contract_cols(product, down_t))).astype(bf16)

    norm_grad, gain_two_grad = norm_back(normed_two_grad, middle, gain_two)
    middle_grad = out_cotangent.astype(f32) + norm_grad

    branch_grad = by_core(middle_grad.astype(bf16))
    out_grad = contract_rows(branch_grad, attended)
    gain_column = jnp.pad(gain_two_grad[:, None], ((0, 0), (0, 127)))
    out_sum = lax.psum_scatter(
        jnp.concatenate([out_grad, gain_column], axis=1).astype(bf16), "dp", scatter_dimension=0, tiled=True
    )
    attended_grad = matmul(branch_grad, out_t).astype(bf16)
    dq, dk, dv = attn_bwd(plan, q_rot, attended_grad, attended, lse, k_tree, v_tree, scale)
    pair_grads = jnp.concatenate([dk, dv], axis=1)
    total = lax.dynamic_slice_in_dim(pair_grads, member * local_tok, local_tok)
    for bits in range(1, members):
        piece = lax.dynamic_slice_in_dim(pair_grads, (member ^ bits) * local_tok, local_tok)
        total = total + swap(piece.astype(bf16), "dp", dp_size, bits).astype(f32)
    q_grad = turn(dq.reshape(local_tok, heads, head_dim), cosines, -sines).astype(bf16)
    q_grad = q_grad.reshape(local_tok, q_width)
    k_grad = turn((total[:, :128] * scale)[:, None], cosines, -sines).astype(bf16)[:, 0]
    grads = jnp.concatenate([q_grad, k_grad, total[:, 128:].astype(bf16)], axis=1)
    first_grad = contract_rows(normed, grads)
    bias_grad = jnp.sum(grads.astype(f32), axis=0)
    normed_grad = to_tokens(contract_cols(grads, first_all[:, : q_width + 256]))
    input_norm_grad, gain_one_grad = norm_back(normed_grad, input_wide, gain_one)
    input_grad = (middle_grad + input_norm_grad).astype(bf16)
    bias_grad = bias_grad.reshape(heads + 2, dp_size, per_head).transpose(1, 0, 2).reshape(dp_size, per)
    bias_grad = jnp.pad(bias_grad, ((0, 0), (0, pad_to * shard - per)))
    bias_grad = bias_grad.reshape(dp_size, pad_to, shard).transpose(0, 2, 1).reshape(width, pad_to)
    tail = jnp.concatenate([gain_one_grad[:, None], bias_grad], axis=1)
    tail = jnp.pad(tail, ((0, 0), (0, 127 - pad_to)))
    first_sum = lax.psum_scatter(
        jnp.concatenate([first_grad, tail], axis=1).astype(bf16), "dp", scatter_dimension=0, tiled=True
    ).astype(f32)
    out_sum = out_sum.astype(f32)
    gains = jnp.stack([first_sum[:, q_width + 256], out_sum[:, q_width]])
    gains = gains + swap(gains, "tensor", 2, 1)
    bias_sum = first_sum[:, q_width + 257 : q_width + 257 + pad_to].T.reshape(-1)[:per]
    return (
        layer_output,
        input_grad,
        gains[0],
        first_sum[:, :q_width],
        bias_sum[: heads * per_head].reshape(heads, per_head),
        first_sum[:, q_width : q_width + 128],
        bias_sum[heads * per_head : (heads + 1) * per_head].reshape(1, per_head),
        first_sum[:, q_width + 128 : q_width + 256],
        bias_sum[(heads + 1) * per_head :].reshape(1, per_head),
        out_sum[:, :q_width].T,
        gains[1],
        gate_out,
        up_out,
        down_out,
    )


def solution(mesh):
    placed = (
        P(("dp", "tensor"), None),
        P(("dp", "tensor"), None),
        P("dp"),
        P(),
        P(),
        P("dp"),
        P("dp", "tensor"),
        P("tensor", "dp"),
        P("dp", "tensor"),
        P("tensor", "dp"),
        P("dp", "tensor"),
        P("tensor", "dp"),
        P("tensor", "dp"),
        P("dp"),
        P("dp", "tensor"),
        P("dp", "tensor"),
        P("tensor", "dp"),
    )
    return jax.shard_map(
        functools.partial(on_device, mesh.shape["dp"]),
        mesh=mesh,
        in_specs=placed,
        out_specs=(
            P(("dp", "tensor"), None),
            P(("dp", "tensor"), None),
            P("dp"),
            P("dp", "tensor"),
            P("tensor", "dp"),
            P("dp", "tensor"),
            P("tensor", "dp"),
            P("dp", "tensor"),
            P("tensor", "dp"),
            P("tensor", "dp"),
            P("dp"),
            P("dp", "tensor"),
            P("dp", "tensor"),
            P("tensor", "dp"),
        ),
        check_vma=False,
    )
```

```python
import functools

import jax
import jax.numpy as jnp
from jax import lax
from jax.experimental import pallas as pl
from jax.experimental.pallas import tpu as pltpu
from jax.sharding import PartitionSpec as P

EPS = 1e-06
THETA = 10000.0
TREE_TOK = 5120
TRUNK = 2048
PLANE = 4
NEG = -1e30
QB=128; KC=512; KB=256
LOG2E=1.4426950408889634

MESH = pl.DeviceIdType.MESH


def dot_nt(a,b): return lax.dot_general(a,b,(((1,),(1,)),((),())),preferred_element_type=jnp.float32)
def dot_nn(a,b): return lax.dot_general(a,b,(((1,),(0,)),((),())),preferred_element_type=jnp.float32)

def fwd_kernel(info, q_ref, t_ref, o_ref, l_ref, *, heads, scale):
    blk = pl.program_id(0)
    nfull = info[blk*8]
    rows = heads*QB
    q = jnp.concatenate([q_ref[:, h*128:(h+1)*128] for h in range(heads)], axis=0)
    c2 = scale*LOG2E
    def step(carry, s, v):
        m,l,acc = carry
        mt = s[:, :128]
        for j in range(1, KC//128): mt = jnp.maximum(mt, s[:, j*128:(j+1)*128])
        mn = jnp.maximum(m, jnp.max(mt, axis=1, keepdims=True))
        p = jnp.exp2((s-mn)*c2)
        ps = p[:, :128]
        for j in range(1, KC//128): ps = ps + p[:, j*128:(j+1)*128]
        a = jnp.exp2((m-mn)*c2)
        l = l*a + ps
        acc = acc*a + dot_nn(p.astype(jnp.bfloat16), v)
        return mn,l,acc
    def body(c, carry):
        k = t_ref[pl.ds(pl.multiple_of(c*KC,KC),KC),0:128]
        v = t_ref[pl.ds(pl.multiple_of(c*KC,KC),KC),128:256]
        return step(carry, dot_nt(q,k), v)
    init = (jnp.full((rows,1),NEG,jnp.float32), jnp.zeros((rows,128),jnp.float32), jnp.zeros((rows,128),jnp.float32))
    b0 = pl.multiple_of(info[blk*8+1]*KB,KB); b1 = pl.multiple_of(info[blk*8+2]*KB,KB)
    k = jnp.concatenate([t_ref[pl.ds(b0,KB),0:128], t_ref[pl.ds(b1,KB),0:128]],axis=0)
    v = jnp.concatenate([t_ref[pl.ds(b0,KB),128:256], t_ref[pl.ds(b1,KB),128:256]],axis=0)
    s = dot_nt(q,k)
    col = lax.broadcasted_iota(jnp.int32,(QB,KC),1)
    row = lax.broadcasted_iota(jnp.int32,(QB,KC),0)
    base = jnp.where(col<KB, info[blk*8+3], info[blk*8+4]-KB)
    ok = col+base <= row
    s = jnp.concatenate([jnp.where(ok, s[h*QB:(h+1)*QB], NEG) for h in range(heads)],axis=0)
    carry = step(init, s, v)
    m,l,acc = lax.fori_loop(0,nfull,body,carry)
    lsum = jnp.sum(l,axis=1,keepdims=True)
    out = (acc/lsum).astype(jnp.bfloat16)
    o_ref[...] = jnp.concatenate([out[h*QB:(h+1)*QB] for h in range(heads)],axis=1)
    lse2 = m*c2+jnp.log2(lsum)
    t = jnp.broadcast_to(lse2,(rows,128)).T
    l_ref[...] = t[:8,:].reshape(1,8,rows)

def attn_fwd(info, q, tree, scale):
    T=q.shape[0]; heads=q.shape[1]//128; nb=T//QB; rows=heads*QB
    return pl.pallas_call(functools.partial(fwd_kernel,heads=heads,scale=scale),
        grid_spec=pltpu.PrefetchScalarGridSpec(num_scalar_prefetch=1,grid=(nb,),
            in_specs=[pl.BlockSpec((QB,heads*128),lambda i,s:(i,0)),
                      pl.BlockSpec(tree.shape,lambda i,s:(0,0))],
            out_specs=[pl.BlockSpec((QB,heads*128),lambda i,s:(i,0)),pl.BlockSpec((1,8,rows),lambda i,s:(i,0,0))]),
        out_shape=[jax.ShapeDtypeStruct((T,heads*128),jnp.bfloat16),jax.ShapeDtypeStruct((nb,8,rows),jnp.float32)],
        compiler_params=pltpu.CompilerParams(vmem_limit_bytes=56<<20),
        name="attention_forward",
        cost_estimate=pl.CostEstimate(flops=4*T*heads*128*2304,bytes_accessed=6<<20,transcendentals=T*heads*2304),
    )(info,q,tree)

def bwd_kernel(info, q_ref, do_ref, o_ref, l_ref, t_ref, dq_ref, dt_ref, sum_ref, *, heads, scale):
    blk = pl.program_id(0)
    @pl.when(blk==0)
    def _():
        sum_ref[...] = jnp.zeros_like(sum_ref)
    nfull = info[blk*8]
    rows = heads*QB
    cat = lambda ref: jnp.concatenate([ref[:, h*128:(h+1)*128] for h in range(heads)], axis=0)
    q = cat(q_ref); do = cat(do_ref); o = cat(o_ref)
    c2 = scale*LOG2E
    delta = jnp.sum((do.astype(jnp.float32)*o.astype(jnp.float32)).T, axis=0, keepdims=True)
    lse2 = l_ref[0,0:1,:]
    def tile(k, v, ok):
        s = dot_nt(k,q)
        p = jnp.exp2(s*c2-lse2)
        if ok is not None:
            p = jnp.concatenate([jnp.where(ok, p[:, h*QB:(h+1)*QB], 0.0) for h in range(heads)],axis=1)
        dp = dot_nt(v,do)
        ds = (p*(dp-delta)).astype(jnp.bfloat16)
        dv = dot_nn(p.astype(jnp.bfloat16), do)
        dk = dot_nn(ds, q)
        dq = lax.dot_general(ds,k,(((0,),(0,)),((),())),preferred_element_type=jnp.float32)
        return dq,dk,dv
    def body(c, acc):
        at = pl.ds(pl.multiple_of(c*KC,KC),KC)
        dq,dk,dv = tile(t_ref[at,0:128], t_ref[at,128:256], None)
        sum_ref[at,0:128] += dk
        sum_ref[at,128:256] += dv
        return acc+dq
    b0 = pl.multiple_of(info[blk*8+1]*KB,KB); b1 = pl.multiple_of(info[blk*8+2]*KB,KB)
    k = jnp.concatenate([t_ref[pl.ds(b0,KB),0:128], t_ref[pl.ds(b1,KB),0:128]],axis=0)
    v = jnp.concatenate([t_ref[pl.ds(b0,KB),128:256], t_ref[pl.ds(b1,KB),128:256]],axis=0)
    col = lax.broadcasted_iota(jnp.int32,(KC,QB),0)
    row = lax.broadcasted_iota(jnp.int32,(KC,QB),1)
    base = jnp.where(col<KB, info[blk*8+3], info[blk*8+4]-KB)
    dq,dk,dv = tile(k,v,col+base<=row)
    sum_ref[pl.ds(b0,KB),0:128] += dk[:KB]
    sum_ref[pl.ds(b0,KB),128:256] += dv[:KB]
    sum_ref[pl.ds(b1,KB),0:128] += dk[KB:]
    sum_ref[pl.ds(b1,KB),128:256] += dv[KB:]
    dq = lax.fori_loop(0,nfull,body,dq)
    dq = dq*scale
    dq_ref[...] = jnp.concatenate([dq[h*QB:(h+1)*QB] for h in range(heads)],axis=1)

    @pl.when(blk == pl.num_programs(0) - 1)
    def _():
        dt_ref[...] = sum_ref[...].astype(jnp.bfloat16)


def attn_bwd(info,q,do,o,lse,tree,scale):
    T=q.shape[0]; heads=q.shape[1]//128; nb=T//QB; rows=heads*QB
    qspec=pl.BlockSpec((QB,heads*128),lambda i,s:(i,0))
    full=pl.BlockSpec(tree.shape,lambda i,s:(0,0))
    return pl.pallas_call(functools.partial(bwd_kernel,heads=heads,scale=scale),
        grid_spec=pltpu.PrefetchScalarGridSpec(num_scalar_prefetch=1,grid=(nb,),
            in_specs=[qspec,qspec,qspec,pl.BlockSpec((1,8,rows),lambda i,s:(i,0,0)),full],
            out_specs=[qspec,full],
            scratch_shapes=[pltpu.VMEM(tree.shape,jnp.float32)]),
        out_shape=[jax.ShapeDtypeStruct((T,heads*128),jnp.float32),jax.ShapeDtypeStruct(tree.shape,jnp.bfloat16)],
        compiler_params=pltpu.CompilerParams(vmem_limit_bytes=56<<20),
        name="attention_backward",
        cost_estimate=pl.CostEstimate(flops=10*T*heads*128*2304,bytes_accessed=12<<20,transcendentals=T*heads*2304),
    )(info,q,do,o,lse,tree)


def plane_partner(dp, bits):
    one = dp + 1 - 2 * lax.rem(dp, 2)
    if bits == 1:
        return one
    two = 2 - 4 * lax.rem(dp // 2, 2)
    return (dp if bits == 2 else one) + two


def line_partner(dp):
    return dp + PLANE - 2 * PLANE * lax.rem(dp // PLANE, 2)


def greet(dp, core, lines):
    z_at = dp // PLANE
    barrier = pltpu.get_barrier_semaphore()
    for bits in range(1, PLANE):
        pl.semaphore_signal(barrier, inc=1, device_id={"dp": plane_partner(dp, bits)}, device_id_type=MESH)
    pl.semaphore_signal(barrier, inc=1, device_id={"tensor": 1 - core}, device_id_type=MESH)

    @pl.when(z_at > 0)
    def _():
        pl.semaphore_signal(barrier, inc=1, device_id={"dp": dp - PLANE}, device_id_type=MESH)

    @pl.when(z_at < lines - 1)
    def _():
        pl.semaphore_signal(barrier, inc=1, device_id={"dp": dp + PLANE}, device_id_type=MESH)

    beside = jnp.minimum(z_at, 1) + jnp.minimum(lines - 1 - z_at, 1)
    pl.semaphore_wait(barrier, PLANE + beside)


class Gather:
    def __init__(self, own, whole, sems, dp, lines):
        self.own, self.whole, self.dp, self.lines = own, whole, dp, lines
        self.z_at = dp // PLANE
        self.local_sem, self.line_send, self.line_recv, self.plane_send, self.plane_recv = sems
        self.rows_per = own.shape[0]

    def rows(self, owner):
        return pl.ds(pl.multiple_of(owner * self.rows_per, self.rows_per), self.rows_per)

    def local(self):
        return pltpu.make_async_copy(self.own, self.whole.at[self.rows(self.dp)], self.local_sem)

    def place(self, sign):
        return self.z_at if sign == 1 else self.lines - 1 - self.z_at

    def line_copy(self, sign, step):
        owner = self.dp - sign * step * PLANE
        way = (1 - sign) // 2
        return pltpu.make_async_remote_copy(
            src_ref=self.own if step == 0 else self.whole.at[self.rows(owner)],
            dst_ref=self.whole.at[self.rows(owner)],
            send_sem=self.line_send.at[way, step], recv_sem=self.line_recv.at[way, step],
            device_id={"dp": self.dp + sign * PLANE}, device_id_type=MESH)

    def line_start(self, sign, step):
        place = self.place(sign)

        @pl.when((place >= step) & (place < self.lines - 1))
        def _():
            self.line_copy(sign, step).start()

    def line_wait_send(self, sign, step):
        place = self.place(sign)

        @pl.when((place >= step) & (place < self.lines - 1))
        def _():
            self.line_copy(sign, step).wait_send()

    def plane_copy(self, bits, owner, own=False):
        z = owner // PLANE
        return pltpu.make_async_remote_copy(
            src_ref=self.own if own else self.whole.at[self.rows(owner)],
            dst_ref=self.whole.at[self.rows(owner)],
            send_sem=self.plane_send.at[bits - 1, z], recv_sem=self.plane_recv.at[bits - 1, z],
            device_id={"dp": plane_partner(self.dp, bits)}, device_id_type=MESH)

    def plane_start_own(self):
        for bits in range(1, PLANE):
            self.plane_copy(bits, self.dp, True).start()

    def arrived(self, sign, step):
        place = self.place(sign)

        @pl.when(place >= step + 1)
        def _():
            owner = self.dp - sign * (step + 1) * PLANE
            pltpu.make_async_remote_copy(
                src_ref=self.own, dst_ref=self.whole.at[self.rows(owner)],
                send_sem=self.line_send.at[(1 - sign) // 2, step],
                recv_sem=self.line_recv.at[(1 - sign) // 2, step],
                device_id={"dp": self.dp - sign * PLANE}, device_id_type=MESH).wait_recv()
            if step + 1 < self.lines - 1:

                @pl.when(place < self.lines - 1)
                def _():
                    self.line_copy(sign, step + 1).start()

            for bits in range(1, PLANE):
                self.plane_copy(bits, owner).start()

    def plane_wait_recv(self):
        for bits in range(1, PLANE):
            for z in range(self.lines):
                owner = z * PLANE + lax.rem(plane_partner(self.dp, bits), PLANE)
                self.plane_copy(bits, owner).wait_recv()

    def finish(self):
        for sign in (1, -1):
            for step in range(self.lines - 1):
                self.line_wait_send(sign, step)
        for bits in range(1, PLANE):
            for z in range(self.lines):
                self.plane_copy(bits, z * PLANE + lax.rem(self.dp, PLANE)).wait_send()


def front_kernel(*refs, lines, members, steps):
    (
        ff_in, first_in, out_in, extra_in, x_in, cos_in, sin_in,
        own_out, *slab_outs,
    ) = refs[: 8 + 2 * steps]
    (
        first_out, out_t, q_out, tree_out, normed_out, rows_out,
        first_all, extra_all, x_all, normed, pair,
        first_local, first_ls, first_lr, first_ps, first_pr,
        extra_local, extra_ls, extra_lr, extra_ps, extra_pr,
        out_local, out_ls, out_lr, out_ps, out_pr,
        spread_local, spread_send, spread_recv, hop_send, hop_recv,
        x_local, x_send, x_recv, keep_sem, pair_local, pair_send, pair_recv,
    ) = refs[8 + 2 * steps :]
    bf16, f32 = jnp.bfloat16, jnp.float32
    dp = lax.axis_index("dp")
    core = lax.axis_index("tensor")
    z_at = dp // PLANE
    j_at = lax.rem(dp, PLANE)
    half, width = x_in.shape
    shard = first_in.shape[0]
    local_tok = 2 * half
    slab_rows = PLANE * shard
    ups, downs = slab_outs[:steps], slab_outs[steps:]
    mate = {"tensor": 1 - core}

    first = Gather(first_in, first_all, (first_local, first_ls, first_lr, first_ps, first_pr), dp, lines)
    extra = Gather(extra_in, extra_all, (extra_local, extra_ls, extra_lr, extra_ps, extra_pr), dp, lines)
    outer = Gather(out_in, out_t, (out_local, out_ls, out_lr, out_ps, out_pr), dp, lines)

    token_rows = lambda c: pl.ds(pl.multiple_of(c * half, half), half)
    x_keep = pltpu.make_async_copy(x_in, x_all.at[token_rows(core)], x_local)
    x_copy = pltpu.make_async_remote_copy(
        src_ref=x_in, dst_ref=x_all.at[token_rows(core)], send_sem=x_send, recv_sem=x_recv,
        device_id=mate, device_id_type=MESH)
    shard_rows = lambda j: pl.ds(pl.multiple_of(j * shard, shard), shard)

    def spread(which, bits):
        there = lax.rem(plane_partner(dp, bits), PLANE)
        return pltpu.make_async_remote_copy(
            src_ref=ff_in.at[which, there], dst_ref=own_out.at[which, shard_rows(j_at)],
            send_sem=spread_send.at[which, bits - 1], recv_sem=spread_recv.at[which, bits - 1],
            device_id={"dp": plane_partner(dp, bits)}, device_id_type=MESH)

    def spread_keep(which):
        return pltpu.make_async_copy(ff_in.at[which, j_at], own_out.at[which, shard_rows(j_at)], spread_local.at[which])

    def hop(which, sign, step):
        way = (1 - sign) // 2
        outs = ups if sign == 1 else downs
        return pltpu.make_async_remote_copy(
            src_ref=(own_out if step == 0 else outs[step - 1]).at[which], dst_ref=outs[step].at[which],
            send_sem=hop_send.at[which, way, step], recv_sem=hop_recv.at[which, way, step],
            device_id={"dp": dp + sign * PLANE}, device_id_type=MESH)

    for one in (first, extra, outer):
        one.local().start()
    x_keep.start()
    for which in range(3):
        spread_keep(which).start()
    greet(dp, core, lines)
    x_copy.start()
    for sign in (1, -1):
        first.line_start(sign, 0)
        extra.line_start(sign, 0)
    for bits in range(1, PLANE):
        spread(2, bits).start()
    first.plane_start_own()
    extra.plane_start_own()
    for which in (0, 1):
        for bits in range(1, PLANE):
            spread(which, bits).start()

    x_keep.wait()
    x_copy.wait_recv()
    wide = x_all[...].astype(f32)
    scale = lax.rsqrt(jnp.mean(wide * wide, axis=1, keepdims=True) + EPS)

    def hop_start(which):
        spread_keep(which).wait()
        for bits in range(1, PLANE):
            spread(which, bits).wait_recv()
        for sign in (1, -1):
            place = z_at if sign == 1 else lines - 1 - z_at

            @pl.when(place < lines - 1)
            def _():
                hop(which, sign, 0).start()

    for step in range(lines - 1):
        for sign in (1, -1):
            first.arrived(sign, step)
            extra.arrived(sign, step)
        if step == 0:
            hop_start(2)
    hop_start(0)
    hop_start(1)
    first.local().wait()
    extra.local().wait()
    for sign in (1, -1):
        outer.line_start(sign, 0)
    outer.plane_start_own()
    extra.plane_wait_recv()
    first.plane_wait_recv()
    keep = pltpu.make_async_copy(first_all, first_out, keep_sem)
    keep.start()
    small = extra_all[0:16, :].astype(f32)
    for owner in range(1, lines * PLANE):
        small = small + extra_all[16 * owner : 16 * (owner + 1), :].astype(f32)
    rows_out[...] = small
    normed[...] = (x_all[...].astype(f32) * scale * small[0:1, :]).astype(bf16)
    normed_out[...] = normed[...]
    columns = first_all.shape[1]
    q_width = columns - 256
    cosines, sines = cos_in[...], sin_in[...]

    def project(at, count):
        part = dot_nn(normed[...], first_all[:, at : at + count])
        return part + small[2:3, at : at + count]

    def turned(part):
        return (part * cosines + pltpu.roll(part, 64, 1) * sines).astype(bf16)

    both = project(q_width, 256)
    pair[:, 0:128] = turned(both[:, 0:128])
    pair[:, 128:256] = both[:, 128:256].astype(bf16)
    member = lax.rem(dp, members)
    tree_rows = lambda m: pl.ds(pl.multiple_of(m * local_tok, local_tok), local_tok)
    partner = lax.rem(line_partner(dp), members)
    pair_keep = pltpu.make_async_copy(pair, tree_out.at[tree_rows(member)], pair_local)
    pair_keep.start()

    def pair_copy(bits, forward=False):
        at = tree_rows(partner if forward else member)
        index = PLANE + bits - 1 if forward else bits
        return pltpu.make_async_remote_copy(
            src_ref=tree_out.at[at] if forward else pair, dst_ref=tree_out.at[at],
            send_sem=pair_send.at[index], recv_sem=pair_recv.at[index],
            device_id={"dp": plane_partner(dp, bits) if bits else line_partner(dp)}, device_id_type=MESH)

    for bits in range(PLANE):
        pair_copy(bits).start()
    for at in range(0, q_width, 256):
        part = project(at, 256)
        q_out[:, at : at + 128] = turned(part[:, 0:128])
        q_out[:, at + 128 : at + 256] = turned(part[:, 128:256])
    pltpu.make_async_remote_copy(
        src_ref=pair, dst_ref=tree_out.at[tree_rows(partner)], send_sem=pair_send.at[0],
        recv_sem=pair_recv.at[0], device_id={"dp": line_partner(dp)}, device_id_type=MESH).wait_recv()
    for bits in range(1, PLANE):
        pair_copy(bits, True).start()
    for step in range(lines - 1):
        for sign in (1, -1):
            outer.arrived(sign, step)
    for step in range(steps):
        for which in (2, 0, 1):
            for sign in (1, -1):
                place = z_at if sign == 1 else lines - 1 - z_at

                @pl.when(place >= step + 1)
                def _():
                    hop(which, sign, step).wait_recv()
                    if step + 1 < steps:

                        @pl.when(place < lines - 1)
                        def _():
                            hop(which, sign, step + 1).start()
    for bits in range(1, PLANE):
        pair_copy(bits).wait_recv()
        pair_copy(bits, True).wait_recv()
    outer.plane_wait_recv()

    for one in (first, extra, outer):
        one.finish()
    outer.local().wait()
    x_copy.wait_send()
    keep.wait()
    pair_keep.wait()
    for bits in range(PLANE):
        pair_copy(bits).wait_send()
        if bits:
            pair_copy(bits, True).wait_send()
    for which in range(3):
        for bits in range(1, PLANE):
            spread(which, bits).wait_send()
        for sign in (1, -1):
            for step in range(steps):
                place = z_at if sign == 1 else lines - 1 - z_at

                @pl.when((place >= step) & (place < lines - 1))
                def _():
                    hop(which, sign, step).wait_send()


def front(ff_blocks, first, out_t, extra, x, cosines, sines, lines, members):
    bf16, f32 = jnp.bfloat16, jnp.float32
    half, width = x.shape
    local_tok = 2 * half
    shard, columns = first.shape
    block = ff_blocks.shape[-1]
    q_width = out_t.shape[1]
    count = lines * PLANE
    steps = max(lines - 3, 1)
    anywhere = pl.BlockSpec(memory_space=pl.ANY)
    inside = pl.BlockSpec(memory_space=pltpu.VMEM)
    dma = pltpu.SemaphoreType.DMA
    slab = jax.ShapeDtypeStruct((3, PLANE * shard, block), bf16)
    gather_sems = [dma, dma((2, lines)), dma((2, lines)), dma((PLANE - 1, lines)), dma((PLANE - 1, lines))]
    return pl.pallas_call(
        functools.partial(front_kernel, lines=lines, members=members, steps=steps),
        out_shape=(slab,) * (1 + 2 * steps)
        + (
            jax.ShapeDtypeStruct((width, columns), bf16),
            jax.ShapeDtypeStruct((width, q_width), bf16),
            jax.ShapeDtypeStruct((local_tok, q_width), bf16),
            jax.ShapeDtypeStruct((members * local_tok, 256), bf16),
            jax.ShapeDtypeStruct((local_tok, width), bf16),
            jax.ShapeDtypeStruct((16, width), f32),
        ),
        in_specs=[anywhere] * 5 + [inside] * 2,
        out_specs=(anywhere,) * (1 + 2 * steps) + (anywhere, anywhere, inside, anywhere, inside, inside),
        scratch_shapes=[
            pltpu.VMEM((width, columns), bf16), pltpu.VMEM((16 * count, width), bf16),
            pltpu.VMEM((local_tok, width), bf16), pltpu.VMEM((local_tok, width), bf16),
            pltpu.VMEM((local_tok, 256), bf16),
        ]
        + gather_sems * 3
        + [
            dma((3,)), dma((3, PLANE - 1)), dma((3, PLANE - 1)), dma((3, 2, steps)), dma((3, 2, steps)),
            dma, dma, dma, dma, dma, dma((2 * PLANE - 1,)), dma((2 * PLANE - 1,)),
        ],
        compiler_params=pltpu.CompilerParams(vmem_limit_bytes=56 << 20, collective_id=1, has_side_effects=True),
        name="front",
        cost_estimate=pl.CostEstimate(flops=2 * local_tok * width * columns, bytes_accessed=30 << 20, transcendentals=0),
    )(ff_blocks, first, out_t, extra, x, cosines, sines)


def ff_kernel(
    *refs, tile_h, tile_n, tile_m, lines,
):
    spread = 1 + 2 * (lines - 2)
    x_in, cots, slabs = refs[0], refs[1 : 1 + PLANE], refs[1 + PLANE : 1 + PLANE + spread]
    (
        dx_out, y_out, parts_out, top_out, bottom_out,
        x_all, cot_all, gate_w, up_w, down_w, prod, gate_g, up_g, far, near, back, y_stage,
        x_send, x_recv, fwd_send, fwd_recv, pair_send, pair_recv, dx_send, dx_recv,
        x_load, cot_load, cot_send, cot_recv, weight_sem, hop_send, hop_recv, y_sem, out_sem,
    ) = refs[1 + PLANE + spread :]
    bf16 = jnp.bfloat16
    half = x_in.shape[0]
    width = x_in.shape[1]
    block = gate_w.shape[1]
    chunk = 2 * half
    dp = lax.axis_index("dp")
    core = lax.axis_index("tensor")
    chip = [None] + [{"dp": plane_partner(dp, bits)} for bits in range(1, PLANE)]
    mate = {"tensor": 1 - core}
    rows = lambda k, r, n=1: pl.ds((2 * k + r) * half, n * half)

    z_at = dp // PLANE
    slab_rows = width // lines
    weights = (gate_w, up_w, down_w)
    ways = ((1, 0), (-1, 1))
    place_of = lambda sign: z_at if sign == 1 else lines - 1 - z_at
    place_rows = lambda z: pl.ds(pl.multiple_of(z * slab_rows, slab_rows), slab_rows)

    def weight_loads(which, act):
        for sign, way in ways:
            for step in range(lines - 2):
                piece = 1 + way * (lines - 2) + step

                @pl.when(place_of(sign) >= step + 1)
                def _():
                    act(pltpu.make_async_copy(
                        slabs[piece].at[which], weights[which].at[place_rows(z_at - sign * (step + 1))],
                        weight_sem.at[which, piece]))

        act(pltpu.make_async_copy(slabs[0].at[which], weights[which].at[place_rows(z_at)], weight_sem.at[which, 0]))

    def last_hop(which, sign, way):
        origin = 0 if sign == 1 else lines - 1
        return pltpu.make_async_remote_copy(
            src_ref=slabs[(way + 1) * (lines - 2)].at[which],
            dst_ref=weights[which].at[pl.ds(origin * slab_rows, slab_rows)],
            send_sem=hop_send.at[which, way], recv_sem=hop_recv.at[which, way],
            device_id={"dp": dp + sign * PLANE}, device_id_type=MESH)

    def weight_wait(which):
        weight_loads(which, lambda copy: copy.wait())
        for sign, way in ways:

            @pl.when(place_of(sign) == lines - 1)
            def _():
                last_hop(which, sign, way).wait_recv()

    x_keep = pltpu.make_async_copy(x_in, x_all.at[rows(0, 0)], x_load)
    x_keep.start()

    def cot_keep(k):
        return pltpu.make_async_copy(cots[k], cot_all.at[rows(k, 0)], cot_load.at[k])

    def cot_copy(k):
        return pltpu.make_async_remote_copy(
            src_ref=cots[k], dst_ref=cot_all.at[rows(k, 1)], send_sem=cot_send.at[k], recv_sem=cot_recv.at[k],
            device_id=mate, device_id_type=MESH)

    for k in range(PLANE):
        cot_keep(k).start()
    for which in (2, 0, 1):
        weight_loads(which, lambda copy: copy.start())
    greet(dp, core, lines)
    for which in (2, 0, 1):
        for sign, way in ways:

            @pl.when(place_of(sign) == lines - 2)
            def _():
                last_hop(which, sign, way).start()

    def x_copy(k):
        return pltpu.make_async_remote_copy(
            src_ref=x_in, dst_ref=x_all.at[rows(k, 0) if k else rows(0, 1)],
            send_sem=x_send.at[k], recv_sem=x_recv.at[k],
            device_id=chip[k] if k else mate, device_id_type=MESH)

    def x_forward(k):
        return pltpu.make_async_remote_copy(
            src_ref=x_all.at[rows(k, 0)], dst_ref=x_all.at[rows(k, 1)],
            send_sem=fwd_send.at[k - 1], recv_sem=fwd_recv.at[k - 1],
            device_id=mate, device_id_type=MESH)

    def pair_copy(k):
        return pltpu.make_async_remote_copy(
            src_ref=far.at[k], dst_ref=near.at[k],
            send_sem=pair_send.at[k], recv_sem=pair_recv.at[k],
            device_id=mate, device_id_type=MESH)

    def dx_copy(k):
        return pltpu.make_async_remote_copy(
            src_ref=near.at[k], dst_ref=back.at[k - 1],
            send_sem=dx_send.at[k - 1], recv_sem=dx_recv.at[k - 1],
            device_id=chip[k], device_id_type=MESH)

    x_copy(0).start()
    x_copy(1).start()
    x_copy(2).start()
    for k in range(PLANE):
        cot_copy(k).start()
    for k in range(PLANE):
        cot_keep(k).wait()
        cot_copy(k).wait_recv()
    weight_wait(2)

    @pl.loop(0, PLANE)
    def _(k):
        at = pl.ds(pl.multiple_of(k * chunk, chunk), chunk)

        @pl.loop(0, block // tile_h)
        def _(t):
            cols = pl.ds(pl.multiple_of(t * tile_h, tile_h), tile_h)
            up_g[at, cols] = dot_nn(cot_all[at, :], down_w[:, cols]).astype(bf16)

    def gate_up(k):
        at = rows(k, 0, 2)

        @pl.loop(0, block // tile_h)
        def _(t):
            cols = pl.ds(pl.multiple_of(t * tile_h, tile_h), tile_h)
            gate = dot_nn(x_all[at, :], gate_w[:, cols])
            up = dot_nn(x_all[at, :], up_w[:, cols])
            pg = up_g[at, cols].astype(jnp.float32)
            sig = 0.5 * jnp.tanh(0.5 * gate) + 0.5
            silu = gate * sig
            prod[at, cols] = (silu * up).astype(bf16)
            up_g[at, cols] = (pg * silu).astype(bf16)
            gate_g[at, cols] = (pg * up * (sig + silu * (1.0 - sig))).astype(bf16)

    def dx_half(k, r):
        at = rows(k, r)

        @pl.loop(0, width // tile_n)
        def _(t):
            cols = pl.ds(pl.multiple_of(t * tile_n, tile_n), tile_n)
            part = dot_nt(gate_g[at, :], gate_w[cols, :]) + dot_nt(up_g[at, :], up_w[cols, :])
            if r:
                far[k, :, cols] = part.astype(bf16)
            else:
                near[k, :, cols] = (part + near[k, :, cols].astype(jnp.float32)).astype(bf16)

    def dx_first(k):
        dx_half(k, 1)
        pair_copy(k).start()

    def dx_second(k):
        pair_copy(k).wait_recv()
        dx_half(k, 0)
        if k:
            dx_copy(k).start()

    def y_copies(k, act):
        for r in range(2):
            act(pltpu.make_async_copy(y_stage.at[pl.ds(r * half, half)], y_out.at[r, k], y_sem.at[r]))

    def y_part(k):
        if k:
            y_copies(k - 1, lambda copy: copy.wait())

        @pl.loop(0, width // tile_n)
        def _(t):
            cols = pl.ds(pl.multiple_of(t * tile_n, tile_n), tile_n)
            y_stage[:, cols] = dot_nt(prod[rows(k, 0, 2), :], down_w[cols, :]).astype(bf16)

        y_copies(k, lambda copy: copy.start())

    x_keep.wait()
    weight_wait(0)
    weight_wait(1)
    x_copy(0).wait_recv()
    gate_up(0)
    dx_first(0)
    x_copy(3).start()
    x_copy(1).wait_recv()
    x_forward(1).start()
    x_copy(2).wait_recv()
    x_forward(2).start()
    dx_second(0)
    x_forward(1).wait_recv()
    gate_up(1)
    dx_first(1)
    y_part(0)
    dx_second(1)
    x_forward(2).wait_recv()
    gate_up(2)
    dx_first(2)
    y_part(1)
    x_copy(3).wait_recv()
    x_forward(3).start()
    dx_second(2)
    x_forward(3).wait_recv()
    gate_up(3)
    dx_first(3)
    y_part(2)
    dx_second(3)
    y_part(3)

    def out_copies(which, act):
        for z in range(lines):
            at = pl.ds(z * slab_rows, slab_rows)
            act(pltpu.make_async_copy(weights[which].at[at], parts_out.at[which, z], out_sem.at[which, z]))
        for index, out in ((lines, top_out), (lines + 1, bottom_out)):
            at = pl.ds((lines - 1) * slab_rows if out is top_out else 0, slab_rows)
            act(pltpu.make_async_copy(weights[which].at[at], out.at[which], out_sem.at[which, index]))

    @pl.loop(0, width // tile_m)
    def _(m):
        at = pl.ds(pl.multiple_of(m * tile_m, tile_m), tile_m)
        turned = cot_all[:, at].T
        down_w[at, :] = dot_nn(turned, prod[...]).astype(bf16)

    out_copies(2, lambda copy: copy.start())

    @pl.loop(0, width // tile_m)
    def _(m):
        at = pl.ds(pl.multiple_of(m * tile_m, tile_m), tile_m)
        turned = x_all[:, at].T
        gate_w[at, :] = dot_nn(turned, gate_g[...]).astype(bf16)
        up_w[at, :] = dot_nn(turned, up_g[...]).astype(bf16)

    out_copies(0, lambda copy: copy.start())
    out_copies(1, lambda copy: copy.start())

    for k in range(1, PLANE):
        dx_copy(k).wait_recv()
    total = near[0].astype(jnp.float32)
    for k in range(PLANE - 1):
        total = total + back[k].astype(jnp.float32)
    dx_out[...] = total

    for k in range(PLANE):
        x_copy(k).wait_send()
        pair_copy(k).wait_send()
        if k:
            x_forward(k).wait_send()
            dx_copy(k).wait_send()
    y_copies(PLANE - 1, lambda copy: copy.wait())
    for which in range(3):
        out_copies(which, lambda copy: copy.wait())
        for sign, way in ways:

            @pl.when(place_of(sign) == lines - 2)
            def _():
                last_hop(which, sign, way).wait_send()

    for k in range(PLANE):
        cot_copy(k).wait_send()


def feed_forward(x, cots, slabs, lines, tile_h=384, tile_n=512, tile_m=256):
    half, width = x.shape
    block = slabs[0].shape[-1]
    slab_rows = width // lines
    tokens = 2 * PLANE * half
    bf16 = jnp.bfloat16
    anywhere = pl.BlockSpec(memory_space=pl.ANY)
    dma = pltpu.SemaphoreType.DMA
    slab = jax.ShapeDtypeStruct((3, slab_rows, block), bf16)
    return pl.pallas_call(
        functools.partial(ff_kernel, tile_h=tile_h, tile_n=tile_n, tile_m=tile_m, lines=lines),
        out_shape=(
            jax.ShapeDtypeStruct((half, width), jnp.float32),
            jax.ShapeDtypeStruct((2, PLANE, half, width), bf16),
            jax.ShapeDtypeStruct((3, lines, slab_rows, block), bf16),
            slab,
            slab,
        ),
        in_specs=[anywhere] * (1 + PLANE + len(slabs)),
        out_specs=(pl.BlockSpec(memory_space=pltpu.VMEM),) + (anywhere,) * 4,
        scratch_shapes=[
            pltpu.VMEM((tokens, width), bf16), pltpu.VMEM((tokens, width), bf16),
            pltpu.VMEM((width, block), bf16), pltpu.VMEM((width, block), bf16), pltpu.VMEM((width, block), bf16),
            pltpu.VMEM((tokens, block), bf16), pltpu.VMEM((tokens, block), bf16), pltpu.VMEM((tokens, block), bf16),
            pltpu.VMEM((PLANE, half, width), bf16), pltpu.VMEM((PLANE, half, width), bf16), pltpu.VMEM((PLANE - 1, half, width), bf16),
            pltpu.VMEM((2 * half, width), bf16),
            dma((PLANE,)), dma((PLANE,)), dma((PLANE - 1,)), dma((PLANE - 1,)), dma((PLANE,)), dma((PLANE,)),
            dma((PLANE - 1,)), dma((PLANE - 1,)), dma, dma((PLANE,)), dma((PLANE,)), dma((PLANE,)), dma((3, 2 * lines)), dma((3, 2)), dma((3, 2)), dma((2,)), dma((3, lines + 2)),
        ],
        compiler_params=pltpu.CompilerParams(vmem_limit_bytes=62 << 20, collective_id=0, has_side_effects=True),
        name="feed_forward",
        cost_estimate=pl.CostEstimate(flops=18 * tokens * width * block, bytes_accessed=60 << 20, transcendentals=tokens * block),
    )(x, *cots, *slabs)


def back_kernel(
    dkv_in, dq_in, cos_in, sin_in, normed_in, first_in, out_part, x_in, rows_in, gain_row_in, middle_grad_in,
    ff_in, carried_up, carried_down, y_in,
    input_grad_out, sums_out, small_out, ff_out, y_out,
    kv_own, kv_other, kv_plane, kv_merged, kv_line, grads, part_q, part_kv, own_o,
    recv_q, recv_kv, recv_o, line_q, line_kv, line_o, from_q, from_kv, from_o,
    far, near, small_own, small_mate, small_plane, small_line,
    own_buf, recv_buf, first_buf, total_buf,
    kv_local, kv_send, kv_recv, kv_line_send, kv_line_recv,
    plane_send, plane_recv, line_send, line_recv, own_o_sem,
    mate_send, mate_recv, small_mate_sem, small_plane_send, small_plane_recv, small_line_send, small_line_recv,
    load_sem, own_sem, carry_sem, hop_send, hop_recv, spread_local, spread_send, spread_recv, y_send, y_recv,
    *, lines, members, scale,
):
    bf16, f32 = jnp.bfloat16, jnp.float32
    dp = lax.axis_index("dp")
    core = lax.axis_index("tensor")
    z_at, j_at = dp // PLANE, lax.rem(dp, PLANE)
    half, width = x_in.shape
    local_tok = 2 * half
    slab_rows = width // lines
    shard = slab_rows // PLANE
    q_width = dq_in.shape[1]
    block = total_buf.shape[-1]
    mate = {"tensor": 1 - core}
    chip = [None] + [{"dp": plane_partner(dp, bits)} for bits in range(1, PLANE)]
    there = [j_at] + [lax.rem(plane_partner(dp, bits), PLANE) for bits in range(1, PLANE)]
    side = lax.rem(z_at, 2) * PLANE
    other_side = PLANE - side
    member = lax.rem(dp, members)
    del member
    ways = ((1, 0), (-1, 1))
    place_of = lambda sign: z_at if sign == 1 else lines - 1 - z_at
    tree_rows = lambda m: pl.ds(pl.multiple_of(m * local_tok, local_tok), local_tok)

    kv_loads = [
        pltpu.make_async_copy(dkv_in.at[tree_rows(side + j_at)], kv_own, kv_local.at[0]),
        pltpu.make_async_copy(dkv_in.at[tree_rows(other_side + j_at)], kv_other, kv_local.at[1]),
    ]
    for load in kv_loads:
        load.start()
    o_load = pltpu.make_async_copy(out_part.at[:, j_at], own_o, own_o_sem)
    o_load.start()

    def slab_load(which, sign, way, step):
        target = lines - 1 - step + place_of(sign)
        slab = target if sign == 1 else lines - 1 - target
        return pltpu.make_async_copy(ff_in.at[which, slab], own_buf.at[which, way], load_sem.at[which, way])

    def own_load(which):
        return pltpu.make_async_copy(ff_in.at[which, z_at], total_buf.at[which], own_sem.at[which])

    def carry_load(which, sign, way):
        return pltpu.make_async_copy(
            (carried_up if sign == 1 else carried_down).at[which], first_buf.at[which, way], carry_sem.at[which, way])

    order = (2, 0, 1)
    for which in order:
        for sign, way in ways:
            carry_load(which, sign, way).start()

            @pl.when(place_of(sign) == 1)
            def _():
                slab_load(which, sign, way, 1).start()

        own_load(which).start()

    barrier = pltpu.get_barrier_semaphore()
    for bits in range(1, PLANE):
        pl.semaphore_signal(barrier, inc=1, device_id=chip[bits], device_id_type=MESH)
    pl.semaphore_signal(barrier, inc=1, device_id=mate, device_id_type=MESH)
    for apart in range(1, lines):
        pl.semaphore_signal(
            barrier, inc=1, device_id={"dp": lax.rem(z_at + apart, lines) * PLANE + j_at}, device_id_type=MESH)
    pl.semaphore_wait(barrier, PLANE + lines - 1)

    def kv_copy(bits, part):
        at = tree_rows((side if part == 0 else other_side) + there[bits])
        return pltpu.make_async_remote_copy(
            src_ref=dkv_in.at[at], dst_ref=kv_plane.at[bits - 1, part],
            send_sem=kv_send.at[bits - 1, part], recv_sem=kv_recv.at[bits - 1, part],
            device_id=chip[bits], device_id_type=MESH)

    for part in (1, 0):
        for bits in range(1, PLANE):
            kv_copy(bits, part).start()

    def hop(which, sign, way, step, first_place=False):
        slab = lines - 1 - step if sign == 1 else step
        carried = first_buf.at[which, way] if step == 1 else recv_buf.at[which, way, step - 2]
        return pltpu.make_async_remote_copy(
            src_ref=ff_in.at[which, slab] if first_place else carried, dst_ref=recv_buf.at[which, way, step - 1],
            send_sem=hop_send.at[which, way, step - 1], recv_sem=hop_recv.at[which, way, step - 1],
            device_id={"dp": dp + sign * PLANE}, device_id_type=MESH)

    def hop_step(which, step):
        for sign, way in ways:
            place = place_of(sign)
            if step == 1:
                carry_load(which, sign, way).wait()

            @pl.when(place == 0)
            def _():
                hop(which, sign, way, step, True).start()

            @pl.when((place >= 1) & (place <= step))
            def _():
                if step > 1:
                    hop(which, sign, way, step - 1).wait_recv()
                slab_load(which, sign, way, step).wait()
                mine = own_buf[which, way].astype(f32)
                if step == 1:
                    first_buf[which, way] = (mine + first_buf[which, way].astype(f32)).astype(bf16)
                else:
                    recv_buf[which, way, step - 2] = (mine + recv_buf[which, way, step - 2].astype(f32)).astype(bf16)
                hop(which, sign, way, step).start()

            if step < lines - 2:

                @pl.when((place >= 1) & (place <= step + 1))
                def _():
                    slab_load(which, sign, way, step + 1).start()

    for which in order:
        hop_step(which, 1)

    groups = {
        "o": (0, out_part, own_o, recv_o, line_o, from_o, q_width + 256, q_width),
        "q": (1, part_q, None, recv_q, line_q, from_q, 0, q_width),
        "kv": (2, part_kv, None, recv_kv, line_kv, from_kv, q_width, 256),
    }

    def plane_copy(name, bits):
        index, part, _, recv, *_ = groups[name]
        return pltpu.make_async_remote_copy(
            src_ref=part.at[:, there[bits]], dst_ref=recv.at[bits - 1],
            send_sem=plane_send.at[index, bits - 1], recv_sem=plane_recv.at[index, bits - 1],
            device_id=chip[bits], device_id_type=MESH)

    def line_copy(name, apart):
        index, _, _, _, line, came, *_ = groups[name]
        target = lax.rem(z_at + apart, lines)
        return pltpu.make_async_remote_copy(
            src_ref=line.at[target], dst_ref=came.at[apart - 1],
            send_sem=line_send.at[index, apart - 1], recv_sem=line_recv.at[index, apart - 1],
            device_id={"dp": target * PLANE + j_at}, device_id_type=MESH)

    def plane_start(name):
        for bits in range(1, PLANE):
            plane_copy(name, bits).start()

    def plane_sum(name):
        _, part, own, recv, line, *_ = groups[name]
        for bits in range(1, PLANE):
            plane_copy(name, bits).wait_recv()
        for z in range(lines):
            total = (part[z, j_at] if own is None else own[z]).astype(f32)
            for bits in range(1, PLANE):
                total = total + recv[bits - 1, z].astype(f32)
            line[z] = total.astype(bf16)
        for apart in range(1, lines):
            line_copy(name, apart).start()

    def line_sum(name):
        *_, line, came, at, size = groups[name]
        for apart in range(1, lines):
            line_copy(name, apart).wait_recv()
        total = line[z_at].astype(f32)
        for apart in range(1, lines):
            total = total + came[apart - 1].astype(f32)
        sums_out[:, at : at + size] = total

    plane_start("o")
    cosines, sines = cos_in[...], sin_in[...]

    def turned_back(part):
        return (part * cosines - pltpu.roll(part, 64, 1) * sines).astype(bf16)

    for at in range(0, q_width, 128):
        grads[:, at : at + 128] = turned_back(dq_in[:, at : at + 128])

    def y_copy(bits):
        return pltpu.make_async_remote_copy(
            src_ref=y_in.at[bits], dst_ref=y_out.at[bits - 1], send_sem=y_send.at[bits - 1], recv_sem=y_recv.at[bits - 1],
            device_id=chip[bits], device_id_type=MESH)

    def weight_part(part, at, size):
        for z in range(lines):
            turned = normed_in[:, z * slab_rows : (z + 1) * slab_rows].T
            tile = dot_nn(turned, grads[:, at : at + size]).astype(bf16)
            for j in range(PLANE):
                part[z, j] = tile[j * shard : (j + 1) * shard]

    weight_part(part_q, 0, q_width)
    plane_start("q")

    for load in kv_loads:
        load.wait()
    for bits in range(1, PLANE):
        kv_copy(bits, 1).wait_recv()
    total = kv_other[...].astype(f32)
    for bits in range(1, PLANE):
        total = total + kv_plane[bits - 1, 1].astype(f32)
    kv_merged[...] = total.astype(bf16)
    kv_across = pltpu.make_async_remote_copy(
        src_ref=kv_merged, dst_ref=kv_line, send_sem=kv_line_send, recv_sem=kv_line_recv,
        device_id={"dp": line_partner(dp)}, device_id_type=MESH)
    kv_across.start()
    for step in range(2, lines - 1):
        hop_step(order[0], step)
    for bits in range(1, PLANE):
        kv_copy(bits, 0).wait_recv()
    kv_across.wait_recv()
    total = kv_own[...].astype(f32) + kv_line[...].astype(f32)
    for bits in range(1, PLANE):
        total = total + kv_plane[bits - 1, 0].astype(f32)
    grads[:, q_width : q_width + 128] = turned_back(total[:, 0:128] * scale)
    grads[:, q_width + 128 :] = total[:, 128:256].astype(bf16)
    weight_part(part_kv, q_width, 256)
    plane_start("kv")
    for bits in range(1, PLANE):
        y_copy(bits).start()

    def normed_grad(c):
        at = pl.ds(pl.multiple_of(c * half, half), half)
        return dot_nt(grads[at, :], first_in[...])

    far[...] = normed_grad(1 - core).astype(bf16)
    mate_copy = pltpu.make_async_remote_copy(
        src_ref=far, dst_ref=near, send_sem=mate_send, recv_sem=mate_recv, device_id=mate, device_id_type=MESH)
    mate_copy.start()
    mine = normed_grad(core)
    o_load.wait()
    plane_sum("o")
    mate_copy.wait_recv()
    mine = mine + near[...].astype(f32)
    wide = x_in[...].astype(f32)
    norm = lax.rsqrt(jnp.mean(wide * wide, axis=1, keepdims=True) + EPS)
    z_own = wide * norm
    w = mine * gain_row_in[...]
    back = norm * (w - z_own * jnp.mean(w * z_own, axis=1, keepdims=True))
    input_grad_out[...] = (middle_grad_in[...] + back).astype(bf16)
    bias = jnp.sum(grads[...].astype(f32), axis=0, keepdims=True)
    small_own[...] = jnp.concatenate(
        [
            jnp.sum(mine * z_own, axis=0, keepdims=True),
            rows_in[...],
            jnp.concatenate([bias, jnp.zeros((1, width - q_width - 256), f32)], axis=1),
            jnp.zeros((5, width), f32),
        ],
        axis=0,
    )
    small_copy = pltpu.make_async_remote_copy(
        src_ref=small_own, dst_ref=small_mate, send_sem=small_mate_sem.at[0], recv_sem=small_mate_sem.at[1],
        device_id=mate, device_id_type=MESH)
    small_copy.start()
    for step in range(2, lines - 1):
        hop_step(order[1], step)
    plane_sum("q")
    for step in range(2, lines - 1):
        hop_step(order[2], step)
    plane_sum("kv")

    small_copy.wait_recv()
    gain_rows = lax.broadcasted_iota(jnp.int32, (8, width), 0) < 2
    small_plane[0] = small_own[...] + jnp.where(gain_rows, small_mate[...], 0.0)

    def small_plane_copy(bits):
        return pltpu.make_async_remote_copy(
            src_ref=small_plane.at[0], dst_ref=small_plane.at[bits],
            send_sem=small_plane_send.at[bits - 1], recv_sem=small_plane_recv.at[bits - 1],
            device_id=chip[bits], device_id_type=MESH)

    def small_line_copy(apart):
        return pltpu.make_async_remote_copy(
            src_ref=small_line.at[0], dst_ref=small_line.at[apart],
            send_sem=small_line_send.at[apart - 1], recv_sem=small_line_recv.at[apart - 1],
            device_id={"dp": lax.rem(z_at + apart, lines) * PLANE + j_at}, device_id_type=MESH)

    for bits in range(1, PLANE):
        small_plane_copy(bits).start()
    for bits in range(1, PLANE):
        small_plane_copy(bits).wait_recv()
    total = small_plane[0]
    for bits in range(1, PLANE):
        total = total + small_plane[bits]
    small_line[0] = total
    for apart in range(1, lines):
        small_line_copy(apart).start()
    line_sum("o")
    line_sum("q")
    line_sum("kv")
    for apart in range(1, lines):
        small_line_copy(apart).wait_recv()
    total = small_line[0]
    for apart in range(1, lines):
        total = total + small_line[apart]
    small_out[...] = total

    columns = lambda j: pl.ds(pl.multiple_of(j * block, block), block)

    def spread(which, bits):
        rows = pl.ds(pl.multiple_of(there[bits] * shard, shard), shard)
        return pltpu.make_async_remote_copy(
            src_ref=total_buf.at[which, rows], dst_ref=ff_out.at[which, :, columns(j_at)],
            send_sem=spread_send.at[which, bits - 1], recv_sem=spread_recv.at[which, bits - 1],
            device_id=chip[bits], device_id_type=MESH)

    def spread_keep(which):
        rows = pl.ds(pl.multiple_of(j_at * shard, shard), shard)
        return pltpu.make_async_copy(
            total_buf.at[which, rows], ff_out.at[which, :, columns(j_at)], spread_local.at[which])

    for which in order:
        own_load(which).wait()
        for sign, way in ways:

            @pl.when(place_of(sign) >= 1)
            def _():
                hop(which, sign, way, lines - 2).wait_recv()
                came = recv_buf[which, way, lines - 3].astype(f32)
                total_buf[which] = (total_buf[which].astype(f32) + came).astype(bf16)

        for bits in range(1, PLANE):
            spread(which, bits).start()
        spread_keep(which).start()

    for which in order:
        for bits in range(1, PLANE):
            spread(which, bits).wait_recv()
            spread(which, bits).wait_send()
        spread_keep(which).wait()
        for sign, way in ways:
            for step in range(1, lines - 1):

                @pl.when(place_of(sign) <= step)
                def _():
                    hop(which, sign, way, step).wait_send()

    for bits in range(1, PLANE):
        y_copy(bits).wait_recv()
        y_copy(bits).wait_send()
        small_plane_copy(bits).wait_send()
        for part in range(2):
            kv_copy(bits, part).wait_send()
        for name in groups:
            plane_copy(name, bits).wait_send()
    for apart in range(1, lines):
        small_line_copy(apart).wait_send()
        for name in groups:
            line_copy(name, apart).wait_send()
    kv_across.wait_send()
    mate_copy.wait_send()
    small_copy.wait_send()


def finish(dkv, dq, cosines, sines, normed, first, out_part, x, gain_rows, gain_row, middle_grad, ff_parts, up, down, y_parts, lines, members, scale):
    bf16, f32 = jnp.bfloat16, jnp.float32
    half, width = x.shape
    local_tok = 2 * half
    q_width = dq.shape[1]
    slab_rows = width // lines
    shard = slab_rows // PLANE
    block = ff_parts.shape[-1]
    anywhere = pl.BlockSpec(memory_space=pl.ANY)
    inside = pl.BlockSpec(memory_space=pltpu.VMEM)
    dma = pltpu.SemaphoreType.DMA
    near = PLANE - 1
    vmem = lambda *shape: pltpu.VMEM(shape, bf16)
    wide = lambda *shape: pltpu.VMEM(shape, f32)
    pair = (local_tok, 256)
    return pl.pallas_call(
        functools.partial(back_kernel, lines=lines, members=members, scale=scale),
        out_shape=(
            jax.ShapeDtypeStruct((half, width), bf16),
            jax.ShapeDtypeStruct((shard, 2 * q_width + 256), f32),
            jax.ShapeDtypeStruct((8, width), f32),
            jax.ShapeDtypeStruct((3, shard, PLANE * block), bf16),
            jax.ShapeDtypeStruct((PLANE - 1, half, width), bf16),
        ),
        in_specs=[anywhere] + [inside] * 5 + [anywhere] + [inside] * 4 + [anywhere] * 4,
        out_specs=(inside, inside, inside, anywhere, anywhere),
        scratch_shapes=[
            vmem(*pair), vmem(*pair), vmem(near, 2, *pair), vmem(*pair), vmem(*pair),
            vmem(local_tok, q_width + 256), vmem(lines, PLANE, shard, q_width), vmem(lines, PLANE, shard, 256), vmem(lines, shard, q_width),
            vmem(near, lines, shard, q_width), vmem(near, lines, shard, 256), vmem(near, lines, shard, q_width),
            vmem(lines, shard, q_width), vmem(lines, shard, 256), vmem(lines, shard, q_width),
            vmem(lines - 1, shard, q_width), vmem(lines - 1, shard, 256), vmem(lines - 1, shard, q_width),
            vmem(half, width), vmem(half, width), wide(8, width), wide(8, width), wide(PLANE, 8, width), wide(lines, 8, width),
            vmem(3, 2, slab_rows, block), vmem(3, 2, lines - 2, slab_rows, block), vmem(3, 2, slab_rows, block), vmem(3, slab_rows, block),
            dma((2,)), dma((near, 2)), dma((near, 2)), dma, dma,
            dma((3, near)), dma((3, near)), dma((3, lines - 1)), dma((3, lines - 1)), dma,
            dma, dma, dma((2,)), dma((near,)), dma((near,)), dma((lines - 1,)), dma((lines - 1,)),
            dma((3, 2)), dma((3,)), dma((3, 2)), dma((3, 2, lines - 2)), dma((3, 2, lines - 2)), dma((3,)), dma((3, near)), dma((3, near)), dma((near,)), dma((near,)),
        ],
        compiler_params=pltpu.CompilerParams(vmem_limit_bytes=62 << 20, collective_id=2, has_side_effects=True),
        name="back",
        cost_estimate=pl.CostEstimate(flops=6 * local_tok * width * (q_width + 256), bytes_accessed=40 << 20, transcendentals=0),
    )(dkv, dq, cosines, sines, normed, first, out_part, x, gain_rows, gain_row, middle_grad, ff_parts, up, down, y_parts)


def swap(block, axis, count, bits):
    return lax.ppermute(block, axis, [(i, i ^ bits) for i in range(count)])


def rms_scale(values):
    return lax.rsqrt(jnp.mean(values * values, axis=1, keepdims=True) + EPS)


def norm_back(grad, values, gain):
    scale = rms_scale(values)
    z = values * scale
    w = grad * gain
    gain_grad = jnp.sum(grad * z, axis=0)
    return scale * (w - z * jnp.mean(w * z, axis=1, keepdims=True)), gain_grad


def rope_tables(positions):
    exponents = jnp.arange(64, dtype=jnp.float32) * (2.0 / 128)
    frequency = jnp.power(THETA, -exponents)
    angles = positions.astype(jnp.float32)[:, None] * frequency[None, :]
    cosines, sines = jnp.cos(angles), jnp.sin(angles)
    return (
        jnp.concatenate([cosines, cosines], axis=1),
        jnp.concatenate([-sines, sines], axis=1),
    )


def contract_rows(left, right):
    return lax.dot_general(
        left, right, (((0,), (0,)), ((), ())), preferred_element_type=jnp.float32
    )


def contract_cols(left, right):
    return lax.dot_general(
        left, right, (((1,), (1,)), ((), ())), preferred_element_type=jnp.float32
    )


def matmul(left, right):
    return jnp.dot(left, right, preferred_element_type=jnp.float32)


def attention_plan(segment_ids, parent_ids, dp_index, local_tok):
    members = TREE_TOK // local_tok
    first = dp_index // members * TREE_TOK
    slots = lax.dynamic_slice_in_dim(segment_ids, first, TREE_TOK)[::KB]
    numbers = jnp.arange(parent_ids.shape[0], dtype=jnp.int32)
    parents = jnp.sum(jnp.where(slots[:, None] == numbers[None, :], parent_ids[None, :], 0), axis=1)
    places = jnp.arange(slots.shape[0], dtype=jnp.int32)
    holder = jnp.sum(jnp.where(parents[:, None] == slots[None, :], places[None, :], 0), axis=1)
    starts = dp_index % members * local_tok + QB * jnp.arange(local_tok // QB, dtype=jnp.int32)
    slot = starts // KB
    chosen = slot[:, None] == places[None, :]
    pick = lambda table: jnp.sum(jnp.where(chosen, table[None, :], 0), axis=1)
    in_trunk = starts < TRUNK
    is_leaf = pick(parents) != slots[0]
    chunk = jnp.minimum(starts, TRUNK) // KC
    far = jnp.int32(1 << 20)
    block0 = jnp.where(in_trunk, 2 * chunk, jnp.where(is_leaf, pick(holder), TRUNK // KB))
    block1 = jnp.where(in_trunk, 2 * chunk + 1, slot)
    shift0 = jnp.where(in_trunk, block0 * KB - starts, jnp.where(is_leaf, -far, far))
    shift1 = block1 * KB - starts
    zero = jnp.zeros_like(chunk)
    return jnp.stack([chunk, block0, block1, shift0, shift1, zero, zero, zero], axis=1).reshape(-1)


def on_device(
    dp_size,
    layer_input,
    out_cotangent,
    positions,
    segment_ids,
    parent_ids,
    attention_gain,
    query_weight,
    query_bias,
    key_weight,
    key_bias,
    value_weight,
    value_bias,
    output_weight,
    feedforward_gain,
    gate_weight,
    up_weight,
    down_weight,
):
    bf16, f32 = jnp.bfloat16, jnp.float32
    local_tok = positions.shape[0]
    half_tok, width = layer_input.shape
    shard = attention_gain.shape[0]
    heads, head_dim = query_bias.shape[0], 128
    per_head = query_bias.shape[1]
    q_width = heads * head_dim
    hidden = gate_weight.shape[1]
    block = -(-hidden // (PLANE * 128)) * 128
    lines = dp_size // PLANE
    members = TREE_TOK // local_tok
    dp_index = lax.axis_index("dp")
    core = lax.axis_index("tensor")
    scale = head_dim ** (-0.5)

    def line_route(sign, first, last):
        route = []
        for place in range(first, last + 1):
            z = place if sign == 1 else lines - 1 - place
            route += [(z * PLANE + j, (z + sign) * PLANE + j) for j in range(PLANE)]
        return route

    def by_core(mine):
        other = swap(mine, "tensor", 2, 1)
        first = jnp.where(core == 0, mine, other)
        second = jnp.where(core == 0, other, mine)
        return jnp.concatenate([first, second], axis=0)

    def to_tokens(values):
        halves = values.reshape(2, half_tok, width)
        mine = lax.dynamic_index_in_dim(halves, core, 0, keepdims=False)
        theirs = lax.dynamic_index_in_dim(halves, 1 - core, 0, keepdims=False)
        return mine + swap(theirs.astype(bf16), "tensor", 2, 1).astype(f32)

    blocked = lambda w: jnp.pad(w, ((0, 0), (0, PLANE * block - hidden))).reshape(shard, PLANE, block).transpose(1, 0, 2)
    ff_blocks = jnp.stack([blocked(gate_weight), blocked(up_weight), blocked(down_weight.T)])
    first_own = jnp.concatenate([query_weight, key_weight, value_weight], axis=1)
    biases = jnp.concatenate([query_bias, key_bias, value_bias], axis=0)
    bias_row = lax.dynamic_update_slice(
        jnp.zeros((heads + 2, head_dim), bf16), biases, (0, dp_index * per_head)
    ).reshape(1, -1)
    gains = lax.dynamic_update_slice(
        jnp.zeros((2, width), bf16), jnp.stack([attention_gain, feedforward_gain]), (0, dp_index * shard)
    )
    extra = jnp.concatenate(
        [gains, jnp.pad(bias_row, ((0, 0), (0, width - bias_row.shape[1]))), jnp.zeros((13, width), bf16)], axis=0
    )
    cosines, sines = rope_tables(positions)
    plan = attention_plan(segment_ids, parent_ids, dp_index, local_tok)
    steps = lines - 3
    outs = front(ff_blocks, first_own, output_weight.T, extra, layer_input, cosines, sines, lines, members)
    slab, ups, downs = outs[0], list(outs[1 : 1 + steps]), list(outs[1 + steps : 1 + 2 * steps])
    first_all, out_t, q_rot, tree, normed, rows = outs[1 + 2 * steps :]
    gain_one, gain_two = rows[0:1], rows[1:2]

    ups.append(lax.ppermute(ups[-1], "dp", line_route(1, lines - 3, lines - 2)))
    downs.append(lax.ppermute(downs[-1], "dp", line_route(-1, lines - 3, lines - 2)))
    cot_late = lax.optimization_barrier((out_cotangent, rows))[0]
    cots = [out_cotangent] + [swap(cot_late, "dp", dp_size, bits) for bits in range(1, PLANE)]
    attended, lse = attn_fwd(plan, q_rot, tree, scale)
    input_wide = layer_input.astype(f32)
    middle = input_wide + to_tokens(contract_cols(attended, out_t))
    normed_two = (middle * rms_scale(middle) * gain_two).astype(bf16)

    normed_two_grad, y_parts, ff_parts, top, bottom = feed_forward(
        normed_two, cots, [slab] + ups + downs, lines
    )
    up_first = lax.ppermute(top, "dp", line_route(1, 0, 0))
    down_first = lax.ppermute(bottom, "dp", line_route(-1, 0, 0))
    norm_grad, gain_two_grad = norm_back(normed_two_grad, middle, gain_two)
    middle_grad = out_cotangent.astype(f32) + norm_grad

    branch_grad = by_core(middle_grad.astype(bf16))
    out_part = contract_rows(branch_grad, attended).astype(bf16).reshape(lines, PLANE, shard, q_width)
    attended_grad = matmul(branch_grad, out_t).astype(bf16)
    dq, dtree = attn_bwd(plan, q_rot, attended_grad, attended, lse, tree, scale)
    y_other = lax.optimization_barrier((swap(y_parts[1], "tensor", 2, 1), dq))[0]
    y_sums = y_parts[0].astype(f32) + y_other.astype(f32)
    y_low, dq = lax.optimization_barrier((y_sums.astype(bf16), dq))

    input_grad, sums, small, ff_sums, y_came = finish(
        dtree, dq, cosines, sines, normed, first_all, out_part, layer_input, gain_two_grad[None], gain_one,
        middle_grad, ff_parts, up_first, down_first, y_low, lines, members, scale,
    )
    layer_output = (middle + y_sums[0] + jnp.sum(y_came.astype(f32), axis=0)).astype(bf16)
    ff_sums = ff_sums[:, :, :hidden].astype(f32)
    gains_out = lax.dynamic_slice(small[0:2], (0, dp_index * shard), (2, shard))
    bias_out = lax.dynamic_slice(
        small[2, : (heads + 2) * head_dim].reshape(heads + 2, head_dim), (0, dp_index * per_head), (heads + 2, per_head)
    )
    return (
        layer_output,
        input_grad,
        gains_out[0],
        sums[:, :q_width],
        bias_out[:heads],
        sums[:, q_width : q_width + 128],
        bias_out[heads : heads + 1],
        sums[:, q_width + 128 : q_width + 256],
        bias_out[heads + 1 :],
        sums[:, q_width + 256 :].T,
        gains_out[1],
        ff_sums[0],
        ff_sums[1],
        ff_sums[2].T,
    )


def solution(mesh):
    placed = (
        P(("dp", "tensor"), None),
        P(("dp", "tensor"), None),
        P("dp"),
        P(),
        P(),
        P("dp"),
        P("dp", "tensor"),
        P("tensor", "dp"),
        P("dp", "tensor"),
        P("tensor", "dp"),
        P("dp", "tensor"),
        P("tensor", "dp"),
        P("tensor", "dp"),
        P("dp"),
        P("dp", "tensor"),
        P("dp", "tensor"),
        P("tensor", "dp"),
    )
    return jax.shard_map(
        functools.partial(on_device, mesh.shape["dp"]),
        mesh=mesh,
        in_specs=placed,
        out_specs=(
            P(("dp", "tensor"), None),
            P(("dp", "tensor"), None),
            P("dp"),
            P("dp", "tensor"),
            P("tensor", "dp"),
            P("dp", "tensor"),
            P("tensor", "dp"),
            P("dp", "tensor"),
            P("tensor", "dp"),
            P("tensor", "dp"),
            P("dp"),
            P("dp", "tensor"),
            P("dp", "tensor"),
            P("tensor", "dp"),
        ),
        check_vma=False,
    )
```

```python
import functools

import jax
import jax.numpy as jnp
from jax import lax
from jax.experimental import pallas as pl
from jax.experimental.pallas import tpu as pltpu
from jax.sharding import PartitionSpec as P

EPS = 1e-06
THETA = 10000.0
TREE_TOK = 5120
TRUNK = 2048
PLANE = 4
NEG = -1e30
LATE = (2, 0)
QB=128; KC=512; KB=256
LOG2E=1.4426950408889634

MESH = pl.DeviceIdType.MESH


def dot_nt(a,b): return lax.dot_general(a,b,(((1,),(1,)),((),())),preferred_element_type=jnp.float32)
def dot_nn(a,b): return lax.dot_general(a,b,(((1,),(0,)),((),())),preferred_element_type=jnp.float32)

def plane_partner(dp, bits):
    one = dp + 1 - 2 * lax.rem(dp, 2)
    if bits == 1:
        return one
    two = 2 - 4 * lax.rem(dp // 2, 2)
    return (dp if bits == 2 else one) + two


def line_partner(dp):
    return dp + PLANE - 2 * PLANE * lax.rem(dp // PLANE, 2)


def greet(dp, core, lines):
    z_at = dp // PLANE
    barrier = pltpu.get_barrier_semaphore()
    for bits in range(1, PLANE):
        pl.semaphore_signal(barrier, inc=1, device_id={"dp": plane_partner(dp, bits)}, device_id_type=MESH)
    pl.semaphore_signal(barrier, inc=1, device_id={"tensor": 1 - core}, device_id_type=MESH)

    @pl.when(z_at > 0)
    def _():
        pl.semaphore_signal(barrier, inc=1, device_id={"dp": dp - PLANE}, device_id_type=MESH)

    @pl.when(z_at < lines - 1)
    def _():
        pl.semaphore_signal(barrier, inc=1, device_id={"dp": dp + PLANE}, device_id_type=MESH)

    beside = jnp.minimum(z_at, 1) + jnp.minimum(lines - 1 - z_at, 1)
    pl.semaphore_wait(barrier, PLANE + beside)


def second_block(start):
    return jnp.where(start < TRUNK, start // KC * (KC // KB) + 1, start // KB)


def masked_chunk(tree_ref, other_ref, blk, start):
    at = pl.ds(pl.multiple_of(second_block(start) * KB, KB), KB)
    k = jnp.concatenate([other_ref[blk, :, 0:128], tree_ref[at, 0:128]], axis=0)
    v = jnp.concatenate([other_ref[blk, :, 128:256], tree_ref[at, 128:256]], axis=0)
    return k, v


def attend_kernel(
    info, hot, q_ref, tree_ref, out_t, x_in, rows_in, cot_in, up_in, down_in, late_up, late_down,
    att_out, lse_out, middle_out, normed_out, other_ref, cot_out, mid_up, mid_down, last_up, last_down,
    far, near, pair_send, pair_recv, cot_send, cot_recv, half_send, half_recv, mid_send, mid_recv, last_send, last_recv,
    *, lines, members, scale,
):
    bf16, f32 = jnp.bfloat16, jnp.float32
    dp = lax.axis_index("dp")
    core = lax.axis_index("tensor")
    z_at = dp // PLANE
    half, width = x_in.shape
    local_tok, q_width = q_ref.shape
    heads = q_width // 128
    rows = heads * QB
    c2 = scale * LOG2E
    mate = {"tensor": 1 - core}
    chip = [None] + [{"dp": plane_partner(dp, bits)} for bits in range(1, PLANE)]
    ways = ((1, 0), (-1, 1))
    place_of = lambda sign: z_at if sign == 1 else lines - 1 - z_at

    def mid_hop(sign, way):
        return pltpu.make_async_remote_copy(
            src_ref=(up_in, down_in)[way].at[1], dst_ref=(mid_up, mid_down)[way],
            send_sem=mid_send.at[way], recv_sem=mid_recv.at[way],
            device_id={"dp": dp + sign * PLANE}, device_id_type=MESH)

    def last_hop(sign, way):
        return pltpu.make_async_remote_copy(
            src_ref=(late_up, late_down)[way].at[0], dst_ref=(last_up, last_down)[way],
            send_sem=last_send.at[way], recv_sem=last_recv.at[way],
            device_id={"dp": dp + sign * PLANE}, device_id_type=MESH)

    def cot_copy(bits):
        return pltpu.make_async_remote_copy(
            src_ref=cot_in, dst_ref=cot_out.at[bits - 1], send_sem=cot_send.at[bits - 1], recv_sem=cot_recv.at[bits - 1],
            device_id=chip[bits], device_id_type=MESH)

    def cot_half(bits):
        at = pl.ds((bits - 1) * (half // 2), half // 2)
        return pltpu.make_async_remote_copy(
            src_ref=cot_out.at[2 - bits, at], dst_ref=cot_out.at[2, at],
            send_sem=half_send.at[bits - 1], recv_sem=half_recv.at[bits - 1],
            device_id=chip[bits], device_id_type=MESH)

    greet(dp, core, lines)
    for sign, way in ways:
        place = place_of(sign)

        @pl.when((place >= lines - 3) & (place < lines - 1))
        def _():
            mid_hop(sign, way).start()

        @pl.when(place == lines - 2)
        def _():
            last_hop(sign, way).start()

    for bits in (1, 2):
        cot_copy(bits).start()

    def step(carry, s, v):
        m, l, acc = carry
        mt = s[:, :128]
        for j in range(1, KC // 128):
            mt = jnp.maximum(mt, s[:, j * 128 : (j + 1) * 128])
        mn = jnp.maximum(m, jnp.max(mt, axis=1, keepdims=True))
        p = jnp.exp2((s - mn) * c2)
        ps = p[:, :128]
        for j in range(1, KC // 128):
            ps = ps + p[:, j * 128 : (j + 1) * 128]
        a = jnp.exp2((m - mn) * c2)
        return mn, l * a + ps, acc * a + dot_nn(p.astype(bf16), v)

    @pl.loop(0, local_tok // QB)
    def _(blk):
        start = lax.rem(dp, members) * local_tok + blk * QB
        nfull = jnp.minimum(start, TRUNK) // KC
        mine = pl.ds(pl.multiple_of(blk * QB, QB), QB)
        slots = members * local_tok // KB
        at = pl.ds(pl.multiple_of(jnp.minimum(start, TRUNK - KC) // KC * KC, KC), KB)
        first = tree_ref[at, :].astype(f32) * jnp.where(start < TRUNK, 1.0, 0.0)
        for slot in range(TRUNK // KB, slots):
            first = first + hot[blk * slots + slot] * tree_ref[slot * KB : (slot + 1) * KB, :].astype(f32)
        other_ref[blk] = first.astype(bf16)
        q = jnp.concatenate([q_ref[mine, h * 128 : (h + 1) * 128] for h in range(heads)], axis=0)

        def body(c, carry):
            at = pl.ds(pl.multiple_of(c * KC, KC), KC)
            return step(carry, dot_nt(q, tree_ref[at, 0:128]), tree_ref[at, 128:256])

        init = (jnp.full((rows, 1), NEG, f32), jnp.zeros((rows, 128), f32), jnp.zeros((rows, 128), f32))
        k, v = masked_chunk(tree_ref, other_ref, blk, start)
        s = dot_nt(q, k)
        col = lax.broadcasted_iota(jnp.int32, (QB, KC), 1)
        row = lax.broadcasted_iota(jnp.int32, (QB, KC), 0)
        ok = col + jnp.where(col < KB, info[2 * blk], info[2 * blk + 1] - KB) <= row
        s = jnp.concatenate([jnp.where(ok, s[h * QB : (h + 1) * QB], NEG) for h in range(heads)], axis=0)
        m, l, acc = lax.fori_loop(0, nfull, body, step(init, s, v))
        lsum = jnp.sum(l, axis=1, keepdims=True)
        out = (acc / lsum).astype(bf16)
        for h in range(heads):
            att_out[mine, h * 128 : (h + 1) * 128] = out[h * QB : (h + 1) * QB]
        lse = jnp.broadcast_to(m * c2 + jnp.log2(lsum), (rows, 128)).T
        lse_out[blk] = lse[0:8, :]

    for bits in (1, 2):
        cot_copy(bits).wait_recv()
    for bits in (1, 2):
        cot_half(bits).start()

    def projected(c):
        at = pl.ds(pl.multiple_of(c * half, half), half)
        return dot_nt(att_out[at, :], out_t[...])

    far[...] = projected(1 - core).astype(bf16)
    pair = pltpu.make_async_remote_copy(
        src_ref=far, dst_ref=near, send_sem=pair_send, recv_sem=pair_recv, device_id=mate, device_id_type=MESH)
    pair.start()
    own = projected(core) + x_in[...].astype(f32)
    pair.wait_recv()
    middle = own + near[...].astype(f32)
    middle_out[...] = middle
    norm = lax.rsqrt(jnp.mean(middle * middle, axis=1, keepdims=True) + EPS)
    normed_out[...] = (middle * norm * rows_in[1:2, :]).astype(bf16)

    pair.wait_send()
    for bits in (1, 2):
        cot_half(bits).wait_recv()
        cot_copy(bits).wait_send()
        cot_half(bits).wait_send()
    for sign, way in ways:
        place = place_of(sign)

        @pl.when(place >= lines - 2)
        def _():
            mid_hop(sign, way).wait_recv()

        @pl.when((place >= lines - 3) & (place < lines - 1))
        def _():
            mid_hop(sign, way).wait_send()

        @pl.when(place == lines - 1)
        def _():
            last_hop(sign, way).wait_recv()

        @pl.when(place == lines - 2)
        def _():
            last_hop(sign, way).wait_send()


def attend(info, hot, q, tree, out_t, x, rows, cot, up, down, late_up, late_down, lines, members, scale):
    bf16, f32 = jnp.bfloat16, jnp.float32
    local_tok, q_width = q.shape
    half, width = x.shape
    anywhere = pl.BlockSpec(memory_space=pl.ANY)
    inside = pl.BlockSpec(memory_space=pltpu.VMEM)
    dma = pltpu.SemaphoreType.DMA
    slab = jax.ShapeDtypeStruct(up.shape[1:], bf16)
    return pl.pallas_call(
        functools.partial(attend_kernel, lines=lines, members=members, scale=scale),
        out_shape=(
            jax.ShapeDtypeStruct((local_tok, q_width), bf16),
            jax.ShapeDtypeStruct((local_tok // QB, 8, q_width // 128 * QB), f32),
            jax.ShapeDtypeStruct((half, width), f32),
            jax.ShapeDtypeStruct((half, width), bf16),
            jax.ShapeDtypeStruct((local_tok // QB, KB, 256), bf16),
            jax.ShapeDtypeStruct((PLANE - 1, half, width), bf16),
            slab, slab, slab, slab,
        ),
        in_specs=[pl.BlockSpec(memory_space=pltpu.SMEM)] * 2 + [inside] * 5 + [anywhere] * 5,
        out_specs=(inside,) * 5 + (anywhere,) * 5,
        scratch_shapes=[
            pltpu.VMEM((half, width), bf16), pltpu.VMEM((half, width), bf16),
            dma, dma, dma((2,)), dma((2,)), dma((2,)), dma((2,)), dma((2,)), dma((2,)), dma((2,)), dma((2,)),
        ],
        compiler_params=pltpu.CompilerParams(vmem_limit_bytes=56 << 20, collective_id=3, has_side_effects=True),
        name="attend",
        cost_estimate=pl.CostEstimate(
            flops=4 * local_tok * q_width * 2304, bytes_accessed=12 << 20, transcendentals=local_tok * q_width * 18
        ),
    )(info, hot, q, tree, out_t, x, rows, cot, up, down, late_up, late_down)


def attend_back_kernel(
    info, hot, q_ref, att_ref, lse_ref, tree_ref, other_ref, out_t, dx_in, middle_in, cot_in, gain_in, cos_in, sin_in,
    y_own, y_other, ff_in, carried_up, carried_down,
    dq_out, dtree_out, middle_grad_out, gain_out, part_out, layer_out, next_up, next_down,
    sum_ref, parent_ref, branch, att_grad, y_sum, y_tmp, y_came, own_buf, sum_buf,
    branch_send, branch_recv, y_load, y_send, y_recv, load_sem, hop_send, hop_recv,
    *, lines, members, scale,
):
    bf16, f32 = jnp.bfloat16, jnp.float32
    dp = lax.axis_index("dp")
    core = lax.axis_index("tensor")
    z_at = dp // PLANE
    half, width = cot_in.shape
    local_tok, q_width = q_ref.shape
    heads = q_width // 128
    slab_rows = width // lines
    shard = slab_rows // PLANE
    rows = heads * QB
    c2 = scale * LOG2E
    mate = {"tensor": 1 - core}
    chip = [None] + [{"dp": plane_partner(dp, bits)} for bits in range(1, PLANE)]
    ways = ((1, 0), (-1, 1))
    place_of = lambda sign: z_at if sign == 1 else lines - 1 - z_at

    def own_slab(which, sign):
        return ff_in.at[which, lines - 1 if sign == 1 else 0]

    def own_load(which, sign):
        return pltpu.make_async_copy(own_slab(which, sign), own_buf.at[which], load_sem.at[which, 0])

    def carry_load(which, way):
        return pltpu.make_async_copy((carried_up, carried_down)[way].at[which], sum_buf.at[which], load_sem.at[which, 1])

    def hop(which, sign, way, first_place):
        slab = lines - 2 if sign == 1 else 1
        return pltpu.make_async_remote_copy(
            src_ref=ff_in.at[which, slab] if first_place else sum_buf.at[which],
            dst_ref=(next_up, next_down)[way].at[which],
            send_sem=hop_send.at[which, way], recv_sem=hop_recv.at[which, way],
            device_id={"dp": dp + sign * PLANE}, device_id_type=MESH)

    for sign, way in ways:

        @pl.when(place_of(sign) == 1)
        def _():
            for which in (2, 0, 1):
                own_load(which, sign).start()
                carry_load(which, way).start()

    def y_loads(k, act):
        act(pltpu.make_async_copy(y_own.at[k], y_sum.at[k], y_load.at[k, 0]))
        act(pltpu.make_async_copy(y_other.at[k], y_tmp.at[k], y_load.at[k, 1]))

    for k in range(PLANE):
        y_loads(k, lambda copy: copy.start())
    greet(dp, core, lines)
    for sign, way in ways:

        @pl.when(place_of(sign) == 0)
        def _():
            for which in (2, 0, 1):
                hop(which, sign, way, True).start()

        @pl.when(place_of(sign) == 1)
        def _():
            for which in (2, 0, 1):
                own_load(which, sign).wait()
                carry_load(which, way).wait()
                sum_buf[which] = (own_buf[which].astype(f32) + sum_buf[which].astype(f32)).astype(bf16)
                hop(which, sign, way, False).start()

    middle = middle_in[...]
    norm = lax.rsqrt(jnp.mean(middle * middle, axis=1, keepdims=True) + EPS)
    z_own = middle * norm
    gain_out[...] = jnp.sum(dx_in[...] * z_own, axis=0, keepdims=True)
    w = dx_in[...] * gain_in[1:2, :]
    middle_grad = cot_in[...].astype(f32) + norm * (w - z_own * jnp.mean(w * z_own, axis=1, keepdims=True))
    middle_grad_out[...] = middle_grad
    token_rows = pl.ds(pl.multiple_of(core * half, half), half)
    branch[token_rows, :] = middle_grad.astype(bf16)
    branch_copy = pltpu.make_async_remote_copy(
        src_ref=branch.at[token_rows], dst_ref=branch.at[token_rows], send_sem=branch_send, recv_sem=branch_recv,
        device_id=mate, device_id_type=MESH)
    branch_copy.start()

    def y_copy(bits):
        return pltpu.make_async_remote_copy(
            src_ref=y_sum.at[bits], dst_ref=y_came.at[bits - 1], send_sem=y_send.at[bits - 1], recv_sem=y_recv.at[bits - 1],
            device_id=chip[bits], device_id_type=MESH)

    for k in (1, 2, 3, 0):
        y_loads(k, lambda copy: copy.wait())
        y_sum[k] = (y_sum[k].astype(f32) + y_tmp[k].astype(f32)).astype(bf16)
        if k:
            y_copy(k).start()
    branch_copy.wait_recv()
    att_grad[...] = dot_nn(branch[...], out_t[...]).astype(bf16)
    for z in range(lines):
        tile = dot_nn(branch[:, z * slab_rows : (z + 1) * slab_rows].T, att_ref[...]).astype(bf16)
        for j in range(PLANE):
            part_out[z, j] = tile[j * shard : (j + 1) * shard]

    sum_ref[...] = jnp.zeros_like(sum_ref)
    cosines, sines = cos_in[...], sin_in[...]

    @pl.loop(0, local_tok // QB)
    def _(blk):
        start = lax.rem(dp, members) * local_tok + blk * QB
        nfull = jnp.minimum(start, TRUNK) // KC
        mine = pl.ds(pl.multiple_of(blk * QB, QB), QB)
        stacked = lambda ref: jnp.concatenate([ref[mine, h * 128 : (h + 1) * 128] for h in range(heads)], axis=0)
        q, do, o = stacked(q_ref), stacked(att_grad), stacked(att_ref)
        delta = jnp.sum((do.astype(f32) * o.astype(f32)).T, axis=0, keepdims=True)
        lse = lse_ref[blk][0:1, :]

        def tile(k, v, ok):
            p = jnp.exp2(dot_nt(k, q) * c2 - lse)
            if ok is not None:
                p = jnp.concatenate([jnp.where(ok, p[:, h * QB : (h + 1) * QB], 0.0) for h in range(heads)], axis=1)
            ds = (p * (dot_nt(v, do) - delta)).astype(bf16)
            dq = lax.dot_general(ds, k, (((0,), (0,)), ((), ())), preferred_element_type=f32)
            return dq, dot_nn(ds, q), dot_nn(p.astype(bf16), do)

        def body(c, acc):
            at = pl.ds(pl.multiple_of(c * KC, KC), KC)
            dq, dk, dv = tile(tree_ref[at, 0:128], tree_ref[at, 128:256], None)
            sum_ref[at, 0:128] += dk
            sum_ref[at, 128:256] += dv
            return acc + dq

        k, v = masked_chunk(tree_ref, other_ref, blk, start)
        col = lax.broadcasted_iota(jnp.int32, (KC, QB), 0)
        row = lax.broadcasted_iota(jnp.int32, (KC, QB), 1)
        ok = col + jnp.where(col < KB, info[2 * blk], info[2 * blk + 1] - KB) <= row
        dq, dk, dv = tile(k, v, ok)
        at = pl.ds(pl.multiple_of(second_block(start) * KB, KB), KB)
        sum_ref[at, 0:128] += dk[KB:]
        sum_ref[at, 128:256] += dv[KB:]
        parent_ref[blk, :, 0:128] = dk[:KB]
        parent_ref[blk, :, 128:256] = dv[:KB]

        @pl.when(start < TRUNK)
        def _():
            at = pl.ds(pl.multiple_of(start // KC * KC, KC), KB)
            sum_ref[at, 0:128] += dk[:KB]
            sum_ref[at, 128:256] += dv[:KB]

        dq = lax.fori_loop(0, nfull, body, dq) * scale
        place = pl.ds(pl.multiple_of(blk * QB, QB), QB)
        for h in range(heads):
            part = dq[h * QB : (h + 1) * QB]
            turned = part * cos_in[place, :] - pltpu.roll(part, 64, 1) * sin_in[place, :]
            dq_out[mine, h * 128 : (h + 1) * 128] = turned.astype(bf16)

    dtree_out[0:TRUNK, :] = sum_ref[0:TRUNK, :].astype(bf16)

    @pl.loop(TRUNK // KB, members * local_tok // KB)
    def _(slot):
        at = pl.ds(pl.multiple_of(slot * KB, KB), KB)
        total = sum_ref[at, :]
        for blk in range(local_tok // QB):
            total = total + hot[blk * (members * local_tok // KB) + slot] * parent_ref[blk]
        dtree_out[at, :] = total.astype(bf16)

    for bits in range(1, PLANE):
        y_copy(bits).wait_recv()
    total = middle_in[...] + y_sum[0].astype(f32)
    for bits in range(1, PLANE):
        total = total + y_came[bits - 1].astype(f32)
    layer_out[...] = total.astype(bf16)
    branch_copy.wait_send()
    for bits in range(1, PLANE):
        y_copy(bits).wait_send()
    for sign, way in ways:

        @pl.when(place_of(sign) <= 1)
        def _():
            for which in range(3):
                hop(which, sign, way, False).wait_send()

        @pl.when((place_of(sign) >= 1) & (place_of(sign) <= 2))
        def _():
            for which in range(3):
                hop(which, sign, way, False).wait_recv()


def attend_back(info, hot, q, attended, lse, tree, other, out_t, dx, middle, cot, rows, cosines, sines, y_own, y_other, ff_parts, up, down, lines, members, scale):
    bf16, f32 = jnp.bfloat16, jnp.float32
    local_tok, q_width = q.shape
    half, width = cot.shape
    slab_rows = width // lines
    shard = slab_rows // PLANE
    block = up.shape[-1]
    anywhere = pl.BlockSpec(memory_space=pl.ANY)
    inside = pl.BlockSpec(memory_space=pltpu.VMEM)
    dma = pltpu.SemaphoreType.DMA
    slab = jax.ShapeDtypeStruct((3, slab_rows, block), bf16)
    return pl.pallas_call(
        functools.partial(attend_back_kernel, lines=lines, members=members, scale=scale),
        out_shape=(
            jax.ShapeDtypeStruct((local_tok, q_width), bf16),
            jax.ShapeDtypeStruct(tree.shape, bf16),
            jax.ShapeDtypeStruct((half, width), f32),
            jax.ShapeDtypeStruct((1, width), f32),
            jax.ShapeDtypeStruct((lines, PLANE, shard, q_width), bf16),
            jax.ShapeDtypeStruct((half, width), bf16),
            slab, slab,
        ),
        in_specs=[pl.BlockSpec(memory_space=pltpu.SMEM)] * 2 + [inside] * 12 + [anywhere] * 5,
        out_specs=(inside,) * 6 + (anywhere,) * 2,
        scratch_shapes=[
            pltpu.VMEM(tree.shape, f32), pltpu.VMEM((local_tok // QB, KB, 256), f32),
            pltpu.VMEM((local_tok, width), bf16), pltpu.VMEM((local_tok, q_width), bf16),
            pltpu.VMEM((PLANE, half, width), bf16), pltpu.VMEM((PLANE, half, width), bf16), pltpu.VMEM((PLANE - 1, half, width), bf16),
            pltpu.VMEM((3, slab_rows, block), bf16), pltpu.VMEM((3, slab_rows, block), bf16),
            dma, dma, dma((PLANE, 2)), dma((PLANE - 1,)), dma((PLANE - 1,)), dma((3, 2)), dma((3, 2)), dma((3, 2)),
        ],
        compiler_params=pltpu.CompilerParams(vmem_limit_bytes=62 << 20, collective_id=4, has_side_effects=True),
        name="attend_back",
        cost_estimate=pl.CostEstimate(
            flops=10 * local_tok * q_width * 2304, bytes_accessed=30 << 20, transcendentals=local_tok * q_width * 18
        ),
    )(info, hot, q, attended, lse, tree, other, out_t, dx, middle, cot, rows, cosines, sines, y_own, y_other, ff_parts, up, down)


class Gather:
    def __init__(self, own, whole, sems, dp, lines):
        self.own, self.whole, self.dp, self.lines = own, whole, dp, lines
        self.z_at = dp // PLANE
        self.local_sem, self.line_send, self.line_recv, self.plane_send, self.plane_recv = sems
        self.rows_per = own.shape[0]

    def rows(self, owner):
        return pl.ds(pl.multiple_of(owner * self.rows_per, self.rows_per), self.rows_per)

    def local(self):
        return pltpu.make_async_copy(self.own, self.whole.at[self.rows(self.dp)], self.local_sem)

    def place(self, sign):
        return self.z_at if sign == 1 else self.lines - 1 - self.z_at

    def line_copy(self, sign, step):
        owner = self.dp - sign * step * PLANE
        way = (1 - sign) // 2
        return pltpu.make_async_remote_copy(
            src_ref=self.own if step == 0 else self.whole.at[self.rows(owner)],
            dst_ref=self.whole.at[self.rows(owner)],
            send_sem=self.line_send.at[way, step], recv_sem=self.line_recv.at[way, step],
            device_id={"dp": self.dp + sign * PLANE}, device_id_type=MESH)

    def line_start(self, sign, step):
        place = self.place(sign)

        @pl.when((place >= step) & (place < self.lines - 1))
        def _():
            self.line_copy(sign, step).start()

    def line_wait_send(self, sign, step):
        place = self.place(sign)

        @pl.when((place >= step) & (place < self.lines - 1))
        def _():
            self.line_copy(sign, step).wait_send()

    def plane_copy(self, bits, owner, own=False):
        z = owner // PLANE
        return pltpu.make_async_remote_copy(
            src_ref=self.own if own else self.whole.at[self.rows(owner)],
            dst_ref=self.whole.at[self.rows(owner)],
            send_sem=self.plane_send.at[bits - 1, z], recv_sem=self.plane_recv.at[bits - 1, z],
            device_id={"dp": plane_partner(self.dp, bits)}, device_id_type=MESH)

    def plane_start_own(self):
        for bits in range(1, PLANE):
            self.plane_copy(bits, self.dp, True).start()

    def arrived(self, sign, step):
        place = self.place(sign)

        @pl.when(place >= step + 1)
        def _():
            owner = self.dp - sign * (step + 1) * PLANE
            pltpu.make_async_remote_copy(
                src_ref=self.own, dst_ref=self.whole.at[self.rows(owner)],
                send_sem=self.line_send.at[(1 - sign) // 2, step],
                recv_sem=self.line_recv.at[(1 - sign) // 2, step],
                device_id={"dp": self.dp - sign * PLANE}, device_id_type=MESH).wait_recv()
            if step + 1 < self.lines - 1:

                @pl.when(place < self.lines - 1)
                def _():
                    self.line_copy(sign, step + 1).start()

            for bits in range(1, PLANE):
                self.plane_copy(bits, owner).start()

    def plane_wait_recv(self):
        for bits in range(1, PLANE):
            for z in range(self.lines):
                owner = z * PLANE + lax.rem(plane_partner(self.dp, bits), PLANE)
                self.plane_copy(bits, owner).wait_recv()

    def finish(self):
        for sign in (1, -1):
            for step in range(self.lines - 1):
                self.line_wait_send(sign, step)
        for bits in range(1, PLANE):
            for z in range(self.lines):
                self.plane_copy(bits, z * PLANE + lax.rem(self.dp, PLANE)).wait_send()


def front_kernel(*refs, lines, members, steps):
    (
        ff_in, first_in, out_in, extra_in, x_in, cos_in, sin_in,
        own_out, *slab_outs,
    ) = refs[: 8 + 2 * steps]
    (
        late_up, late_down, first_out, out_t, q_out, tree_out, normed_out, rows_out,
        first_all, extra_all, x_all, normed, pair,
        first_local, first_ls, first_lr, first_ps, first_pr,
        extra_local, extra_ls, extra_lr, extra_ps, extra_pr,
        out_local, out_ls, out_lr, out_ps, out_pr,
        spread_local, spread_send, spread_recv, hop_send, hop_recv,
        x_local, x_send, x_recv, keep_sem, pair_local, pair_send, pair_recv, late_send, late_recv,
    ) = refs[8 + 2 * steps :]
    bf16, f32 = jnp.bfloat16, jnp.float32
    dp = lax.axis_index("dp")
    core = lax.axis_index("tensor")
    z_at = dp // PLANE
    j_at = lax.rem(dp, PLANE)
    half, width = x_in.shape
    shard = first_in.shape[0]
    local_tok = 2 * half
    slab_rows = PLANE * shard
    ups, downs = slab_outs[:steps], slab_outs[steps:]
    mate = {"tensor": 1 - core}

    first = Gather(first_in, first_all, (first_local, first_ls, first_lr, first_ps, first_pr), dp, lines)
    extra = Gather(extra_in, extra_all, (extra_local, extra_ls, extra_lr, extra_ps, extra_pr), dp, lines)
    outer = Gather(out_in, out_t, (out_local, out_ls, out_lr, out_ps, out_pr), dp, lines)

    token_rows = lambda c: pl.ds(pl.multiple_of(c * half, half), half)
    x_keep = pltpu.make_async_copy(x_in, x_all.at[token_rows(core)], x_local)
    x_copy = pltpu.make_async_remote_copy(
        src_ref=x_in, dst_ref=x_all.at[token_rows(core)], send_sem=x_send, recv_sem=x_recv,
        device_id=mate, device_id_type=MESH)
    shard_rows = lambda j: pl.ds(pl.multiple_of(j * shard, shard), shard)

    def spread(which, bits):
        there = lax.rem(plane_partner(dp, bits), PLANE)
        return pltpu.make_async_remote_copy(
            src_ref=ff_in.at[which, there], dst_ref=own_out.at[which, shard_rows(j_at)],
            send_sem=spread_send.at[which, bits - 1], recv_sem=spread_recv.at[which, bits - 1],
            device_id={"dp": plane_partner(dp, bits)}, device_id_type=MESH)

    def spread_keep(which):
        return pltpu.make_async_copy(ff_in.at[which, j_at], own_out.at[which, shard_rows(j_at)], spread_local.at[which])

    def hop(which, sign, step):
        way = (1 - sign) // 2
        outs = ups if sign == 1 else downs
        return pltpu.make_async_remote_copy(
            src_ref=(own_out if step == 0 else outs[step - 1]).at[which], dst_ref=outs[step].at[which],
            send_sem=hop_send.at[which, way, step], recv_sem=hop_recv.at[which, way, step],
            device_id={"dp": dp + sign * PLANE}, device_id_type=MESH)

    def late_hop(index, sign):
        way = (1 - sign) // 2
        return pltpu.make_async_remote_copy(
            src_ref=(ups if sign == 1 else downs)[steps - 1].at[LATE[index]],
            dst_ref=(late_up if sign == 1 else late_down).at[index],
            send_sem=late_send.at[index, way], recv_sem=late_recv.at[index, way],
            device_id={"dp": dp + sign * PLANE}, device_id_type=MESH)

    for one in (first, extra, outer):
        one.local().start()
    x_keep.start()
    for which in range(3):
        spread_keep(which).start()
    greet(dp, core, lines)
    x_copy.start()
    for sign in (1, -1):
        first.line_start(sign, 0)
        extra.line_start(sign, 0)
    for bits in range(1, PLANE):
        spread(2, bits).start()
    first.plane_start_own()
    extra.plane_start_own()
    for which in (0, 1):
        for bits in range(1, PLANE):
            spread(which, bits).start()

    x_keep.wait()
    x_copy.wait_recv()
    wide = x_all[...].astype(f32)
    scale = lax.rsqrt(jnp.mean(wide * wide, axis=1, keepdims=True) + EPS)

    def hop_start(which):
        spread_keep(which).wait()
        for bits in range(1, PLANE):
            spread(which, bits).wait_recv()
        for sign in (1, -1):
            place = z_at if sign == 1 else lines - 1 - z_at

            @pl.when(place < lines - 1)
            def _():
                hop(which, sign, 0).start()

    for step in range(lines - 1):
        for sign in (1, -1):
            first.arrived(sign, step)
            extra.arrived(sign, step)
        if step == 0:
            hop_start(2)
    hop_start(0)
    hop_start(1)
    first.local().wait()
    extra.local().wait()
    for sign in (1, -1):
        outer.line_start(sign, 0)
    outer.plane_start_own()
    extra.plane_wait_recv()
    first.plane_wait_recv()
    keep = pltpu.make_async_copy(first_all, first_out, keep_sem)
    keep.start()
    small = extra_all[0:16, :].astype(f32)
    for owner in range(1, lines * PLANE):
        small = small + extra_all[16 * owner : 16 * (owner + 1), :].astype(f32)
    rows_out[...] = small
    normed[...] = (x_all[...].astype(f32) * scale * small[0:1, :]).astype(bf16)
    normed_out[...] = normed[...]
    columns = first_all.shape[1]
    q_width = columns - 256
    cosines, sines = cos_in[...], sin_in[...]

    def project(at, count):
        part = dot_nn(normed[...], first_all[:, at : at + count])
        return part + small[2:3, at : at + count]

    def turned(part):
        return (part * cosines + pltpu.roll(part, 64, 1) * sines).astype(bf16)

    both = project(q_width, 256)
    pair[:, 0:128] = turned(both[:, 0:128])
    pair[:, 128:256] = both[:, 128:256].astype(bf16)
    member = lax.rem(dp, members)
    tree_rows = lambda m: pl.ds(pl.multiple_of(m * local_tok, local_tok), local_tok)
    partner = lax.rem(line_partner(dp), members)
    pair_keep = pltpu.make_async_copy(pair, tree_out.at[tree_rows(member)], pair_local)
    pair_keep.start()

    def pair_copy(bits, forward=False):
        at = tree_rows(partner if forward else member)
        index = PLANE + bits - 1 if forward else bits
        return pltpu.make_async_remote_copy(
            src_ref=tree_out.at[at] if forward else pair, dst_ref=tree_out.at[at],
            send_sem=pair_send.at[index], recv_sem=pair_recv.at[index],
            device_id={"dp": plane_partner(dp, bits) if bits else line_partner(dp)}, device_id_type=MESH)

    for bits in range(PLANE):
        pair_copy(bits).start()
    for at in range(0, q_width, 256):
        part = project(at, 256)
        q_out[:, at : at + 128] = turned(part[:, 0:128])
        q_out[:, at + 128 : at + 256] = turned(part[:, 128:256])
    pltpu.make_async_remote_copy(
        src_ref=pair, dst_ref=tree_out.at[tree_rows(partner)], send_sem=pair_send.at[0],
        recv_sem=pair_recv.at[0], device_id={"dp": line_partner(dp)}, device_id_type=MESH).wait_recv()
    for bits in range(1, PLANE):
        pair_copy(bits, True).start()
    for step in range(lines - 1):
        for sign in (1, -1):
            outer.arrived(sign, step)
    for step in range(steps):
        for which in (2, 0, 1):
            for sign in (1, -1):
                place = z_at if sign == 1 else lines - 1 - z_at

                @pl.when(place >= step + 1)
                def _():
                    hop(which, sign, step).wait_recv()
                    if step + 1 < steps:

                        @pl.when(place < lines - 1)
                        def _():
                            hop(which, sign, step + 1).start()

                    elif which in LATE:

                        @pl.when(place < lines - 1)
                        def _():
                            late_hop(LATE.index(which), sign).start()

    for bits in range(1, PLANE):
        pair_copy(bits).wait_recv()
        pair_copy(bits, True).wait_recv()
    outer.plane_wait_recv()
    for index in range(len(LATE)):
        for sign in (1, -1):
            place = z_at if sign == 1 else lines - 1 - z_at

            @pl.when(place >= lines - 2)
            def _():
                late_hop(index, sign).wait_recv()

            @pl.when((place >= lines - 3) & (place < lines - 1))
            def _():
                late_hop(index, sign).wait_send()

    for one in (first, extra, outer):
        one.finish()
    outer.local().wait()
    x_copy.wait_send()
    keep.wait()
    pair_keep.wait()
    for bits in range(PLANE):
        pair_copy(bits).wait_send()
        if bits:
            pair_copy(bits, True).wait_send()
    for which in range(3):
        for bits in range(1, PLANE):
            spread(which, bits).wait_send()
        for sign in (1, -1):
            for step in range(steps):
                place = z_at if sign == 1 else lines - 1 - z_at

                @pl.when((place >= step) & (place < lines - 1))
                def _():
                    hop(which, sign, step).wait_send()


def front(ff_blocks, first, out_t, extra, x, cosines, sines, lines, members):
    bf16, f32 = jnp.bfloat16, jnp.float32
    half, width = x.shape
    local_tok = 2 * half
    shard, columns = first.shape
    block = ff_blocks.shape[-1]
    q_width = out_t.shape[1]
    count = lines * PLANE
    steps = max(lines - 3, 1)
    anywhere = pl.BlockSpec(memory_space=pl.ANY)
    inside = pl.BlockSpec(memory_space=pltpu.VMEM)
    dma = pltpu.SemaphoreType.DMA
    slab = jax.ShapeDtypeStruct((3, PLANE * shard, block), bf16)
    gather_sems = [dma, dma((2, lines)), dma((2, lines)), dma((PLANE - 1, lines)), dma((PLANE - 1, lines))]
    return pl.pallas_call(
        functools.partial(front_kernel, lines=lines, members=members, steps=steps),
        out_shape=(slab,) * (1 + 2 * steps)
        + (jax.ShapeDtypeStruct((len(LATE), PLANE * shard, block), bf16),) * 2
        + (
            jax.ShapeDtypeStruct((width, columns), bf16),
            jax.ShapeDtypeStruct((width, q_width), bf16),
            jax.ShapeDtypeStruct((local_tok, q_width), bf16),
            jax.ShapeDtypeStruct((members * local_tok, 256), bf16),
            jax.ShapeDtypeStruct((local_tok, width), bf16),
            jax.ShapeDtypeStruct((16, width), f32),
        ),
        in_specs=[anywhere] * 5 + [inside] * 2,
        out_specs=(anywhere,) * (3 + 2 * steps) + (anywhere, anywhere, inside, anywhere, inside, inside),
        scratch_shapes=[
            pltpu.VMEM((width, columns), bf16), pltpu.VMEM((16 * count, width), bf16),
            pltpu.VMEM((local_tok, width), bf16), pltpu.VMEM((local_tok, width), bf16),
            pltpu.VMEM((local_tok, 256), bf16),
        ]
        + gather_sems * 3
        + [
            dma((3,)), dma((3, PLANE - 1)), dma((3, PLANE - 1)), dma((3, 2, steps)), dma((3, 2, steps)),
            dma, dma, dma, dma, dma, dma((2 * PLANE - 1,)), dma((2 * PLANE - 1,)),
            dma((len(LATE), 2)), dma((len(LATE), 2)),
        ],
        compiler_params=pltpu.CompilerParams(vmem_limit_bytes=56 << 20, collective_id=1, has_side_effects=True),
        name="front",
        cost_estimate=pl.CostEstimate(flops=2 * local_tok * width * columns, bytes_accessed=30 << 20, transcendentals=0),
    )(ff_blocks, first, out_t, extra, x, cosines, sines)


def ff_kernel(
    *refs, tile_h, tile_n, tile_m, lines,
):
    early = lines - 3
    x_in, cot_in, cot_came, slab = refs[:4]
    ups, downs = refs[4 : 4 + early], refs[4 + early : 4 + 2 * early]
    late_up, late_down, mid_up, mid_down, last_up, last_down = refs[4 + 2 * early : 10 + 2 * early]
    cots = [cot_in] + [cot_came.at[k] for k in range(PLANE - 1)]
    (
        dx_out, y_own, y_other, parts_out, carried_up, carried_down,
        x_all, cot_all, gate_w, up_w, down_w, prod, gate_g, up_g, far, near, back, y_stage,
        x_send, x_recv, half_send, half_recv, fwd_send, fwd_recv, pair_send, pair_recv, dx_send, dx_recv,
        x_load, cot_load, cot_send, cot_recv, weight_sem, hop_send, hop_recv, y_keep, y_send, y_recv,
        out_sem, first_send, first_recv,
    ) = refs[10 + 2 * early :]
    bf16 = jnp.bfloat16
    half = x_in.shape[0]
    width = x_in.shape[1]
    block = gate_w.shape[1]
    chunk = 2 * half
    dp = lax.axis_index("dp")
    core = lax.axis_index("tensor")
    chip = [None] + [{"dp": plane_partner(dp, bits)} for bits in range(1, PLANE)]
    mate = {"tensor": 1 - core}
    rows = lambda k, r, n=1: pl.ds((2 * k + r) * half, n * half)

    z_at = dp // PLANE
    slab_rows = width // lines
    weights = (gate_w, up_w, down_w)
    grads_of = weights
    down_y = down_w
    ways = ((1, 0), (-1, 1))
    place_of = lambda sign: z_at if sign == 1 else lines - 1 - z_at
    place_rows = lambda z: pl.ds(pl.multiple_of(z * slab_rows, slab_rows), slab_rows)

    def second_to_last(which, way):
        if which == 1:
            return (mid_up, mid_down)[way]
        return (late_up, late_down)[way].at[LATE.index(which)]

    def weight_loads(which, act):
        for sign, way in ways:
            pieces = [piece.at[which] for piece in (ups, downs)[way]] + [second_to_last(which, way)]
            if which == 2:
                pieces.append((last_up, last_down)[way])
            for step, piece in enumerate(pieces):

                @pl.when(place_of(sign) >= step + 1)
                def _():
                    act(pltpu.make_async_copy(
                        piece, weights[which].at[place_rows(z_at - sign * (step + 1))],
                        weight_sem.at[which, 1 + way * (lines - 1) + step]))

        act(pltpu.make_async_copy(slab.at[which], weights[which].at[place_rows(z_at)], weight_sem.at[which, 0]))

    def last_hop(which, sign, way):
        origin = 0 if sign == 1 else lines - 1
        return pltpu.make_async_remote_copy(
            src_ref=second_to_last(which, way),
            dst_ref=weights[which].at[pl.ds(origin * slab_rows, slab_rows)],
            send_sem=hop_send.at[which, way], recv_sem=hop_recv.at[which, way],
            device_id={"dp": dp + sign * PLANE}, device_id_type=MESH)

    def weight_wait(which):
        weight_loads(which, lambda copy: copy.wait())
        for sign, way in ways if which < 2 else ():

            @pl.when(place_of(sign) == lines - 1)
            def _():
                last_hop(which, sign, way).wait_recv()

    x_keep = pltpu.make_async_copy(x_in, x_all.at[rows(0, 0)], x_load)
    x_keep.start()

    def cot_keep(k):
        return pltpu.make_async_copy(cots[k], cot_all.at[rows(k, 0)], cot_load.at[k])

    def cot_copy(k):
        return pltpu.make_async_remote_copy(
            src_ref=cots[k], dst_ref=cot_all.at[rows(k, 1)], send_sem=cot_send.at[k], recv_sem=cot_recv.at[k],
            device_id=mate, device_id_type=MESH)

    for k in range(PLANE):
        cot_keep(k).start()
    for which in (2, 0, 1):
        weight_loads(which, lambda copy: copy.start())
    greet(dp, core, lines)
    for which in (0, 1):
        for sign, way in ways:

            @pl.when(place_of(sign) == lines - 2)
            def _():
                last_hop(which, sign, way).start()

    def x_copy(k):
        return pltpu.make_async_remote_copy(
            src_ref=x_in, dst_ref=x_all.at[rows(k, 0) if k else rows(0, 1)],
            send_sem=x_send.at[k], recv_sem=x_recv.at[k],
            device_id=chip[k] if k else mate, device_id_type=MESH)

    def x_half(k):
        at = lambda j: pl.ds(2 * j * half + (k - 1) * (half // 2), half // 2)
        return pltpu.make_async_remote_copy(
            src_ref=x_all.at[at(PLANE - 1 - k)], dst_ref=x_all.at[at(PLANE - 1)],
            send_sem=half_send.at[k - 1], recv_sem=half_recv.at[k - 1],
            device_id=chip[k], device_id_type=MESH)

    def x_forward(k):
        return pltpu.make_async_remote_copy(
            src_ref=x_all.at[rows(k, 0)], dst_ref=x_all.at[rows(k, 1)],
            send_sem=fwd_send.at[k - 1], recv_sem=fwd_recv.at[k - 1],
            device_id=mate, device_id_type=MESH)

    def pair_copy(k):
        return pltpu.make_async_remote_copy(
            src_ref=far.at[k], dst_ref=near.at[k],
            send_sem=pair_send.at[k], recv_sem=pair_recv.at[k],
            device_id=mate, device_id_type=MESH)

    def dx_copy(k):
        return pltpu.make_async_remote_copy(
            src_ref=near.at[k], dst_ref=back.at[k - 1],
            send_sem=dx_send.at[k - 1], recv_sem=dx_recv.at[k - 1],
            device_id=chip[k], device_id_type=MESH)

    x_copy(0).start()
    x_copy(1).start()
    x_copy(2).start()
    for k in range(PLANE):
        cot_copy(k).start()
    for k in range(PLANE):
        cot_keep(k).wait()
        cot_copy(k).wait_recv()
    weight_wait(2)

    @pl.loop(0, PLANE)
    def _(k):
        at = pl.ds(pl.multiple_of(k * chunk, chunk), chunk)

        @pl.loop(0, block // tile_h)
        def _(t):
            cols = pl.ds(pl.multiple_of(t * tile_h, tile_h), tile_h)
            up_g[at, cols] = dot_nn(cot_all[at, :], down_w[:, cols]).astype(bf16)

    def gate_part(k):
        at = rows(k, 0, 2)

        @pl.loop(0, block // tile_h)
        def _(t):
            cols = pl.ds(pl.multiple_of(t * tile_h, tile_h), tile_h)
            gate_g[at, cols] = dot_nn(x_all[at, :], gate_w[:, cols]).astype(bf16)

    def up_part(k):
        at = rows(k, 0, 2)

        @pl.loop(0, block // tile_h)
        def _(t):
            cols = pl.ds(pl.multiple_of(t * tile_h, tile_h), tile_h)
            up = dot_nn(x_all[at, :], up_w[:, cols])
            gate = gate_g[at, cols].astype(jnp.float32)
            pg = up_g[at, cols].astype(jnp.float32)
            sig = 0.5 * jnp.tanh(0.5 * gate) + 0.5
            silu = gate * sig
            prod[at, cols] = (silu * up).astype(bf16)
            up_g[at, cols] = (pg * silu).astype(bf16)
            gate_g[at, cols] = (pg * up * (sig + silu * (1.0 - sig))).astype(bf16)

    def dx_half(k, r):
        at = rows(k, r)

        @pl.loop(0, width // tile_n)
        def _(t):
            cols = pl.ds(pl.multiple_of(t * tile_n, tile_n), tile_n)
            part = dot_nt(gate_g[at, :], gate_w[cols, :]) + dot_nt(up_g[at, :], up_w[cols, :])
            if r:
                far[k, :, cols] = part.astype(bf16)
            else:
                near[k, :, cols] = (part + near[k, :, cols].astype(jnp.float32)).astype(bf16)

    def dx_first(k):
        dx_half(k, 1)
        pair_copy(k).start()

    def dx_second(k):
        pair_copy(k).wait_recv()
        dx_half(k, 0)
        if k:
            dx_copy(k).start()

    def y_local(k):
        return pltpu.make_async_copy(y_stage.at[pl.ds(0, half)], y_own.at[k], y_keep)

    def y_copy(k):
        return pltpu.make_async_remote_copy(
            src_ref=y_stage.at[pl.ds(half, half)], dst_ref=y_other.at[k],
            send_sem=y_send.at[k], recv_sem=y_recv.at[k], device_id=mate, device_id_type=MESH)

    def y_part(k):
        if k:
            y_local(k - 1).wait()
            y_copy(k - 1).wait_send()

        @pl.loop(0, width // tile_n)
        def _(t):
            cols = pl.ds(pl.multiple_of(t * tile_n, tile_n), tile_n)
            y_stage[:, cols] = dot_nt(prod[rows(k, 0, 2), :], down_y[cols, :]).astype(bf16)

        y_local(k).start()
        y_copy(k).start()

    x_keep.wait()
    x_copy(0).wait_recv()
    weight_wait(0)
    gate_part(0)
    for k in (1, 2):
        x_copy(k).wait_recv()
        x_forward(k).start()
    for k in (1, 2):
        x_half(k).start()
    x_forward(1).wait_recv()
    gate_part(1)
    x_forward(2).wait_recv()
    gate_part(2)
    for k in (1, 2):
        x_half(k).wait_recv()
    x_forward(3).start()
    weight_wait(1)
    up_part(0)
    up_part(1)
    x_forward(3).wait_recv()
    gate_part(3)
    up_part(2)
    up_part(3)

    def first_hop(which, sign, way):
        at = pl.ds((lines - 1) * slab_rows if sign == 1 else 0, slab_rows)
        return pltpu.make_async_remote_copy(
            src_ref=grads_of[which].at[at], dst_ref=(carried_up, carried_down)[way].at[which],
            send_sem=first_send.at[which, way], recv_sem=first_recv.at[which, way],
            device_id={"dp": dp + sign * PLANE}, device_id_type=MESH)

    def out_copies(which, act):
        for z in range(lines):
            at = pl.ds(z * slab_rows, slab_rows)
            act(pltpu.make_async_copy(grads_of[which].at[at], parts_out.at[which, z], out_sem.at[which, z]))

    def weight_grad(which, tokens, grad):
        @pl.loop(0, width // tile_m)
        def _(m):
            at = pl.ds(pl.multiple_of(m * tile_m, tile_m), tile_m)
            grads_of[which][at, :] = dot_nn(tokens[:, at].T, grad[...]).astype(bf16)

        for sign, way in ways:

            @pl.when(place_of(sign) == 0)
            def _():
                first_hop(which, sign, way).start()

        out_copies(which, lambda copy: copy.start())

    for k in range(PLANE):
        y_part(k)
    weight_grad(2, cot_all, prod)
    dx_first(1)
    dx_first(2)
    dx_second(1)
    dx_first(3)
    dx_second(2)
    dx_first(0)
    dx_second(3)
    dx_second(0)
    weight_grad(0, x_all, gate_g)
    weight_grad(1, x_all, up_g)

    for k in range(1, PLANE):
        dx_copy(k).wait_recv()
    total = near[0].astype(jnp.float32)
    for k in range(PLANE - 1):
        total = total + back[k].astype(jnp.float32)
    dx_out[...] = total

    for k in range(PLANE):
        if k < PLANE - 1:
            x_copy(k).wait_send()
        if k in (1, 2):
            x_half(k).wait_send()
        pair_copy(k).wait_send()
        if k:
            x_forward(k).wait_send()
            dx_copy(k).wait_send()
    y_local(PLANE - 1).wait()
    y_copy(PLANE - 1).wait_send()
    for k in range(PLANE):
        y_copy(k).wait_recv()
    for which in range(3):
        out_copies(which, lambda copy: copy.wait())
        for sign, way in ways:
            if which < 2:

                @pl.when(place_of(sign) == lines - 2)
                def _():
                    last_hop(which, sign, way).wait_send()

            @pl.when(place_of(sign) == 0)
            def _():
                first_hop(which, sign, way).wait_send()

            @pl.when(place_of(sign) == 1)
            def _():
                first_hop(which, sign, way).wait_recv()

    for k in range(PLANE):
        cot_copy(k).wait_send()


def feed_forward(x, cot, cot_came, slabs, lines, tile_h=384, tile_n=512, tile_m=256):
    half, width = x.shape
    block = slabs[0].shape[-1]
    slab_rows = width // lines
    tokens = 2 * PLANE * half
    bf16 = jnp.bfloat16
    anywhere = pl.BlockSpec(memory_space=pl.ANY)
    dma = pltpu.SemaphoreType.DMA
    slab = jax.ShapeDtypeStruct((3, slab_rows, block), bf16)
    return pl.pallas_call(
        functools.partial(ff_kernel, tile_h=tile_h, tile_n=tile_n, tile_m=tile_m, lines=lines),
        out_shape=(
            jax.ShapeDtypeStruct((half, width), jnp.float32),
            jax.ShapeDtypeStruct((PLANE, half, width), bf16),
            jax.ShapeDtypeStruct((PLANE, half, width), bf16),
            jax.ShapeDtypeStruct((3, lines, slab_rows, block), bf16),
            slab,
            slab,
        ),
        in_specs=[anywhere] * (3 + len(slabs)),
        out_specs=(pl.BlockSpec(memory_space=pltpu.VMEM),) + (anywhere,) * 5,
        scratch_shapes=[
            pltpu.VMEM((tokens, width), bf16), pltpu.VMEM((tokens, width), bf16),
            pltpu.VMEM((width, block), bf16), pltpu.VMEM((width, block), bf16), pltpu.VMEM((width, block), bf16),
            pltpu.VMEM((tokens, block), bf16), pltpu.VMEM((tokens, block), bf16), pltpu.VMEM((tokens, block), bf16),
            pltpu.VMEM((PLANE, half, width), bf16), pltpu.VMEM((PLANE, half, width), bf16), pltpu.VMEM((PLANE - 1, half, width), bf16),
            pltpu.VMEM((2 * half, width), bf16),
            dma((PLANE - 1,)), dma((PLANE - 1,)), dma((2,)), dma((2,)), dma((PLANE - 1,)), dma((PLANE - 1,)), dma((PLANE,)), dma((PLANE,)),
            dma((PLANE - 1,)), dma((PLANE - 1,)), dma, dma((PLANE,)), dma((PLANE,)), dma((PLANE,)), dma((3, 2 * lines)), dma((3, 2)), dma((3, 2)), dma, dma((PLANE,)), dma((PLANE,)),
            dma((3, lines)), dma((3, 2)), dma((3, 2)),
        ],
        compiler_params=pltpu.CompilerParams(vmem_limit_bytes=62 << 20, collective_id=0, has_side_effects=True),
        name="feed_forward",
        cost_estimate=pl.CostEstimate(flops=18 * tokens * width * block, bytes_accessed=60 << 20, transcendentals=tokens * block),
    )(x, cot, cot_came, *slabs)


def back_kernel(
    dkv_in, dq_in, cos_in, sin_in, normed_in, first_in, out_part, x_in, rows_in, gain_row_in, middle_grad_in,
    ff_in, carried_up, carried_down,
    input_grad_out, sums_out, small_out, ff_out,
    kv_own, kv_other, kv_plane, kv_merged, kv_line, grads, part_q, part_kv, own_o,
    recv_q, recv_kv, recv_o, line_q, line_kv, line_o, from_q, from_kv, from_o,
    far, near, small_own, small_mate, small_plane, small_line,
    own_buf, recv_buf, first_buf, total_buf,
    kv_local, kv_send, kv_recv, kv_line_send, kv_line_recv,
    plane_send, plane_recv, line_send, line_recv, own_o_sem,
    mate_send, mate_recv, small_mate_sem, small_plane_send, small_plane_recv, small_line_send, small_line_recv,
    load_sem, own_sem, carry_sem, hop_send, hop_recv, spread_local, spread_send, spread_recv,
    *, lines, members, scale,
):
    bf16, f32 = jnp.bfloat16, jnp.float32
    dp = lax.axis_index("dp")
    core = lax.axis_index("tensor")
    z_at, j_at = dp // PLANE, lax.rem(dp, PLANE)
    half, width = x_in.shape
    local_tok = 2 * half
    slab_rows = width // lines
    shard = slab_rows // PLANE
    q_width = dq_in.shape[1]
    block = total_buf.shape[-1]
    mate = {"tensor": 1 - core}
    chip = [None] + [{"dp": plane_partner(dp, bits)} for bits in range(1, PLANE)]
    there = [j_at] + [lax.rem(plane_partner(dp, bits), PLANE) for bits in range(1, PLANE)]
    side = lax.rem(z_at, 2) * PLANE
    other_side = PLANE - side
    member = lax.rem(dp, members)
    del member
    ways = ((1, 0), (-1, 1))
    place_of = lambda sign: z_at if sign == 1 else lines - 1 - z_at
    tree_rows = lambda m: pl.ds(pl.multiple_of(m * local_tok, local_tok), local_tok)

    kv_loads = [
        pltpu.make_async_copy(dkv_in.at[tree_rows(side + j_at)], kv_own, kv_local.at[0]),
        pltpu.make_async_copy(dkv_in.at[tree_rows(other_side + j_at)], kv_other, kv_local.at[1]),
    ]
    for load in kv_loads:
        load.start()
    o_load = pltpu.make_async_copy(out_part.at[:, j_at], own_o, own_o_sem)
    o_load.start()

    def slab_load(which, sign, way, step):
        target = lines - 1 - step + place_of(sign)
        slab = target if sign == 1 else lines - 1 - target
        return pltpu.make_async_copy(ff_in.at[which, slab], own_buf.at[which, way], load_sem.at[which, way])

    def own_load(which):
        return pltpu.make_async_copy(ff_in.at[which, z_at], total_buf.at[which], own_sem.at[which])

    def carry_load(which, sign, way):
        return pltpu.make_async_copy(
            (carried_up if sign == 1 else carried_down).at[which], first_buf.at[which, way], carry_sem.at[which, way])

    order = (2, 0, 1)
    for which in order:
        for sign, way in ways:
            carry_load(which, sign, way).start()

            @pl.when((place_of(sign) >= 1) & (place_of(sign) <= 2))
            def _():
                slab_load(which, sign, way, 2).start()

        own_load(which).start()

    barrier = pltpu.get_barrier_semaphore()
    for bits in range(1, PLANE):
        pl.semaphore_signal(barrier, inc=1, device_id=chip[bits], device_id_type=MESH)
    pl.semaphore_signal(barrier, inc=1, device_id=mate, device_id_type=MESH)
    for apart in range(1, lines):
        pl.semaphore_signal(
            barrier, inc=1, device_id={"dp": lax.rem(z_at + apart, lines) * PLANE + j_at}, device_id_type=MESH)
    pl.semaphore_wait(barrier, PLANE + lines - 1)

    def kv_copy(bits, part):
        at = tree_rows((side if part == 0 else other_side) + there[bits])
        return pltpu.make_async_remote_copy(
            src_ref=dkv_in.at[at], dst_ref=kv_plane.at[bits - 1, part],
            send_sem=kv_send.at[bits - 1, part], recv_sem=kv_recv.at[bits - 1, part],
            device_id=chip[bits], device_id_type=MESH)

    for part in (1, 0):
        for bits in range(1, PLANE):
            kv_copy(bits, part).start()

    def hop(which, sign, way, step, first_place=False):
        slab = lines - 1 - step if sign == 1 else step
        carried = first_buf.at[which, way] if step == 2 else recv_buf.at[which, way, step - 3]
        return pltpu.make_async_remote_copy(
            src_ref=ff_in.at[which, slab] if first_place else carried, dst_ref=recv_buf.at[which, way, step - 2],
            send_sem=hop_send.at[which, way, step - 2], recv_sem=hop_recv.at[which, way, step - 2],
            device_id={"dp": dp + sign * PLANE}, device_id_type=MESH)

    def hop_step(which, step):
        for sign, way in ways:
            place = place_of(sign)
            if step == 2:
                carry_load(which, sign, way).wait()

            @pl.when(place == 0)
            def _():
                hop(which, sign, way, step, True).start()

            @pl.when((place >= 1) & (place <= step))
            def _():
                if step > 2:
                    hop(which, sign, way, step - 1).wait_recv()
                slab_load(which, sign, way, step).wait()
                mine = own_buf[which, way].astype(f32)
                if step == 2:
                    first_buf[which, way] = (mine + first_buf[which, way].astype(f32)).astype(bf16)
                else:
                    recv_buf[which, way, step - 3] = (mine + recv_buf[which, way, step - 3].astype(f32)).astype(bf16)
                hop(which, sign, way, step).start()

            if step < lines - 2:

                @pl.when((place >= 1) & (place <= step + 1))
                def _():
                    slab_load(which, sign, way, step + 1).start()

    for which in order:
        hop_step(which, 2)

    groups = {
        "o": (0, out_part, own_o, recv_o, line_o, from_o, q_width + 256, q_width),
        "q": (1, part_q, None, recv_q, line_q, from_q, 0, q_width),
        "kv": (2, part_kv, None, recv_kv, line_kv, from_kv, q_width, 256),
    }

    def plane_copy(name, bits):
        index, part, _, recv, *_ = groups[name]
        return pltpu.make_async_remote_copy(
            src_ref=part.at[:, there[bits]], dst_ref=recv.at[bits - 1],
            send_sem=plane_send.at[index, bits - 1], recv_sem=plane_recv.at[index, bits - 1],
            device_id=chip[bits], device_id_type=MESH)

    def line_copy(name, apart):
        index, _, _, _, line, came, *_ = groups[name]
        target = lax.rem(z_at + apart, lines)
        return pltpu.make_async_remote_copy(
            src_ref=line.at[target], dst_ref=came.at[apart - 1],
            send_sem=line_send.at[index, apart - 1], recv_sem=line_recv.at[index, apart - 1],
            device_id={"dp": target * PLANE + j_at}, device_id_type=MESH)

    def plane_start(name):
        for bits in range(1, PLANE):
            plane_copy(name, bits).start()

    def plane_sum(name):
        _, part, own, recv, line, *_ = groups[name]
        for bits in range(1, PLANE):
            plane_copy(name, bits).wait_recv()
        for z in range(lines):
            total = (part[z, j_at] if own is None else own[z]).astype(f32)
            for bits in range(1, PLANE):
                total = total + recv[bits - 1, z].astype(f32)
            line[z] = total.astype(bf16)
        for apart in range(1, lines):
            line_copy(name, apart).start()

    def line_sum(name):
        *_, line, came, at, size = groups[name]
        for apart in range(1, lines):
            line_copy(name, apart).wait_recv()
        total = line[z_at].astype(f32)
        for apart in range(1, lines):
            total = total + came[apart - 1].astype(f32)
        sums_out[:, at : at + size] = total

    plane_start("o")
    cosines, sines = cos_in[...], sin_in[...]

    def turned_back(part):
        return (part * cosines - pltpu.roll(part, 64, 1) * sines).astype(bf16)

    grads[:, 0:q_width] = dq_in[...]

    def weight_part(part, at, size):
        for z in range(lines):
            turned = normed_in[:, z * slab_rows : (z + 1) * slab_rows].T
            tile = dot_nn(turned, grads[:, at : at + size]).astype(bf16)
            for j in range(PLANE):
                part[z, j] = tile[j * shard : (j + 1) * shard]

    weight_part(part_q, 0, q_width)
    plane_start("q")

    for load in kv_loads:
        load.wait()
    for bits in range(1, PLANE):
        kv_copy(bits, 1).wait_recv()
    total = kv_other[...].astype(f32)
    for bits in range(1, PLANE):
        total = total + kv_plane[bits - 1, 1].astype(f32)
    kv_merged[...] = total.astype(bf16)
    kv_across = pltpu.make_async_remote_copy(
        src_ref=kv_merged, dst_ref=kv_line, send_sem=kv_line_send, recv_sem=kv_line_recv,
        device_id={"dp": line_partner(dp)}, device_id_type=MESH)
    kv_across.start()
    for step in range(3, lines - 1):
        hop_step(order[0], step)
    for bits in range(1, PLANE):
        kv_copy(bits, 0).wait_recv()
    kv_across.wait_recv()
    total = kv_own[...].astype(f32) + kv_line[...].astype(f32)
    for bits in range(1, PLANE):
        total = total + kv_plane[bits - 1, 0].astype(f32)
    grads[:, q_width : q_width + 128] = turned_back(total[:, 0:128] * scale)
    grads[:, q_width + 128 :] = total[:, 128:256].astype(bf16)
    weight_part(part_kv, q_width, 256)
    plane_start("kv")

    def normed_grad(c):
        at = pl.ds(pl.multiple_of(c * half, half), half)
        return dot_nt(grads[at, :], first_in[...])

    far[...] = normed_grad(1 - core).astype(bf16)
    mate_copy = pltpu.make_async_remote_copy(
        src_ref=far, dst_ref=near, send_sem=mate_send, recv_sem=mate_recv, device_id=mate, device_id_type=MESH)
    mate_copy.start()
    mine = normed_grad(core)
    o_load.wait()
    plane_sum("o")
    mate_copy.wait_recv()
    mine = mine + near[...].astype(f32)
    wide = x_in[...].astype(f32)
    norm = lax.rsqrt(jnp.mean(wide * wide, axis=1, keepdims=True) + EPS)
    z_own = wide * norm
    w = mine * gain_row_in[...]
    back = norm * (w - z_own * jnp.mean(w * z_own, axis=1, keepdims=True))
    input_grad_out[...] = (middle_grad_in[...] + back).astype(bf16)
    bias = jnp.sum(grads[...].astype(f32), axis=0, keepdims=True)
    small_own[...] = jnp.concatenate(
        [
            jnp.sum(mine * z_own, axis=0, keepdims=True),
            rows_in[...],
            jnp.concatenate([bias, jnp.zeros((1, width - q_width - 256), f32)], axis=1),
            jnp.zeros((5, width), f32),
        ],
        axis=0,
    )
    small_copy = pltpu.make_async_remote_copy(
        src_ref=small_own, dst_ref=small_mate, send_sem=small_mate_sem.at[0], recv_sem=small_mate_sem.at[1],
        device_id=mate, device_id_type=MESH)
    small_copy.start()
    for step in range(3, lines - 1):
        hop_step(order[1], step)
    plane_sum("q")
    for step in range(3, lines - 1):
        hop_step(order[2], step)
    plane_sum("kv")

    small_copy.wait_recv()
    gain_rows = lax.broadcasted_iota(jnp.int32, (8, width), 0) < 2
    small_plane[0] = small_own[...] + jnp.where(gain_rows, small_mate[...], 0.0)

    def small_plane_copy(bits):
        return pltpu.make_async_remote_copy(
            src_ref=small_plane.at[0], dst_ref=small_plane.at[bits],
            send_sem=small_plane_send.at[bits - 1], recv_sem=small_plane_recv.at[bits - 1],
            device_id=chip[bits], device_id_type=MESH)

    def small_line_copy(apart):
        return pltpu.make_async_remote_copy(
            src_ref=small_line.at[0], dst_ref=small_line.at[apart],
            send_sem=small_line_send.at[apart - 1], recv_sem=small_line_recv.at[apart - 1],
            device_id={"dp": lax.rem(z_at + apart, lines) * PLANE + j_at}, device_id_type=MESH)

    for bits in range(1, PLANE):
        small_plane_copy(bits).start()
    for bits in range(1, PLANE):
        small_plane_copy(bits).wait_recv()
    total = small_plane[0]
    for bits in range(1, PLANE):
        total = total + small_plane[bits]
    small_line[0] = total
    for apart in range(1, lines):
        small_line_copy(apart).start()
    line_sum("o")
    line_sum("q")
    line_sum("kv")
    for apart in range(1, lines):
        small_line_copy(apart).wait_recv()
    total = small_line[0]
    for apart in range(1, lines):
        total = total + small_line[apart]
    small_out[...] = total

    columns = lambda j: pl.ds(pl.multiple_of(j * block, block), block)

    def spread(which, bits):
        rows = pl.ds(pl.multiple_of(there[bits] * shard, shard), shard)
        return pltpu.make_async_remote_copy(
            src_ref=total_buf.at[which, rows], dst_ref=ff_out.at[which, :, columns(j_at)],
            send_sem=spread_send.at[which, bits - 1], recv_sem=spread_recv.at[which, bits - 1],
            device_id=chip[bits], device_id_type=MESH)

    def spread_keep(which):
        rows = pl.ds(pl.multiple_of(j_at * shard, shard), shard)
        return pltpu.make_async_copy(
            total_buf.at[which, rows], ff_out.at[which, :, columns(j_at)], spread_local.at[which])

    for which in order:
        own_load(which).wait()
        for sign, way in ways:

            @pl.when(place_of(sign) >= 1)
            def _():
                hop(which, sign, way, lines - 2).wait_recv()
                came = recv_buf[which, way, lines - 4].astype(f32)
                total_buf[which] = (total_buf[which].astype(f32) + came).astype(bf16)

        for bits in range(1, PLANE):
            spread(which, bits).start()
        spread_keep(which).start()

    for which in order:
        for bits in range(1, PLANE):
            spread(which, bits).wait_recv()
            spread(which, bits).wait_send()
        spread_keep(which).wait()
        for sign, way in ways:
            for step in range(2, lines - 1):

                @pl.when(place_of(sign) <= step)
                def _():
                    hop(which, sign, way, step).wait_send()

    for bits in range(1, PLANE):
        small_plane_copy(bits).wait_send()
        for part in range(2):
            kv_copy(bits, part).wait_send()
        for name in groups:
            plane_copy(name, bits).wait_send()
    for apart in range(1, lines):
        small_line_copy(apart).wait_send()
        for name in groups:
            line_copy(name, apart).wait_send()
    kv_across.wait_send()
    mate_copy.wait_send()
    small_copy.wait_send()


def finish(dkv, dq, cosines, sines, normed, first, out_part, x, gain_rows, gain_row, middle_grad, ff_parts, up, down, lines, members, scale):
    bf16, f32 = jnp.bfloat16, jnp.float32
    half, width = x.shape
    local_tok = 2 * half
    q_width = dq.shape[1]
    slab_rows = width // lines
    shard = slab_rows // PLANE
    block = ff_parts.shape[-1]
    anywhere = pl.BlockSpec(memory_space=pl.ANY)
    inside = pl.BlockSpec(memory_space=pltpu.VMEM)
    dma = pltpu.SemaphoreType.DMA
    near = PLANE - 1
    vmem = lambda *shape: pltpu.VMEM(shape, bf16)
    wide = lambda *shape: pltpu.VMEM(shape, f32)
    pair = (local_tok, 256)
    return pl.pallas_call(
        functools.partial(back_kernel, lines=lines, members=members, scale=scale),
        out_shape=(
            jax.ShapeDtypeStruct((half, width), bf16),
            jax.ShapeDtypeStruct((shard, 2 * q_width + 256), f32),
            jax.ShapeDtypeStruct((8, width), f32),
            jax.ShapeDtypeStruct((3, shard, PLANE * block), bf16),
        ),
        in_specs=[anywhere] + [inside] * 5 + [anywhere] + [inside] * 4 + [anywhere] * 3,
        out_specs=(inside, inside, inside, anywhere),
        scratch_shapes=[
            vmem(*pair), vmem(*pair), vmem(near, 2, *pair), vmem(*pair), vmem(*pair),
            vmem(local_tok, q_width + 256), vmem(lines, PLANE, shard, q_width), vmem(lines, PLANE, shard, 256), vmem(lines, shard, q_width),
            vmem(near, lines, shard, q_width), vmem(near, lines, shard, 256), vmem(near, lines, shard, q_width),
            vmem(lines, shard, q_width), vmem(lines, shard, 256), vmem(lines, shard, q_width),
            vmem(lines - 1, shard, q_width), vmem(lines - 1, shard, 256), vmem(lines - 1, shard, q_width),
            vmem(half, width), vmem(half, width), wide(8, width), wide(8, width), wide(PLANE, 8, width), wide(lines, 8, width),
            vmem(3, 2, slab_rows, block), vmem(3, 2, lines - 3, slab_rows, block), vmem(3, 2, slab_rows, block), vmem(3, slab_rows, block),
            dma((2,)), dma((near, 2)), dma((near, 2)), dma, dma,
            dma((3, near)), dma((3, near)), dma((3, lines - 1)), dma((3, lines - 1)), dma,
            dma, dma, dma((2,)), dma((near,)), dma((near,)), dma((lines - 1,)), dma((lines - 1,)),
            dma((3, 2)), dma((3,)), dma((3, 2)), dma((3, 2, lines - 3)), dma((3, 2, lines - 3)), dma((3,)), dma((3, near)), dma((3, near)),
        ],
        compiler_params=pltpu.CompilerParams(vmem_limit_bytes=62 << 20, collective_id=2, has_side_effects=True),
        name="back",
        cost_estimate=pl.CostEstimate(flops=6 * local_tok * width * (q_width + 256), bytes_accessed=40 << 20, transcendentals=0),
    )(dkv, dq, cosines, sines, normed, first, out_part, x, gain_rows, gain_row, middle_grad, ff_parts, up, down)


def swap(block, axis, count, bits):
    return lax.ppermute(block, axis, [(i, i ^ bits) for i in range(count)])


def rms_scale(values):
    return lax.rsqrt(jnp.mean(values * values, axis=1, keepdims=True) + EPS)


def norm_back(grad, values, gain):
    scale = rms_scale(values)
    z = values * scale
    w = grad * gain
    gain_grad = jnp.sum(grad * z, axis=0)
    return scale * (w - z * jnp.mean(w * z, axis=1, keepdims=True)), gain_grad


def rope_tables(positions):
    exponents = jnp.arange(64, dtype=jnp.float32) * (2.0 / 128)
    frequency = jnp.power(THETA, -exponents)
    angles = positions.astype(jnp.float32)[:, None] * frequency[None, :]
    cosines, sines = jnp.cos(angles), jnp.sin(angles)
    return (
        jnp.concatenate([cosines, cosines], axis=1),
        jnp.concatenate([-sines, sines], axis=1),
    )


def contract_rows(left, right):
    return lax.dot_general(
        left, right, (((0,), (0,)), ((), ())), preferred_element_type=jnp.float32
    )


def contract_cols(left, right):
    return lax.dot_general(
        left, right, (((1,), (1,)), ((), ())), preferred_element_type=jnp.float32
    )


def matmul(left, right):
    return jnp.dot(left, right, preferred_element_type=jnp.float32)


def attention_plan(segment_ids, parent_ids, dp_index, local_tok):
    members = TREE_TOK // local_tok
    first = dp_index // members * TREE_TOK
    slots = lax.dynamic_slice_in_dim(segment_ids, first, TREE_TOK)[::KB]
    numbers = jnp.arange(parent_ids.shape[0], dtype=jnp.int32)
    parents = jnp.sum(jnp.where(slots[:, None] == numbers[None, :], parent_ids[None, :], 0), axis=1)
    places = jnp.arange(slots.shape[0], dtype=jnp.int32)
    holder = jnp.sum(jnp.where(parents[:, None] == slots[None, :], places[None, :], 0), axis=1)
    starts = dp_index % members * local_tok + QB * jnp.arange(local_tok // QB, dtype=jnp.int32)
    slot = starts // KB
    chosen = slot[:, None] == places[None, :]
    pick = lambda table: jnp.sum(jnp.where(chosen, table[None, :], 0), axis=1)
    in_trunk = starts < TRUNK
    is_leaf = pick(parents) != slots[0]
    chunk = jnp.minimum(starts, TRUNK) // KC
    far = jnp.int32(1 << 20)
    block0 = jnp.where(in_trunk, 2 * chunk, jnp.where(is_leaf, pick(holder), TRUNK // KB))
    block1 = jnp.where(in_trunk, 2 * chunk + 1, slot)
    shift0 = jnp.where(in_trunk, block0 * KB - starts, jnp.where(is_leaf, -far, far))
    shift1 = block1 * KB - starts
    hot = jnp.where(~in_trunk[:, None] & (block0[:, None] == places[None, :]), 1.0, 0.0)
    return jnp.stack([shift0, shift1], axis=1).reshape(-1), hot.reshape(-1)


def on_device(
    dp_size,
    layer_input,
    out_cotangent,
    positions,
    segment_ids,
    parent_ids,
    attention_gain,
    query_weight,
    query_bias,
    key_weight,
    key_bias,
    value_weight,
    value_bias,
    output_weight,
    feedforward_gain,
    gate_weight,
    up_weight,
    down_weight,
):
    bf16, f32 = jnp.bfloat16, jnp.float32
    local_tok = positions.shape[0]
    half_tok, width = layer_input.shape
    shard = attention_gain.shape[0]
    heads, head_dim = query_bias.shape[0], 128
    per_head = query_bias.shape[1]
    q_width = heads * head_dim
    hidden = gate_weight.shape[1]
    block = -(-hidden // (PLANE * 128)) * 128
    lines = dp_size // PLANE
    members = TREE_TOK // local_tok
    dp_index = lax.axis_index("dp")
    core = lax.axis_index("tensor")
    scale = head_dim ** (-0.5)

    def line_route(sign, first, last):
        route = []
        for place in range(first, last + 1):
            z = place if sign == 1 else lines - 1 - place
            route += [(z * PLANE + j, (z + sign) * PLANE + j) for j in range(PLANE)]
        return route

    def by_core(mine):
        other = swap(mine, "tensor", 2, 1)
        first = jnp.where(core == 0, mine, other)
        second = jnp.where(core == 0, other, mine)
        return jnp.concatenate([first, second], axis=0)

    blocked = lambda w: jnp.pad(w, ((0, 0), (0, PLANE * block - hidden))).reshape(shard, PLANE, block).transpose(1, 0, 2)
    ff_blocks = jnp.stack([blocked(gate_weight), blocked(up_weight), blocked(down_weight.T)])
    first_own = jnp.concatenate([query_weight, key_weight, value_weight], axis=1)
    biases = jnp.concatenate([query_bias, key_bias, value_bias], axis=0)
    bias_row = lax.dynamic_update_slice(
        jnp.zeros((heads + 2, head_dim), bf16), biases, (0, dp_index * per_head)
    ).reshape(1, -1)
    gains = lax.dynamic_update_slice(
        jnp.zeros((2, width), bf16), jnp.stack([attention_gain, feedforward_gain]), (0, dp_index * shard)
    )
    extra = jnp.concatenate(
        [gains, jnp.pad(bias_row, ((0, 0), (0, width - bias_row.shape[1]))), jnp.zeros((13, width), bf16)], axis=0
    )
    cosines, sines = rope_tables(positions)
    plan, hot = attention_plan(segment_ids, parent_ids, dp_index, local_tok)
    steps = lines - 3
    outs = front(ff_blocks, first_own, output_weight.T, extra, layer_input, cosines, sines, lines, members)
    slab, ups, downs = outs[0], list(outs[1 : 1 + steps]), list(outs[1 + steps : 1 + 2 * steps])
    late_up, late_down, first_all, out_t, q_rot, tree, normed, rows = outs[1 + 2 * steps :]
    gain_one, gain_two = rows[0:1], rows[1:2]

    attended, lse, middle, normed_two, other, cot_came, *more = attend(
        plan, hot, q_rot, tree, out_t, layer_input, rows, out_cotangent, ups[-1], downs[-1], late_up, late_down,
        lines, members, scale,
    )

    normed_two_grad, y_own, y_other, ff_parts, up_first, down_first = feed_forward(
        normed_two, out_cotangent, cot_came, [slab] + ups + downs + [late_up, late_down] + more, lines
    )

    dq, dtree, middle_grad, gain_two_grad, out_part, layer_output, up_next, down_next = attend_back(
        plan, hot, q_rot, attended, lse, tree, other, out_t, normed_two_grad, middle, out_cotangent, rows, cosines, sines,
        y_own, y_other, ff_parts, up_first, down_first, lines, members, scale,
    )
    input_grad, sums, small, ff_sums = finish(
        dtree, dq, cosines, sines, normed, first_all, out_part, layer_input, gain_two_grad, gain_one,
        middle_grad, ff_parts, up_next, down_next, lines, members, scale,
    )
    ff_sums = ff_sums[:, :, :hidden].astype(f32)
    gains_out = lax.dynamic_slice(small[0:2], (0, dp_index * shard), (2, shard))
    bias_out = lax.dynamic_slice(
        small[2, : (heads + 2) * head_dim].reshape(heads + 2, head_dim), (0, dp_index * per_head), (heads + 2, per_head)
    )
    return (
        layer_output,
        input_grad,
        gains_out[0],
        sums[:, :q_width],
        bias_out[:heads],
        sums[:, q_width : q_width + 128],
        bias_out[heads : heads + 1],
        sums[:, q_width + 128 : q_width + 256],
        bias_out[heads + 1 :],
        sums[:, q_width + 256 :].T,
        gains_out[1],
        ff_sums[0],
        ff_sums[1],
        ff_sums[2].T,
    )


def solution(mesh):
    placed = (
        P(("dp", "tensor"), None),
        P(("dp", "tensor"), None),
        P("dp"),
        P(),
        P(),
        P("dp"),
        P("dp", "tensor"),
        P("tensor", "dp"),
        P("dp", "tensor"),
        P("tensor", "dp"),
        P("dp", "tensor"),
        P("tensor", "dp"),
        P("tensor", "dp"),
        P("dp"),
        P("dp", "tensor"),
        P("dp", "tensor"),
        P("tensor", "dp"),
    )
    return jax.shard_map(
        functools.partial(on_device, mesh.shape["dp"]),
        mesh=mesh,
        in_specs=placed,
        out_specs=(
            P(("dp", "tensor"), None),
            P(("dp", "tensor"), None),
            P("dp"),
            P("dp", "tensor"),
            P("tensor", "dp"),
            P("dp", "tensor"),
            P("tensor", "dp"),
            P("dp", "tensor"),
            P("tensor", "dp"),
            P("tensor", "dp"),
            P("dp"),
            P("dp", "tensor"),
            P("dp", "tensor"),
            P("tensor", "dp"),
        ),
        check_vma=False,
    )
```

```python
import functools

import jax
import jax.numpy as jnp
from jax import lax
from jax.experimental import pallas as pl
from jax.experimental.pallas import tpu as pltpu
from jax.sharding import PartitionSpec as P

EPS = 1e-06
THETA = 10000.0
TREE_TOK = 5120
TRUNK = 2048
PLANE = 4
NEG = -1e30
LATE = (2, 0)
QB=128; KC=512; KB=256
LOG2E=1.4426950408889634

MESH = pl.DeviceIdType.MESH


def dot_nt(a,b): return lax.dot_general(a,b,(((1,),(1,)),((),())),preferred_element_type=jnp.float32)
def dot_nn(a,b): return lax.dot_general(a,b,(((1,),(0,)),((),())),preferred_element_type=jnp.float32)

def plane_partner(dp, bits):
    one = dp + 1 - 2 * lax.rem(dp, 2)
    if bits == 1:
        return one
    two = 2 - 4 * lax.rem(dp // 2, 2)
    return (dp if bits == 2 else one) + two


def line_partner(dp):
    return dp + PLANE - 2 * PLANE * lax.rem(dp // PLANE, 2)


def greet(dp, core, lines):
    z_at = dp // PLANE
    barrier = pltpu.get_barrier_semaphore()
    for bits in range(1, PLANE):
        pl.semaphore_signal(barrier, inc=1, device_id={"dp": plane_partner(dp, bits)}, device_id_type=MESH)
    pl.semaphore_signal(barrier, inc=1, device_id={"tensor": 1 - core}, device_id_type=MESH)

    @pl.when(z_at > 0)
    def _():
        pl.semaphore_signal(barrier, inc=1, device_id={"dp": dp - PLANE}, device_id_type=MESH)

    @pl.when(z_at < lines - 1)
    def _():
        pl.semaphore_signal(barrier, inc=1, device_id={"dp": dp + PLANE}, device_id_type=MESH)

    beside = jnp.minimum(z_at, 1) + jnp.minimum(lines - 1 - z_at, 1)
    pl.semaphore_wait(barrier, PLANE + beside)


def second_block(start):
    return jnp.where(start < TRUNK, start // KC * (KC // KB) + 1, start // KB)


def masked_chunk(tree_ref, other_ref, blk, start):
    at = pl.ds(pl.multiple_of(second_block(start) * KB, KB), KB)
    k = jnp.concatenate([other_ref[blk, :, 0:128], tree_ref[at, 0:128]], axis=0)
    v = jnp.concatenate([other_ref[blk, :, 128:256], tree_ref[at, 128:256]], axis=0)
    return k, v


def attend_kernel(
    info, hot, q_ref, tree_ref, out_t, x_in, rows_in, cot_in, up_in, down_in, late_up, late_down,
    att_out, lse_out, middle_out, normed_out, other_ref, cot_out, mid_up, mid_down, last_up, last_down,
    far, near, pair_send, pair_recv, cot_send, cot_recv, half_send, half_recv, mid_send, mid_recv, last_send, last_recv,
    *, lines, members, scale,
):
    bf16, f32 = jnp.bfloat16, jnp.float32
    dp = lax.axis_index("dp")
    core = lax.axis_index("tensor")
    z_at = dp // PLANE
    half, width = x_in.shape
    local_tok, q_width = q_ref.shape
    heads = q_width // 128
    rows = heads * QB
    c2 = scale * LOG2E
    mate = {"tensor": 1 - core}
    chip = [None] + [{"dp": plane_partner(dp, bits)} for bits in range(1, PLANE)]
    ways = ((1, 0), (-1, 1))
    place_of = lambda sign: z_at if sign == 1 else lines - 1 - z_at

    def mid_hop(sign, way):
        return pltpu.make_async_remote_copy(
            src_ref=(up_in, down_in)[way].at[1], dst_ref=(mid_up, mid_down)[way],
            send_sem=mid_send.at[way], recv_sem=mid_recv.at[way],
            device_id={"dp": dp + sign * PLANE}, device_id_type=MESH)

    def last_hop(sign, way):
        return pltpu.make_async_remote_copy(
            src_ref=(late_up, late_down)[way].at[0], dst_ref=(last_up, last_down)[way],
            send_sem=last_send.at[way], recv_sem=last_recv.at[way],
            device_id={"dp": dp + sign * PLANE}, device_id_type=MESH)

    def cot_copy(bits):
        return pltpu.make_async_remote_copy(
            src_ref=cot_in, dst_ref=cot_out.at[bits - 1], send_sem=cot_send.at[bits - 1], recv_sem=cot_recv.at[bits - 1],
            device_id=chip[bits], device_id_type=MESH)

    def cot_half(bits):
        at = pl.ds((bits - 1) * (half // 2), half // 2)
        return pltpu.make_async_remote_copy(
            src_ref=cot_out.at[2 - bits, at], dst_ref=cot_out.at[2, at],
            send_sem=half_send.at[bits - 1], recv_sem=half_recv.at[bits - 1],
            device_id=chip[bits], device_id_type=MESH)

    greet(dp, core, lines)
    for sign, way in ways:
        place = place_of(sign)

        @pl.when((place >= lines - 3) & (place < lines - 1))
        def _():
            mid_hop(sign, way).start()

        @pl.when(place == lines - 2)
        def _():
            last_hop(sign, way).start()

    for bits in (1, 2):
        cot_copy(bits).start()

    def step(carry, s, v):
        m, l, acc = carry
        mt = s[:, :128]
        for j in range(1, KC // 128):
            mt = jnp.maximum(mt, s[:, j * 128 : (j + 1) * 128])
        mn = jnp.maximum(m, jnp.max(mt, axis=1, keepdims=True))
        p = jnp.exp2((s - mn) * c2)
        ps = p[:, :128]
        for j in range(1, KC // 128):
            ps = ps + p[:, j * 128 : (j + 1) * 128]
        a = jnp.exp2((m - mn) * c2)
        return mn, l * a + ps, acc * a + dot_nn(p.astype(bf16), v)

    @pl.loop(0, local_tok // QB)
    def _(blk):
        start = lax.rem(dp, members) * local_tok + blk * QB
        nfull = jnp.minimum(start, TRUNK) // KC
        mine = pl.ds(pl.multiple_of(blk * QB, QB), QB)
        slots = members * local_tok // KB
        at = pl.ds(pl.multiple_of(jnp.minimum(start, TRUNK - KC) // KC * KC, KC), KB)
        first = tree_ref[at, :].astype(f32) * jnp.where(start < TRUNK, 1.0, 0.0)
        for slot in range(TRUNK // KB, slots):
            first = first + hot[blk * slots + slot] * tree_ref[slot * KB : (slot + 1) * KB, :].astype(f32)
        other_ref[blk] = first.astype(bf16)
        q = jnp.concatenate([q_ref[mine, h * 128 : (h + 1) * 128] for h in range(heads)], axis=0)

        def body(c, carry):
            at = pl.ds(pl.multiple_of(c * KC, KC), KC)
            return step(carry, dot_nt(q, tree_ref[at, 0:128]), tree_ref[at, 128:256])

        init = (jnp.full((rows, 1), NEG, f32), jnp.zeros((rows, 128), f32), jnp.zeros((rows, 128), f32))
        k, v = masked_chunk(tree_ref, other_ref, blk, start)
        s = dot_nt(q, k)
        col = lax.broadcasted_iota(jnp.int32, (QB, KC), 1)
        row = lax.broadcasted_iota(jnp.int32, (QB, KC), 0)
        ok = col + jnp.where(col < KB, info[2 * blk], info[2 * blk + 1] - KB) <= row
        s = jnp.concatenate([jnp.where(ok, s[h * QB : (h + 1) * QB], NEG) for h in range(heads)], axis=0)
        m, l, acc = lax.fori_loop(0, nfull, body, step(init, s, v))
        lsum = jnp.sum(l, axis=1, keepdims=True)
        out = (acc / lsum).astype(bf16)
        for h in range(heads):
            att_out[mine, h * 128 : (h + 1) * 128] = out[h * QB : (h + 1) * QB]
        lse = jnp.broadcast_to(m * c2 + jnp.log2(lsum), (rows, 128)).T
        lse_out[blk] = lse[0:8, :]

    for bits in (1, 2):
        cot_copy(bits).wait_recv()
    for bits in (1, 2):
        cot_half(bits).start()

    def projected(c):
        at = pl.ds(pl.multiple_of(c * half, half), half)
        return dot_nt(att_out[at, :], out_t[...])

    far[...] = projected(1 - core).astype(bf16)
    pair = pltpu.make_async_remote_copy(
        src_ref=far, dst_ref=near, send_sem=pair_send, recv_sem=pair_recv, device_id=mate, device_id_type=MESH)
    pair.start()
    own = projected(core) + x_in[...].astype(f32)
    pair.wait_recv()
    middle = own + near[...].astype(f32)
    middle_out[...] = middle
    norm = lax.rsqrt(jnp.mean(middle * middle, axis=1, keepdims=True) + EPS)
    normed_out[...] = (middle * norm * rows_in[1:2, :]).astype(bf16)

    pair.wait_send()
    for bits in (1, 2):
        cot_half(bits).wait_recv()
        cot_copy(bits).wait_send()
        cot_half(bits).wait_send()
    for sign, way in ways:
        place = place_of(sign)

        @pl.when(place >= lines - 2)
        def _():
            mid_hop(sign, way).wait_recv()

        @pl.when((place >= lines - 3) & (place < lines - 1))
        def _():
            mid_hop(sign, way).wait_send()

        @pl.when(place == lines - 1)
        def _():
            last_hop(sign, way).wait_recv()

        @pl.when(place == lines - 2)
        def _():
            last_hop(sign, way).wait_send()


def attend(info, hot, q, tree, out_t, x, rows, cot, up, down, late_up, late_down, lines, members, scale):
    bf16, f32 = jnp.bfloat16, jnp.float32
    local_tok, q_width = q.shape
    half, width = x.shape
    anywhere = pl.BlockSpec(memory_space=pl.ANY)
    inside = pl.BlockSpec(memory_space=pltpu.VMEM)
    dma = pltpu.SemaphoreType.DMA
    slab = jax.ShapeDtypeStruct(up.shape[1:], bf16)
    return pl.pallas_call(
        functools.partial(attend_kernel, lines=lines, members=members, scale=scale),
        out_shape=(
            jax.ShapeDtypeStruct((local_tok, q_width), bf16),
            jax.ShapeDtypeStruct((local_tok // QB, 8, q_width // 128 * QB), f32),
            jax.ShapeDtypeStruct((half, width), f32),
            jax.ShapeDtypeStruct((half, width), bf16),
            jax.ShapeDtypeStruct((local_tok // QB, KB, 256), bf16),
            jax.ShapeDtypeStruct((PLANE - 1, half, width), bf16),
            slab, slab, slab, slab,
        ),
        in_specs=[pl.BlockSpec(memory_space=pltpu.SMEM)] * 2 + [inside] * 5 + [anywhere] * 5,
        out_specs=(inside,) * 5 + (anywhere,) * 5,
        scratch_shapes=[
            pltpu.VMEM((half, width), bf16), pltpu.VMEM((half, width), bf16),
            dma, dma, dma((2,)), dma((2,)), dma((2,)), dma((2,)), dma((2,)), dma((2,)), dma((2,)), dma((2,)),
        ],
        compiler_params=pltpu.CompilerParams(vmem_limit_bytes=56 << 20, collective_id=3, has_side_effects=True),
        name="attend",
        cost_estimate=pl.CostEstimate(
            flops=4 * local_tok * q_width * 2304, bytes_accessed=12 << 20, transcendentals=local_tok * q_width * 18
        ),
    )(info, hot, q, tree, out_t, x, rows, cot, up, down, late_up, late_down)


def attend_back_kernel(
    info, hot, q_ref, att_ref, lse_ref, tree_ref, other_ref, out_t, dx_in, middle_in, cot_in, gain_in, cos_in, sin_in,
    y_own, y_other, ff_in, carried_up, carried_down,
    dq_out, dtree_out, middle_grad_out, gain_out, line_out, layer_out, next_up, next_down,
    part_out, part_came, sum_ref, parent_ref, branch, att_grad, y_sum, y_tmp, y_came, own_buf, sum_buf,
    branch_send, branch_recv, y_load, y_send, y_recv, part_send, part_recv, load_sem, hop_send, hop_recv,
    *, lines, members, scale,
):
    bf16, f32 = jnp.bfloat16, jnp.float32
    dp = lax.axis_index("dp")
    core = lax.axis_index("tensor")
    z_at = dp // PLANE
    half, width = cot_in.shape
    local_tok, q_width = q_ref.shape
    heads = q_width // 128
    slab_rows = width // lines
    shard = slab_rows // PLANE
    rows = heads * QB
    c2 = scale * LOG2E
    mate = {"tensor": 1 - core}
    chip = [None] + [{"dp": plane_partner(dp, bits)} for bits in range(1, PLANE)]
    ways = ((1, 0), (-1, 1))
    place_of = lambda sign: z_at if sign == 1 else lines - 1 - z_at

    def own_slab(which, sign):
        return ff_in.at[which, lines - 1 if sign == 1 else 0]

    def own_load(which, sign):
        return pltpu.make_async_copy(own_slab(which, sign), own_buf.at[which], load_sem.at[which, 0])

    def carry_load(which, way):
        return pltpu.make_async_copy((carried_up, carried_down)[way].at[which], sum_buf.at[which], load_sem.at[which, 1])

    def hop(which, sign, way, first_place):
        slab = lines - 2 if sign == 1 else 1
        return pltpu.make_async_remote_copy(
            src_ref=ff_in.at[which, slab] if first_place else sum_buf.at[which],
            dst_ref=(next_up, next_down)[way].at[which],
            send_sem=hop_send.at[which, way], recv_sem=hop_recv.at[which, way],
            device_id={"dp": dp + sign * PLANE}, device_id_type=MESH)

    for sign, way in ways:

        @pl.when(place_of(sign) == 1)
        def _():
            for which in (2, 0, 1):
                own_load(which, sign).start()
                carry_load(which, way).start()

    def y_loads(k, act):
        act(pltpu.make_async_copy(y_own.at[k], y_sum.at[k], y_load.at[k, 0]))
        act(pltpu.make_async_copy(y_other.at[k], y_tmp.at[k], y_load.at[k, 1]))

    for k in range(PLANE):
        y_loads(k, lambda copy: copy.start())
    greet(dp, core, lines)
    for sign, way in ways:

        @pl.when(place_of(sign) == 0)
        def _():
            for which in (2, 0, 1):
                hop(which, sign, way, True).start()

        @pl.when(place_of(sign) == 1)
        def _():
            for which in (2, 0, 1):
                own_load(which, sign).wait()
                carry_load(which, way).wait()
                sum_buf[which] = (own_buf[which].astype(f32) + sum_buf[which].astype(f32)).astype(bf16)
                hop(which, sign, way, False).start()

    middle = middle_in[...]
    norm = lax.rsqrt(jnp.mean(middle * middle, axis=1, keepdims=True) + EPS)
    z_own = middle * norm
    gain_out[...] = jnp.sum(dx_in[...] * z_own, axis=0, keepdims=True)
    w = dx_in[...] * gain_in[1:2, :]
    middle_grad = cot_in[...].astype(f32) + norm * (w - z_own * jnp.mean(w * z_own, axis=1, keepdims=True))
    middle_grad_out[...] = middle_grad
    token_rows = pl.ds(pl.multiple_of(core * half, half), half)
    branch[token_rows, :] = middle_grad.astype(bf16)
    branch_copy = pltpu.make_async_remote_copy(
        src_ref=branch.at[token_rows], dst_ref=branch.at[token_rows], send_sem=branch_send, recv_sem=branch_recv,
        device_id=mate, device_id_type=MESH)
    branch_copy.start()

    quarter = lambda part: pl.ds(part * (half // 2), half // 2)

    def across_copy(bits):
        part = bits - 1
        return pltpu.make_async_remote_copy(
            src_ref=y_sum.at[3, quarter(part)], dst_ref=y_came.at[2, quarter(part)],
            send_sem=y_send.at[0, part], recv_sem=y_recv.at[0, part], device_id=chip[bits], device_id_type=MESH)

    def y_copy(bits, part):
        return pltpu.make_async_remote_copy(
            src_ref=y_sum.at[bits, quarter(part)], dst_ref=y_came.at[bits - 1, quarter(part)],
            send_sem=y_send.at[bits, part], recv_sem=y_recv.at[bits, part], device_id=chip[bits], device_id_type=MESH)

    for k in (3, 1, 2, 0):
        y_loads(k, lambda copy: copy.wait())
        y_sum[k] = (y_sum[k].astype(f32) + y_tmp[k].astype(f32)).astype(bf16)
        if k == 3:
            across_copy(1).start()
            across_copy(2).start()
        elif k:
            y_copy(k, k - 1).start()
    branch_copy.wait_recv()
    att_grad[...] = dot_nn(branch[...], out_t[...]).astype(bf16)
    for z in range(lines):
        tile = dot_nn(branch[:, z * slab_rows : (z + 1) * slab_rows].T, att_ref[...]).astype(bf16)
        for j in range(PLANE):
            part_out[z, j] = tile[j * shard : (j + 1) * shard]

    def part_copy(bits):
        there = lax.rem(plane_partner(dp, bits), PLANE)
        return pltpu.make_async_remote_copy(
            src_ref=part_out.at[:, there], dst_ref=part_came.at[bits - 1],
            send_sem=part_send.at[bits - 1], recv_sem=part_recv.at[bits - 1],
            device_id=chip[bits], device_id_type=MESH)

    for bits in (1, 2):
        across_copy(bits).wait_recv()
        at = quarter(bits - 1)
        y_sum[PLANE - 1 - bits, at] = (y_sum[PLANE - 1 - bits, at].astype(f32) + y_came[2, at].astype(f32)).astype(bf16)
        y_copy(PLANE - 1 - bits, bits - 1).start()
    for bits in range(1, PLANE):
        part_copy(bits).start()

    sum_ref[...] = jnp.zeros_like(sum_ref)
    cosines, sines = cos_in[...], sin_in[...]

    @pl.loop(0, local_tok // QB)
    def _(blk):
        start = lax.rem(dp, members) * local_tok + blk * QB
        nfull = jnp.minimum(start, TRUNK) // KC
        mine = pl.ds(pl.multiple_of(blk * QB, QB), QB)
        stacked = lambda ref: jnp.concatenate([ref[mine, h * 128 : (h + 1) * 128] for h in range(heads)], axis=0)
        q, do, o = stacked(q_ref), stacked(att_grad), stacked(att_ref)
        delta = jnp.sum((do.astype(f32) * o.astype(f32)).T, axis=0, keepdims=True)
        lse = lse_ref[blk][0:1, :]

        def tile(k, v, ok):
            p = jnp.exp2(dot_nt(k, q) * c2 - lse)
            if ok is not None:
                p = jnp.concatenate([jnp.where(ok, p[:, h * QB : (h + 1) * QB], 0.0) for h in range(heads)], axis=1)
            ds = (p * (dot_nt(v, do) - delta)).astype(bf16)
            dq = lax.dot_general(ds, k, (((0,), (0,)), ((), ())), preferred_element_type=f32)
            return dq, dot_nn(ds, q), dot_nn(p.astype(bf16), do)

        def body(c, acc):
            at = pl.ds(pl.multiple_of(c * KC, KC), KC)
            dq, dk, dv = tile(tree_ref[at, 0:128], tree_ref[at, 128:256], None)
            sum_ref[at, 0:128] += dk
            sum_ref[at, 128:256] += dv
            return acc + dq

        k, v = masked_chunk(tree_ref, other_ref, blk, start)
        col = lax.broadcasted_iota(jnp.int32, (KC, QB), 0)
        row = lax.broadcasted_iota(jnp.int32, (KC, QB), 1)
        ok = col + jnp.where(col < KB, info[2 * blk], info[2 * blk + 1] - KB) <= row
        dq, dk, dv = tile(k, v, ok)
        at = pl.ds(pl.multiple_of(second_block(start) * KB, KB), KB)
        sum_ref[at, 0:128] += dk[KB:]
        sum_ref[at, 128:256] += dv[KB:]
        parent_ref[blk, :, 0:128] = dk[:KB]
        parent_ref[blk, :, 128:256] = dv[:KB]

        @pl.when(start < TRUNK)
        def _():
            at = pl.ds(pl.multiple_of(start // KC * KC, KC), KB)
            sum_ref[at, 0:128] += dk[:KB]
            sum_ref[at, 128:256] += dv[:KB]

        dq = lax.fori_loop(0, nfull, body, dq) * scale
        place = pl.ds(pl.multiple_of(blk * QB, QB), QB)
        for h in range(heads):
            part = dq[h * QB : (h + 1) * QB]
            turned = part * cos_in[place, :] - pltpu.roll(part, 64, 1) * sin_in[place, :]
            dq_out[mine, h * 128 : (h + 1) * 128] = turned.astype(bf16)

    dtree_out[0:TRUNK, :] = sum_ref[0:TRUNK, :].astype(bf16)

    @pl.loop(TRUNK // KB, members * local_tok // KB)
    def _(slot):
        at = pl.ds(pl.multiple_of(slot * KB, KB), KB)
        total = sum_ref[at, :]
        for blk in range(local_tok // QB):
            total = total + hot[blk * (members * local_tok // KB) + slot] * parent_ref[blk]
        dtree_out[at, :] = total.astype(bf16)

    for bits in range(1, PLANE):
        part_copy(bits).wait_recv()
    for z in range(lines):
        total = part_out[z, lax.rem(dp, PLANE)].astype(f32)
        for bits in range(1, PLANE):
            total = total + part_came[bits - 1, z].astype(f32)
        line_out[z] = total.astype(bf16)
    for bits in (1, 2):
        for part in range(2):
            y_copy(bits, part).wait_recv()
    total = middle_in[...] + y_sum[0].astype(f32) + y_came[0].astype(f32) + y_came[1].astype(f32)
    layer_out[...] = total.astype(bf16)
    branch_copy.wait_send()
    for bits in range(1, PLANE):
        part_copy(bits).wait_send()
    for bits in (1, 2):
        across_copy(bits).wait_send()
        for part in range(2):
            y_copy(bits, part).wait_send()
    for sign, way in ways:

        @pl.when(place_of(sign) <= 1)
        def _():
            for which in range(3):
                hop(which, sign, way, False).wait_send()

        @pl.when((place_of(sign) >= 1) & (place_of(sign) <= 2))
        def _():
            for which in range(3):
                hop(which, sign, way, False).wait_recv()


def attend_back(info, hot, q, attended, lse, tree, other, out_t, dx, middle, cot, rows, cosines, sines, y_own, y_other, ff_parts, up, down, lines, members, scale):
    bf16, f32 = jnp.bfloat16, jnp.float32
    local_tok, q_width = q.shape
    half, width = cot.shape
    slab_rows = width // lines
    shard = slab_rows // PLANE
    block = up.shape[-1]
    anywhere = pl.BlockSpec(memory_space=pl.ANY)
    inside = pl.BlockSpec(memory_space=pltpu.VMEM)
    dma = pltpu.SemaphoreType.DMA
    slab = jax.ShapeDtypeStruct((3, slab_rows, block), bf16)
    return pl.pallas_call(
        functools.partial(attend_back_kernel, lines=lines, members=members, scale=scale),
        out_shape=(
            jax.ShapeDtypeStruct((local_tok, q_width), bf16),
            jax.ShapeDtypeStruct(tree.shape, bf16),
            jax.ShapeDtypeStruct((half, width), f32),
            jax.ShapeDtypeStruct((1, width), f32),
            jax.ShapeDtypeStruct((lines, shard, q_width), bf16),
            jax.ShapeDtypeStruct((half, width), bf16),
            slab, slab,
        ),
        in_specs=[pl.BlockSpec(memory_space=pltpu.SMEM)] * 2 + [inside] * 12 + [anywhere] * 5,
        out_specs=(inside,) * 6 + (anywhere,) * 2,
        scratch_shapes=[
            pltpu.VMEM((lines, PLANE, shard, q_width), bf16), pltpu.VMEM((PLANE - 1, lines, shard, q_width), bf16),
            pltpu.VMEM(tree.shape, f32), pltpu.VMEM((local_tok // QB, KB, 256), f32),
            pltpu.VMEM((local_tok, width), bf16), pltpu.VMEM((local_tok, q_width), bf16),
            pltpu.VMEM((PLANE, half, width), bf16), pltpu.VMEM((PLANE, half, width), bf16), pltpu.VMEM((PLANE - 1, half, width), bf16),
            pltpu.VMEM((3, slab_rows, block), bf16), pltpu.VMEM((3, slab_rows, block), bf16),
            dma, dma, dma((PLANE, 2)), dma((3, 2)), dma((3, 2)), dma((PLANE - 1,)), dma((PLANE - 1,)), dma((3, 2)), dma((3, 2)), dma((3, 2)),
        ],
        compiler_params=pltpu.CompilerParams(vmem_limit_bytes=62 << 20, collective_id=4, has_side_effects=True),
        name="attend_back",
        cost_estimate=pl.CostEstimate(
            flops=10 * local_tok * q_width * 2304, bytes_accessed=30 << 20, transcendentals=local_tok * q_width * 18
        ),
    )(info, hot, q, attended, lse, tree, other, out_t, dx, middle, cot, rows, cosines, sines, y_own, y_other, ff_parts, up, down)


class Gather:
    def __init__(self, own, whole, sems, dp, lines):
        self.own, self.whole, self.dp, self.lines = own, whole, dp, lines
        self.z_at = dp // PLANE
        self.local_sem, self.line_send, self.line_recv, self.plane_send, self.plane_recv = sems
        self.rows_per = own.shape[0]

    def rows(self, owner):
        return pl.ds(pl.multiple_of(owner * self.rows_per, self.rows_per), self.rows_per)

    def local(self):
        return pltpu.make_async_copy(self.own, self.whole.at[self.rows(self.dp)], self.local_sem)

    def place(self, sign):
        return self.z_at if sign == 1 else self.lines - 1 - self.z_at

    def line_copy(self, sign, step):
        owner = self.dp - sign * step * PLANE
        way = (1 - sign) // 2
        return pltpu.make_async_remote_copy(
            src_ref=self.own if step == 0 else self.whole.at[self.rows(owner)],
            dst_ref=self.whole.at[self.rows(owner)],
            send_sem=self.line_send.at[way, step], recv_sem=self.line_recv.at[way, step],
            device_id={"dp": self.dp + sign * PLANE}, device_id_type=MESH)

    def line_start(self, sign, step):
        place = self.place(sign)

        @pl.when((place >= step) & (place < self.lines - 1))
        def _():
            self.line_copy(sign, step).start()

    def line_wait_send(self, sign, step):
        place = self.place(sign)

        @pl.when((place >= step) & (place < self.lines - 1))
        def _():
            self.line_copy(sign, step).wait_send()

    def plane_copy(self, bits, owner, own=False):
        z = owner // PLANE
        return pltpu.make_async_remote_copy(
            src_ref=self.own if own else self.whole.at[self.rows(owner)],
            dst_ref=self.whole.at[self.rows(owner)],
            send_sem=self.plane_send.at[bits - 1, z], recv_sem=self.plane_recv.at[bits - 1, z],
            device_id={"dp": plane_partner(self.dp, bits)}, device_id_type=MESH)

    def plane_start_own(self):
        for bits in range(1, PLANE):
            self.plane_copy(bits, self.dp, True).start()

    def arrived(self, sign, step):
        place = self.place(sign)

        @pl.when(place >= step + 1)
        def _():
            owner = self.dp - sign * (step + 1) * PLANE
            pltpu.make_async_remote_copy(
                src_ref=self.own, dst_ref=self.whole.at[self.rows(owner)],
                send_sem=self.line_send.at[(1 - sign) // 2, step],
                recv_sem=self.line_recv.at[(1 - sign) // 2, step],
                device_id={"dp": self.dp - sign * PLANE}, device_id_type=MESH).wait_recv()
            if step + 1 < self.lines - 1:

                @pl.when(place < self.lines - 1)
                def _():
                    self.line_copy(sign, step + 1).start()

            for bits in range(1, PLANE):
                self.plane_copy(bits, owner).start()

    def plane_wait_recv(self):
        for bits in range(1, PLANE):
            for z in range(self.lines):
                owner = z * PLANE + lax.rem(plane_partner(self.dp, bits), PLANE)
                self.plane_copy(bits, owner).wait_recv()

    def finish(self):
        for sign in (1, -1):
            for step in range(self.lines - 1):
                self.line_wait_send(sign, step)
        for bits in range(1, PLANE):
            for z in range(self.lines):
                self.plane_copy(bits, z * PLANE + lax.rem(self.dp, PLANE)).wait_send()


def front_kernel(*refs, lines, members, steps):
    (
        ff_in, first_in, out_in, extra_in, x_in, cos_in, sin_in,
        own_out, *slab_outs,
    ) = refs[: 8 + 2 * steps]
    (
        late_up, late_down, first_out, out_t, q_out, tree_out, normed_out, rows_out,
        first_all, extra_all, x_all, normed, pair,
        first_local, first_ls, first_lr, first_ps, first_pr,
        extra_local, extra_ls, extra_lr, extra_ps, extra_pr,
        out_local, out_ls, out_lr, out_ps, out_pr,
        spread_local, spread_send, spread_recv, hop_send, hop_recv,
        x_local, x_send, x_recv, keep_sem, pair_local, pair_send, pair_recv, late_send, late_recv,
    ) = refs[8 + 2 * steps :]
    bf16, f32 = jnp.bfloat16, jnp.float32
    dp = lax.axis_index("dp")
    core = lax.axis_index("tensor")
    z_at = dp // PLANE
    j_at = lax.rem(dp, PLANE)
    half, width = x_in.shape
    shard = first_in.shape[0]
    local_tok = 2 * half
    slab_rows = PLANE * shard
    ups, downs = slab_outs[:steps], slab_outs[steps:]
    mate = {"tensor": 1 - core}

    first = Gather(first_in, first_all, (first_local, first_ls, first_lr, first_ps, first_pr), dp, lines)
    extra = Gather(extra_in, extra_all, (extra_local, extra_ls, extra_lr, extra_ps, extra_pr), dp, lines)
    outer = Gather(out_in, out_t, (out_local, out_ls, out_lr, out_ps, out_pr), dp, lines)

    token_rows = lambda c: pl.ds(pl.multiple_of(c * half, half), half)
    x_keep = pltpu.make_async_copy(x_in, x_all.at[token_rows(core)], x_local)
    x_copy = pltpu.make_async_remote_copy(
        src_ref=x_in, dst_ref=x_all.at[token_rows(core)], send_sem=x_send, recv_sem=x_recv,
        device_id=mate, device_id_type=MESH)
    shard_rows = lambda j: pl.ds(pl.multiple_of(j * shard, shard), shard)

    def spread(which, bits):
        there = lax.rem(plane_partner(dp, bits), PLANE)
        return pltpu.make_async_remote_copy(
            src_ref=ff_in.at[which, there], dst_ref=own_out.at[which, shard_rows(j_at)],
            send_sem=spread_send.at[which, bits - 1], recv_sem=spread_recv.at[which, bits - 1],
            device_id={"dp": plane_partner(dp, bits)}, device_id_type=MESH)

    def spread_keep(which):
        return pltpu.make_async_copy(ff_in.at[which, j_at], own_out.at[which, shard_rows(j_at)], spread_local.at[which])

    def hop(which, sign, step):
        way = (1 - sign) // 2
        outs = ups if sign == 1 else downs
        return pltpu.make_async_remote_copy(
            src_ref=(own_out if step == 0 else outs[step - 1]).at[which], dst_ref=outs[step].at[which],
            send_sem=hop_send.at[which, way, step], recv_sem=hop_recv.at[which, way, step],
            device_id={"dp": dp + sign * PLANE}, device_id_type=MESH)

    def late_hop(index, sign):
        way = (1 - sign) // 2
        return pltpu.make_async_remote_copy(
            src_ref=(ups if sign == 1 else downs)[steps - 1].at[LATE[index]],
            dst_ref=(late_up if sign == 1 else late_down).at[index],
            send_sem=late_send.at[index, way], recv_sem=late_recv.at[index, way],
            device_id={"dp": dp + sign * PLANE}, device_id_type=MESH)

    for one in (first, extra, outer):
        one.local().start()
    x_keep.start()
    for which in range(3):
        spread_keep(which).start()
    greet(dp, core, lines)
    x_copy.start()
    for sign in (1, -1):
        first.line_start(sign, 0)
        extra.line_start(sign, 0)
    for bits in range(1, PLANE):
        spread(2, bits).start()
    first.plane_start_own()
    extra.plane_start_own()
    for which in (0, 1):
        for bits in range(1, PLANE):
            spread(which, bits).start()

    x_keep.wait()
    x_copy.wait_recv()
    wide = x_all[...].astype(f32)
    scale = lax.rsqrt(jnp.mean(wide * wide, axis=1, keepdims=True) + EPS)

    def hop_start(which):
        spread_keep(which).wait()
        for bits in range(1, PLANE):
            spread(which, bits).wait_recv()
        for sign in (1, -1):
            place = z_at if sign == 1 else lines - 1 - z_at

            @pl.when(place < lines - 1)
            def _():
                hop(which, sign, 0).start()

    for step in range(lines - 1):
        for sign in (1, -1):
            first.arrived(sign, step)
            extra.arrived(sign, step)
        if step == 0:
            hop_start(2)
    hop_start(0)
    hop_start(1)
    first.local().wait()
    extra.local().wait()
    for sign in (1, -1):
        outer.line_start(sign, 0)
    outer.plane_start_own()
    extra.plane_wait_recv()
    first.plane_wait_recv()
    keep = pltpu.make_async_copy(first_all, first_out, keep_sem)
    keep.start()
    small = extra_all[0:16, :].astype(f32)
    for owner in range(1, lines * PLANE):
        small = small + extra_all[16 * owner : 16 * (owner + 1), :].astype(f32)
    rows_out[...] = small
    normed[...] = (x_all[...].astype(f32) * scale * small[0:1, :]).astype(bf16)
    normed_out[...] = normed[...]
    columns = first_all.shape[1]
    q_width = columns - 256
    cosines, sines = cos_in[...], sin_in[...]

    def project(at, count):
        part = dot_nn(normed[...], first_all[:, at : at + count])
        return part + small[2:3, at : at + count]

    def turned(part):
        return (part * cosines + pltpu.roll(part, 64, 1) * sines).astype(bf16)

    both = project(q_width, 256)
    pair[:, 0:128] = turned(both[:, 0:128])
    pair[:, 128:256] = both[:, 128:256].astype(bf16)
    member = lax.rem(dp, members)
    tree_rows = lambda m: pl.ds(pl.multiple_of(m * local_tok, local_tok), local_tok)
    partner = lax.rem(line_partner(dp), members)
    pair_keep = pltpu.make_async_copy(pair, tree_out.at[tree_rows(member)], pair_local)
    pair_keep.start()

    def pair_copy(bits, forward=False):
        at = tree_rows(partner if forward else member)
        index = PLANE + bits - 1 if forward else bits
        return pltpu.make_async_remote_copy(
            src_ref=tree_out.at[at] if forward else pair, dst_ref=tree_out.at[at],
            send_sem=pair_send.at[index], recv_sem=pair_recv.at[index],
            device_id={"dp": plane_partner(dp, bits) if bits else line_partner(dp)}, device_id_type=MESH)

    for bits in range(PLANE):
        pair_copy(bits).start()
    for at in range(0, q_width, 256):
        part = project(at, 256)
        q_out[:, at : at + 128] = turned(part[:, 0:128])
        q_out[:, at + 128 : at + 256] = turned(part[:, 128:256])
    pltpu.make_async_remote_copy(
        src_ref=pair, dst_ref=tree_out.at[tree_rows(partner)], send_sem=pair_send.at[0],
        recv_sem=pair_recv.at[0], device_id={"dp": line_partner(dp)}, device_id_type=MESH).wait_recv()
    for bits in range(1, PLANE):
        pair_copy(bits, True).start()
    for step in range(lines - 1):
        for sign in (1, -1):
            outer.arrived(sign, step)
    for step in range(steps):
        for which in (2, 0, 1):
            for sign in (1, -1):
                place = z_at if sign == 1 else lines - 1 - z_at

                @pl.when(place >= step + 1)
                def _():
                    hop(which, sign, step).wait_recv()
                    if step + 1 < steps:

                        @pl.when(place < lines - 1)
                        def _():
                            hop(which, sign, step + 1).start()

                    elif which in LATE:

                        @pl.when(place < lines - 1)
                        def _():
                            late_hop(LATE.index(which), sign).start()

    for bits in range(1, PLANE):
        pair_copy(bits).wait_recv()
        pair_copy(bits, True).wait_recv()
    outer.plane_wait_recv()
    for index in range(len(LATE)):
        for sign in (1, -1):
            place = z_at if sign == 1 else lines - 1 - z_at

            @pl.when(place >= lines - 2)
            def _():
                late_hop(index, sign).wait_recv()

            @pl.when((place >= lines - 3) & (place < lines - 1))
            def _():
                late_hop(index, sign).wait_send()

    for one in (first, extra, outer):
        one.finish()
    outer.local().wait()
    x_copy.wait_send()
    keep.wait()
    pair_keep.wait()
    for bits in range(PLANE):
        pair_copy(bits).wait_send()
        if bits:
            pair_copy(bits, True).wait_send()
    for which in range(3):
        for bits in range(1, PLANE):
            spread(which, bits).wait_send()
        for sign in (1, -1):
            for step in range(steps):
                place = z_at if sign == 1 else lines - 1 - z_at

                @pl.when((place >= step) & (place < lines - 1))
                def _():
                    hop(which, sign, step).wait_send()


def front(ff_blocks, first, out_t, extra, x, cosines, sines, lines, members):
    bf16, f32 = jnp.bfloat16, jnp.float32
    half, width = x.shape
    local_tok = 2 * half
    shard, columns = first.shape
    block = ff_blocks.shape[-1]
    q_width = out_t.shape[1]
    count = lines * PLANE
    steps = max(lines - 3, 1)
    anywhere = pl.BlockSpec(memory_space=pl.ANY)
    inside = pl.BlockSpec(memory_space=pltpu.VMEM)
    dma = pltpu.SemaphoreType.DMA
    slab = jax.ShapeDtypeStruct((3, PLANE * shard, block), bf16)
    gather_sems = [dma, dma((2, lines)), dma((2, lines)), dma((PLANE - 1, lines)), dma((PLANE - 1, lines))]
    return pl.pallas_call(
        functools.partial(front_kernel, lines=lines, members=members, steps=steps),
        out_shape=(slab,) * (1 + 2 * steps)
        + (jax.ShapeDtypeStruct((len(LATE), PLANE * shard, block), bf16),) * 2
        + (
            jax.ShapeDtypeStruct((width, columns), bf16),
            jax.ShapeDtypeStruct((width, q_width), bf16),
            jax.ShapeDtypeStruct((local_tok, q_width), bf16),
            jax.ShapeDtypeStruct((members * local_tok, 256), bf16),
            jax.ShapeDtypeStruct((local_tok, width), bf16),
            jax.ShapeDtypeStruct((16, width), f32),
        ),
        in_specs=[anywhere] * 5 + [inside] * 2,
        out_specs=(anywhere,) * (3 + 2 * steps) + (anywhere, anywhere, inside, anywhere, inside, inside),
        scratch_shapes=[
            pltpu.VMEM((width, columns), bf16), pltpu.VMEM((16 * count, width), bf16),
            pltpu.VMEM((local_tok, width), bf16), pltpu.VMEM((local_tok, width), bf16),
            pltpu.VMEM((local_tok, 256), bf16),
        ]
        + gather_sems * 3
        + [
            dma((3,)), dma((3, PLANE - 1)), dma((3, PLANE - 1)), dma((3, 2, steps)), dma((3, 2, steps)),
            dma, dma, dma, dma, dma, dma((2 * PLANE - 1,)), dma((2 * PLANE - 1,)),
            dma((len(LATE), 2)), dma((len(LATE), 2)),
        ],
        compiler_params=pltpu.CompilerParams(vmem_limit_bytes=56 << 20, collective_id=1, has_side_effects=True),
        name="front",
        cost_estimate=pl.CostEstimate(flops=2 * local_tok * width * columns, bytes_accessed=30 << 20, transcendentals=0),
    )(ff_blocks, first, out_t, extra, x, cosines, sines)


def ff_kernel(
    *refs, tile_h, tile_n, tile_m, lines,
):
    early = lines - 3
    x_in, cot_in, cot_came, slab = refs[:4]
    ups, downs = refs[4 : 4 + early], refs[4 + early : 4 + 2 * early]
    late_up, late_down, mid_up, mid_down, last_up, last_down = refs[4 + 2 * early : 10 + 2 * early]
    cots = [cot_in] + [cot_came.at[k] for k in range(PLANE - 1)]
    (
        dx_out, y_own, y_other, parts_out, carried_up, carried_down,
        x_all, cot_all, gate_w, up_w, down_w, prod, gate_g, up_g, far, near, back, y_stage, stage,
        x_send, x_recv, half_send, half_recv, fwd_send, fwd_recv, pair_send, pair_recv, dx_send, dx_recv,
        x_load, cot_load, cot_send, cot_recv, weight_sem, hop_send, hop_recv, y_keep, y_send, y_recv,
        stage_sem, first_send, first_recv,
    ) = refs[10 + 2 * early :]
    bf16 = jnp.bfloat16
    half = x_in.shape[0]
    width = x_in.shape[1]
    block = gate_w.shape[1]
    chunk = 2 * half
    dp = lax.axis_index("dp")
    core = lax.axis_index("tensor")
    chip = [None] + [{"dp": plane_partner(dp, bits)} for bits in range(1, PLANE)]
    mate = {"tensor": 1 - core}
    rows = lambda k, r, n=1: pl.ds((2 * k + r) * half, n * half)

    z_at = dp // PLANE
    slab_rows = width // lines
    weights = (gate_w, up_w, down_w)
    ways = ((1, 0), (-1, 1))
    place_of = lambda sign: z_at if sign == 1 else lines - 1 - z_at
    place_rows = lambda z: pl.ds(pl.multiple_of(z * slab_rows, slab_rows), slab_rows)

    def second_to_last(which, way):
        if which == 1:
            return (mid_up, mid_down)[way]
        return (late_up, late_down)[way].at[LATE.index(which)]

    def weight_loads(which, act):
        for sign, way in ways:
            pieces = [piece.at[which] for piece in (ups, downs)[way]] + [second_to_last(which, way)]
            if which == 2:
                pieces.append((last_up, last_down)[way])
            for step, piece in enumerate(pieces):

                @pl.when(place_of(sign) >= step + 1)
                def _():
                    act(pltpu.make_async_copy(
                        piece, weights[which].at[place_rows(z_at - sign * (step + 1))],
                        weight_sem.at[which, 1 + way * (lines - 1) + step]))

        act(pltpu.make_async_copy(slab.at[which], weights[which].at[place_rows(z_at)], weight_sem.at[which, 0]))

    def last_hop(which, sign, way):
        origin = 0 if sign == 1 else lines - 1
        return pltpu.make_async_remote_copy(
            src_ref=second_to_last(which, way),
            dst_ref=weights[which].at[pl.ds(origin * slab_rows, slab_rows)],
            send_sem=hop_send.at[which, way], recv_sem=hop_recv.at[which, way],
            device_id={"dp": dp + sign * PLANE}, device_id_type=MESH)

    def weight_wait(which):
        weight_loads(which, lambda copy: copy.wait())
        for sign, way in ways if which < 2 else ():

            @pl.when(place_of(sign) == lines - 1)
            def _():
                last_hop(which, sign, way).wait_recv()

    x_keep = pltpu.make_async_copy(x_in, x_all.at[rows(0, 0)], x_load)
    x_keep.start()

    def cot_keep(k):
        return pltpu.make_async_copy(cots[k], cot_all.at[rows(k, 0)], cot_load.at[k])

    def cot_copy(k):
        return pltpu.make_async_remote_copy(
            src_ref=cots[k], dst_ref=cot_all.at[rows(k, 1)], send_sem=cot_send.at[k], recv_sem=cot_recv.at[k],
            device_id=mate, device_id_type=MESH)

    for k in range(PLANE):
        cot_keep(k).start()
    for which in (2, 0, 1):
        weight_loads(which, lambda copy: copy.start())
    greet(dp, core, lines)
    for which in (0, 1):
        for sign, way in ways:

            @pl.when(place_of(sign) == lines - 2)
            def _():
                last_hop(which, sign, way).start()

    def x_copy(k):
        return pltpu.make_async_remote_copy(
            src_ref=x_in, dst_ref=x_all.at[rows(k, 0) if k else rows(0, 1)],
            send_sem=x_send.at[k], recv_sem=x_recv.at[k],
            device_id=chip[k] if k else mate, device_id_type=MESH)

    def x_half(k):
        at = lambda j: pl.ds(2 * j * half + (k - 1) * (half // 2), half // 2)
        return pltpu.make_async_remote_copy(
            src_ref=x_all.at[at(PLANE - 1 - k)], dst_ref=x_all.at[at(PLANE - 1)],
            send_sem=half_send.at[k - 1], recv_sem=half_recv.at[k - 1],
            device_id=chip[k], device_id_type=MESH)

    def x_forward(k):
        return pltpu.make_async_remote_copy(
            src_ref=x_all.at[rows(k, 0)], dst_ref=x_all.at[rows(k, 1)],
            send_sem=fwd_send.at[k - 1], recv_sem=fwd_recv.at[k - 1],
            device_id=mate, device_id_type=MESH)

    def pair_copy(k):
        return pltpu.make_async_remote_copy(
            src_ref=far.at[k], dst_ref=near.at[k],
            send_sem=pair_send.at[k], recv_sem=pair_recv.at[k],
            device_id=mate, device_id_type=MESH)

    def dx_copy(k):
        return pltpu.make_async_remote_copy(
            src_ref=near.at[k], dst_ref=back.at[k - 1],
            send_sem=dx_send.at[k - 1], recv_sem=dx_recv.at[k - 1],
            device_id=chip[k], device_id_type=MESH)

    x_copy(0).start()
    x_copy(1).start()
    x_copy(2).start()
    for k in range(PLANE):
        cot_copy(k).start()
    for k in range(PLANE):
        cot_keep(k).wait()
        cot_copy(k).wait_recv()
    weight_wait(2)

    @pl.loop(0, PLANE)
    def _(k):
        at = pl.ds(pl.multiple_of(k * chunk, chunk), chunk)

        @pl.loop(0, block // tile_h)
        def _(t):
            cols = pl.ds(pl.multiple_of(t * tile_h, tile_h), tile_h)
            up_g[at, cols] = dot_nn(cot_all[at, :], down_w[:, cols]).astype(bf16)

    def gate_part(k):
        at = rows(k, 0, 2)

        @pl.loop(0, block // tile_h)
        def _(t):
            cols = pl.ds(pl.multiple_of(t * tile_h, tile_h), tile_h)
            gate_g[at, cols] = dot_nn(x_all[at, :], gate_w[:, cols]).astype(bf16)

    def up_part(k):
        at = rows(k, 0, 2)

        @pl.loop(0, block // tile_h)
        def _(t):
            cols = pl.ds(pl.multiple_of(t * tile_h, tile_h), tile_h)
            up = dot_nn(x_all[at, :], up_w[:, cols])
            gate = gate_g[at, cols].astype(jnp.float32)
            pg = up_g[at, cols].astype(jnp.float32)
            sig = 0.5 * jnp.tanh(0.5 * gate) + 0.5
            silu = gate * sig
            prod[at, cols] = (silu * up).astype(bf16)
            up_g[at, cols] = (pg * silu).astype(bf16)
            gate_g[at, cols] = (pg * up * (sig + silu * (1.0 - sig))).astype(bf16)

    def dx_half(k, r):
        at = rows(k, r)

        @pl.loop(0, width // tile_n)
        def _(t):
            cols = pl.ds(pl.multiple_of(t * tile_n, tile_n), tile_n)
            part = dot_nt(gate_g[at, :], gate_w[cols, :]) + dot_nt(up_g[at, :], up_w[cols, :])
            if r:
                far[k, :, cols] = part.astype(bf16)
            else:
                near[k, :, cols] = (part + near[k, :, cols].astype(jnp.float32)).astype(bf16)

    def dx_first(k):
        dx_half(k, 1)
        pair_copy(k).start()

    def dx_second(k):
        pair_copy(k).wait_recv()
        dx_half(k, 0)
        if k:
            dx_copy(k).start()

    def y_local(k):
        return pltpu.make_async_copy(y_stage.at[pl.ds(0, half)], y_own.at[k], y_keep)

    def y_copy(k):
        return pltpu.make_async_remote_copy(
            src_ref=y_stage.at[pl.ds(half, half)], dst_ref=y_other.at[k],
            send_sem=y_send.at[k], recv_sem=y_recv.at[k], device_id=mate, device_id_type=MESH)

    def y_part(k):
        if k:
            y_local(k - 1).wait()
            y_copy(k - 1).wait_send()

        @pl.loop(0, width // tile_n)
        def _(t):
            cols = pl.ds(pl.multiple_of(t * tile_n, tile_n), tile_n)
            y_stage[:, cols] = dot_nt(prod[rows(k, 0, 2), :], down_w[cols, :]).astype(bf16)

        y_local(k).start()
        y_copy(k).start()

    x_keep.wait()
    x_copy(0).wait_recv()
    weight_wait(0)
    gate_part(0)
    for k in (1, 2):
        x_copy(k).wait_recv()
        x_forward(k).start()
    for k in (1, 2):
        x_half(k).start()
    x_forward(1).wait_recv()
    gate_part(1)
    x_forward(2).wait_recv()
    gate_part(2)
    for k in (1, 2):
        x_half(k).wait_recv()
    x_forward(3).start()
    weight_wait(1)
    up_part(0)
    up_part(1)
    x_forward(3).wait_recv()
    gate_part(3)
    up_part(2)
    up_part(3)

    def first_hop(which, sign, way):
        at = pl.ds((lines - 1) * slab_rows if sign == 1 else 0, slab_rows)
        return pltpu.make_async_remote_copy(
            src_ref=parts_out.at[which, at], dst_ref=(carried_up, carried_down)[way].at[which],
            send_sem=first_send.at[which, way], recv_sem=first_recv.at[which, way],
            device_id={"dp": dp + sign * PLANE}, device_id_type=MESH)

    tiles = width // tile_m

    def stage_copy(which, m, slot):
        at = pl.ds(pl.multiple_of(m * tile_m, tile_m), tile_m)
        return pltpu.make_async_copy(stage.at[slot], parts_out.at[which, at], stage_sem.at[slot])

    def weight_grad(which, tokens, grad):
        @pl.loop(0, tiles)
        def _(m):
            at = pl.ds(pl.multiple_of(m * tile_m, tile_m), tile_m)
            tile = dot_nn(tokens[:, at].T, grad[...]).astype(bf16)
            slot = lax.rem(m, 2)

            @pl.when(m >= 2)
            def _():
                stage_copy(which, m - 2, slot).wait()

            stage[slot] = tile
            stage_copy(which, m, slot).start()

        for m in (tiles - 2, tiles - 1):
            stage_copy(which, m, m % 2).wait()
        for sign, way in ways:

            @pl.when(place_of(sign) == 0)
            def _():
                first_hop(which, sign, way).start()

    weight_grad(2, cot_all, prod)
    dx_first(1)
    dx_first(2)
    dx_second(1)
    dx_first(3)
    dx_second(2)
    dx_first(0)
    dx_second(3)
    dx_second(0)
    weight_grad(0, x_all, gate_g)
    weight_grad(1, x_all, up_g)
    for k in range(PLANE):
        y_part(k)

    for k in range(1, PLANE):
        dx_copy(k).wait_recv()
    total = near[0].astype(jnp.float32)
    for k in range(PLANE - 1):
        total = total + back[k].astype(jnp.float32)
    dx_out[...] = total

    for k in range(PLANE):
        if k < PLANE - 1:
            x_copy(k).wait_send()
        if k in (1, 2):
            x_half(k).wait_send()
        pair_copy(k).wait_send()
        if k:
            x_forward(k).wait_send()
            dx_copy(k).wait_send()
    y_local(PLANE - 1).wait()
    y_copy(PLANE - 1).wait_send()
    for k in range(PLANE):
        y_copy(k).wait_recv()
    for which in range(3):
        for sign, way in ways:
            if which < 2:

                @pl.when(place_of(sign) == lines - 2)
                def _():
                    last_hop(which, sign, way).wait_send()

            @pl.when(place_of(sign) == 0)
            def _():
                first_hop(which, sign, way).wait_send()

            @pl.when(place_of(sign) == 1)
            def _():
                first_hop(which, sign, way).wait_recv()

    for k in range(PLANE):
        cot_copy(k).wait_send()


def feed_forward(x, cot, cot_came, slabs, lines, tile_h=384, tile_n=512, tile_m=256):
    half, width = x.shape
    block = slabs[0].shape[-1]
    slab_rows = width // lines
    tokens = 2 * PLANE * half
    bf16 = jnp.bfloat16
    anywhere = pl.BlockSpec(memory_space=pl.ANY)
    dma = pltpu.SemaphoreType.DMA
    slab = jax.ShapeDtypeStruct((3, slab_rows, block), bf16)
    return pl.pallas_call(
        functools.partial(ff_kernel, tile_h=tile_h, tile_n=tile_n, tile_m=tile_m, lines=lines),
        out_shape=(
            jax.ShapeDtypeStruct((half, width), jnp.float32),
            jax.ShapeDtypeStruct((PLANE, half, width), bf16),
            jax.ShapeDtypeStruct((PLANE, half, width), bf16),
            jax.ShapeDtypeStruct((3, width, block), bf16),
            slab,
            slab,
        ),
        in_specs=[anywhere] * (3 + len(slabs)),
        out_specs=(pl.BlockSpec(memory_space=pltpu.VMEM),) + (anywhere,) * 5,
        scratch_shapes=[
            pltpu.VMEM((tokens, width), bf16), pltpu.VMEM((tokens, width), bf16),
            pltpu.VMEM((width, block), bf16), pltpu.VMEM((width, block), bf16), pltpu.VMEM((width, block), bf16),
            pltpu.VMEM((tokens, block), bf16), pltpu.VMEM((tokens, block), bf16), pltpu.VMEM((tokens, block), bf16),
            pltpu.VMEM((PLANE, half, width), bf16), pltpu.VMEM((PLANE, half, width), bf16), pltpu.VMEM((PLANE - 1, half, width), bf16),
            pltpu.VMEM((2 * half, width), bf16), pltpu.VMEM((2, tile_m, block), bf16),
            dma((PLANE - 1,)), dma((PLANE - 1,)), dma((2,)), dma((2,)), dma((PLANE - 1,)), dma((PLANE - 1,)), dma((PLANE,)), dma((PLANE,)),
            dma((PLANE - 1,)), dma((PLANE - 1,)), dma, dma((PLANE,)), dma((PLANE,)), dma((PLANE,)), dma((3, 2 * lines)), dma((3, 2)), dma((3, 2)), dma, dma((PLANE,)), dma((PLANE,)),
            dma((2,)), dma((3, 2)), dma((3, 2)),
        ],
        compiler_params=pltpu.CompilerParams(vmem_limit_bytes=62 << 20, collective_id=0, has_side_effects=True),
        name="feed_forward",
        cost_estimate=pl.CostEstimate(flops=18 * tokens * width * block, bytes_accessed=60 << 20, transcendentals=tokens * block),
    )(x, cot, cot_came, *slabs)


def back_kernel(
    dkv_in, dq_in, cos_in, sin_in, normed_in, first_in, line_o, x_in, rows_in, gain_row_in, middle_grad_in,
    ff_in, carried_up, carried_down,
    input_grad_out, sums_out, small_out, ff_out,
    kv_own, kv_other, kv_plane, kv_merged, kv_line, grads, part_q, part_kv,
    recv_q, recv_kv, line_q, line_kv, from_q, from_kv, from_o,
    far, near, small_own, small_mate, small_plane, small_line,
    own_buf, recv_buf, first_buf, total_buf,
    kv_local, kv_send, kv_recv, kv_line_send, kv_line_recv,
    plane_send, plane_recv, line_send, line_recv,
    mate_send, mate_recv, small_mate_sem, small_plane_send, small_plane_recv, small_line_send, small_line_recv,
    load_sem, own_sem, carry_sem, hop_send, hop_recv, spread_local, spread_send, spread_recv,
    *, lines, members, scale,
):
    bf16, f32 = jnp.bfloat16, jnp.float32
    dp = lax.axis_index("dp")
    core = lax.axis_index("tensor")
    z_at, j_at = dp // PLANE, lax.rem(dp, PLANE)
    half, width = x_in.shape
    local_tok = 2 * half
    slab_rows = width // lines
    shard = slab_rows // PLANE
    q_width = dq_in.shape[1]
    block = total_buf.shape[-1]
    mate = {"tensor": 1 - core}
    chip = [None] + [{"dp": plane_partner(dp, bits)} for bits in range(1, PLANE)]
    there = [j_at] + [lax.rem(plane_partner(dp, bits), PLANE) for bits in range(1, PLANE)]
    side = lax.rem(z_at, 2) * PLANE
    other_side = PLANE - side
    member = lax.rem(dp, members)
    del member
    ways = ((1, 0), (-1, 1))
    place_of = lambda sign: z_at if sign == 1 else lines - 1 - z_at
    tree_rows = lambda m: pl.ds(pl.multiple_of(m * local_tok, local_tok), local_tok)

    kv_loads = [
        pltpu.make_async_copy(dkv_in.at[tree_rows(side + j_at)], kv_own, kv_local.at[0]),
        pltpu.make_async_copy(dkv_in.at[tree_rows(other_side + j_at)], kv_other, kv_local.at[1]),
    ]
    for load in kv_loads:
        load.start()

    def slab_load(which, sign, way, step):
        target = lines - 1 - step + place_of(sign)
        slab = target if sign == 1 else lines - 1 - target
        return pltpu.make_async_copy(ff_in.at[which, slab], own_buf.at[which, way], load_sem.at[which, way])

    def own_load(which):
        return pltpu.make_async_copy(ff_in.at[which, z_at], total_buf.at[which], own_sem.at[which])

    def carry_load(which, sign, way):
        return pltpu.make_async_copy(
            (carried_up if sign == 1 else carried_down).at[which], first_buf.at[which, way], carry_sem.at[which, way])

    order = (2, 0, 1)
    for which in order:
        for sign, way in ways:
            carry_load(which, sign, way).start()

            @pl.when((place_of(sign) >= 1) & (place_of(sign) <= 2))
            def _():
                slab_load(which, sign, way, 2).start()

        own_load(which).start()

    barrier = pltpu.get_barrier_semaphore()
    for bits in range(1, PLANE):
        pl.semaphore_signal(barrier, inc=1, device_id=chip[bits], device_id_type=MESH)
    pl.semaphore_signal(barrier, inc=1, device_id=mate, device_id_type=MESH)
    for apart in range(1, lines):
        pl.semaphore_signal(
            barrier, inc=1, device_id={"dp": lax.rem(z_at + apart, lines) * PLANE + j_at}, device_id_type=MESH)
    pl.semaphore_wait(barrier, PLANE + lines - 1)

    def kv_copy(bits, part):
        at = tree_rows((side if part == 0 else other_side) + there[bits])
        return pltpu.make_async_remote_copy(
            src_ref=dkv_in.at[at], dst_ref=kv_plane.at[bits - 1, part],
            send_sem=kv_send.at[bits - 1, part], recv_sem=kv_recv.at[bits - 1, part],
            device_id=chip[bits], device_id_type=MESH)

    for part in (1, 0):
        for bits in range(1, PLANE):
            kv_copy(bits, part).start()

    def hop(which, sign, way, step, first_place=False):
        slab = lines - 1 - step if sign == 1 else step
        carried = first_buf.at[which, way] if step == 2 else recv_buf.at[which, way, step - 3]
        return pltpu.make_async_remote_copy(
            src_ref=ff_in.at[which, slab] if first_place else carried, dst_ref=recv_buf.at[which, way, step - 2],
            send_sem=hop_send.at[which, way, step - 2], recv_sem=hop_recv.at[which, way, step - 2],
            device_id={"dp": dp + sign * PLANE}, device_id_type=MESH)

    def hop_step(which, step):
        for sign, way in ways:
            place = place_of(sign)
            if step == 2:
                carry_load(which, sign, way).wait()

            @pl.when(place == 0)
            def _():
                hop(which, sign, way, step, True).start()

            @pl.when((place >= 1) & (place <= step))
            def _():
                if step > 2:
                    hop(which, sign, way, step - 1).wait_recv()
                slab_load(which, sign, way, step).wait()
                mine = own_buf[which, way].astype(f32)
                if step == 2:
                    first_buf[which, way] = (mine + first_buf[which, way].astype(f32)).astype(bf16)
                else:
                    recv_buf[which, way, step - 3] = (mine + recv_buf[which, way, step - 3].astype(f32)).astype(bf16)
                hop(which, sign, way, step).start()

            if step < lines - 2:

                @pl.when((place >= 1) & (place <= step + 1))
                def _():
                    slab_load(which, sign, way, step + 1).start()

    for which in order:
        hop_step(which, 2)

    groups = {
        "o": (0, None, None, line_o, from_o, q_width + 256, q_width),
        "q": (1, part_q, recv_q, line_q, from_q, 0, q_width),
        "kv": (2, part_kv, recv_kv, line_kv, from_kv, q_width, 256),
    }

    def plane_copy(name, bits):
        index, part, recv, *_ = groups[name]
        return pltpu.make_async_remote_copy(
            src_ref=part.at[:, there[bits]], dst_ref=recv.at[bits - 1],
            send_sem=plane_send.at[index, bits - 1], recv_sem=plane_recv.at[index, bits - 1],
            device_id=chip[bits], device_id_type=MESH)

    def line_copy(name, apart):
        index, _, _, line, came, *_ = groups[name]
        target = lax.rem(z_at + apart, lines)
        return pltpu.make_async_remote_copy(
            src_ref=line.at[target], dst_ref=came.at[apart - 1],
            send_sem=line_send.at[index, apart - 1], recv_sem=line_recv.at[index, apart - 1],
            device_id={"dp": target * PLANE + j_at}, device_id_type=MESH)

    def plane_start(name):
        for bits in range(1, PLANE):
            plane_copy(name, bits).start()

    def plane_sum(name):
        _, part, recv, line, *_ = groups[name]
        for bits in range(1, PLANE):
            plane_copy(name, bits).wait_recv()
        for z in range(lines):
            total = part[z, j_at].astype(f32)
            for bits in range(1, PLANE):
                total = total + recv[bits - 1, z].astype(f32)
            line[z] = total.astype(bf16)
        line_start(name)

    def line_start(name):
        for apart in range(1, lines):
            line_copy(name, apart).start()

    def line_sum(name):
        *_, line, came, at, size = groups[name]
        for apart in range(1, lines):
            line_copy(name, apart).wait_recv()
        total = line[z_at].astype(f32)
        for apart in range(1, lines):
            total = total + came[apart - 1].astype(f32)
        sums_out[:, at : at + size] = total

    line_start("o")
    cosines, sines = cos_in[...], sin_in[...]

    def turned_back(part):
        return (part * cosines - pltpu.roll(part, 64, 1) * sines).astype(bf16)

    grads[:, 0:q_width] = dq_in[...]

    def weight_part(part, at, size):
        for z in range(lines):
            turned = normed_in[:, z * slab_rows : (z + 1) * slab_rows].T
            tile = dot_nn(turned, grads[:, at : at + size]).astype(bf16)
            for j in range(PLANE):
                part[z, j] = tile[j * shard : (j + 1) * shard]

    weight_part(part_q, 0, q_width)

    columns = lambda j: pl.ds(pl.multiple_of(j * block, block), block)

    def spread(which, bits):
        rows = pl.ds(pl.multiple_of(there[bits] * shard, shard), shard)
        return pltpu.make_async_remote_copy(
            src_ref=total_buf.at[which, rows], dst_ref=ff_out.at[which, :, columns(j_at)],
            send_sem=spread_send.at[which, bits - 1], recv_sem=spread_recv.at[which, bits - 1],
            device_id=chip[bits], device_id_type=MESH)

    def spread_keep(which):
        rows = pl.ds(pl.multiple_of(j_at * shard, shard), shard)
        return pltpu.make_async_copy(
            total_buf.at[which, rows], ff_out.at[which, :, columns(j_at)], spread_local.at[which])

    def line_done(which):
        for step in range(3, lines - 1):
            hop_step(which, step)
        own_load(which).wait()
        for sign, way in ways:

            @pl.when(place_of(sign) >= 1)
            def _():
                hop(which, sign, way, lines - 2).wait_recv()
                came = recv_buf[which, way, lines - 4].astype(f32)
                total_buf[which] = (total_buf[which].astype(f32) + came).astype(bf16)

        for bits in range(1, PLANE):
            spread(which, bits).start()
        spread_keep(which).start()

    for load in kv_loads:
        load.wait()
    for bits in range(1, PLANE):
        kv_copy(bits, 1).wait_recv()
    total = kv_other[...].astype(f32)
    for bits in range(1, PLANE):
        total = total + kv_plane[bits - 1, 1].astype(f32)
    kv_merged[...] = total.astype(bf16)
    kv_across = pltpu.make_async_remote_copy(
        src_ref=kv_merged, dst_ref=kv_line, send_sem=kv_line_send, recv_sem=kv_line_recv,
        device_id={"dp": line_partner(dp)}, device_id_type=MESH)
    kv_across.start()
    plane_start("q")
    line_done(2)
    for bits in range(1, PLANE):
        kv_copy(bits, 0).wait_recv()
    kv_across.wait_recv()
    total = kv_own[...].astype(f32) + kv_line[...].astype(f32)
    for bits in range(1, PLANE):
        total = total + kv_plane[bits - 1, 0].astype(f32)
    grads[:, q_width : q_width + 128] = turned_back(total[:, 0:128] * scale)
    grads[:, q_width + 128 :] = total[:, 128:256].astype(bf16)
    weight_part(part_kv, q_width, 256)
    plane_start("kv")

    def normed_grad(c):
        at = pl.ds(pl.multiple_of(c * half, half), half)
        return dot_nt(grads[at, :], first_in[...])

    far[...] = normed_grad(1 - core).astype(bf16)
    mate_copy = pltpu.make_async_remote_copy(
        src_ref=far, dst_ref=near, send_sem=mate_send, recv_sem=mate_recv, device_id=mate, device_id_type=MESH)
    mate_copy.start()
    mine = normed_grad(core)
    line_done(0)
    mate_copy.wait_recv()
    mine = mine + near[...].astype(f32)
    wide = x_in[...].astype(f32)
    norm = lax.rsqrt(jnp.mean(wide * wide, axis=1, keepdims=True) + EPS)
    z_own = wide * norm
    w = mine * gain_row_in[...]
    back = norm * (w - z_own * jnp.mean(w * z_own, axis=1, keepdims=True))
    input_grad_out[...] = (middle_grad_in[...] + back).astype(bf16)
    bias = jnp.sum(grads[...].astype(f32), axis=0, keepdims=True)
    small_own[...] = jnp.concatenate(
        [
            jnp.sum(mine * z_own, axis=0, keepdims=True),
            rows_in[...],
            jnp.concatenate([bias, jnp.zeros((1, width - q_width - 256), f32)], axis=1),
            jnp.zeros((5, width), f32),
        ],
        axis=0,
    )
    small_copy = pltpu.make_async_remote_copy(
        src_ref=small_own, dst_ref=small_mate, send_sem=small_mate_sem.at[0], recv_sem=small_mate_sem.at[1],
        device_id=mate, device_id_type=MESH)
    small_copy.start()
    plane_sum("q")
    plane_sum("kv")
    line_done(1)

    small_copy.wait_recv()
    gain_rows = lax.broadcasted_iota(jnp.int32, (8, width), 0) < 2
    small_plane[0] = small_own[...] + jnp.where(gain_rows, small_mate[...], 0.0)

    def small_plane_copy(bits):
        return pltpu.make_async_remote_copy(
            src_ref=small_plane.at[0], dst_ref=small_plane.at[bits],
            send_sem=small_plane_send.at[bits - 1], recv_sem=small_plane_recv.at[bits - 1],
            device_id=chip[bits], device_id_type=MESH)

    def small_line_copy(apart):
        return pltpu.make_async_remote_copy(
            src_ref=small_line.at[0], dst_ref=small_line.at[apart],
            send_sem=small_line_send.at[apart - 1], recv_sem=small_line_recv.at[apart - 1],
            device_id={"dp": lax.rem(z_at + apart, lines) * PLANE + j_at}, device_id_type=MESH)

    for bits in range(1, PLANE):
        small_plane_copy(bits).start()
    for bits in range(1, PLANE):
        small_plane_copy(bits).wait_recv()
    total = small_plane[0]
    for bits in range(1, PLANE):
        total = total + small_plane[bits]
    small_line[0] = total
    for apart in range(1, lines):
        small_line_copy(apart).start()
    line_sum("o")
    line_sum("q")
    line_sum("kv")
    for apart in range(1, lines):
        small_line_copy(apart).wait_recv()
    total = small_line[0]
    for apart in range(1, lines):
        total = total + small_line[apart]
    small_out[...] = total

    for which in order:
        for bits in range(1, PLANE):
            spread(which, bits).wait_recv()
            spread(which, bits).wait_send()
        spread_keep(which).wait()
        for sign, way in ways:
            for step in range(2, lines - 1):

                @pl.when(place_of(sign) <= step)
                def _():
                    hop(which, sign, way, step).wait_send()

    for bits in range(1, PLANE):
        small_plane_copy(bits).wait_send()
        for part in range(2):
            kv_copy(bits, part).wait_send()
        for name in ("q", "kv"):
            plane_copy(name, bits).wait_send()
    for apart in range(1, lines):
        small_line_copy(apart).wait_send()
        for name in groups:
            line_copy(name, apart).wait_send()
    kv_across.wait_send()
    mate_copy.wait_send()
    small_copy.wait_send()


def finish(dkv, dq, cosines, sines, normed, first, line_o, x, gain_rows, gain_row, middle_grad, ff_parts, up, down, lines, members, scale):
    bf16, f32 = jnp.bfloat16, jnp.float32
    half, width = x.shape
    local_tok = 2 * half
    q_width = dq.shape[1]
    slab_rows = width // lines
    shard = slab_rows // PLANE
    block = ff_parts.shape[-1]
    anywhere = pl.BlockSpec(memory_space=pl.ANY)
    inside = pl.BlockSpec(memory_space=pltpu.VMEM)
    dma = pltpu.SemaphoreType.DMA
    near = PLANE - 1
    vmem = lambda *shape: pltpu.VMEM(shape, bf16)
    wide = lambda *shape: pltpu.VMEM(shape, f32)
    pair = (local_tok, 256)
    return pl.pallas_call(
        functools.partial(back_kernel, lines=lines, members=members, scale=scale),
        out_shape=(
            jax.ShapeDtypeStruct((half, width), bf16),
            jax.ShapeDtypeStruct((shard, 2 * q_width + 256), f32),
            jax.ShapeDtypeStruct((8, width), f32),
            jax.ShapeDtypeStruct((3, shard, PLANE * block), bf16),
        ),
        in_specs=[anywhere] + [inside] * 10 + [anywhere] * 3,
        out_specs=(inside, inside, inside, anywhere),
        scratch_shapes=[
            vmem(*pair), vmem(*pair), vmem(near, 2, *pair), vmem(*pair), vmem(*pair),
            vmem(local_tok, q_width + 256), vmem(lines, PLANE, shard, q_width), vmem(lines, PLANE, shard, 256),
            vmem(near, lines, shard, q_width), vmem(near, lines, shard, 256),
            vmem(lines, shard, q_width), vmem(lines, shard, 256),
            vmem(lines - 1, shard, q_width), vmem(lines - 1, shard, 256), vmem(lines - 1, shard, q_width),
            vmem(half, width), vmem(half, width), wide(8, width), wide(8, width), wide(PLANE, 8, width), wide(lines, 8, width),
            vmem(3, 2, slab_rows, block), vmem(3, 2, lines - 3, slab_rows, block), vmem(3, 2, slab_rows, block), vmem(3, slab_rows, block),
            dma((2,)), dma((near, 2)), dma((near, 2)), dma, dma,
            dma((3, near)), dma((3, near)), dma((3, lines - 1)), dma((3, lines - 1)),
            dma, dma, dma((2,)), dma((near,)), dma((near,)), dma((lines - 1,)), dma((lines - 1,)),
            dma((3, 2)), dma((3,)), dma((3, 2)), dma((3, 2, lines - 3)), dma((3, 2, lines - 3)), dma((3,)), dma((3, near)), dma((3, near)),
        ],
        compiler_params=pltpu.CompilerParams(vmem_limit_bytes=62 << 20, collective_id=2, has_side_effects=True),
        name="back",
        cost_estimate=pl.CostEstimate(flops=6 * local_tok * width * (q_width + 256), bytes_accessed=40 << 20, transcendentals=0),
    )(dkv, dq, cosines, sines, normed, first, line_o, x, gain_rows, gain_row, middle_grad, ff_parts, up, down)


def swap(block, axis, count, bits):
    return lax.ppermute(block, axis, [(i, i ^ bits) for i in range(count)])


def rms_scale(values):
    return lax.rsqrt(jnp.mean(values * values, axis=1, keepdims=True) + EPS)


def norm_back(grad, values, gain):
    scale = rms_scale(values)
    z = values * scale
    w = grad * gain
    gain_grad = jnp.sum(grad * z, axis=0)
    return scale * (w - z * jnp.mean(w * z, axis=1, keepdims=True)), gain_grad


def rope_tables(positions):
    exponents = jnp.arange(64, dtype=jnp.float32) * (2.0 / 128)
    frequency = jnp.power(THETA, -exponents)
    angles = positions.astype(jnp.float32)[:, None] * frequency[None, :]
    cosines, sines = jnp.cos(angles), jnp.sin(angles)
    return (
        jnp.concatenate([cosines, cosines], axis=1),
        jnp.concatenate([-sines, sines], axis=1),
    )


def contract_rows(left, right):
    return lax.dot_general(
        left, right, (((0,), (0,)), ((), ())), preferred_element_type=jnp.float32
    )


def contract_cols(left, right):
    return lax.dot_general(
        left, right, (((1,), (1,)), ((), ())), preferred_element_type=jnp.float32
    )


def matmul(left, right):
    return jnp.dot(left, right, preferred_element_type=jnp.float32)


def attention_plan(segment_ids, parent_ids, dp_index, local_tok):
    members = TREE_TOK // local_tok
    first = dp_index // members * TREE_TOK
    slots = lax.dynamic_slice_in_dim(segment_ids, first, TREE_TOK)[::KB]
    numbers = jnp.arange(parent_ids.shape[0], dtype=jnp.int32)
    parents = jnp.sum(jnp.where(slots[:, None] == numbers[None, :], parent_ids[None, :], 0), axis=1)
    places = jnp.arange(slots.shape[0], dtype=jnp.int32)
    holder = jnp.sum(jnp.where(parents[:, None] == slots[None, :], places[None, :], 0), axis=1)
    starts = dp_index % members * local_tok + QB * jnp.arange(local_tok // QB, dtype=jnp.int32)
    slot = starts // KB
    chosen = slot[:, None] == places[None, :]
    pick = lambda table: jnp.sum(jnp.where(chosen, table[None, :], 0), axis=1)
    in_trunk = starts < TRUNK
    is_leaf = pick(parents) != slots[0]
    chunk = jnp.minimum(starts, TRUNK) // KC
    far = jnp.int32(1 << 20)
    block0 = jnp.where(in_trunk, 2 * chunk, jnp.where(is_leaf, pick(holder), TRUNK // KB))
    block1 = jnp.where(in_trunk, 2 * chunk + 1, slot)
    shift0 = jnp.where(in_trunk, block0 * KB - starts, jnp.where(is_leaf, -far, far))
    shift1 = block1 * KB - starts
    hot = jnp.where(~in_trunk[:, None] & (block0[:, None] == places[None, :]), 1.0, 0.0)
    return jnp.stack([shift0, shift1], axis=1).reshape(-1), hot.reshape(-1)


def on_device(
    dp_size,
    layer_input,
    out_cotangent,
    positions,
    segment_ids,
    parent_ids,
    attention_gain,
    query_weight,
    query_bias,
    key_weight,
    key_bias,
    value_weight,
    value_bias,
    output_weight,
    feedforward_gain,
    gate_weight,
    up_weight,
    down_weight,
):
    bf16, f32 = jnp.bfloat16, jnp.float32
    local_tok = positions.shape[0]
    half_tok, width = layer_input.shape
    shard = attention_gain.shape[0]
    heads, head_dim = query_bias.shape[0], 128
    per_head = query_bias.shape[1]
    q_width = heads * head_dim
    hidden = gate_weight.shape[1]
    block = -(-hidden // (PLANE * 128)) * 128
    lines = dp_size // PLANE
    members = TREE_TOK // local_tok
    dp_index = lax.axis_index("dp")
    core = lax.axis_index("tensor")
    scale = head_dim ** (-0.5)

    def line_route(sign, first, last):
        route = []
        for place in range(first, last + 1):
            z = place if sign == 1 else lines - 1 - place
            route += [(z * PLANE + j, (z + sign) * PLANE + j) for j in range(PLANE)]
        return route

    def by_core(mine):
        other = swap(mine, "tensor", 2, 1)
        first = jnp.where(core == 0, mine, other)
        second = jnp.where(core == 0, other, mine)
        return jnp.concatenate([first, second], axis=0)

    blocked = lambda w: jnp.pad(w, ((0, 0), (0, PLANE * block - hidden))).reshape(shard, PLANE, block).transpose(1, 0, 2)
    ff_blocks = jnp.stack([blocked(gate_weight), blocked(up_weight), blocked(down_weight.T)])
    first_own = jnp.concatenate([query_weight, key_weight, value_weight], axis=1)
    biases = jnp.concatenate([query_bias, key_bias, value_bias], axis=0)
    bias_row = lax.dynamic_update_slice(
        jnp.zeros((heads + 2, head_dim), bf16), biases, (0, dp_index * per_head)
    ).reshape(1, -1)
    gains = lax.dynamic_update_slice(
        jnp.zeros((2, width), bf16), jnp.stack([attention_gain, feedforward_gain]), (0, dp_index * shard)
    )
    extra = jnp.concatenate(
        [gains, jnp.pad(bias_row, ((0, 0), (0, width - bias_row.shape[1]))), jnp.zeros((13, width), bf16)], axis=0
    )
    cosines, sines = rope_tables(positions)
    plan, hot = attention_plan(segment_ids, parent_ids, dp_index, local_tok)
    steps = lines - 3
    outs = front(ff_blocks, first_own, output_weight.T, extra, layer_input, cosines, sines, lines, members)
    slab, ups, downs = outs[0], list(outs[1 : 1 + steps]), list(outs[1 + steps : 1 + 2 * steps])
    late_up, late_down, first_all, out_t, q_rot, tree, normed, rows = outs[1 + 2 * steps :]
    gain_one, gain_two = rows[0:1], rows[1:2]

    attended, lse, middle, normed_two, other, cot_came, *more = attend(
        plan, hot, q_rot, tree, out_t, layer_input, rows, out_cotangent, ups[-1], downs[-1], late_up, late_down,
        lines, members, scale,
    )

    normed_two_grad, y_own, y_other, ff_parts, up_first, down_first = feed_forward(
        normed_two, out_cotangent, cot_came, [slab] + ups + downs + [late_up, late_down] + more, lines
    )

    ff_parts = ff_parts.reshape(3, lines, width // lines, block)

    dq, dtree, middle_grad, gain_two_grad, line_o, layer_output, up_next, down_next = attend_back(
        plan, hot, q_rot, attended, lse, tree, other, out_t, normed_two_grad, middle, out_cotangent, rows, cosines, sines,
        y_own, y_other, ff_parts, up_first, down_first, lines, members, scale,
    )
    input_grad, sums, small, ff_sums = finish(
        dtree, dq, cosines, sines, normed, first_all, line_o, layer_input, gain_two_grad, gain_one,
        middle_grad, ff_parts, up_next, down_next, lines, members, scale,
    )
    ff_sums = ff_sums[:, :, :hidden].astype(f32)
    gains_out = lax.dynamic_slice(small[0:2], (0, dp_index * shard), (2, shard))
    bias_out = lax.dynamic_slice(
        small[2, : (heads + 2) * head_dim].reshape(heads + 2, head_dim), (0, dp_index * per_head), (heads + 2, per_head)
    )
    return (
        layer_output,
        input_grad,
        gains_out[0],
        sums[:, :q_width],
        bias_out[:heads],
        sums[:, q_width : q_width + 128],
        bias_out[heads : heads + 1],
        sums[:, q_width + 128 : q_width + 256],
        bias_out[heads + 1 :],
        sums[:, q_width + 256 :].T,
        gains_out[1],
        ff_sums[0],
        ff_sums[1],
        ff_sums[2].T,
    )


def solution(mesh):
    placed = (
        P(("dp", "tensor"), None),
        P(("dp", "tensor"), None),
        P("dp"),
        P(),
        P(),
        P("dp"),
        P("dp", "tensor"),
        P("tensor", "dp"),
        P("dp", "tensor"),
        P("tensor", "dp"),
        P("dp", "tensor"),
        P("tensor", "dp"),
        P("tensor", "dp"),
        P("dp"),
        P("dp", "tensor"),
        P("dp", "tensor"),
        P("tensor", "dp"),
    )
    return jax.shard_map(
        functools.partial(on_device, mesh.shape["dp"]),
        mesh=mesh,
        in_specs=placed,
        out_specs=(
            P(("dp", "tensor"), None),
            P(("dp", "tensor"), None),
            P("dp"),
            P("dp", "tensor"),
            P("tensor", "dp"),
            P("dp", "tensor"),
            P("tensor", "dp"),
            P("dp", "tensor"),
            P("tensor", "dp"),
            P("tensor", "dp"),
            P("dp"),
            P("dp", "tensor"),
            P("dp", "tensor"),
            P("tensor", "dp"),
        ),
        check_vma=False,
    )
```

```python
import functools

import jax
import jax.numpy as jnp
from jax import lax
from jax.experimental import pallas as pl
from jax.experimental.pallas import tpu as pltpu
from jax.sharding import PartitionSpec as P

EPS = 1e-06
THETA = 10000.0
TREE_TOK = 5120
TRUNK = 2048
PLANE = 4
NEG = -1e30
LATE = (2, 0)
QB=128; KC=512; KB=256
LOG2E=1.4426950408889634

MESH = pl.DeviceIdType.MESH


def dot_nt(a,b): return lax.dot_general(a,b,(((1,),(1,)),((),())),preferred_element_type=jnp.float32)
def dot_nn(a,b): return lax.dot_general(a,b,(((1,),(0,)),((),())),preferred_element_type=jnp.float32)

def plane_partner(dp, bits):
    one = dp + 1 - 2 * lax.rem(dp, 2)
    if bits == 1:
        return one
    two = 2 - 4 * lax.rem(dp // 2, 2)
    return (dp if bits == 2 else one) + two


def line_partner(dp):
    return dp + PLANE - 2 * PLANE * lax.rem(dp // PLANE, 2)


def greet(dp, core, lines):
    z_at = dp // PLANE
    barrier = pltpu.get_barrier_semaphore()
    for bits in range(1, PLANE):
        pl.semaphore_signal(barrier, inc=1, device_id={"dp": plane_partner(dp, bits)}, device_id_type=MESH)
    pl.semaphore_signal(barrier, inc=1, device_id={"tensor": 1 - core}, device_id_type=MESH)

    @pl.when(z_at > 0)
    def _():
        pl.semaphore_signal(barrier, inc=1, device_id={"dp": dp - PLANE}, device_id_type=MESH)

    @pl.when(z_at < lines - 1)
    def _():
        pl.semaphore_signal(barrier, inc=1, device_id={"dp": dp + PLANE}, device_id_type=MESH)

    beside = jnp.minimum(z_at, 1) + jnp.minimum(lines - 1 - z_at, 1)
    pl.semaphore_wait(barrier, PLANE + beside)


def second_block(start):
    return jnp.where(start < TRUNK, start // KC * (KC // KB) + 1, start // KB)


def masked_chunk(tree_ref, other_ref, blk, start):
    at = pl.ds(pl.multiple_of(second_block(start) * KB, KB), KB)
    k = jnp.concatenate([other_ref[blk, :, 0:128], tree_ref[at, 0:128]], axis=0)
    v = jnp.concatenate([other_ref[blk, :, 128:256], tree_ref[at, 128:256]], axis=0)
    return k, v


def attend_kernel(
    info, hot, q_ref, tree_ref, out_t, x_in, rows_in, cot_in, up_in, down_in, late_up, late_down,
    att_out, lse_out, middle_out, normed_out, other_ref, cot_out, mid_up, mid_down, last_up, last_down,
    far, near, pair_send, pair_recv, cot_send, cot_recv, half_send, half_recv, mid_send, mid_recv, last_send, last_recv,
    *, lines, members, scale,
):
    bf16, f32 = jnp.bfloat16, jnp.float32
    dp = lax.axis_index("dp")
    core = lax.axis_index("tensor")
    z_at = dp // PLANE
    half, width = x_in.shape
    local_tok, q_width = q_ref.shape
    heads = q_width // 128
    rows = heads * QB
    c2 = scale * LOG2E
    mate = {"tensor": 1 - core}
    chip = [None] + [{"dp": plane_partner(dp, bits)} for bits in range(1, PLANE)]
    ways = ((1, 0), (-1, 1))
    place_of = lambda sign: z_at if sign == 1 else lines - 1 - z_at

    def mid_hop(sign, way):
        return pltpu.make_async_remote_copy(
            src_ref=(up_in, down_in)[way].at[1], dst_ref=(mid_up, mid_down)[way],
            send_sem=mid_send.at[way], recv_sem=mid_recv.at[way],
            device_id={"dp": dp + sign * PLANE}, device_id_type=MESH)

    def last_hop(sign, way):
        return pltpu.make_async_remote_copy(
            src_ref=(late_up, late_down)[way].at[0], dst_ref=(last_up, last_down)[way],
            send_sem=last_send.at[way], recv_sem=last_recv.at[way],
            device_id={"dp": dp + sign * PLANE}, device_id_type=MESH)

    def cot_copy(bits):
        return pltpu.make_async_remote_copy(
            src_ref=cot_in, dst_ref=cot_out.at[bits - 1], send_sem=cot_send.at[bits - 1], recv_sem=cot_recv.at[bits - 1],
            device_id=chip[bits], device_id_type=MESH)

    def cot_half(bits):
        at = pl.ds((bits - 1) * (half // 2), half // 2)
        return pltpu.make_async_remote_copy(
            src_ref=cot_out.at[2 - bits, at], dst_ref=cot_out.at[2, at],
            send_sem=half_send.at[bits - 1], recv_sem=half_recv.at[bits - 1],
            device_id=chip[bits], device_id_type=MESH)

    greet(dp, core, lines)
    for sign, way in ways:
        place = place_of(sign)

        @pl.when((place >= lines - 3) & (place < lines - 1))
        def _():
            mid_hop(sign, way).start()

        @pl.when(place == lines - 2)
        def _():
            last_hop(sign, way).start()

    for bits in (1, 2):
        cot_copy(bits).start()

    def step(carry, s, v):
        m, l, acc = carry
        mt = s[:, :128]
        for j in range(1, KC // 128):
            mt = jnp.maximum(mt, s[:, j * 128 : (j + 1) * 128])
        mn = jnp.maximum(m, jnp.max(mt, axis=1, keepdims=True))
        p = jnp.exp2((s - mn) * c2)
        ps = p[:, :128]
        for j in range(1, KC // 128):
            ps = ps + p[:, j * 128 : (j + 1) * 128]
        a = jnp.exp2((m - mn) * c2)
        return mn, l * a + ps, acc * a + dot_nn(p.astype(bf16), v)

    @pl.loop(0, local_tok // QB)
    def _(blk):
        start = lax.rem(dp, members) * local_tok + blk * QB
        nfull = jnp.minimum(start, TRUNK) // KC
        mine = pl.ds(pl.multiple_of(blk * QB, QB), QB)
        slots = members * local_tok // KB
        at = pl.ds(pl.multiple_of(jnp.minimum(start, TRUNK - KC) // KC * KC, KC), KB)
        first = tree_ref[at, :].astype(f32) * jnp.where(start < TRUNK, 1.0, 0.0)
        for slot in range(TRUNK // KB, slots):
            first = first + hot[blk * slots + slot] * tree_ref[slot * KB : (slot + 1) * KB, :].astype(f32)
        other_ref[blk] = first.astype(bf16)
        q = jnp.concatenate([q_ref[mine, h * 128 : (h + 1) * 128] for h in range(heads)], axis=0)

        def body(c, carry):
            at = pl.ds(pl.multiple_of(c * KC, KC), KC)
            return step(carry, dot_nt(q, tree_ref[at, 0:128]), tree_ref[at, 128:256])

        init = (jnp.full((rows, 1), NEG, f32), jnp.zeros((rows, 128), f32), jnp.zeros((rows, 128), f32))
        k, v = masked_chunk(tree_ref, other_ref, blk, start)
        s = dot_nt(q, k)
        col = lax.broadcasted_iota(jnp.int32, (QB, KC), 1)
        row = lax.broadcasted_iota(jnp.int32, (QB, KC), 0)
        ok = col + jnp.where(col < KB, info[2 * blk], info[2 * blk + 1] - KB) <= row
        s = jnp.concatenate([jnp.where(ok, s[h * QB : (h + 1) * QB], NEG) for h in range(heads)], axis=0)
        m, l, acc = lax.fori_loop(0, nfull, body, step(init, s, v))
        lsum = jnp.sum(l, axis=1, keepdims=True)
        out = (acc / lsum).astype(bf16)
        for h in range(heads):
            att_out[mine, h * 128 : (h + 1) * 128] = out[h * QB : (h + 1) * QB]
        lse = jnp.broadcast_to(m * c2 + jnp.log2(lsum), (rows, 128)).T
        lse_out[blk] = lse[0:8, :]

    for bits in (1, 2):
        cot_copy(bits).wait_recv()
    for bits in (1, 2):
        cot_half(bits).start()

    def projected(c):
        at = pl.ds(pl.multiple_of(c * half, half), half)
        return dot_nt(att_out[at, :], out_t[...])

    far[...] = projected(1 - core).astype(bf16)
    pair = pltpu.make_async_remote_copy(
        src_ref=far, dst_ref=near, send_sem=pair_send, recv_sem=pair_recv, device_id=mate, device_id_type=MESH)
    pair.start()
    own = projected(core) + x_in[...].astype(f32)
    pair.wait_recv()
    middle = own + near[...].astype(f32)
    middle_out[...] = middle
    norm = lax.rsqrt(jnp.mean(middle * middle, axis=1, keepdims=True) + EPS)
    normed_out[...] = (middle * norm * rows_in[1:2, :]).astype(bf16)

    pair.wait_send()
    for bits in (1, 2):
        cot_half(bits).wait_recv()
        cot_copy(bits).wait_send()
        cot_half(bits).wait_send()
    for sign, way in ways:
        place = place_of(sign)

        @pl.when(place >= lines - 2)
        def _():
            mid_hop(sign, way).wait_recv()

        @pl.when((place >= lines - 3) & (place < lines - 1))
        def _():
            mid_hop(sign, way).wait_send()

        @pl.when(place == lines - 1)
        def _():
            last_hop(sign, way).wait_recv()

        @pl.when(place == lines - 2)
        def _():
            last_hop(sign, way).wait_send()


def attend(info, hot, q, tree, out_t, x, rows, cot, up, down, late_up, late_down, lines, members, scale):
    bf16, f32 = jnp.bfloat16, jnp.float32
    local_tok, q_width = q.shape
    half, width = x.shape
    anywhere = pl.BlockSpec(memory_space=pl.ANY)
    inside = pl.BlockSpec(memory_space=pltpu.VMEM)
    dma = pltpu.SemaphoreType.DMA
    slab = jax.ShapeDtypeStruct(up.shape[1:], bf16)
    return pl.pallas_call(
        functools.partial(attend_kernel, lines=lines, members=members, scale=scale),
        out_shape=(
            jax.ShapeDtypeStruct((local_tok, q_width), bf16),
            jax.ShapeDtypeStruct((local_tok // QB, 8, q_width // 128 * QB), f32),
            jax.ShapeDtypeStruct((half, width), f32),
            jax.ShapeDtypeStruct((half, width), bf16),
            jax.ShapeDtypeStruct((local_tok // QB, KB, 256), bf16),
            jax.ShapeDtypeStruct((PLANE - 1, half, width), bf16),
            slab, slab, slab, slab,
        ),
        in_specs=[pl.BlockSpec(memory_space=pltpu.SMEM)] * 2 + [inside] * 5 + [anywhere] * 5,
        out_specs=(inside,) * 5 + (anywhere,) * 5,
        scratch_shapes=[
            pltpu.VMEM((half, width), bf16), pltpu.VMEM((half, width), bf16),
            dma, dma, dma((2,)), dma((2,)), dma((2,)), dma((2,)), dma((2,)), dma((2,)), dma((2,)), dma((2,)),
        ],
        compiler_params=pltpu.CompilerParams(vmem_limit_bytes=56 << 20, collective_id=3, has_side_effects=True),
        name="attend",
        cost_estimate=pl.CostEstimate(
            flops=4 * local_tok * q_width * 2304, bytes_accessed=12 << 20, transcendentals=local_tok * q_width * 18
        ),
    )(info, hot, q, tree, out_t, x, rows, cot, up, down, late_up, late_down)


def attend_back_kernel(
    info, hot, q_ref, att_ref, lse_ref, tree_ref, other_ref, out_t, dx_in, middle_in, cot_in, gain_in, cos_in, sin_in,
    y_own, y_other, ff_in, carried_up, carried_down,
    dq_out, dtree_out, middle_grad_out, gain_out, line_out, layer_out, next_up, next_down,
    part_out, part_came, sum_ref, parent_ref, branch, att_grad, y_sum, y_tmp, y_came, own_buf, sum_buf,
    branch_send, branch_recv, y_load, y_send, y_recv, part_send, part_recv, load_sem, hop_send, hop_recv,
    *, lines, members, scale,
):
    bf16, f32 = jnp.bfloat16, jnp.float32
    dp = lax.axis_index("dp")
    core = lax.axis_index("tensor")
    z_at = dp // PLANE
    half, width = cot_in.shape
    local_tok, q_width = q_ref.shape
    heads = q_width // 128
    slab_rows = width // lines
    shard = slab_rows // PLANE
    rows = heads * QB
    c2 = scale * LOG2E
    mate = {"tensor": 1 - core}
    chip = [None] + [{"dp": plane_partner(dp, bits)} for bits in range(1, PLANE)]
    ways = ((1, 0), (-1, 1))
    place_of = lambda sign: z_at if sign == 1 else lines - 1 - z_at

    def own_slab(which, sign):
        return ff_in.at[which, lines - 1 if sign == 1 else 0]

    def own_load(which, sign):
        return pltpu.make_async_copy(own_slab(which, sign), own_buf.at[which], load_sem.at[which, 0])

    def carry_load(which, way):
        return pltpu.make_async_copy((carried_up, carried_down)[way].at[which], sum_buf.at[which], load_sem.at[which, 1])

    def hop(which, sign, way, first_place):
        slab = lines - 2 if sign == 1 else 1
        return pltpu.make_async_remote_copy(
            src_ref=ff_in.at[which, slab] if first_place else sum_buf.at[which],
            dst_ref=(next_up, next_down)[way].at[which],
            send_sem=hop_send.at[which, way], recv_sem=hop_recv.at[which, way],
            device_id={"dp": dp + sign * PLANE}, device_id_type=MESH)

    for sign, way in ways:

        @pl.when(place_of(sign) == 1)
        def _():
            for which in (2, 0, 1):
                own_load(which, sign).start()
                carry_load(which, way).start()

    def y_loads(k, act):
        act(pltpu.make_async_copy(y_own.at[k], y_sum.at[k], y_load.at[k, 0]))
        act(pltpu.make_async_copy(y_other.at[k], y_tmp.at[k], y_load.at[k, 1]))

    for k in range(PLANE):
        y_loads(k, lambda copy: copy.start())
    greet(dp, core, lines)
    for sign, way in ways:

        @pl.when(place_of(sign) == 0)
        def _():
            for which in (2, 0, 1):
                hop(which, sign, way, True).start()

        @pl.when(place_of(sign) == 1)
        def _():
            for which in (2, 0, 1):
                own_load(which, sign).wait()
                carry_load(which, way).wait()
                sum_buf[which] = (own_buf[which].astype(f32) + sum_buf[which].astype(f32)).astype(bf16)
                hop(which, sign, way, False).start()

    middle = middle_in[...]
    norm = lax.rsqrt(jnp.mean(middle * middle, axis=1, keepdims=True) + EPS)
    z_own = middle * norm
    gain_out[...] = jnp.sum(dx_in[...] * z_own, axis=0, keepdims=True)
    w = dx_in[...] * gain_in[1:2, :]
    middle_grad = cot_in[...].astype(f32) + norm * (w - z_own * jnp.mean(w * z_own, axis=1, keepdims=True))
    middle_grad_out[...] = middle_grad
    token_rows = pl.ds(pl.multiple_of(core * half, half), half)
    branch[token_rows, :] = middle_grad.astype(bf16)
    branch_copy = pltpu.make_async_remote_copy(
        src_ref=branch.at[token_rows], dst_ref=branch.at[token_rows], send_sem=branch_send, recv_sem=branch_recv,
        device_id=mate, device_id_type=MESH)
    branch_copy.start()

    quarter = lambda part: pl.ds(part * (half // 2), half // 2)

    def across_copy(bits):
        part = bits - 1
        return pltpu.make_async_remote_copy(
            src_ref=y_sum.at[3, quarter(part)], dst_ref=y_came.at[2, quarter(part)],
            send_sem=y_send.at[0, part], recv_sem=y_recv.at[0, part], device_id=chip[bits], device_id_type=MESH)

    def y_copy(bits, part):
        return pltpu.make_async_remote_copy(
            src_ref=y_sum.at[bits, quarter(part)], dst_ref=y_came.at[bits - 1, quarter(part)],
            send_sem=y_send.at[bits, part], recv_sem=y_recv.at[bits, part], device_id=chip[bits], device_id_type=MESH)

    for k in (3, 1, 2, 0):
        y_loads(k, lambda copy: copy.wait())
        y_sum[k] = (y_sum[k].astype(f32) + y_tmp[k].astype(f32)).astype(bf16)
        if k == 3:
            across_copy(1).start()
            across_copy(2).start()
        elif k:
            y_copy(k, k - 1).start()
    branch_copy.wait_recv()
    att_grad[...] = dot_nn(branch[...], out_t[...]).astype(bf16)
    for z in range(lines):
        tile = dot_nn(branch[:, z * slab_rows : (z + 1) * slab_rows].T, att_ref[...]).astype(bf16)
        for j in range(PLANE):
            part_out[z, j] = tile[j * shard : (j + 1) * shard]

    def part_copy(bits):
        there = lax.rem(plane_partner(dp, bits), PLANE)
        return pltpu.make_async_remote_copy(
            src_ref=part_out.at[:, there], dst_ref=part_came.at[bits - 1],
            send_sem=part_send.at[bits - 1], recv_sem=part_recv.at[bits - 1],
            device_id=chip[bits], device_id_type=MESH)

    for bits in (1, 2):
        across_copy(bits).wait_recv()
        at = quarter(bits - 1)
        y_sum[PLANE - 1 - bits, at] = (y_sum[PLANE - 1 - bits, at].astype(f32) + y_came[2, at].astype(f32)).astype(bf16)
        y_copy(PLANE - 1 - bits, bits - 1).start()
    for bits in range(1, PLANE):
        part_copy(bits).start()

    sum_ref[...] = jnp.zeros_like(sum_ref)
    cosines, sines = cos_in[...], sin_in[...]

    @pl.loop(0, local_tok // QB)
    def _(blk):
        start = lax.rem(dp, members) * local_tok + blk * QB
        nfull = jnp.minimum(start, TRUNK) // KC
        mine = pl.ds(pl.multiple_of(blk * QB, QB), QB)
        stacked = lambda ref: jnp.concatenate([ref[mine, h * 128 : (h + 1) * 128] for h in range(heads)], axis=0)
        q, do, o = stacked(q_ref), stacked(att_grad), stacked(att_ref)
        delta = jnp.sum((do.astype(f32) * o.astype(f32)).T, axis=0, keepdims=True)
        lse = lse_ref[blk][0:1, :]

        def tile(k, v, ok):
            p = jnp.exp2(dot_nt(k, q) * c2 - lse)
            if ok is not None:
                p = jnp.concatenate([jnp.where(ok, p[:, h * QB : (h + 1) * QB], 0.0) for h in range(heads)], axis=1)
            ds = (p * (dot_nt(v, do) - delta)).astype(bf16)
            dq = lax.dot_general(ds, k, (((0,), (0,)), ((), ())), preferred_element_type=f32)
            return dq, dot_nn(ds, q), dot_nn(p.astype(bf16), do)

        def body(c, acc):
            at = pl.ds(pl.multiple_of(c * KC, KC), KC)
            dq, dk, dv = tile(tree_ref[at, 0:128], tree_ref[at, 128:256], None)
            sum_ref[at, 0:128] += dk
            sum_ref[at, 128:256] += dv
            return acc + dq

        k, v = masked_chunk(tree_ref, other_ref, blk, start)
        col = lax.broadcasted_iota(jnp.int32, (KC, QB), 0)
        row = lax.broadcasted_iota(jnp.int32, (KC, QB), 1)
        ok = col + jnp.where(col < KB, info[2 * blk], info[2 * blk + 1] - KB) <= row
        dq, dk, dv = tile(k, v, ok)
        at = pl.ds(pl.multiple_of(second_block(start) * KB, KB), KB)
        sum_ref[at, 0:128] += dk[KB:]
        sum_ref[at, 128:256] += dv[KB:]
        parent_ref[blk, :, 0:128] = dk[:KB]
        parent_ref[blk, :, 128:256] = dv[:KB]

        @pl.when(start < TRUNK)
        def _():
            at = pl.ds(pl.multiple_of(start // KC * KC, KC), KB)
            sum_ref[at, 0:128] += dk[:KB]
            sum_ref[at, 128:256] += dv[:KB]

        dq = lax.fori_loop(0, nfull, body, dq) * scale
        place = pl.ds(pl.multiple_of(blk * QB, QB), QB)
        for h in range(heads):
            part = dq[h * QB : (h + 1) * QB]
            turned = part * cos_in[place, :] - pltpu.roll(part, 64, 1) * sin_in[place, :]
            dq_out[mine, h * 128 : (h + 1) * 128] = turned.astype(bf16)

    dtree_out[0:TRUNK, :] = sum_ref[0:TRUNK, :].astype(bf16)

    @pl.loop(TRUNK // KB, members * local_tok // KB)
    def _(slot):
        at = pl.ds(pl.multiple_of(slot * KB, KB), KB)
        total = sum_ref[at, :]
        for blk in range(local_tok // QB):
            total = total + hot[blk * (members * local_tok // KB) + slot] * parent_ref[blk]
        dtree_out[at, :] = total.astype(bf16)

    for bits in range(1, PLANE):
        part_copy(bits).wait_recv()
    for z in range(lines):
        total = part_out[z, lax.rem(dp, PLANE)].astype(f32)
        for bits in range(1, PLANE):
            total = total + part_came[bits - 1, z].astype(f32)
        line_out[z] = total.astype(bf16)
    for bits in (1, 2):
        for part in range(2):
            y_copy(bits, part).wait_recv()
    total = middle_in[...] + y_sum[0].astype(f32) + y_came[0].astype(f32) + y_came[1].astype(f32)
    layer_out[...] = total.astype(bf16)
    branch_copy.wait_send()
    for bits in range(1, PLANE):
        part_copy(bits).wait_send()
    for bits in (1, 2):
        across_copy(bits).wait_send()
        for part in range(2):
            y_copy(bits, part).wait_send()
    for sign, way in ways:

        @pl.when(place_of(sign) <= 1)
        def _():
            for which in range(3):
                hop(which, sign, way, False).wait_send()

        @pl.when((place_of(sign) >= 1) & (place_of(sign) <= 2))
        def _():
            for which in range(3):
                hop(which, sign, way, False).wait_recv()


def attend_back(info, hot, q, attended, lse, tree, other, out_t, dx, middle, cot, rows, cosines, sines, y_own, y_other, ff_parts, up, down, lines, members, scale):
    bf16, f32 = jnp.bfloat16, jnp.float32
    local_tok, q_width = q.shape
    half, width = cot.shape
    slab_rows = width // lines
    shard = slab_rows // PLANE
    block = up.shape[-1]
    anywhere = pl.BlockSpec(memory_space=pl.ANY)
    inside = pl.BlockSpec(memory_space=pltpu.VMEM)
    dma = pltpu.SemaphoreType.DMA
    slab = jax.ShapeDtypeStruct((3, slab_rows, block), bf16)
    return pl.pallas_call(
        functools.partial(attend_back_kernel, lines=lines, members=members, scale=scale),
        out_shape=(
            jax.ShapeDtypeStruct((local_tok, q_width), bf16),
            jax.ShapeDtypeStruct(tree.shape, bf16),
            jax.ShapeDtypeStruct((half, width), f32),
            jax.ShapeDtypeStruct((1, width), f32),
            jax.ShapeDtypeStruct((lines, shard, q_width), bf16),
            jax.ShapeDtypeStruct((half, width), bf16),
            slab, slab,
        ),
        in_specs=[pl.BlockSpec(memory_space=pltpu.SMEM)] * 2 + [inside] * 12 + [anywhere] * 5,
        out_specs=(inside,) * 6 + (anywhere,) * 2,
        scratch_shapes=[
            pltpu.VMEM((lines, PLANE, shard, q_width), bf16), pltpu.VMEM((PLANE - 1, lines, shard, q_width), bf16),
            pltpu.VMEM(tree.shape, f32), pltpu.VMEM((local_tok // QB, KB, 256), f32),
            pltpu.VMEM((local_tok, width), bf16), pltpu.VMEM((local_tok, q_width), bf16),
            pltpu.VMEM((PLANE, half, width), bf16), pltpu.VMEM((PLANE, half, width), bf16), pltpu.VMEM((PLANE - 1, half, width), bf16),
            pltpu.VMEM((3, slab_rows, block), bf16), pltpu.VMEM((3, slab_rows, block), bf16),
            dma, dma, dma((PLANE, 2)), dma((3, 2)), dma((3, 2)), dma((PLANE - 1,)), dma((PLANE - 1,)), dma((3, 2)), dma((3, 2)), dma((3, 2)),
        ],
        compiler_params=pltpu.CompilerParams(vmem_limit_bytes=62 << 20, collective_id=4, has_side_effects=True),
        name="attend_back",
        cost_estimate=pl.CostEstimate(
            flops=10 * local_tok * q_width * 2304, bytes_accessed=30 << 20, transcendentals=local_tok * q_width * 18
        ),
    )(info, hot, q, attended, lse, tree, other, out_t, dx, middle, cot, rows, cosines, sines, y_own, y_other, ff_parts, up, down)


class Gather:
    def __init__(self, own, whole, sems, dp, lines):
        self.own, self.whole, self.dp, self.lines = own, whole, dp, lines
        self.z_at = dp // PLANE
        self.local_sem, self.line_send, self.line_recv, self.plane_send, self.plane_recv = sems
        self.rows_per = own.shape[0]

    def rows(self, owner):
        return pl.ds(pl.multiple_of(owner * self.rows_per, self.rows_per), self.rows_per)

    def local(self):
        return pltpu.make_async_copy(self.own, self.whole.at[self.rows(self.dp)], self.local_sem)

    def place(self, sign):
        return self.z_at if sign == 1 else self.lines - 1 - self.z_at

    def line_copy(self, sign, step):
        owner = self.dp - sign * step * PLANE
        way = (1 - sign) // 2
        return pltpu.make_async_remote_copy(
            src_ref=self.own if step == 0 else self.whole.at[self.rows(owner)],
            dst_ref=self.whole.at[self.rows(owner)],
            send_sem=self.line_send.at[way, step], recv_sem=self.line_recv.at[way, step],
            device_id={"dp": self.dp + sign * PLANE}, device_id_type=MESH)

    def line_start(self, sign, step):
        place = self.place(sign)

        @pl.when((place >= step) & (place < self.lines - 1))
        def _():
            self.line_copy(sign, step).start()

    def line_wait_send(self, sign, step):
        place = self.place(sign)

        @pl.when((place >= step) & (place < self.lines - 1))
        def _():
            self.line_copy(sign, step).wait_send()

    def plane_copy(self, bits, owner, own=False):
        z = owner // PLANE
        return pltpu.make_async_remote_copy(
            src_ref=self.own if own else self.whole.at[self.rows(owner)],
            dst_ref=self.whole.at[self.rows(owner)],
            send_sem=self.plane_send.at[bits - 1, z], recv_sem=self.plane_recv.at[bits - 1, z],
            device_id={"dp": plane_partner(self.dp, bits)}, device_id_type=MESH)

    def plane_start_own(self):
        for bits in range(1, PLANE):
            self.plane_copy(bits, self.dp, True).start()

    def arrived(self, sign, step):
        place = self.place(sign)

        @pl.when(place >= step + 1)
        def _():
            owner = self.dp - sign * (step + 1) * PLANE
            pltpu.make_async_remote_copy(
                src_ref=self.own, dst_ref=self.whole.at[self.rows(owner)],
                send_sem=self.line_send.at[(1 - sign) // 2, step],
                recv_sem=self.line_recv.at[(1 - sign) // 2, step],
                device_id={"dp": self.dp - sign * PLANE}, device_id_type=MESH).wait_recv()
            if step + 1 < self.lines - 1:

                @pl.when(place < self.lines - 1)
                def _():
                    self.line_copy(sign, step + 1).start()

            for bits in range(1, PLANE):
                self.plane_copy(bits, owner).start()

    def plane_wait_recv(self):
        for bits in range(1, PLANE):
            for z in range(self.lines):
                owner = z * PLANE + lax.rem(plane_partner(self.dp, bits), PLANE)
                self.plane_copy(bits, owner).wait_recv()

    def finish(self):
        for sign in (1, -1):
            for step in range(self.lines - 1):
                self.line_wait_send(sign, step)
        for bits in range(1, PLANE):
            for z in range(self.lines):
                self.plane_copy(bits, z * PLANE + lax.rem(self.dp, PLANE)).wait_send()


def front_kernel(*refs, lines, members, steps):
    (
        gate_in, up_in, down_in, first_in, out_in, extra_in, x_in, cos_in, sin_in,
        own_out, *slab_outs,
    ) = refs[: 10 + 2 * steps]
    (
        late_up, late_down, first_out, out_t, q_out, tree_out, normed_out, rows_out,
        first_all, extra_all, x_all, normed, pair,
        first_local, first_ls, first_lr, first_ps, first_pr,
        extra_local, extra_ls, extra_lr, extra_ps, extra_pr,
        out_local, out_ls, out_lr, out_ps, out_pr,
        spread_local, spread_send, spread_recv, hop_send, hop_recv,
        x_local, x_send, x_recv, keep_sem, pair_local, pair_send, pair_recv, late_send, late_recv,
    ) = refs[10 + 2 * steps :]
    bf16, f32 = jnp.bfloat16, jnp.float32
    dp = lax.axis_index("dp")
    core = lax.axis_index("tensor")
    z_at = dp // PLANE
    j_at = lax.rem(dp, PLANE)
    half, width = x_in.shape
    shard = first_in.shape[0]
    local_tok = 2 * half
    slab_rows = PLANE * shard
    ups, downs = slab_outs[:steps], slab_outs[steps:]
    mate = {"tensor": 1 - core}

    first = Gather(first_in, first_all, (first_local, first_ls, first_lr, first_ps, first_pr), dp, lines)
    extra = Gather(extra_in, extra_all, (extra_local, extra_ls, extra_lr, extra_ps, extra_pr), dp, lines)
    outer = Gather(out_in, out_t, (out_local, out_ls, out_lr, out_ps, out_pr), dp, lines)

    token_rows = lambda c: pl.ds(pl.multiple_of(c * half, half), half)
    x_keep = pltpu.make_async_copy(x_in, x_all.at[token_rows(core)], x_local)
    x_copy = pltpu.make_async_remote_copy(
        src_ref=x_in, dst_ref=x_all.at[token_rows(core)], send_sem=x_send, recv_sem=x_recv,
        device_id=mate, device_id_type=MESH)
    shard_rows = lambda j: pl.ds(pl.multiple_of(j * shard, shard), shard)

    block = own_out.shape[-1]
    last = gate_in.shape[1] - (PLANE - 1) * block

    def by_width(owner, act):
        @pl.when(owner < PLANE - 1)
        def _():
            act(block)

        @pl.when(owner == PLANE - 1)
        def _():
            act(last)

    def piece(which, owner, size):
        at = pl.ds(pl.multiple_of(owner * block, 128), size)
        return (gate_in, up_in, down_in)[which].at[:, at], own_out.at[which, shard_rows(j_at), pl.ds(0, size)]

    def spread(which, bits, owner, size):
        src, dst = piece(which, owner, size)
        return pltpu.make_async_remote_copy(
            src_ref=src, dst_ref=dst,
            send_sem=spread_send.at[which, bits - 1], recv_sem=spread_recv.at[which, bits - 1],
            device_id={"dp": plane_partner(dp, bits)}, device_id_type=MESH)

    def spread_start(which):
        for bits in range(1, PLANE):
            owner = lax.rem(plane_partner(dp, bits), PLANE)
            by_width(owner, lambda size: spread(which, bits, owner, size).start())

    def spread_wait_send(which):
        for bits in range(1, PLANE):
            owner = lax.rem(plane_partner(dp, bits), PLANE)
            by_width(owner, lambda size: spread(which, bits, owner, size).wait_send())

    def spread_wait_recv(which):
        for bits in range(1, PLANE):
            by_width(j_at, lambda size: spread(which, bits, j_at, size).wait_recv())

    def spread_keep(which, act):
        def with_size(size):
            src, dst = piece(which, j_at, size)
            act(pltpu.make_async_copy(src, dst, spread_local.at[which]))

        by_width(j_at, with_size)

    def hop(which, sign, step):
        way = (1 - sign) // 2
        outs = ups if sign == 1 else downs
        return pltpu.make_async_remote_copy(
            src_ref=(own_out if step == 0 else outs[step - 1]).at[which], dst_ref=outs[step].at[which],
            send_sem=hop_send.at[which, way, step], recv_sem=hop_recv.at[which, way, step],
            device_id={"dp": dp + sign * PLANE}, device_id_type=MESH)

    def late_hop(index, sign):
        way = (1 - sign) // 2
        return pltpu.make_async_remote_copy(
            src_ref=(ups if sign == 1 else downs)[steps - 1].at[LATE[index]],
            dst_ref=(late_up if sign == 1 else late_down).at[index],
            send_sem=late_send.at[index, way], recv_sem=late_recv.at[index, way],
            device_id={"dp": dp + sign * PLANE}, device_id_type=MESH)

    for one in (first, extra, outer):
        one.local().start()
    x_keep.start()
    for which in range(3):
        spread_keep(which, lambda copy: copy.start())
    greet(dp, core, lines)
    x_copy.start()
    for sign in (1, -1):
        first.line_start(sign, 0)
        extra.line_start(sign, 0)
    spread_start(2)
    first.plane_start_own()
    extra.plane_start_own()
    for which in (0, 1):
        spread_start(which)

    x_keep.wait()
    x_copy.wait_recv()
    wide = x_all[...].astype(f32)
    scale = lax.rsqrt(jnp.mean(wide * wide, axis=1, keepdims=True) + EPS)

    def hop_start(which):
        spread_keep(which, lambda copy: copy.wait())
        spread_wait_recv(which)
        for sign in (1, -1):
            place = z_at if sign == 1 else lines - 1 - z_at

            @pl.when(place < lines - 1)
            def _():
                hop(which, sign, 0).start()

    for step in range(lines - 1):
        for sign in (1, -1):
            first.arrived(sign, step)
            extra.arrived(sign, step)
        if step == 0:
            hop_start(2)
    hop_start(0)
    hop_start(1)
    first.local().wait()
    extra.local().wait()
    for sign in (1, -1):
        outer.line_start(sign, 0)
    outer.plane_start_own()
    extra.plane_wait_recv()
    first.plane_wait_recv()
    keep = pltpu.make_async_copy(first_all, first_out, keep_sem)
    keep.start()
    small = extra_all[0:16, :].astype(f32)
    for owner in range(1, lines * PLANE):
        small = small + extra_all[16 * owner : 16 * (owner + 1), :].astype(f32)
    rows_out[...] = small
    normed[...] = (x_all[...].astype(f32) * scale * small[0:1, :]).astype(bf16)
    normed_out[...] = normed[...]
    columns = first_all.shape[1]
    q_width = columns - 256
    cosines, sines = cos_in[...], sin_in[...]

    def project(at, count):
        part = dot_nn(normed[...], first_all[:, at : at + count])
        return part + small[2:3, at : at + count]

    def turned(part):
        return (part * cosines + pltpu.roll(part, 64, 1) * sines).astype(bf16)

    both = project(q_width, 256)
    pair[:, 0:128] = turned(both[:, 0:128])
    pair[:, 128:256] = both[:, 128:256].astype(bf16)
    member = lax.rem(dp, members)
    tree_rows = lambda m: pl.ds(pl.multiple_of(m * local_tok, local_tok), local_tok)
    partner = lax.rem(line_partner(dp), members)
    pair_keep = pltpu.make_async_copy(pair, tree_out.at[tree_rows(member)], pair_local)
    pair_keep.start()

    def pair_copy(bits, forward=False):
        at = tree_rows(partner if forward else member)
        index = PLANE + bits - 1 if forward else bits
        return pltpu.make_async_remote_copy(
            src_ref=tree_out.at[at] if forward else pair, dst_ref=tree_out.at[at],
            send_sem=pair_send.at[index], recv_sem=pair_recv.at[index],
            device_id={"dp": plane_partner(dp, bits) if bits else line_partner(dp)}, device_id_type=MESH)

    for bits in range(PLANE):
        pair_copy(bits).start()
    for at in range(0, q_width, 256):
        part = project(at, 256)
        q_out[:, at : at + 128] = turned(part[:, 0:128])
        q_out[:, at + 128 : at + 256] = turned(part[:, 128:256])
    pltpu.make_async_remote_copy(
        src_ref=pair, dst_ref=tree_out.at[tree_rows(partner)], send_sem=pair_send.at[0],
        recv_sem=pair_recv.at[0], device_id={"dp": line_partner(dp)}, device_id_type=MESH).wait_recv()
    for bits in range(1, PLANE):
        pair_copy(bits, True).start()
    for step in range(lines - 1):
        for sign in (1, -1):
            outer.arrived(sign, step)
    for step in range(steps):
        for which in (2, 0, 1):
            for sign in (1, -1):
                place = z_at if sign == 1 else lines - 1 - z_at

                @pl.when(place >= step + 1)
                def _():
                    hop(which, sign, step).wait_recv()
                    if step + 1 < steps:

                        @pl.when(place < lines - 1)
                        def _():
                            hop(which, sign, step + 1).start()

                    elif which in LATE:

                        @pl.when(place < lines - 1)
                        def _():
                            late_hop(LATE.index(which), sign).start()

    for bits in range(1, PLANE):
        pair_copy(bits).wait_recv()
        pair_copy(bits, True).wait_recv()
    outer.plane_wait_recv()
    for index in range(len(LATE)):
        for sign in (1, -1):
            place = z_at if sign == 1 else lines - 1 - z_at

            @pl.when(place >= lines - 2)
            def _():
                late_hop(index, sign).wait_recv()

            @pl.when((place >= lines - 3) & (place < lines - 1))
            def _():
                late_hop(index, sign).wait_send()

    for one in (first, extra, outer):
        one.finish()
    outer.local().wait()
    x_copy.wait_send()
    keep.wait()
    pair_keep.wait()
    for bits in range(PLANE):
        pair_copy(bits).wait_send()
        if bits:
            pair_copy(bits, True).wait_send()
    for which in range(3):
        spread_wait_send(which)
        for sign in (1, -1):
            for step in range(steps):
                place = z_at if sign == 1 else lines - 1 - z_at

                @pl.when((place >= step) & (place < lines - 1))
                def _():
                    hop(which, sign, step).wait_send()


def front(gate, up, down, first, out_t, extra, x, cosines, sines, lines, members):
    bf16, f32 = jnp.bfloat16, jnp.float32
    half, width = x.shape
    local_tok = 2 * half
    shard, columns = first.shape
    block = -(-gate.shape[1] // (PLANE * 128)) * 128
    q_width = out_t.shape[1]
    count = lines * PLANE
    steps = max(lines - 3, 1)
    anywhere = pl.BlockSpec(memory_space=pl.ANY)
    inside = pl.BlockSpec(memory_space=pltpu.VMEM)
    dma = pltpu.SemaphoreType.DMA
    slab = jax.ShapeDtypeStruct((3, PLANE * shard, block), bf16)
    gather_sems = [dma, dma((2, lines)), dma((2, lines)), dma((PLANE - 1, lines)), dma((PLANE - 1, lines))]
    return pl.pallas_call(
        functools.partial(front_kernel, lines=lines, members=members, steps=steps),
        out_shape=(slab,) * (1 + 2 * steps)
        + (jax.ShapeDtypeStruct((len(LATE), PLANE * shard, block), bf16),) * 2
        + (
            jax.ShapeDtypeStruct((width, columns), bf16),
            jax.ShapeDtypeStruct((width, q_width), bf16),
            jax.ShapeDtypeStruct((local_tok, q_width), bf16),
            jax.ShapeDtypeStruct((members * local_tok, 256), bf16),
            jax.ShapeDtypeStruct((local_tok, width), bf16),
            jax.ShapeDtypeStruct((16, width), f32),
        ),
        in_specs=[anywhere] * 7 + [inside] * 2,
        out_specs=(anywhere,) * (3 + 2 * steps) + (anywhere, anywhere, inside, anywhere, inside, inside),
        scratch_shapes=[
            pltpu.VMEM((width, columns), bf16), pltpu.VMEM((16 * count, width), bf16),
            pltpu.VMEM((local_tok, width), bf16), pltpu.VMEM((local_tok, width), bf16),
            pltpu.VMEM((local_tok, 256), bf16),
        ]
        + gather_sems * 3
        + [
            dma((3,)), dma((3, PLANE - 1)), dma((3, PLANE - 1)), dma((3, 2, steps)), dma((3, 2, steps)),
            dma, dma, dma, dma, dma, dma((2 * PLANE - 1,)), dma((2 * PLANE - 1,)),
            dma((len(LATE), 2)), dma((len(LATE), 2)),
        ],
        compiler_params=pltpu.CompilerParams(vmem_limit_bytes=56 << 20, collective_id=1, has_side_effects=True),
        name="front",
        cost_estimate=pl.CostEstimate(flops=2 * local_tok * width * columns, bytes_accessed=30 << 20, transcendentals=0),
    )(gate, up, down, first, out_t, extra, x, cosines, sines)


def ff_kernel(
    *refs, tile_h, tile_n, tile_m, lines, hidden,
):
    early = lines - 3
    x_in, cot_in, cot_came, slab = refs[:4]
    ups, downs = refs[4 : 4 + early], refs[4 + early : 4 + 2 * early]
    late_up, late_down, mid_up, mid_down, last_up, last_down = refs[4 + 2 * early : 10 + 2 * early]
    cots = [cot_in] + [cot_came.at[k] for k in range(PLANE - 1)]
    (
        dx_out, y_own, y_other, parts_out, carried_up, carried_down,
        x_all, cot_all, gate_w, up_w, down_w, prod, gate_g, up_g, far, near, back, y_stage, stage,
        x_send, x_recv, half_send, half_recv, fwd_send, fwd_recv, pair_send, pair_recv, dx_send, dx_recv,
        x_load, cot_load, cot_send, cot_recv, weight_sem, hop_send, hop_recv, y_keep, y_send, y_recv,
        stage_sem, first_send, first_recv,
    ) = refs[10 + 2 * early :]
    bf16 = jnp.bfloat16
    half = x_in.shape[0]
    width = x_in.shape[1]
    block = gate_w.shape[1]
    dp = lax.axis_index("dp")
    core = lax.axis_index("tensor")
    chip = [None] + [{"dp": plane_partner(dp, bits)} for bits in range(1, PLANE)]
    mate = {"tensor": 1 - core}
    rows = lambda k, r, n=1: pl.ds((2 * k + r) * half, n * half)

    z_at = dp // PLANE
    slab_rows = width // lines
    weights = (gate_w, up_w, down_w)
    ways = ((1, 0), (-1, 1))
    place_of = lambda sign: z_at if sign == 1 else lines - 1 - z_at
    place_rows = lambda z: pl.ds(pl.multiple_of(z * slab_rows, slab_rows), slab_rows)

    def second_to_last(which, way):
        if which == 1:
            return (mid_up, mid_down)[way]
        return (late_up, late_down)[way].at[LATE.index(which)]

    def weight_loads(which, act):
        for sign, way in ways:
            pieces = [piece.at[which] for piece in (ups, downs)[way]] + [second_to_last(which, way)]
            if which == 2:
                pieces.append((last_up, last_down)[way])
            for step, piece in enumerate(pieces):

                @pl.when(place_of(sign) >= step + 1)
                def _():
                    act(pltpu.make_async_copy(
                        piece, weights[which].at[place_rows(z_at - sign * (step + 1))],
                        weight_sem.at[which, 1 + way * (lines - 1) + step]))

        act(pltpu.make_async_copy(slab.at[which], weights[which].at[place_rows(z_at)], weight_sem.at[which, 0]))

    def last_hop(which, sign, way):
        origin = 0 if sign == 1 else lines - 1
        return pltpu.make_async_remote_copy(
            src_ref=second_to_last(which, way),
            dst_ref=weights[which].at[pl.ds(origin * slab_rows, slab_rows)],
            send_sem=hop_send.at[which, way], recv_sem=hop_recv.at[which, way],
            device_id={"dp": dp + sign * PLANE}, device_id_type=MESH)

    def weight_wait(which):
        weight_loads(which, lambda copy: copy.wait())
        for sign, way in ways if which < 2 else ():

            @pl.when(place_of(sign) == lines - 1)
            def _():
                last_hop(which, sign, way).wait_recv()

        last = hidden - (PLANE - 1) * block
        if last < block:

            @pl.when(lax.rem(dp, PLANE) == PLANE - 1)
            def _():
                weights[which][:, last:] = jnp.zeros((width, block - last), bf16)

    x_keep = pltpu.make_async_copy(x_in, x_all.at[rows(0, 0)], x_load)
    x_keep.start()

    def cot_keep(k):
        return pltpu.make_async_copy(cots[k], cot_all.at[rows(k, 0)], cot_load.at[k])

    def cot_copy(k):
        return pltpu.make_async_remote_copy(
            src_ref=cots[k], dst_ref=cot_all.at[rows(k, 1)], send_sem=cot_send.at[k], recv_sem=cot_recv.at[k],
            device_id=mate, device_id_type=MESH)

    for k in range(PLANE):
        cot_keep(k).start()
    for which in (2, 0, 1):
        weight_loads(which, lambda copy: copy.start())
    greet(dp, core, lines)
    for which in (0, 1):
        for sign, way in ways:

            @pl.when(place_of(sign) == lines - 2)
            def _():
                last_hop(which, sign, way).start()

    def x_copy(k):
        return pltpu.make_async_remote_copy(
            src_ref=x_in, dst_ref=x_all.at[rows(k, 0) if k else rows(0, 1)],
            send_sem=x_send.at[k], recv_sem=x_recv.at[k],
            device_id=chip[k] if k else mate, device_id_type=MESH)

    def x_half(k):
        at = lambda j: pl.ds(2 * j * half + (k - 1) * (half // 2), half // 2)
        return pltpu.make_async_remote_copy(
            src_ref=x_all.at[at(PLANE - 1 - k)], dst_ref=x_all.at[at(PLANE - 1)],
            send_sem=half_send.at[k - 1], recv_sem=half_recv.at[k - 1],
            device_id=chip[k], device_id_type=MESH)

    def x_forward(k):
        return pltpu.make_async_remote_copy(
            src_ref=x_all.at[rows(k, 0)], dst_ref=x_all.at[rows(k, 1)],
            send_sem=fwd_send.at[k - 1], recv_sem=fwd_recv.at[k - 1],
            device_id=mate, device_id_type=MESH)

    def pair_copy(k):
        return pltpu.make_async_remote_copy(
            src_ref=far.at[k], dst_ref=near.at[k],
            send_sem=pair_send.at[k], recv_sem=pair_recv.at[k],
            device_id=mate, device_id_type=MESH)

    def dx_copy(k):
        return pltpu.make_async_remote_copy(
            src_ref=near.at[k], dst_ref=back.at[k - 1],
            send_sem=dx_send.at[k - 1], recv_sem=dx_recv.at[k - 1],
            device_id=chip[k], device_id_type=MESH)

    x_copy(0).start()
    x_copy(1).start()
    x_copy(2).start()
    for k in range(PLANE):
        cot_copy(k).start()
    for k in range(PLANE):
        cot_keep(k).wait()
        cot_copy(k).wait_recv()
    weight_wait(2)

    starts = list(range(0, max(block - 1023, 0), tile_h)) or [0]
    if block - starts[-1] >= 2 * tile_h:
        starts.append(starts[-1] + tile_h)
    cuts = [pl.ds(at, end - at) for at, end in zip(starts, starts[1:] + [block])]

    @pl.loop(0, 2 * PLANE)
    def _(k):
        at = pl.ds(pl.multiple_of(k * half, half), half)
        for cols in cuts:
            up_g[at, cols] = dot_nn(cot_all[at, :], down_w[:, cols]).astype(bf16)

    def gate_part(k):
        @pl.loop(0, 2)
        def _(r):
            at = pl.ds(pl.multiple_of(2 * k * half + r * half, half), half)
            for cols in cuts:
                gate_g[at, cols] = dot_nn(x_all[at, :], gate_w[:, cols]).astype(bf16)

    def up_part(k):
        @pl.loop(0, 2)
        def _(r):
            at = pl.ds(pl.multiple_of(2 * k * half + r * half, half), half)
            for cols in cuts:
                up = dot_nn(x_all[at, :], up_w[:, cols])
                gate = gate_g[at, cols].astype(jnp.float32)
                pg = up_g[at, cols].astype(jnp.float32)
                sig = 0.5 * jnp.tanh(0.5 * gate) + 0.5
                silu = gate * sig
                prod[at, cols] = (silu * up).astype(bf16)
                up_g[at, cols] = (pg * silu).astype(bf16)
                gate_g[at, cols] = (pg * up * (sig + silu * (1.0 - sig))).astype(bf16)

    def dx_half(k, r):
        at = rows(k, r)

        @pl.loop(0, width // tile_n)
        def _(t):
            cols = pl.ds(pl.multiple_of(t * tile_n, tile_n), tile_n)
            part = dot_nt(gate_g[at, :], gate_w[cols, :]) + dot_nt(up_g[at, :], up_w[cols, :])
            if r:
                far[k, :, cols] = part.astype(bf16)
            else:
                near[k, :, cols] = (part + near[k, :, cols].astype(jnp.float32)).astype(bf16)

    def dx_first(k):
        dx_half(k, 1)
        pair_copy(k).start()

    def dx_second(k):
        pair_copy(k).wait_recv()
        dx_half(k, 0)
        if k:
            dx_copy(k).start()

    def y_local(k):
        return pltpu.make_async_copy(y_stage.at[pl.ds(0, half)], y_own.at[k], y_keep)

    def y_copy(k):
        return pltpu.make_async_remote_copy(
            src_ref=y_stage.at[pl.ds(half, half)], dst_ref=y_other.at[k],
            send_sem=y_send.at[k], recv_sem=y_recv.at[k], device_id=mate, device_id_type=MESH)

    def y_part(k):
        if k:
            y_local(k - 1).wait()
            y_copy(k - 1).wait_send()

        @pl.loop(0, width // tile_n)
        def _(t):
            cols = pl.ds(pl.multiple_of(t * tile_n, tile_n), tile_n)
            y_stage[:, cols] = dot_nt(prod[rows(k, 0, 2), :], down_w[cols, :]).astype(bf16)

        y_local(k).start()
        y_copy(k).start()

    x_keep.wait()
    x_copy(0).wait_recv()
    weight_wait(0)
    gate_part(0)
    for k in (1, 2):
        x_copy(k).wait_recv()
        x_forward(k).start()
    for k in (1, 2):
        x_half(k).start()
    x_forward(1).wait_recv()
    gate_part(1)
    x_forward(2).wait_recv()
    gate_part(2)
    for k in (1, 2):
        x_half(k).wait_recv()
    x_forward(3).start()
    weight_wait(1)
    up_part(0)
    up_part(1)
    x_forward(3).wait_recv()
    gate_part(3)
    up_part(2)
    up_part(3)

    def first_hop(which, sign, way):
        at = pl.ds((lines - 1) * slab_rows if sign == 1 else 0, slab_rows)
        return pltpu.make_async_remote_copy(
            src_ref=parts_out.at[which, at], dst_ref=(carried_up, carried_down)[way].at[which],
            send_sem=first_send.at[which, way], recv_sem=first_recv.at[which, way],
            device_id={"dp": dp + sign * PLANE}, device_id_type=MESH)

    tiles = width // tile_m

    def stage_copy(which, m, slot):
        at = pl.ds(pl.multiple_of(m * tile_m, tile_m), tile_m)
        return pltpu.make_async_copy(stage.at[slot], parts_out.at[which, at], stage_sem.at[slot])

    def weight_grad(which, tokens, grad):
        @pl.loop(0, tiles)
        def _(m):
            at = pl.ds(pl.multiple_of(m * tile_m, tile_m), tile_m)
            tile = dot_nn(tokens[:, at].T, grad[...]).astype(bf16)
            slot = lax.rem(m, 2)

            @pl.when(m >= 2)
            def _():
                stage_copy(which, m - 2, slot).wait()

            stage[slot] = tile
            stage_copy(which, m, slot).start()

        for m in (tiles - 2, tiles - 1):
            stage_copy(which, m, m % 2).wait()
        for sign, way in ways:

            @pl.when(place_of(sign) == 0)
            def _():
                first_hop(which, sign, way).start()

    weight_grad(2, cot_all, prod)
    weight_grad(0, x_all, gate_g)
    dx_first(1)
    dx_first(2)
    dx_second(1)
    dx_first(3)
    dx_second(2)
    dx_first(0)
    dx_second(3)
    dx_second(0)
    weight_grad(1, x_all, up_g)
    for k in range(PLANE):
        y_part(k)

    for k in range(1, PLANE):
        dx_copy(k).wait_recv()
    total = near[0].astype(jnp.float32)
    for k in range(PLANE - 1):
        total = total + back[k].astype(jnp.float32)
    dx_out[...] = total

    for k in range(PLANE):
        if k < PLANE - 1:
            x_copy(k).wait_send()
        if k in (1, 2):
            x_half(k).wait_send()
        pair_copy(k).wait_send()
        if k:
            x_forward(k).wait_send()
            dx_copy(k).wait_send()
    y_local(PLANE - 1).wait()
    y_copy(PLANE - 1).wait_send()
    for k in range(PLANE):
        y_copy(k).wait_recv()
    for which in range(3):
        for sign, way in ways:
            if which < 2:

                @pl.when(place_of(sign) == lines - 2)
                def _():
                    last_hop(which, sign, way).wait_send()

            @pl.when(place_of(sign) == 0)
            def _():
                first_hop(which, sign, way).wait_send()

            @pl.when(place_of(sign) == 1)
            def _():
                first_hop(which, sign, way).wait_recv()

    for k in range(PLANE):
        cot_copy(k).wait_send()


def feed_forward(x, cot, cot_came, slabs, lines, hidden, tile_h=512, tile_n=768, tile_m=256):
    half, width = x.shape
    block = slabs[0].shape[-1]
    slab_rows = width // lines
    tokens = 2 * PLANE * half
    bf16 = jnp.bfloat16
    anywhere = pl.BlockSpec(memory_space=pl.ANY)
    dma = pltpu.SemaphoreType.DMA
    slab = jax.ShapeDtypeStruct((3, slab_rows, block), bf16)
    return pl.pallas_call(
        functools.partial(ff_kernel, tile_h=tile_h, tile_n=tile_n, tile_m=tile_m, lines=lines, hidden=hidden),
        out_shape=(
            jax.ShapeDtypeStruct((half, width), jnp.float32),
            jax.ShapeDtypeStruct((PLANE, half, width), bf16),
            jax.ShapeDtypeStruct((PLANE, half, width), bf16),
            jax.ShapeDtypeStruct((3, width, block), bf16),
            slab,
            slab,
        ),
        in_specs=[anywhere] * (3 + len(slabs)),
        out_specs=(pl.BlockSpec(memory_space=pltpu.VMEM),) + (anywhere,) * 5,
        scratch_shapes=[
            pltpu.VMEM((tokens, width), bf16), pltpu.VMEM((tokens, width), bf16),
            pltpu.VMEM((width, block), bf16), pltpu.VMEM((width, block), bf16), pltpu.VMEM((width, block), bf16),
            pltpu.VMEM((tokens, block), bf16), pltpu.VMEM((tokens, block), bf16), pltpu.VMEM((tokens, block), bf16),
            pltpu.VMEM((PLANE, half, width), bf16), pltpu.VMEM((PLANE, half, width), bf16), pltpu.VMEM((PLANE - 1, half, width), bf16),
            pltpu.VMEM((2 * half, width), bf16), pltpu.VMEM((2, tile_m, block), bf16),
            dma((PLANE - 1,)), dma((PLANE - 1,)), dma((2,)), dma((2,)), dma((PLANE - 1,)), dma((PLANE - 1,)), dma((PLANE,)), dma((PLANE,)),
            dma((PLANE - 1,)), dma((PLANE - 1,)), dma, dma((PLANE,)), dma((PLANE,)), dma((PLANE,)), dma((3, 2 * lines)), dma((3, 2)), dma((3, 2)), dma, dma((PLANE,)), dma((PLANE,)),
            dma((2,)), dma((3, 2)), dma((3, 2)),
        ],
        compiler_params=pltpu.CompilerParams(vmem_limit_bytes=62 << 20, collective_id=0, has_side_effects=True),
        name="feed_forward",
        cost_estimate=pl.CostEstimate(flops=18 * tokens * width * block, bytes_accessed=60 << 20, transcendentals=tokens * block),
    )(x, cot, cot_came, *slabs)


def back_kernel(
    dkv_in, dq_in, cos_in, sin_in, normed_in, first_in, line_o, x_in, rows_in, gain_row_in, middle_grad_in,
    ff_in, carried_up, carried_down,
    input_grad_out, sums_out, small_out, ff_out,
    kv_own, kv_other, kv_plane, kv_merged, kv_line, grads, part_q, part_kv,
    recv_q, recv_kv, line_q, line_kv, from_q, from_kv, from_o,
    far, near, small_own, small_mate, small_plane, small_line,
    own_buf, recv_buf, first_buf, total_buf,
    kv_local, kv_send, kv_recv, kv_line_send, kv_line_recv,
    plane_send, plane_recv, line_send, line_recv,
    mate_send, mate_recv, small_mate_sem, small_plane_send, small_plane_recv, small_line_send, small_line_recv,
    load_sem, own_sem, carry_sem, hop_send, hop_recv, spread_local, spread_send, spread_recv,
    *, lines, members, scale,
):
    bf16, f32 = jnp.bfloat16, jnp.float32
    dp = lax.axis_index("dp")
    core = lax.axis_index("tensor")
    z_at, j_at = dp // PLANE, lax.rem(dp, PLANE)
    half, width = x_in.shape
    local_tok = 2 * half
    slab_rows = width // lines
    shard = slab_rows // PLANE
    q_width = dq_in.shape[1]
    block = total_buf.shape[-1]
    mate = {"tensor": 1 - core}
    chip = [None] + [{"dp": plane_partner(dp, bits)} for bits in range(1, PLANE)]
    there = [j_at] + [lax.rem(plane_partner(dp, bits), PLANE) for bits in range(1, PLANE)]
    side = lax.rem(z_at, 2) * PLANE
    other_side = PLANE - side
    member = lax.rem(dp, members)
    del member
    ways = ((1, 0), (-1, 1))
    place_of = lambda sign: z_at if sign == 1 else lines - 1 - z_at
    tree_rows = lambda m: pl.ds(pl.multiple_of(m * local_tok, local_tok), local_tok)

    kv_loads = [
        pltpu.make_async_copy(dkv_in.at[tree_rows(side + j_at)], kv_own, kv_local.at[0]),
        pltpu.make_async_copy(dkv_in.at[tree_rows(other_side + j_at)], kv_other, kv_local.at[1]),
    ]
    for load in kv_loads:
        load.start()

    def slab_load(which, sign, way, step):
        target = lines - 1 - step + place_of(sign)
        slab = target if sign == 1 else lines - 1 - target
        return pltpu.make_async_copy(ff_in.at[which, slab], own_buf.at[which, way], load_sem.at[which, way])

    def own_load(which):
        return pltpu.make_async_copy(ff_in.at[which, z_at], total_buf.at[which], own_sem.at[which])

    def carry_load(which, sign, way):
        return pltpu.make_async_copy(
            (carried_up if sign == 1 else carried_down).at[which], first_buf.at[which, way], carry_sem.at[which, way])

    order = (2, 0, 1)
    for which in order:
        for sign, way in ways:
            carry_load(which, sign, way).start()

            @pl.when((place_of(sign) >= 1) & (place_of(sign) <= 2))
            def _():
                slab_load(which, sign, way, 2).start()

        own_load(which).start()

    barrier = pltpu.get_barrier_semaphore()
    for bits in range(1, PLANE):
        pl.semaphore_signal(barrier, inc=1, device_id=chip[bits], device_id_type=MESH)
    pl.semaphore_signal(barrier, inc=1, device_id=mate, device_id_type=MESH)
    for apart in range(1, lines):
        pl.semaphore_signal(
            barrier, inc=1, device_id={"dp": lax.rem(z_at + apart, lines) * PLANE + j_at}, device_id_type=MESH)
    pl.semaphore_wait(barrier, PLANE + lines - 1)

    def kv_copy(bits, part):
        at = tree_rows((side if part == 0 else other_side) + there[bits])
        return pltpu.make_async_remote_copy(
            src_ref=dkv_in.at[at], dst_ref=kv_plane.at[bits - 1, part],
            send_sem=kv_send.at[bits - 1, part], recv_sem=kv_recv.at[bits - 1, part],
            device_id=chip[bits], device_id_type=MESH)

    for part in (1, 0):
        for bits in range(1, PLANE):
            kv_copy(bits, part).start()

    def hop(which, sign, way, step, first_place=False):
        slab = lines - 1 - step if sign == 1 else step
        carried = first_buf.at[which, way] if step == 2 else recv_buf.at[which, way, step - 3]
        return pltpu.make_async_remote_copy(
            src_ref=ff_in.at[which, slab] if first_place else carried, dst_ref=recv_buf.at[which, way, step - 2],
            send_sem=hop_send.at[which, way, step - 2], recv_sem=hop_recv.at[which, way, step - 2],
            device_id={"dp": dp + sign * PLANE}, device_id_type=MESH)

    def hop_step(which, step):
        for sign, way in ways:
            place = place_of(sign)
            if step == 2:
                carry_load(which, sign, way).wait()

            @pl.when(place == 0)
            def _():
                hop(which, sign, way, step, True).start()

            @pl.when((place >= 1) & (place <= step))
            def _():
                if step > 2:
                    hop(which, sign, way, step - 1).wait_recv()
                slab_load(which, sign, way, step).wait()
                mine = own_buf[which, way].astype(f32)
                if step == 2:
                    first_buf[which, way] = (mine + first_buf[which, way].astype(f32)).astype(bf16)
                else:
                    recv_buf[which, way, step - 3] = (mine + recv_buf[which, way, step - 3].astype(f32)).astype(bf16)
                hop(which, sign, way, step).start()

            if step < lines - 2:

                @pl.when((place >= 1) & (place <= step + 1))
                def _():
                    slab_load(which, sign, way, step + 1).start()

    for which in order:
        hop_step(which, 2)

    groups = {
        "o": (0, None, None, line_o, from_o, q_width + 256, q_width),
        "q": (1, part_q, recv_q, line_q, from_q, 0, q_width),
        "kv": (2, part_kv, recv_kv, line_kv, from_kv, q_width, 256),
    }

    def plane_copy(name, bits):
        index, part, recv, *_ = groups[name]
        return pltpu.make_async_remote_copy(
            src_ref=part.at[:, there[bits]], dst_ref=recv.at[bits - 1],
            send_sem=plane_send.at[index, bits - 1], recv_sem=plane_recv.at[index, bits - 1],
            device_id=chip[bits], device_id_type=MESH)

    def line_copy(name, apart):
        index, _, _, line, came, *_ = groups[name]
        target = lax.rem(z_at + apart, lines)
        return pltpu.make_async_remote_copy(
            src_ref=line.at[target], dst_ref=came.at[apart - 1],
            send_sem=line_send.at[index, apart - 1], recv_sem=line_recv.at[index, apart - 1],
            device_id={"dp": target * PLANE + j_at}, device_id_type=MESH)

    def plane_start(name):
        for bits in range(1, PLANE):
            plane_copy(name, bits).start()

    def plane_sum(name):
        _, part, recv, line, *_ = groups[name]
        for bits in range(1, PLANE):
            plane_copy(name, bits).wait_recv()
        for z in range(lines):
            total = part[z, j_at].astype(f32)
            for bits in range(1, PLANE):
                total = total + recv[bits - 1, z].astype(f32)
            line[z] = total.astype(bf16)
        line_start(name)

    def line_start(name):
        for apart in range(1, lines):
            line_copy(name, apart).start()

    def line_sum(name):
        *_, line, came, at, size = groups[name]
        for apart in range(1, lines):
            line_copy(name, apart).wait_recv()
        total = line[z_at].astype(f32)
        for apart in range(1, lines):
            total = total + came[apart - 1].astype(f32)
        sums_out[:, at : at + size] = total

    line_start("o")
    cosines, sines = cos_in[...], sin_in[...]

    def turned_back(part):
        return (part * cosines - pltpu.roll(part, 64, 1) * sines).astype(bf16)

    grads[:, 0:q_width] = dq_in[...]

    def weight_part(part, at, size):
        for z in range(lines):
            turned = normed_in[:, z * slab_rows : (z + 1) * slab_rows].T
            tile = dot_nn(turned, grads[:, at : at + size]).astype(bf16)
            for j in range(PLANE):
                part[z, j] = tile[j * shard : (j + 1) * shard]

    weight_part(part_q, 0, q_width)

    columns = lambda j: pl.ds(pl.multiple_of(j * block, block), block)

    def spread(which, bits):
        rows = pl.ds(pl.multiple_of(there[bits] * shard, shard), shard)
        return pltpu.make_async_remote_copy(
            src_ref=total_buf.at[which, rows], dst_ref=ff_out.at[which, :, columns(j_at)],
            send_sem=spread_send.at[which, bits - 1], recv_sem=spread_recv.at[which, bits - 1],
            device_id=chip[bits], device_id_type=MESH)

    def spread_keep(which):
        rows = pl.ds(pl.multiple_of(j_at * shard, shard), shard)
        return pltpu.make_async_copy(
            total_buf.at[which, rows], ff_out.at[which, :, columns(j_at)], spread_local.at[which])

    def line_done(which):
        for step in range(3, lines - 1):
            hop_step(which, step)
        own_load(which).wait()
        for sign, way in ways:

            @pl.when(place_of(sign) >= 1)
            def _():
                hop(which, sign, way, lines - 2).wait_recv()
                came = recv_buf[which, way, lines - 4].astype(f32)
                total_buf[which] = (total_buf[which].astype(f32) + came).astype(bf16)

        for bits in range(1, PLANE):
            spread(which, bits).start()
        spread_keep(which).start()

    for load in kv_loads:
        load.wait()
    for bits in range(1, PLANE):
        kv_copy(bits, 1).wait_recv()
    total = kv_other[...].astype(f32)
    for bits in range(1, PLANE):
        total = total + kv_plane[bits - 1, 1].astype(f32)
    kv_merged[...] = total.astype(bf16)
    kv_across = pltpu.make_async_remote_copy(
        src_ref=kv_merged, dst_ref=kv_line, send_sem=kv_line_send, recv_sem=kv_line_recv,
        device_id={"dp": line_partner(dp)}, device_id_type=MESH)
    kv_across.start()
    plane_start("q")
    line_done(2)
    for bits in range(1, PLANE):
        kv_copy(bits, 0).wait_recv()
    kv_across.wait_recv()
    total = kv_own[...].astype(f32) + kv_line[...].astype(f32)
    for bits in range(1, PLANE):
        total = total + kv_plane[bits - 1, 0].astype(f32)
    grads[:, q_width : q_width + 128] = turned_back(total[:, 0:128] * scale)
    grads[:, q_width + 128 :] = total[:, 128:256].astype(bf16)
    weight_part(part_kv, q_width, 256)
    plane_start("kv")

    def normed_grad(c):
        at = pl.ds(pl.multiple_of(c * half, half), half)
        return dot_nt(grads[at, :], first_in[...])

    far[...] = normed_grad(1 - core).astype(bf16)
    mate_copy = pltpu.make_async_remote_copy(
        src_ref=far, dst_ref=near, send_sem=mate_send, recv_sem=mate_recv, device_id=mate, device_id_type=MESH)
    mate_copy.start()
    mine = normed_grad(core)
    line_done(0)
    mate_copy.wait_recv()
    mine = mine + near[...].astype(f32)
    wide = x_in[...].astype(f32)
    norm = lax.rsqrt(jnp.mean(wide * wide, axis=1, keepdims=True) + EPS)
    z_own = wide * norm
    w = mine * gain_row_in[0:1, :]
    back = norm * (w - z_own * jnp.mean(w * z_own, axis=1, keepdims=True))
    input_grad_out[...] = (middle_grad_in[...] + back).astype(bf16)
    bias = jnp.sum(grads[...].astype(f32), axis=0, keepdims=True)
    small_own[...] = jnp.concatenate(
        [
            jnp.sum(mine * z_own, axis=0, keepdims=True),
            rows_in[...],
            jnp.concatenate([bias, jnp.zeros((1, width - q_width - 256), f32)], axis=1),
            jnp.zeros((5, width), f32),
        ],
        axis=0,
    )
    small_copy = pltpu.make_async_remote_copy(
        src_ref=small_own, dst_ref=small_mate, send_sem=small_mate_sem.at[0], recv_sem=small_mate_sem.at[1],
        device_id=mate, device_id_type=MESH)
    small_copy.start()
    plane_sum("q")
    plane_sum("kv")
    line_done(1)

    small_copy.wait_recv()
    gain_rows = lax.broadcasted_iota(jnp.int32, (8, width), 0) < 2
    small_plane[0] = small_own[...] + jnp.where(gain_rows, small_mate[...], 0.0)

    def small_plane_copy(bits):
        return pltpu.make_async_remote_copy(
            src_ref=small_plane.at[0], dst_ref=small_plane.at[bits],
            send_sem=small_plane_send.at[bits - 1], recv_sem=small_plane_recv.at[bits - 1],
            device_id=chip[bits], device_id_type=MESH)

    def small_line_copy(apart):
        return pltpu.make_async_remote_copy(
            src_ref=small_line.at[0], dst_ref=small_line.at[apart],
            send_sem=small_line_send.at[apart - 1], recv_sem=small_line_recv.at[apart - 1],
            device_id={"dp": lax.rem(z_at + apart, lines) * PLANE + j_at}, device_id_type=MESH)

    for bits in range(1, PLANE):
        small_plane_copy(bits).start()
    for bits in range(1, PLANE):
        small_plane_copy(bits).wait_recv()
    total = small_plane[0]
    for bits in range(1, PLANE):
        total = total + small_plane[bits]
    small_line[0] = total
    for apart in range(1, lines):
        small_line_copy(apart).start()
    line_sum("o")
    line_sum("q")
    line_sum("kv")
    for apart in range(1, lines):
        small_line_copy(apart).wait_recv()
    total = small_line[0]
    for apart in range(1, lines):
        total = total + small_line[apart]
    small_out[...] = total

    for which in order:
        for bits in range(1, PLANE):
            spread(which, bits).wait_recv()
            spread(which, bits).wait_send()
        spread_keep(which).wait()
        for sign, way in ways:
            for step in range(2, lines - 1):

                @pl.when(place_of(sign) <= step)
                def _():
                    hop(which, sign, way, step).wait_send()

    for bits in range(1, PLANE):
        small_plane_copy(bits).wait_send()
        for part in range(2):
            kv_copy(bits, part).wait_send()
        for name in ("q", "kv"):
            plane_copy(name, bits).wait_send()
    for apart in range(1, lines):
        small_line_copy(apart).wait_send()
        for name in groups:
            line_copy(name, apart).wait_send()
    kv_across.wait_send()
    mate_copy.wait_send()
    small_copy.wait_send()


def finish(dkv, dq, cosines, sines, normed, first, line_o, x, gain_rows, gain_row, middle_grad, ff_parts, up, down, lines, members, scale):
    bf16, f32 = jnp.bfloat16, jnp.float32
    half, width = x.shape
    local_tok = 2 * half
    q_width = dq.shape[1]
    slab_rows = width // lines
    shard = slab_rows // PLANE
    block = ff_parts.shape[-1]
    anywhere = pl.BlockSpec(memory_space=pl.ANY)
    inside = pl.BlockSpec(memory_space=pltpu.VMEM)
    dma = pltpu.SemaphoreType.DMA
    near = PLANE - 1
    vmem = lambda *shape: pltpu.VMEM(shape, bf16)
    wide = lambda *shape: pltpu.VMEM(shape, f32)
    pair = (local_tok, 256)
    return pl.pallas_call(
        functools.partial(back_kernel, lines=lines, members=members, scale=scale),
        out_shape=(
            jax.ShapeDtypeStruct((half, width), bf16),
            jax.ShapeDtypeStruct((shard, 2 * q_width + 256), f32),
            jax.ShapeDtypeStruct((8, width), f32),
            jax.ShapeDtypeStruct((3, shard, PLANE * block), bf16),
        ),
        in_specs=[anywhere] + [inside] * 10 + [anywhere] * 3,
        out_specs=(inside, inside, inside, anywhere),
        scratch_shapes=[
            vmem(*pair), vmem(*pair), vmem(near, 2, *pair), vmem(*pair), vmem(*pair),
            vmem(local_tok, q_width + 256), vmem(lines, PLANE, shard, q_width), vmem(lines, PLANE, shard, 256),
            vmem(near, lines, shard, q_width), vmem(near, lines, shard, 256),
            vmem(lines, shard, q_width), vmem(lines, shard, 256),
            vmem(lines - 1, shard, q_width), vmem(lines - 1, shard, 256), vmem(lines - 1, shard, q_width),
            vmem(half, width), vmem(half, width), wide(8, width), wide(8, width), wide(PLANE, 8, width), wide(lines, 8, width),
            vmem(3, 2, slab_rows, block), vmem(3, 2, lines - 3, slab_rows, block), vmem(3, 2, slab_rows, block), vmem(3, slab_rows, block),
            dma((2,)), dma((near, 2)), dma((near, 2)), dma, dma,
            dma((3, near)), dma((3, near)), dma((3, lines - 1)), dma((3, lines - 1)),
            dma, dma, dma((2,)), dma((near,)), dma((near,)), dma((lines - 1,)), dma((lines - 1,)),
            dma((3, 2)), dma((3,)), dma((3, 2)), dma((3, 2, lines - 3)), dma((3, 2, lines - 3)), dma((3,)), dma((3, near)), dma((3, near)),
        ],
        compiler_params=pltpu.CompilerParams(vmem_limit_bytes=62 << 20, collective_id=2, has_side_effects=True),
        name="back",
        cost_estimate=pl.CostEstimate(flops=6 * local_tok * width * (q_width + 256), bytes_accessed=40 << 20, transcendentals=0),
    )(dkv, dq, cosines, sines, normed, first, line_o, x, gain_rows, gain_row, middle_grad, ff_parts, up, down)


def swap(block, axis, count, bits):
    return lax.ppermute(block, axis, [(i, i ^ bits) for i in range(count)])


def rms_scale(values):
    return lax.rsqrt(jnp.mean(values * values, axis=1, keepdims=True) + EPS)


def norm_back(grad, values, gain):
    scale = rms_scale(values)
    z = values * scale
    w = grad * gain
    gain_grad = jnp.sum(grad * z, axis=0)
    return scale * (w - z * jnp.mean(w * z, axis=1, keepdims=True)), gain_grad


def rope_tables(positions):
    exponents = jnp.arange(64, dtype=jnp.float32) * (2.0 / 128)
    frequency = jnp.power(THETA, -exponents)
    angles = positions.astype(jnp.float32)[:, None] * frequency[None, :]
    cosines, sines = jnp.cos(angles), jnp.sin(angles)
    return (
        jnp.concatenate([cosines, cosines], axis=1),
        jnp.concatenate([-sines, sines], axis=1),
    )


def contract_rows(left, right):
    return lax.dot_general(
        left, right, (((0,), (0,)), ((), ())), preferred_element_type=jnp.float32
    )


def contract_cols(left, right):
    return lax.dot_general(
        left, right, (((1,), (1,)), ((), ())), preferred_element_type=jnp.float32
    )


def matmul(left, right):
    return jnp.dot(left, right, preferred_element_type=jnp.float32)


def attention_plan(segment_ids, parent_ids, dp_index, local_tok):
    members = TREE_TOK // local_tok
    first = dp_index // members * TREE_TOK
    slots = lax.dynamic_slice_in_dim(segment_ids, first, TREE_TOK)[::KB]
    numbers = jnp.arange(parent_ids.shape[0], dtype=jnp.int32)
    parents = jnp.sum(jnp.where(slots[:, None] == numbers[None, :], parent_ids[None, :], 0), axis=1)
    places = jnp.arange(slots.shape[0], dtype=jnp.int32)
    holder = jnp.sum(jnp.where(parents[:, None] == slots[None, :], places[None, :], 0), axis=1)
    starts = dp_index % members * local_tok + QB * jnp.arange(local_tok // QB, dtype=jnp.int32)
    slot = starts // KB
    chosen = slot[:, None] == places[None, :]
    pick = lambda table: jnp.sum(jnp.where(chosen, table[None, :], 0), axis=1)
    in_trunk = starts < TRUNK
    is_leaf = pick(parents) != slots[0]
    chunk = jnp.minimum(starts, TRUNK) // KC
    far = jnp.int32(1 << 20)
    block0 = jnp.where(in_trunk, 2 * chunk, jnp.where(is_leaf, pick(holder), TRUNK // KB))
    block1 = jnp.where(in_trunk, 2 * chunk + 1, slot)
    shift0 = jnp.where(in_trunk, block0 * KB - starts, jnp.where(is_leaf, -far, far))
    shift1 = block1 * KB - starts
    hot = jnp.where(~in_trunk[:, None] & (block0[:, None] == places[None, :]), 1.0, 0.0)
    return jnp.stack([shift0, shift1], axis=1).reshape(-1), hot.reshape(-1)


def on_device(
    dp_size,
    layer_input,
    out_cotangent,
    positions,
    segment_ids,
    parent_ids,
    attention_gain,
    query_weight,
    query_bias,
    key_weight,
    key_bias,
    value_weight,
    value_bias,
    output_weight,
    feedforward_gain,
    gate_weight,
    up_weight,
    down_weight,
):
    bf16, f32 = jnp.bfloat16, jnp.float32
    local_tok = positions.shape[0]
    half_tok, width = layer_input.shape
    shard = attention_gain.shape[0]
    heads, head_dim = query_bias.shape[0], 128
    per_head = query_bias.shape[1]
    q_width = heads * head_dim
    hidden = gate_weight.shape[1]
    lines = dp_size // PLANE
    members = TREE_TOK // local_tok
    dp_index = lax.axis_index("dp")
    core = lax.axis_index("tensor")
    scale = head_dim ** (-0.5)

    def line_route(sign, first, last):
        route = []
        for place in range(first, last + 1):
            z = place if sign == 1 else lines - 1 - place
            route += [(z * PLANE + j, (z + sign) * PLANE + j) for j in range(PLANE)]
        return route

    def by_core(mine):
        other = swap(mine, "tensor", 2, 1)
        first = jnp.where(core == 0, mine, other)
        second = jnp.where(core == 0, other, mine)
        return jnp.concatenate([first, second], axis=0)

    first_own = jnp.concatenate([query_weight, key_weight, value_weight], axis=1)
    biases = jnp.concatenate([query_bias, key_bias, value_bias], axis=0)
    bias_row = lax.dynamic_update_slice(
        jnp.zeros((heads + 2, head_dim), bf16), biases, (0, dp_index * per_head)
    ).reshape(1, -1)
    gains = lax.dynamic_update_slice(
        jnp.zeros((2, width), bf16), jnp.stack([attention_gain, feedforward_gain]), (0, dp_index * shard)
    )
    extra = jnp.concatenate(
        [gains, jnp.pad(bias_row, ((0, 0), (0, width - bias_row.shape[1]))), jnp.zeros((13, width), bf16)], axis=0
    )
    cosines, sines = rope_tables(positions)
    plan, hot = attention_plan(segment_ids, parent_ids, dp_index, local_tok)
    steps = lines - 3
    outs = front(
        gate_weight, up_weight, down_weight.T, first_own, output_weight.T, extra, layer_input, cosines, sines, lines, members
    )
    slab, ups, downs = outs[0], list(outs[1 : 1 + steps]), list(outs[1 + steps : 1 + 2 * steps])
    late_up, late_down, first_all, out_t, q_rot, tree, normed, rows = outs[1 + 2 * steps :]

    attended, lse, middle, normed_two, other, cot_came, *more = attend(
        plan, hot, q_rot, tree, out_t, layer_input, rows, out_cotangent, ups[-1], downs[-1], late_up, late_down,
        lines, members, scale,
    )

    normed_two_grad, y_own, y_other, ff_parts, up_first, down_first = feed_forward(
        normed_two, out_cotangent, cot_came, [slab] + ups + downs + [late_up, late_down] + more, lines, hidden
    )

    ff_parts = ff_parts.reshape(3, lines, width // lines, ff_parts.shape[-1])

    dq, dtree, middle_grad, gain_two_grad, line_o, layer_output, up_next, down_next = attend_back(
        plan, hot, q_rot, attended, lse, tree, other, out_t, normed_two_grad, middle, out_cotangent, rows, cosines, sines,
        y_own, y_other, ff_parts, up_first, down_first, lines, members, scale,
    )
    input_grad, sums, small, ff_sums = finish(
        dtree, dq, cosines, sines, normed, first_all, line_o, layer_input, gain_two_grad, rows,
        middle_grad, ff_parts, up_next, down_next, lines, members, scale,
    )
    ff_sums = ff_sums[:, :, :hidden].astype(f32)
    gains_out = lax.dynamic_slice(small[0:2], (0, dp_index * shard), (2, shard))
    bias_out = lax.dynamic_slice(
        small[2, : (heads + 2) * head_dim].reshape(heads + 2, head_dim), (0, dp_index * per_head), (heads + 2, per_head)
    )
    return (
        layer_output,
        input_grad,
        gains_out[0],
        sums[:, :q_width],
        bias_out[:heads],
        sums[:, q_width : q_width + 128],
        bias_out[heads : heads + 1],
        sums[:, q_width + 128 : q_width + 256],
        bias_out[heads + 1 :],
        sums[:, q_width + 256 :].T,
        gains_out[1],
        ff_sums[0],
        ff_sums[1],
        ff_sums[2].T,
    )


def solution(mesh):
    placed = (
        P(("dp", "tensor"), None),
        P(("dp", "tensor"), None),
        P("dp"),
        P(),
        P(),
        P("dp"),
        P("dp", "tensor"),
        P("tensor", "dp"),
        P("dp", "tensor"),
        P("tensor", "dp"),
        P("dp", "tensor"),
        P("tensor", "dp"),
        P("tensor", "dp"),
        P("dp"),
        P("dp", "tensor"),
        P("dp", "tensor"),
        P("tensor", "dp"),
    )
    return jax.shard_map(
        functools.partial(on_device, mesh.shape["dp"]),
        mesh=mesh,
        in_specs=placed,
        out_specs=(
            P(("dp", "tensor"), None),
            P(("dp", "tensor"), None),
            P("dp"),
            P("dp", "tensor"),
            P("tensor", "dp"),
            P("dp", "tensor"),
            P("tensor", "dp"),
            P("dp", "tensor"),
            P("tensor", "dp"),
            P("tensor", "dp"),
            P("dp"),
            P("dp", "tensor"),
            P("dp", "tensor"),
            P("tensor", "dp"),
        ),
        check_vma=False,
    )
```

```python
import functools

import jax
import jax.numpy as jnp
from jax import lax
from jax.experimental import pallas as pl
from jax.experimental.pallas import tpu as pltpu
from jax.sharding import PartitionSpec as P

EPS = 1e-06
THETA = 10000.0
TREE_TOK = 5120
TRUNK = 2048
PLANE = 4
NEG = -1e30
LATE = (2, 0)
QB=128; KC=512; KB=256
LOG2E=1.4426950408889634

MESH = pl.DeviceIdType.MESH


def dot_nt(a,b): return lax.dot_general(a,b,(((1,),(1,)),((),())),preferred_element_type=jnp.float32)
def dot_nn(a,b): return lax.dot_general(a,b,(((1,),(0,)),((),())),preferred_element_type=jnp.float32)

def plane_partner(dp, bits):
    one = dp + 1 - 2 * lax.rem(dp, 2)
    if bits == 1:
        return one
    two = 2 - 4 * lax.rem(dp // 2, 2)
    return (dp if bits == 2 else one) + two


def line_partner(dp):
    return dp + PLANE - 2 * PLANE * lax.rem(dp // PLANE, 2)


def greet(dp, core, lines):
    z_at = dp // PLANE
    barrier = pltpu.get_barrier_semaphore()
    for bits in range(1, PLANE):
        pl.semaphore_signal(barrier, inc=1, device_id={"dp": plane_partner(dp, bits)}, device_id_type=MESH)
    pl.semaphore_signal(barrier, inc=1, device_id={"tensor": 1 - core}, device_id_type=MESH)

    @pl.when(z_at > 0)
    def _():
        pl.semaphore_signal(barrier, inc=1, device_id={"dp": dp - PLANE}, device_id_type=MESH)

    @pl.when(z_at < lines - 1)
    def _():
        pl.semaphore_signal(barrier, inc=1, device_id={"dp": dp + PLANE}, device_id_type=MESH)

    beside = jnp.minimum(z_at, 1) + jnp.minimum(lines - 1 - z_at, 1)
    pl.semaphore_wait(barrier, PLANE + beside)


def second_block(start):
    return jnp.where(start < TRUNK, start // KC * (KC // KB) + 1, start // KB)


def masked_chunk(tree_ref, other_ref, blk, start):
    at = pl.ds(pl.multiple_of(second_block(start) * KB, KB), KB)
    k = jnp.concatenate([other_ref[blk, :, 0:128], tree_ref[at, 0:128]], axis=0)
    v = jnp.concatenate([other_ref[blk, :, 128:256], tree_ref[at, 128:256]], axis=0)
    return k, v


def attend_kernel(
    info, hot, q_ref, tree_ref, out_t, x_in, rows_in, cot_in, up_in, down_in, late_up, late_down,
    att_out, lse_out, middle_out, normed_out, other_ref, cot_out, mid_up, mid_down, last_up, last_down,
    far, near, pair_send, pair_recv, cot_send, cot_recv, half_send, half_recv, mid_send, mid_recv, last_send, last_recv,
    *, lines, members, scale,
):
    bf16, f32 = jnp.bfloat16, jnp.float32
    dp = lax.axis_index("dp")
    core = lax.axis_index("tensor")
    z_at = dp // PLANE
    half, width = x_in.shape
    local_tok, q_width = q_ref.shape
    heads = q_width // 128
    rows = heads * QB
    c2 = scale * LOG2E
    mate = {"tensor": 1 - core}
    chip = [None] + [{"dp": plane_partner(dp, bits)} for bits in range(1, PLANE)]
    ways = ((1, 0), (-1, 1))
    place_of = lambda sign: z_at if sign == 1 else lines - 1 - z_at

    def mid_hop(sign, way):
        return pltpu.make_async_remote_copy(
            src_ref=(up_in, down_in)[way].at[1], dst_ref=(mid_up, mid_down)[way],
            send_sem=mid_send.at[way], recv_sem=mid_recv.at[way],
            device_id={"dp": dp + sign * PLANE}, device_id_type=MESH)

    def last_hop(sign, way):
        return pltpu.make_async_remote_copy(
            src_ref=(late_up, late_down)[way].at[0], dst_ref=(last_up, last_down)[way],
            send_sem=last_send.at[way], recv_sem=last_recv.at[way],
            device_id={"dp": dp + sign * PLANE}, device_id_type=MESH)

    def cot_copy(bits):
        return pltpu.make_async_remote_copy(
            src_ref=cot_in, dst_ref=cot_out.at[bits - 1], send_sem=cot_send.at[bits - 1], recv_sem=cot_recv.at[bits - 1],
            device_id=chip[bits], device_id_type=MESH)

    def cot_half(bits):
        at = pl.ds((bits - 1) * (half // 2), half // 2)
        return pltpu.make_async_remote_copy(
            src_ref=cot_out.at[2 - bits, at], dst_ref=cot_out.at[2, at],
            send_sem=half_send.at[bits - 1], recv_sem=half_recv.at[bits - 1],
            device_id=chip[bits], device_id_type=MESH)

    greet(dp, core, lines)
    for sign, way in ways:
        place = place_of(sign)

        @pl.when((place >= lines - 3) & (place < lines - 1))
        def _():
            mid_hop(sign, way).start()

        @pl.when(place == lines - 2)
        def _():
            last_hop(sign, way).start()

    for bits in (1, 2):
        cot_copy(bits).start()

    def step(carry, s, v):
        m, l, acc = carry
        mt = s[:, :128]
        for j in range(1, KC // 128):
            mt = jnp.maximum(mt, s[:, j * 128 : (j + 1) * 128])
        mn = jnp.maximum(m, jnp.max(mt, axis=1, keepdims=True))
        p = jnp.exp2((s - mn) * c2)
        ps = p[:, :128]
        for j in range(1, KC // 128):
            ps = ps + p[:, j * 128 : (j + 1) * 128]
        a = jnp.exp2((m - mn) * c2)
        return mn, l * a + ps, acc * a + dot_nn(p.astype(bf16), v)

    @pl.loop(0, local_tok // QB)
    def _(blk):
        start = lax.rem(dp, members) * local_tok + blk * QB
        nfull = jnp.minimum(start, TRUNK) // KC
        mine = pl.ds(pl.multiple_of(blk * QB, QB), QB)
        slots = members * local_tok // KB
        at = pl.ds(pl.multiple_of(jnp.minimum(start, TRUNK - KC) // KC * KC, KC), KB)
        first = tree_ref[at, :].astype(f32) * jnp.where(start < TRUNK, 1.0, 0.0)
        for slot in range(TRUNK // KB, slots):
            first = first + hot[blk * slots + slot] * tree_ref[slot * KB : (slot + 1) * KB, :].astype(f32)
        other_ref[blk] = first.astype(bf16)
        q = jnp.concatenate([q_ref[mine, h * 128 : (h + 1) * 128] for h in range(heads)], axis=0)

        def body(c, carry):
            at = pl.ds(pl.multiple_of(c * KC, KC), KC)
            return step(carry, dot_nt(q, tree_ref[at, 0:128]), tree_ref[at, 128:256])

        init = (jnp.full((rows, 1), NEG, f32), jnp.zeros((rows, 128), f32), jnp.zeros((rows, 128), f32))
        k, v = masked_chunk(tree_ref, other_ref, blk, start)
        s = dot_nt(q, k)
        col = lax.broadcasted_iota(jnp.int32, (QB, KC), 1)
        row = lax.broadcasted_iota(jnp.int32, (QB, KC), 0)
        ok = col + jnp.where(col < KB, info[2 * blk], info[2 * blk + 1] - KB) <= row
        s = jnp.concatenate([jnp.where(ok, s[h * QB : (h + 1) * QB], NEG) for h in range(heads)], axis=0)
        m, l, acc = lax.fori_loop(0, nfull, body, step(init, s, v))
        lsum = jnp.sum(l, axis=1, keepdims=True)
        out = (acc / lsum).astype(bf16)
        for h in range(heads):
            att_out[mine, h * 128 : (h + 1) * 128] = out[h * QB : (h + 1) * QB]
        lse = jnp.broadcast_to(m * c2 + jnp.log2(lsum), (rows, 128)).T
        lse_out[blk] = lse[0:8, :]

    for bits in (1, 2):
        cot_copy(bits).wait_recv()
    for bits in (1, 2):
        cot_half(bits).start()

    def projected(c):
        at = pl.ds(pl.multiple_of(c * half, half), half)
        return dot_nt(att_out[at, :], out_t[...])

    far[...] = projected(1 - core).astype(bf16)
    pair = pltpu.make_async_remote_copy(
        src_ref=far, dst_ref=near, send_sem=pair_send, recv_sem=pair_recv, device_id=mate, device_id_type=MESH)
    pair.start()
    own = projected(core) + x_in[...].astype(f32)
    pair.wait_recv()
    middle = own + near[...].astype(f32)
    middle_out[...] = middle
    norm = lax.rsqrt(jnp.mean(middle * middle, axis=1, keepdims=True) + EPS)
    normed_out[...] = (middle * norm * rows_in[1:2, :]).astype(bf16)

    pair.wait_send()
    for bits in (1, 2):
        cot_half(bits).wait_recv()
        cot_copy(bits).wait_send()
        cot_half(bits).wait_send()
    for sign, way in ways:
        place = place_of(sign)

        @pl.when(place >= lines - 2)
        def _():
            mid_hop(sign, way).wait_recv()

        @pl.when((place >= lines - 3) & (place < lines - 1))
        def _():
            mid_hop(sign, way).wait_send()

        @pl.when(place == lines - 1)
        def _():
            last_hop(sign, way).wait_recv()

        @pl.when(place == lines - 2)
        def _():
            last_hop(sign, way).wait_send()


def attend(info, hot, q, tree, out_t, x, rows, cot, up, down, late_up, late_down, lines, members, scale):
    bf16, f32 = jnp.bfloat16, jnp.float32
    local_tok, q_width = q.shape
    half, width = x.shape
    anywhere = pl.BlockSpec(memory_space=pl.ANY)
    inside = pl.BlockSpec(memory_space=pltpu.VMEM)
    dma = pltpu.SemaphoreType.DMA
    slab = jax.ShapeDtypeStruct(up.shape[1:], bf16)
    return pl.pallas_call(
        functools.partial(attend_kernel, lines=lines, members=members, scale=scale),
        out_shape=(
            jax.ShapeDtypeStruct((local_tok, q_width), bf16),
            jax.ShapeDtypeStruct((local_tok // QB, 8, q_width // 128 * QB), f32),
            jax.ShapeDtypeStruct((half, width), f32),
            jax.ShapeDtypeStruct((half, width), bf16),
            jax.ShapeDtypeStruct((local_tok // QB, KB, 256), bf16),
            jax.ShapeDtypeStruct((PLANE - 1, half, width), bf16),
            slab, slab, slab, slab,
        ),
        in_specs=[pl.BlockSpec(memory_space=pltpu.SMEM)] * 2 + [inside] * 5 + [anywhere] * 5,
        out_specs=(inside,) * 5 + (anywhere,) * 5,
        scratch_shapes=[
            pltpu.VMEM((half, width), bf16), pltpu.VMEM((half, width), bf16),
            dma, dma, dma((2,)), dma((2,)), dma((2,)), dma((2,)), dma((2,)), dma((2,)), dma((2,)), dma((2,)),
        ],
        compiler_params=pltpu.CompilerParams(vmem_limit_bytes=56 << 20, collective_id=3, has_side_effects=True),
        name="attend",
        cost_estimate=pl.CostEstimate(
            flops=4 * local_tok * q_width * 2304, bytes_accessed=12 << 20, transcendentals=local_tok * q_width * 18
        ),
    )(info, hot, q, tree, out_t, x, rows, cot, up, down, late_up, late_down)


def attend_back_kernel(
    info, hot, q_ref, att_ref, lse_ref, tree_ref, other_ref, out_t, dx_in, middle_in, cot_in, gain_in, cos_in, sin_in,
    y_own, y_other, ff_in, carried_up, carried_down,
    dq_out, dtree_out, middle_grad_out, gain_out, line_out, layer_out, next_up, next_down,
    part_out, part_came, sum_ref, parent_ref, branch, att_grad, y_sum, y_tmp, y_came, own_buf, sum_buf,
    branch_send, branch_recv, y_load, y_send, y_recv, part_send, part_recv, load_sem, hop_send, hop_recv,
    *, lines, members, scale,
):
    bf16, f32 = jnp.bfloat16, jnp.float32
    dp = lax.axis_index("dp")
    core = lax.axis_index("tensor")
    z_at = dp // PLANE
    half, width = cot_in.shape
    local_tok, q_width = q_ref.shape
    heads = q_width // 128
    slab_rows = width // lines
    shard = slab_rows // PLANE
    rows = heads * QB
    c2 = scale * LOG2E
    mate = {"tensor": 1 - core}
    chip = [None] + [{"dp": plane_partner(dp, bits)} for bits in range(1, PLANE)]
    ways = ((1, 0), (-1, 1))
    place_of = lambda sign: z_at if sign == 1 else lines - 1 - z_at

    def own_slab(which, sign):
        return ff_in.at[which, lines - 1 if sign == 1 else 0]

    def own_load(which, sign):
        return pltpu.make_async_copy(own_slab(which, sign), own_buf.at[which], load_sem.at[which, 0])

    def carry_load(which, way):
        return pltpu.make_async_copy((carried_up, carried_down)[way].at[which], sum_buf.at[which], load_sem.at[which, 1])

    def hop(which, sign, way, first_place):
        slab = lines - 2 if sign == 1 else 1
        return pltpu.make_async_remote_copy(
            src_ref=ff_in.at[which, slab] if first_place else sum_buf.at[which],
            dst_ref=(next_up, next_down)[way].at[which],
            send_sem=hop_send.at[which, way], recv_sem=hop_recv.at[which, way],
            device_id={"dp": dp + sign * PLANE}, device_id_type=MESH)

    for sign, way in ways:

        @pl.when(place_of(sign) == 1)
        def _():
            for which in (2, 0, 1):
                own_load(which, sign).start()
                carry_load(which, way).start()

    def y_loads(k, act):
        act(pltpu.make_async_copy(y_own.at[k], y_sum.at[k], y_load.at[k, 0]))
        act(pltpu.make_async_copy(y_other.at[k], y_tmp.at[k], y_load.at[k, 1]))

    for k in range(PLANE):
        y_loads(k, lambda copy: copy.start())
    greet(dp, core, lines)
    for sign, way in ways:

        @pl.when(place_of(sign) == 0)
        def _():
            for which in (2, 0, 1):
                hop(which, sign, way, True).start()

        @pl.when(place_of(sign) == 1)
        def _():
            for which in (2, 0, 1):
                own_load(which, sign).wait()
                carry_load(which, way).wait()
                sum_buf[which] = (own_buf[which].astype(f32) + sum_buf[which].astype(f32)).astype(bf16)
                hop(which, sign, way, False).start()

    middle = middle_in[...]
    norm = lax.rsqrt(jnp.mean(middle * middle, axis=1, keepdims=True) + EPS)
    z_own = middle * norm
    gain_out[...] = jnp.sum(dx_in[...] * z_own, axis=0, keepdims=True)
    w = dx_in[...] * gain_in[1:2, :]
    middle_grad = cot_in[...].astype(f32) + norm * (w - z_own * jnp.mean(w * z_own, axis=1, keepdims=True))
    middle_grad_out[...] = middle_grad
    token_rows = pl.ds(pl.multiple_of(core * half, half), half)
    branch[token_rows, :] = middle_grad.astype(bf16)
    branch_copy = pltpu.make_async_remote_copy(
        src_ref=branch.at[token_rows], dst_ref=branch.at[token_rows], send_sem=branch_send, recv_sem=branch_recv,
        device_id=mate, device_id_type=MESH)
    branch_copy.start()

    quarter = lambda part: pl.ds(part * (half // 2), half // 2)

    def across_copy(bits):
        part = bits - 1
        return pltpu.make_async_remote_copy(
            src_ref=y_sum.at[3, quarter(part)], dst_ref=y_came.at[2, quarter(part)],
            send_sem=y_send.at[0, part], recv_sem=y_recv.at[0, part], device_id=chip[bits], device_id_type=MESH)

    def y_copy(bits, part):
        return pltpu.make_async_remote_copy(
            src_ref=y_sum.at[bits, quarter(part)], dst_ref=y_came.at[bits - 1, quarter(part)],
            send_sem=y_send.at[bits, part], recv_sem=y_recv.at[bits, part], device_id=chip[bits], device_id_type=MESH)

    for k in (3, 1, 2, 0):
        y_loads(k, lambda copy: copy.wait())
        y_sum[k] = (y_sum[k].astype(f32) + y_tmp[k].astype(f32)).astype(bf16)
        if k == 3:
            across_copy(1).start()
            across_copy(2).start()
        elif k:
            y_copy(k, k - 1).start()
    branch_copy.wait_recv()
    att_grad[...] = dot_nn(branch[...], out_t[...]).astype(bf16)
    for z in range(lines):
        tile = dot_nn(branch[:, z * slab_rows : (z + 1) * slab_rows].T, att_ref[...]).astype(bf16)
        for j in range(PLANE):
            part_out[z, j] = tile[j * shard : (j + 1) * shard]

    def part_copy(bits):
        there = lax.rem(plane_partner(dp, bits), PLANE)
        return pltpu.make_async_remote_copy(
            src_ref=part_out.at[:, there], dst_ref=part_came.at[bits - 1],
            send_sem=part_send.at[bits - 1], recv_sem=part_recv.at[bits - 1],
            device_id=chip[bits], device_id_type=MESH)

    for bits in (1, 2):
        across_copy(bits).wait_recv()
        at = quarter(bits - 1)
        y_sum[PLANE - 1 - bits, at] = (y_sum[PLANE - 1 - bits, at].astype(f32) + y_came[2, at].astype(f32)).astype(bf16)
        y_copy(PLANE - 1 - bits, bits - 1).start()
    for bits in range(1, PLANE):
        part_copy(bits).start()

    sum_ref[...] = jnp.zeros_like(sum_ref)
    cosines, sines = cos_in[...], sin_in[...]

    @pl.loop(0, local_tok // QB)
    def _(blk):
        start = lax.rem(dp, members) * local_tok + blk * QB
        nfull = jnp.minimum(start, TRUNK) // KC
        mine = pl.ds(pl.multiple_of(blk * QB, QB), QB)
        stacked = lambda ref: jnp.concatenate([ref[mine, h * 128 : (h + 1) * 128] for h in range(heads)], axis=0)
        q, do, o = stacked(q_ref), stacked(att_grad), stacked(att_ref)
        delta = jnp.sum((do.astype(f32) * o.astype(f32)).T, axis=0, keepdims=True)
        lse = lse_ref[blk][0:1, :]

        def tile(k, v, ok):
            p = jnp.exp2(dot_nt(k, q) * c2 - lse)
            if ok is not None:
                p = jnp.concatenate([jnp.where(ok, p[:, h * QB : (h + 1) * QB], 0.0) for h in range(heads)], axis=1)
            ds = (p * (dot_nt(v, do) - delta)).astype(bf16)
            dq = lax.dot_general(ds, k, (((0,), (0,)), ((), ())), preferred_element_type=f32)
            return dq, dot_nn(ds, q), dot_nn(p.astype(bf16), do)

        def body(c, acc):
            at = pl.ds(pl.multiple_of(c * KC, KC), KC)
            dq, dk, dv = tile(tree_ref[at, 0:128], tree_ref[at, 128:256], None)
            sum_ref[at, 0:128] += dk
            sum_ref[at, 128:256] += dv
            return acc + dq

        k, v = masked_chunk(tree_ref, other_ref, blk, start)
        col = lax.broadcasted_iota(jnp.int32, (KC, QB), 0)
        row = lax.broadcasted_iota(jnp.int32, (KC, QB), 1)
        ok = col + jnp.where(col < KB, info[2 * blk], info[2 * blk + 1] - KB) <= row
        dq, dk, dv = tile(k, v, ok)
        at = pl.ds(pl.multiple_of(second_block(start) * KB, KB), KB)
        sum_ref[at, 0:128] += dk[KB:]
        sum_ref[at, 128:256] += dv[KB:]
        parent_ref[blk, :, 0:128] = dk[:KB]
        parent_ref[blk, :, 128:256] = dv[:KB]

        @pl.when(start < TRUNK)
        def _():
            at = pl.ds(pl.multiple_of(start // KC * KC, KC), KB)
            sum_ref[at, 0:128] += dk[:KB]
            sum_ref[at, 128:256] += dv[:KB]

        dq = lax.fori_loop(0, nfull, body, dq) * scale
        place = pl.ds(pl.multiple_of(blk * QB, QB), QB)
        for h in range(heads):
            part = dq[h * QB : (h + 1) * QB]
            turned = part * cos_in[place, :] - pltpu.roll(part, 64, 1) * sin_in[place, :]
            dq_out[mine, h * 128 : (h + 1) * 128] = turned.astype(bf16)

    dtree_out[0:TRUNK, :] = sum_ref[0:TRUNK, :].astype(bf16)

    @pl.loop(TRUNK // KB, members * local_tok // KB)
    def _(slot):
        at = pl.ds(pl.multiple_of(slot * KB, KB), KB)
        total = sum_ref[at, :]
        for blk in range(local_tok // QB):
            total = total + hot[blk * (members * local_tok // KB) + slot] * parent_ref[blk]
        dtree_out[at, :] = total.astype(bf16)

    for bits in range(1, PLANE):
        part_copy(bits).wait_recv()
    for z in range(lines):
        total = part_out[z, lax.rem(dp, PLANE)].astype(f32)
        for bits in range(1, PLANE):
            total = total + part_came[bits - 1, z].astype(f32)
        line_out[z] = total.astype(bf16)
    for bits in (1, 2):
        for part in range(2):
            y_copy(bits, part).wait_recv()
    total = middle_in[...] + y_sum[0].astype(f32) + y_came[0].astype(f32) + y_came[1].astype(f32)
    layer_out[...] = total.astype(bf16)
    branch_copy.wait_send()
    for bits in range(1, PLANE):
        part_copy(bits).wait_send()
    for bits in (1, 2):
        across_copy(bits).wait_send()
        for part in range(2):
            y_copy(bits, part).wait_send()
    for sign, way in ways:

        @pl.when(place_of(sign) <= 1)
        def _():
            for which in range(3):
                hop(which, sign, way, False).wait_send()

        @pl.when((place_of(sign) >= 1) & (place_of(sign) <= 2))
        def _():
            for which in range(3):
                hop(which, sign, way, False).wait_recv()


def attend_back(info, hot, q, attended, lse, tree, other, out_t, dx, middle, cot, rows, cosines, sines, y_own, y_other, ff_parts, up, down, lines, members, scale):
    bf16, f32 = jnp.bfloat16, jnp.float32
    local_tok, q_width = q.shape
    half, width = cot.shape
    slab_rows = width // lines
    shard = slab_rows // PLANE
    block = up.shape[-1]
    anywhere = pl.BlockSpec(memory_space=pl.ANY)
    inside = pl.BlockSpec(memory_space=pltpu.VMEM)
    dma = pltpu.SemaphoreType.DMA
    slab = jax.ShapeDtypeStruct((3, slab_rows, block), bf16)
    return pl.pallas_call(
        functools.partial(attend_back_kernel, lines=lines, members=members, scale=scale),
        out_shape=(
            jax.ShapeDtypeStruct((local_tok, q_width), bf16),
            jax.ShapeDtypeStruct(tree.shape, bf16),
            jax.ShapeDtypeStruct((half, width), f32),
            jax.ShapeDtypeStruct((1, width), f32),
            jax.ShapeDtypeStruct((lines, shard, q_width), bf16),
            jax.ShapeDtypeStruct((half, width), bf16),
            slab, slab,
        ),
        in_specs=[pl.BlockSpec(memory_space=pltpu.SMEM)] * 2 + [inside] * 12 + [anywhere] * 5,
        out_specs=(inside,) * 6 + (anywhere,) * 2,
        scratch_shapes=[
            pltpu.VMEM((lines, PLANE, shard, q_width), bf16), pltpu.VMEM((PLANE - 1, lines, shard, q_width), bf16),
            pltpu.VMEM(tree.shape, f32), pltpu.VMEM((local_tok // QB, KB, 256), f32),
            pltpu.VMEM((local_tok, width), bf16), pltpu.VMEM((local_tok, q_width), bf16),
            pltpu.VMEM((PLANE, half, width), bf16), pltpu.VMEM((PLANE, half, width), bf16), pltpu.VMEM((PLANE - 1, half, width), bf16),
            pltpu.VMEM((3, slab_rows, block), bf16), pltpu.VMEM((3, slab_rows, block), bf16),
            dma, dma, dma((PLANE, 2)), dma((3, 2)), dma((3, 2)), dma((PLANE - 1,)), dma((PLANE - 1,)), dma((3, 2)), dma((3, 2)), dma((3, 2)),
        ],
        compiler_params=pltpu.CompilerParams(vmem_limit_bytes=62 << 20, collective_id=4, has_side_effects=True),
        name="attend_back",
        cost_estimate=pl.CostEstimate(
            flops=10 * local_tok * q_width * 2304, bytes_accessed=30 << 20, transcendentals=local_tok * q_width * 18
        ),
    )(info, hot, q, attended, lse, tree, other, out_t, dx, middle, cot, rows, cosines, sines, y_own, y_other, ff_parts, up, down)


class Gather:
    def __init__(self, own, whole, sems, dp, lines):
        self.own, self.whole, self.dp, self.lines = own, whole, dp, lines
        self.z_at = dp // PLANE
        self.local_sem, self.line_send, self.line_recv, self.plane_send, self.plane_recv = sems
        self.rows_per = own.shape[0]

    def rows(self, owner):
        return pl.ds(pl.multiple_of(owner * self.rows_per, self.rows_per), self.rows_per)

    def local(self):
        return pltpu.make_async_copy(self.own, self.whole.at[self.rows(self.dp)], self.local_sem)

    def place(self, sign):
        return self.z_at if sign == 1 else self.lines - 1 - self.z_at

    def line_copy(self, sign, step):
        owner = self.dp - sign * step * PLANE
        way = (1 - sign) // 2
        return pltpu.make_async_remote_copy(
            src_ref=self.own if step == 0 else self.whole.at[self.rows(owner)],
            dst_ref=self.whole.at[self.rows(owner)],
            send_sem=self.line_send.at[way, step], recv_sem=self.line_recv.at[way, step],
            device_id={"dp": self.dp + sign * PLANE}, device_id_type=MESH)

    def line_start(self, sign, step):
        place = self.place(sign)

        @pl.when((place >= step) & (place < self.lines - 1))
        def _():
            self.line_copy(sign, step).start()

    def line_wait_send(self, sign, step):
        place = self.place(sign)

        @pl.when((place >= step) & (place < self.lines - 1))
        def _():
            self.line_copy(sign, step).wait_send()

    def plane_copy(self, bits, owner, own=False):
        z = owner // PLANE
        return pltpu.make_async_remote_copy(
            src_ref=self.own if own else self.whole.at[self.rows(owner)],
            dst_ref=self.whole.at[self.rows(owner)],
            send_sem=self.plane_send.at[bits - 1, z], recv_sem=self.plane_recv.at[bits - 1, z],
            device_id={"dp": plane_partner(self.dp, bits)}, device_id_type=MESH)

    def plane_start_own(self):
        for bits in range(1, PLANE):
            self.plane_copy(bits, self.dp, True).start()

    def arrived(self, sign, step):
        place = self.place(sign)

        @pl.when(place >= step + 1)
        def _():
            owner = self.dp - sign * (step + 1) * PLANE
            pltpu.make_async_remote_copy(
                src_ref=self.own, dst_ref=self.whole.at[self.rows(owner)],
                send_sem=self.line_send.at[(1 - sign) // 2, step],
                recv_sem=self.line_recv.at[(1 - sign) // 2, step],
                device_id={"dp": self.dp - sign * PLANE}, device_id_type=MESH).wait_recv()
            if step + 1 < self.lines - 1:

                @pl.when(place < self.lines - 1)
                def _():
                    self.line_copy(sign, step + 1).start()

            for bits in range(1, PLANE):
                self.plane_copy(bits, owner).start()

    def plane_wait_recv(self):
        for bits in range(1, PLANE):
            for z in range(self.lines):
                owner = z * PLANE + lax.rem(plane_partner(self.dp, bits), PLANE)
                self.plane_copy(bits, owner).wait_recv()

    def finish(self):
        for sign in (1, -1):
            for step in range(self.lines - 1):
                self.line_wait_send(sign, step)
        for bits in range(1, PLANE):
            for z in range(self.lines):
                self.plane_copy(bits, z * PLANE + lax.rem(self.dp, PLANE)).wait_send()


def front_kernel(*refs, lines, members, steps):
    (
        gate_in, up_in, down_in, first_in, out_in, extra_in, x_in, cos_in, sin_in,
        own_out, *slab_outs,
    ) = refs[: 10 + 2 * steps]
    (
        late_up, late_down, first_out, out_t, q_out, tree_out, normed_out, rows_out,
        first_all, extra_all, x_all, normed, pair,
        first_local, first_ls, first_lr, first_ps, first_pr,
        extra_local, extra_ls, extra_lr, extra_ps, extra_pr,
        out_local, out_ls, out_lr, out_ps, out_pr,
        spread_local, spread_send, spread_recv, hop_send, hop_recv,
        x_local, x_send, x_recv, keep_sem, pair_local, pair_send, pair_recv, late_send, late_recv,
    ) = refs[10 + 2 * steps :]
    bf16, f32 = jnp.bfloat16, jnp.float32
    dp = lax.axis_index("dp")
    core = lax.axis_index("tensor")
    z_at = dp // PLANE
    j_at = lax.rem(dp, PLANE)
    half, width = x_in.shape
    shard = first_in.shape[0]
    local_tok = 2 * half
    slab_rows = PLANE * shard
    ups, downs = slab_outs[:steps], slab_outs[steps:]
    mate = {"tensor": 1 - core}

    first = Gather(first_in, first_all, (first_local, first_ls, first_lr, first_ps, first_pr), dp, lines)
    extra = Gather(extra_in, extra_all, (extra_local, extra_ls, extra_lr, extra_ps, extra_pr), dp, lines)
    outer = Gather(out_in, out_t, (out_local, out_ls, out_lr, out_ps, out_pr), dp, lines)

    token_rows = lambda c: pl.ds(pl.multiple_of(c * half, half), half)
    x_keep = pltpu.make_async_copy(x_in, x_all.at[token_rows(core)], x_local)
    x_copy = pltpu.make_async_remote_copy(
        src_ref=x_in, dst_ref=x_all.at[token_rows(core)], send_sem=x_send, recv_sem=x_recv,
        device_id=mate, device_id_type=MESH)
    shard_rows = lambda j: pl.ds(pl.multiple_of(j * shard, shard), shard)

    block = own_out.shape[-1]
    last = gate_in.shape[1] - (PLANE - 1) * block

    def by_width(owner, act):
        @pl.when(owner < PLANE - 1)
        def _():
            act(block)

        @pl.when(owner == PLANE - 1)
        def _():
            act(last)

    def piece(which, owner, size):
        at = pl.ds(pl.multiple_of(owner * block, 128), size)
        return (gate_in, up_in, down_in)[which].at[:, at], own_out.at[which, shard_rows(j_at), pl.ds(0, size)]

    def spread(which, bits, owner, size):
        src, dst = piece(which, owner, size)
        return pltpu.make_async_remote_copy(
            src_ref=src, dst_ref=dst,
            send_sem=spread_send.at[which, bits - 1], recv_sem=spread_recv.at[which, bits - 1],
            device_id={"dp": plane_partner(dp, bits)}, device_id_type=MESH)

    def spread_start(which):
        for bits in range(1, PLANE):
            owner = lax.rem(plane_partner(dp, bits), PLANE)
            by_width(owner, lambda size: spread(which, bits, owner, size).start())

    def spread_wait_send(which):
        for bits in range(1, PLANE):
            owner = lax.rem(plane_partner(dp, bits), PLANE)
            by_width(owner, lambda size: spread(which, bits, owner, size).wait_send())

    def spread_wait_recv(which):
        for bits in range(1, PLANE):
            by_width(j_at, lambda size: spread(which, bits, j_at, size).wait_recv())

    def spread_keep(which, act):
        def with_size(size):
            src, dst = piece(which, j_at, size)
            act(pltpu.make_async_copy(src, dst, spread_local.at[which]))

        by_width(j_at, with_size)

    def hop(which, sign, step):
        way = (1 - sign) // 2
        outs = ups if sign == 1 else downs
        return pltpu.make_async_remote_copy(
            src_ref=(own_out if step == 0 else outs[step - 1]).at[which], dst_ref=outs[step].at[which],
            send_sem=hop_send.at[which, way, step], recv_sem=hop_recv.at[which, way, step],
            device_id={"dp": dp + sign * PLANE}, device_id_type=MESH)

    def late_hop(index, sign):
        way = (1 - sign) // 2
        return pltpu.make_async_remote_copy(
            src_ref=(ups if sign == 1 else downs)[steps - 1].at[LATE[index]],
            dst_ref=(late_up if sign == 1 else late_down).at[index],
            send_sem=late_send.at[index, way], recv_sem=late_recv.at[index, way],
            device_id={"dp": dp + sign * PLANE}, device_id_type=MESH)

    for one in (first, extra, outer):
        one.local().start()
    x_keep.start()
    for which in range(3):
        spread_keep(which, lambda copy: copy.start())
    greet(dp, core, lines)
    x_copy.start()
    for sign in (1, -1):
        first.line_start(sign, 0)
        extra.line_start(sign, 0)
    spread_start(2)
    first.plane_start_own()
    extra.plane_start_own()
    for which in (0, 1):
        spread_start(which)

    x_keep.wait()
    x_copy.wait_recv()
    wide = x_all[...].astype(f32)
    scale = lax.rsqrt(jnp.mean(wide * wide, axis=1, keepdims=True) + EPS)

    def hop_start(which):
        spread_keep(which, lambda copy: copy.wait())
        spread_wait_recv(which)
        for sign in (1, -1):
            place = z_at if sign == 1 else lines - 1 - z_at

            @pl.when(place < lines - 1)
            def _():
                hop(which, sign, 0).start()

    for step in range(lines - 1):
        for sign in (1, -1):
            first.arrived(sign, step)
            extra.arrived(sign, step)
        if step == 0:
            hop_start(2)
    hop_start(0)
    hop_start(1)
    first.local().wait()
    extra.local().wait()
    for sign in (1, -1):
        outer.line_start(sign, 0)
    outer.plane_start_own()
    extra.plane_wait_recv()
    first.plane_wait_recv()
    keep = pltpu.make_async_copy(first_all, first_out, keep_sem)
    keep.start()
    small = extra_all[0:16, :].astype(f32)
    for owner in range(1, lines * PLANE):
        small = small + extra_all[16 * owner : 16 * (owner + 1), :].astype(f32)
    rows_out[...] = small
    normed[...] = (x_all[...].astype(f32) * scale * small[0:1, :]).astype(bf16)
    normed_out[...] = normed[...]
    columns = first_all.shape[1]
    q_width = columns - 256
    cosines, sines = cos_in[...], sin_in[...]

    def project(at, count):
        part = dot_nn(normed[...], first_all[:, at : at + count])
        return part + small[2:3, at : at + count]

    def turned(part):
        return (part * cosines + pltpu.roll(part, 64, 1) * sines).astype(bf16)

    both = project(q_width, 256)
    pair[:, 0:128] = turned(both[:, 0:128])
    pair[:, 128:256] = both[:, 128:256].astype(bf16)
    member = lax.rem(dp, members)
    tree_rows = lambda m: pl.ds(pl.multiple_of(m * local_tok, local_tok), local_tok)
    partner = lax.rem(line_partner(dp), members)
    pair_keep = pltpu.make_async_copy(pair, tree_out.at[tree_rows(member)], pair_local)
    pair_keep.start()

    def pair_copy(bits, forward=False):
        at = tree_rows(partner if forward else member)
        index = PLANE + bits - 1 if forward else bits
        return pltpu.make_async_remote_copy(
            src_ref=tree_out.at[at] if forward else pair, dst_ref=tree_out.at[at],
            send_sem=pair_send.at[index], recv_sem=pair_recv.at[index],
            device_id={"dp": plane_partner(dp, bits) if bits else line_partner(dp)}, device_id_type=MESH)

    for bits in range(PLANE):
        pair_copy(bits).start()
    for at in range(0, q_width, 256):
        part = project(at, 256)
        q_out[:, at : at + 128] = turned(part[:, 0:128])
        q_out[:, at + 128 : at + 256] = turned(part[:, 128:256])
    pltpu.make_async_remote_copy(
        src_ref=pair, dst_ref=tree_out.at[tree_rows(partner)], send_sem=pair_send.at[0],
        recv_sem=pair_recv.at[0], device_id={"dp": line_partner(dp)}, device_id_type=MESH).wait_recv()
    for bits in range(1, PLANE):
        pair_copy(bits, True).start()

    def pass_on(which):
        for step in range(steps):
            for sign in (1, -1):
                place = z_at if sign == 1 else lines - 1 - z_at

                @pl.when(place >= step + 1)
                def _():
                    hop(which, sign, step).wait_recv()
                    if step + 1 < steps:

                        @pl.when(place < lines - 1)
                        def _():
                            hop(which, sign, step + 1).start()

                    elif which in LATE:

                        @pl.when(place < lines - 1)
                        def _():
                            late_hop(LATE.index(which), sign).start()

    pass_on(2)
    for step in range(lines - 1):
        for sign in (1, -1):
            outer.arrived(sign, step)
    pass_on(0)
    pass_on(1)
    for bits in range(1, PLANE):
        pair_copy(bits).wait_recv()
        pair_copy(bits, True).wait_recv()
    outer.plane_wait_recv()
    for index in range(len(LATE)):
        for sign in (1, -1):
            place = z_at if sign == 1 else lines - 1 - z_at

            @pl.when(place >= lines - 2)
            def _():
                late_hop(index, sign).wait_recv()

            @pl.when((place >= lines - 3) & (place < lines - 1))
            def _():
                late_hop(index, sign).wait_send()

    for one in (first, extra, outer):
        one.finish()
    outer.local().wait()
    x_copy.wait_send()
    keep.wait()
    pair_keep.wait()
    for bits in range(PLANE):
        pair_copy(bits).wait_send()
        if bits:
            pair_copy(bits, True).wait_send()
    for which in range(3):
        spread_wait_send(which)
        for sign in (1, -1):
            for step in range(steps):
                place = z_at if sign == 1 else lines - 1 - z_at

                @pl.when((place >= step) & (place < lines - 1))
                def _():
                    hop(which, sign, step).wait_send()


def front(gate, up, down, first, out_t, extra, x, cosines, sines, lines, members):
    bf16, f32 = jnp.bfloat16, jnp.float32
    half, width = x.shape
    local_tok = 2 * half
    shard, columns = first.shape
    block = -(-gate.shape[1] // (PLANE * 128)) * 128
    q_width = out_t.shape[1]
    count = lines * PLANE
    steps = max(lines - 3, 1)
    anywhere = pl.BlockSpec(memory_space=pl.ANY)
    inside = pl.BlockSpec(memory_space=pltpu.VMEM)
    dma = pltpu.SemaphoreType.DMA
    slab = jax.ShapeDtypeStruct((3, PLANE * shard, block), bf16)
    gather_sems = [dma, dma((2, lines)), dma((2, lines)), dma((PLANE - 1, lines)), dma((PLANE - 1, lines))]
    return pl.pallas_call(
        functools.partial(front_kernel, lines=lines, members=members, steps=steps),
        out_shape=(slab,) * (1 + 2 * steps)
        + (jax.ShapeDtypeStruct((len(LATE), PLANE * shard, block), bf16),) * 2
        + (
            jax.ShapeDtypeStruct((width, columns), bf16),
            jax.ShapeDtypeStruct((width, q_width), bf16),
            jax.ShapeDtypeStruct((local_tok, q_width), bf16),
            jax.ShapeDtypeStruct((members * local_tok, 256), bf16),
            jax.ShapeDtypeStruct((local_tok, width), bf16),
            jax.ShapeDtypeStruct((16, width), f32),
        ),
        in_specs=[anywhere] * 7 + [inside] * 2,
        out_specs=(anywhere,) * (3 + 2 * steps) + (anywhere, anywhere, inside, anywhere, inside, inside),
        scratch_shapes=[
            pltpu.VMEM((width, columns), bf16), pltpu.VMEM((16 * count, width), bf16),
            pltpu.VMEM((local_tok, width), bf16), pltpu.VMEM((local_tok, width), bf16),
            pltpu.VMEM((local_tok, 256), bf16),
        ]
        + gather_sems * 3
        + [
            dma((3,)), dma((3, PLANE - 1)), dma((3, PLANE - 1)), dma((3, 2, steps)), dma((3, 2, steps)),
            dma, dma, dma, dma, dma, dma((2 * PLANE - 1,)), dma((2 * PLANE - 1,)),
            dma((len(LATE), 2)), dma((len(LATE), 2)),
        ],
        compiler_params=pltpu.CompilerParams(vmem_limit_bytes=56 << 20, collective_id=1, has_side_effects=True),
        name="front",
        cost_estimate=pl.CostEstimate(flops=2 * local_tok * width * columns, bytes_accessed=30 << 20, transcendentals=0),
    )(gate, up, down, first, out_t, extra, x, cosines, sines)


def ff_kernel(
    *refs, tile_h, tile_n, tile_m, lines, hidden,
):
    early = lines - 3
    x_in, cot_in, cot_came, slab = refs[:4]
    ups, downs = refs[4 : 4 + early], refs[4 + early : 4 + 2 * early]
    late_up, late_down, mid_up, mid_down, last_up, last_down = refs[4 + 2 * early : 10 + 2 * early]
    cots = [cot_in] + [cot_came.at[k] for k in range(PLANE - 1)]
    (
        dx_out, y_own, y_other, parts_out, carried_up, carried_down,
        x_all, cot_all, gate_w, up_w, down_w, prod, gate_g, up_g, far, near, back, y_stage, stage,
        x_send, x_recv, half_send, half_recv, fwd_send, fwd_recv, pair_send, pair_recv, dx_send, dx_recv,
        x_load, cot_load, cot_send, cot_recv, weight_sem, hop_send, hop_recv, y_keep, y_send, y_recv,
        stage_sem, first_send, first_recv,
    ) = refs[10 + 2 * early :]
    bf16 = jnp.bfloat16
    half = x_in.shape[0]
    width = x_in.shape[1]
    block = gate_w.shape[1]
    dp = lax.axis_index("dp")
    core = lax.axis_index("tensor")
    chip = [None] + [{"dp": plane_partner(dp, bits)} for bits in range(1, PLANE)]
    mate = {"tensor": 1 - core}
    rows = lambda k, r, n=1: pl.ds((2 * k + r) * half, n * half)

    z_at = dp // PLANE
    slab_rows = width // lines
    weights = (gate_w, up_w, down_w)
    ways = ((1, 0), (-1, 1))
    place_of = lambda sign: z_at if sign == 1 else lines - 1 - z_at
    place_rows = lambda z: pl.ds(pl.multiple_of(z * slab_rows, slab_rows), slab_rows)

    def second_to_last(which, way):
        if which == 1:
            return (mid_up, mid_down)[way]
        return (late_up, late_down)[way].at[LATE.index(which)]

    def weight_loads(which, act):
        for sign, way in ways:
            pieces = [piece.at[which] for piece in (ups, downs)[way]] + [second_to_last(which, way)]
            if which == 2:
                pieces.append((last_up, last_down)[way])
            for step, piece in enumerate(pieces):

                @pl.when(place_of(sign) >= step + 1)
                def _():
                    act(pltpu.make_async_copy(
                        piece, weights[which].at[place_rows(z_at - sign * (step + 1))],
                        weight_sem.at[which, 1 + way * (lines - 1) + step]))

        act(pltpu.make_async_copy(slab.at[which], weights[which].at[place_rows(z_at)], weight_sem.at[which, 0]))

    def last_hop(which, sign, way):
        origin = 0 if sign == 1 else lines - 1
        return pltpu.make_async_remote_copy(
            src_ref=second_to_last(which, way),
            dst_ref=weights[which].at[pl.ds(origin * slab_rows, slab_rows)],
            send_sem=hop_send.at[which, way], recv_sem=hop_recv.at[which, way],
            device_id={"dp": dp + sign * PLANE}, device_id_type=MESH)

    def weight_wait(which):
        weight_loads(which, lambda copy: copy.wait())
        for sign, way in ways if which < 2 else ():

            @pl.when(place_of(sign) == lines - 1)
            def _():
                last_hop(which, sign, way).wait_recv()

        last = hidden - (PLANE - 1) * block
        if last < block:

            @pl.when(lax.rem(dp, PLANE) == PLANE - 1)
            def _():
                weights[which][:, last:] = jnp.zeros((width, block - last), bf16)

    x_keep = pltpu.make_async_copy(x_in, x_all.at[rows(0, 0)], x_load)
    x_keep.start()

    def cot_keep(k):
        return pltpu.make_async_copy(cots[k], cot_all.at[rows(k, 0)], cot_load.at[k])

    def cot_copy(k):
        return pltpu.make_async_remote_copy(
            src_ref=cots[k], dst_ref=cot_all.at[rows(k, 1)], send_sem=cot_send.at[k], recv_sem=cot_recv.at[k],
            device_id=mate, device_id_type=MESH)

    for k in range(PLANE):
        cot_keep(k).start()
    for which in (2, 0, 1):
        weight_loads(which, lambda copy: copy.start())
    greet(dp, core, lines)
    for which in (0, 1):
        for sign, way in ways:

            @pl.when(place_of(sign) == lines - 2)
            def _():
                last_hop(which, sign, way).start()

    def x_copy(k):
        return pltpu.make_async_remote_copy(
            src_ref=x_in, dst_ref=x_all.at[rows(k, 0) if k else rows(0, 1)],
            send_sem=x_send.at[k], recv_sem=x_recv.at[k],
            device_id=chip[k] if k else mate, device_id_type=MESH)

    def x_half(k):
        at = lambda j: pl.ds(2 * j * half + (k - 1) * (half // 2), half // 2)
        return pltpu.make_async_remote_copy(
            src_ref=x_all.at[at(PLANE - 1 - k)], dst_ref=x_all.at[at(PLANE - 1)],
            send_sem=half_send.at[k - 1], recv_sem=half_recv.at[k - 1],
            device_id=chip[k], device_id_type=MESH)

    def x_forward(k):
        return pltpu.make_async_remote_copy(
            src_ref=x_all.at[rows(k, 0)], dst_ref=x_all.at[rows(k, 1)],
            send_sem=fwd_send.at[k - 1], recv_sem=fwd_recv.at[k - 1],
            device_id=mate, device_id_type=MESH)

    def pair_copy(k):
        return pltpu.make_async_remote_copy(
            src_ref=far.at[k], dst_ref=near.at[k],
            send_sem=pair_send.at[k], recv_sem=pair_recv.at[k],
            device_id=mate, device_id_type=MESH)

    def dx_copy(k):
        return pltpu.make_async_remote_copy(
            src_ref=near.at[k], dst_ref=back.at[k - 1],
            send_sem=dx_send.at[k - 1], recv_sem=dx_recv.at[k - 1],
            device_id=chip[k], device_id_type=MESH)

    x_copy(0).start()
    x_copy(1).start()
    x_copy(2).start()
    for k in range(PLANE):
        cot_copy(k).start()
    for k in range(PLANE):
        cot_keep(k).wait()
        cot_copy(k).wait_recv()
    weight_wait(2)

    starts = list(range(0, max(block - 1023, 0), tile_h)) or [0]
    if block - starts[-1] >= 2 * tile_h:
        starts.append(starts[-1] + tile_h)
    cuts = [pl.ds(at, end - at) for at, end in zip(starts, starts[1:] + [block])]

    @pl.loop(0, 2 * PLANE)
    def _(k):
        at = pl.ds(pl.multiple_of(k * half, half), half)
        for cols in cuts:
            up_g[at, cols] = dot_nn(cot_all[at, :], down_w[:, cols]).astype(bf16)

    def gate_part(k):
        @pl.loop(0, 2)
        def _(r):
            at = pl.ds(pl.multiple_of(2 * k * half + r * half, half), half)
            for cols in cuts:
                gate_g[at, cols] = dot_nn(x_all[at, :], gate_w[:, cols]).astype(bf16)

    def up_part(k):
        @pl.loop(0, 2)
        def _(r):
            at = pl.ds(pl.multiple_of(2 * k * half + r * half, half), half)
            for cols in cuts:
                up = dot_nn(x_all[at, :], up_w[:, cols])
                gate = gate_g[at, cols].astype(jnp.float32)
                pg = up_g[at, cols].astype(jnp.float32)
                sig = 0.5 * jnp.tanh(0.5 * gate) + 0.5
                silu = gate * sig
                prod[at, cols] = (silu * up).astype(bf16)
                up_g[at, cols] = (pg * silu).astype(bf16)
                gate_g[at, cols] = (pg * up * (sig + silu * (1.0 - sig))).astype(bf16)

    def dx_half(k, r):
        at = rows(k, r)

        @pl.loop(0, width // tile_n)
        def _(t):
            cols = pl.ds(pl.multiple_of(t * tile_n, tile_n), tile_n)
            part = dot_nt(gate_g[at, :], gate_w[cols, :]) + dot_nt(up_g[at, :], up_w[cols, :])
            if r:
                far[k, :, cols] = part.astype(bf16)
            else:
                near[k, :, cols] = (part + near[k, :, cols].astype(jnp.float32)).astype(bf16)

    def dx_first(k):
        dx_half(k, 1)
        pair_copy(k).start()

    def dx_second(k):
        pair_copy(k).wait_recv()
        dx_half(k, 0)
        if k:
            dx_copy(k).start()

    def y_local(k):
        return pltpu.make_async_copy(y_stage.at[pl.ds(0, half)], y_own.at[k], y_keep)

    def y_copy(k):
        return pltpu.make_async_remote_copy(
            src_ref=y_stage.at[pl.ds(half, half)], dst_ref=y_other.at[k],
            send_sem=y_send.at[k], recv_sem=y_recv.at[k], device_id=mate, device_id_type=MESH)

    def y_part(k):
        if k:
            y_local(k - 1).wait()
            y_copy(k - 1).wait_send()

        @pl.loop(0, width // tile_n)
        def _(t):
            cols = pl.ds(pl.multiple_of(t * tile_n, tile_n), tile_n)
            y_stage[:, cols] = dot_nt(prod[rows(k, 0, 2), :], down_w[cols, :]).astype(bf16)

        y_local(k).start()
        y_copy(k).start()

    x_keep.wait()
    x_copy(0).wait_recv()
    weight_wait(0)
    gate_part(0)
    for k in (1, 2):
        x_copy(k).wait_recv()
        x_forward(k).start()
    for k in (1, 2):
        x_half(k).start()
    x_forward(1).wait_recv()
    gate_part(1)
    x_forward(2).wait_recv()
    gate_part(2)
    for k in (1, 2):
        x_half(k).wait_recv()
    x_forward(3).start()
    weight_wait(1)
    up_part(0)
    up_part(1)
    x_forward(3).wait_recv()
    gate_part(3)
    up_part(2)
    up_part(3)

    def first_hop(which, sign, way):
        at = pl.ds((lines - 1) * slab_rows if sign == 1 else 0, slab_rows)
        return pltpu.make_async_remote_copy(
            src_ref=parts_out.at[which, at], dst_ref=(carried_up, carried_down)[way].at[which],
            send_sem=first_send.at[which, way], recv_sem=first_recv.at[which, way],
            device_id={"dp": dp + sign * PLANE}, device_id_type=MESH)

    tiles = width // tile_m

    def stage_copy(which, m, slot):
        at = pl.ds(pl.multiple_of(m * tile_m, tile_m), tile_m)
        return pltpu.make_async_copy(stage.at[slot], parts_out.at[which, at], stage_sem.at[slot])

    def weight_grad(which, tokens, grad):
        @pl.loop(0, tiles)
        def _(m):
            at = pl.ds(pl.multiple_of(m * tile_m, tile_m), tile_m)
            tile = dot_nn(tokens[:, at].T, grad[...]).astype(bf16)
            slot = lax.rem(m, 2)

            @pl.when(m >= 2)
            def _():
                stage_copy(which, m - 2, slot).wait()

            stage[slot] = tile
            stage_copy(which, m, slot).start()

        for m in (tiles - 2, tiles - 1):
            stage_copy(which, m, m % 2).wait()
        for sign, way in ways:

            @pl.when(place_of(sign) == 0)
            def _():
                first_hop(which, sign, way).start()

    weight_grad(2, cot_all, prod)
    weight_grad(0, x_all, gate_g)
    dx_first(1)
    dx_first(2)
    dx_second(1)
    dx_first(3)
    dx_second(2)
    dx_first(0)
    dx_second(3)
    dx_second(0)
    weight_grad(1, x_all, up_g)
    for k in range(PLANE):
        y_part(k)

    for k in range(1, PLANE):
        dx_copy(k).wait_recv()
    total = near[0].astype(jnp.float32)
    for k in range(PLANE - 1):
        total = total + back[k].astype(jnp.float32)
    dx_out[...] = total

    for k in range(PLANE):
        if k < PLANE - 1:
            x_copy(k).wait_send()
        if k in (1, 2):
            x_half(k).wait_send()
        pair_copy(k).wait_send()
        if k:
            x_forward(k).wait_send()
            dx_copy(k).wait_send()
    y_local(PLANE - 1).wait()
    y_copy(PLANE - 1).wait_send()
    for k in range(PLANE):
        y_copy(k).wait_recv()
    for which in range(3):
        for sign, way in ways:
            if which < 2:

                @pl.when(place_of(sign) == lines - 2)
                def _():
                    last_hop(which, sign, way).wait_send()

            @pl.when(place_of(sign) == 0)
            def _():
                first_hop(which, sign, way).wait_send()

            @pl.when(place_of(sign) == 1)
            def _():
                first_hop(which, sign, way).wait_recv()

    for k in range(PLANE):
        cot_copy(k).wait_send()


def feed_forward(x, cot, cot_came, slabs, lines, hidden, tile_h=512, tile_n=768, tile_m=256):
    half, width = x.shape
    block = slabs[0].shape[-1]
    slab_rows = width // lines
    tokens = 2 * PLANE * half
    bf16 = jnp.bfloat16
    anywhere = pl.BlockSpec(memory_space=pl.ANY)
    dma = pltpu.SemaphoreType.DMA
    slab = jax.ShapeDtypeStruct((3, slab_rows, block), bf16)
    return pl.pallas_call(
        functools.partial(ff_kernel, tile_h=tile_h, tile_n=tile_n, tile_m=tile_m, lines=lines, hidden=hidden),
        out_shape=(
            jax.ShapeDtypeStruct((half, width), jnp.float32),
            jax.ShapeDtypeStruct((PLANE, half, width), bf16),
            jax.ShapeDtypeStruct((PLANE, half, width), bf16),
            jax.ShapeDtypeStruct((3, width, block), bf16),
            slab,
            slab,
        ),
        in_specs=[anywhere] * (3 + len(slabs)),
        out_specs=(pl.BlockSpec(memory_space=pltpu.VMEM),) + (anywhere,) * 5,
        scratch_shapes=[
            pltpu.VMEM((tokens, width), bf16), pltpu.VMEM((tokens, width), bf16),
            pltpu.VMEM((width, block), bf16), pltpu.VMEM((width, block), bf16), pltpu.VMEM((width, block), bf16),
            pltpu.VMEM((tokens, block), bf16), pltpu.VMEM((tokens, block), bf16), pltpu.VMEM((tokens, block), bf16),
            pltpu.VMEM((PLANE, half, width), bf16), pltpu.VMEM((PLANE, half, width), bf16), pltpu.VMEM((PLANE - 1, half, width), bf16),
            pltpu.VMEM((2 * half, width), bf16), pltpu.VMEM((2, tile_m, block), bf16),
            dma((PLANE - 1,)), dma((PLANE - 1,)), dma((2,)), dma((2,)), dma((PLANE - 1,)), dma((PLANE - 1,)), dma((PLANE,)), dma((PLANE,)),
            dma((PLANE - 1,)), dma((PLANE - 1,)), dma, dma((PLANE,)), dma((PLANE,)), dma((PLANE,)), dma((3, 2 * lines)), dma((3, 2)), dma((3, 2)), dma, dma((PLANE,)), dma((PLANE,)),
            dma((2,)), dma((3, 2)), dma((3, 2)),
        ],
        compiler_params=pltpu.CompilerParams(vmem_limit_bytes=62 << 20, collective_id=0, has_side_effects=True),
        name="feed_forward",
        cost_estimate=pl.CostEstimate(flops=18 * tokens * width * block, bytes_accessed=60 << 20, transcendentals=tokens * block),
    )(x, cot, cot_came, *slabs)


def back_kernel(
    dkv_in, dq_in, cos_in, sin_in, normed_in, first_in, line_o, x_in, rows_in, gain_row_in, middle_grad_in,
    ff_in, carried_up, carried_down,
    input_grad_out, sums_out, small_out, ff_out,
    kv_own, kv_other, kv_plane, kv_merged, kv_line, grads, part_q, part_kv,
    recv_q, recv_kv, line_q, line_kv, from_q, from_kv, from_o,
    far, near, small_own, small_mate, small_plane, small_line,
    own_buf, recv_buf, first_buf, total_buf,
    kv_local, kv_send, kv_recv, kv_line_send, kv_line_recv,
    plane_send, plane_recv, line_send, line_recv,
    mate_send, mate_recv, small_mate_sem, small_plane_send, small_plane_recv, small_line_send, small_line_recv,
    load_sem, own_sem, carry_sem, hop_send, hop_recv, spread_local, spread_send, spread_recv,
    *, lines, members, scale,
):
    bf16, f32 = jnp.bfloat16, jnp.float32
    dp = lax.axis_index("dp")
    core = lax.axis_index("tensor")
    z_at, j_at = dp // PLANE, lax.rem(dp, PLANE)
    half, width = x_in.shape
    local_tok = 2 * half
    slab_rows = width // lines
    shard = slab_rows // PLANE
    q_width = dq_in.shape[1]
    block = total_buf.shape[-1]
    mate = {"tensor": 1 - core}
    chip = [None] + [{"dp": plane_partner(dp, bits)} for bits in range(1, PLANE)]
    there = [j_at] + [lax.rem(plane_partner(dp, bits), PLANE) for bits in range(1, PLANE)]
    side = lax.rem(z_at, 2) * PLANE
    other_side = PLANE - side
    member = lax.rem(dp, members)
    del member
    ways = ((1, 0), (-1, 1))
    place_of = lambda sign: z_at if sign == 1 else lines - 1 - z_at
    tree_rows = lambda m: pl.ds(pl.multiple_of(m * local_tok, local_tok), local_tok)

    kv_loads = [
        pltpu.make_async_copy(dkv_in.at[tree_rows(side + j_at)], kv_own, kv_local.at[0]),
        pltpu.make_async_copy(dkv_in.at[tree_rows(other_side + j_at)], kv_other, kv_local.at[1]),
    ]
    for load in kv_loads:
        load.start()

    def slab_load(which, sign, way, step):
        target = lines - 1 - step + place_of(sign)
        slab = target if sign == 1 else lines - 1 - target
        return pltpu.make_async_copy(ff_in.at[which, slab], own_buf.at[which, way], load_sem.at[which, way])

    def own_load(which):
        return pltpu.make_async_copy(ff_in.at[which, z_at], total_buf.at[which], own_sem.at[which])

    def carry_load(which, sign, way):
        return pltpu.make_async_copy(
            (carried_up if sign == 1 else carried_down).at[which], first_buf.at[which, way], carry_sem.at[which, way])

    order = (2, 0, 1)
    for which in order:
        for sign, way in ways:
            carry_load(which, sign, way).start()

            @pl.when((place_of(sign) >= 1) & (place_of(sign) <= 2))
            def _():
                slab_load(which, sign, way, 2).start()

        own_load(which).start()

    barrier = pltpu.get_barrier_semaphore()
    for bits in range(1, PLANE):
        pl.semaphore_signal(barrier, inc=1, device_id=chip[bits], device_id_type=MESH)
    pl.semaphore_signal(barrier, inc=1, device_id=mate, device_id_type=MESH)
    for apart in range(1, lines):
        pl.semaphore_signal(
            barrier, inc=1, device_id={"dp": lax.rem(z_at + apart, lines) * PLANE + j_at}, device_id_type=MESH)
    pl.semaphore_wait(barrier, PLANE + lines - 1)

    def kv_copy(bits, part):
        at = tree_rows((side if part == 0 else other_side) + there[bits])
        return pltpu.make_async_remote_copy(
            src_ref=dkv_in.at[at], dst_ref=kv_plane.at[bits - 1, part],
            send_sem=kv_send.at[bits - 1, part], recv_sem=kv_recv.at[bits - 1, part],
            device_id=chip[bits], device_id_type=MESH)

    for part in (1, 0):
        for bits in range(1, PLANE):
            kv_copy(bits, part).start()

    def hop(which, sign, way, step, first_place=False):
        slab = lines - 1 - step if sign == 1 else step
        carried = first_buf.at[which, way] if step == 2 else recv_buf.at[which, way, step - 3]
        return pltpu.make_async_remote_copy(
            src_ref=ff_in.at[which, slab] if first_place else carried, dst_ref=recv_buf.at[which, way, step - 2],
            send_sem=hop_send.at[which, way, step - 2], recv_sem=hop_recv.at[which, way, step - 2],
            device_id={"dp": dp + sign * PLANE}, device_id_type=MESH)

    def hop_step(which, step):
        for sign, way in ways:
            place = place_of(sign)
            if step == 2:
                carry_load(which, sign, way).wait()

            @pl.when(place == 0)
            def _():
                hop(which, sign, way, step, True).start()

            @pl.when((place >= 1) & (place <= step))
            def _():
                if step > 2:
                    hop(which, sign, way, step - 1).wait_recv()
                slab_load(which, sign, way, step).wait()
                mine = own_buf[which, way].astype(f32)
                if step == 2:
                    first_buf[which, way] = (mine + first_buf[which, way].astype(f32)).astype(bf16)
                else:
                    recv_buf[which, way, step - 3] = (mine + recv_buf[which, way, step - 3].astype(f32)).astype(bf16)
                hop(which, sign, way, step).start()

            if step < lines - 2:

                @pl.when((place >= 1) & (place <= step + 1))
                def _():
                    slab_load(which, sign, way, step + 1).start()

    for which in order:
        hop_step(which, 2)

    groups = {
        "o": (0, None, None, line_o, from_o, q_width + 256, q_width),
        "q": (1, part_q, recv_q, line_q, from_q, 0, q_width),
        "kv": (2, part_kv, recv_kv, line_kv, from_kv, q_width, 256),
    }

    def plane_copy(name, bits):
        index, part, recv, *_ = groups[name]
        return pltpu.make_async_remote_copy(
            src_ref=part.at[:, there[bits]], dst_ref=recv.at[bits - 1],
            send_sem=plane_send.at[index, bits - 1], recv_sem=plane_recv.at[index, bits - 1],
            device_id=chip[bits], device_id_type=MESH)

    def line_copy(name, apart):
        index, _, _, line, came, *_ = groups[name]
        target = lax.rem(z_at + apart, lines)
        return pltpu.make_async_remote_copy(
            src_ref=line.at[target], dst_ref=came.at[apart - 1],
            send_sem=line_send.at[index, apart - 1], recv_sem=line_recv.at[index, apart - 1],
            device_id={"dp": target * PLANE + j_at}, device_id_type=MESH)

    def plane_start(name):
        for bits in range(1, PLANE):
            plane_copy(name, bits).start()

    def plane_sum(name):
        _, part, recv, line, *_ = groups[name]
        for bits in range(1, PLANE):
            plane_copy(name, bits).wait_recv()
        for z in range(lines):
            total = part[z, j_at].astype(f32)
            for bits in range(1, PLANE):
                total = total + recv[bits - 1, z].astype(f32)
            line[z] = total.astype(bf16)
        line_start(name)

    def line_start(name):
        for apart in range(1, lines):
            line_copy(name, apart).start()

    def line_sum(name):
        *_, line, came, at, size = groups[name]
        for apart in range(1, lines):
            line_copy(name, apart).wait_recv()
        total = line[z_at].astype(f32)
        for apart in range(1, lines):
            total = total + came[apart - 1].astype(f32)
        sums_out[:, at : at + size] = total

    line_start("o")
    cosines, sines = cos_in[...], sin_in[...]

    def turned_back(part):
        return (part * cosines - pltpu.roll(part, 64, 1) * sines).astype(bf16)

    grads[:, 0:q_width] = dq_in[...]

    def weight_part(part, at, size):
        for z in range(lines):
            turned = normed_in[:, z * slab_rows : (z + 1) * slab_rows].T
            tile = dot_nn(turned, grads[:, at : at + size]).astype(bf16)
            for j in range(PLANE):
                part[z, j] = tile[j * shard : (j + 1) * shard]

    weight_part(part_q, 0, q_width)

    columns = lambda j: pl.ds(pl.multiple_of(j * block, block), block)

    def spread(which, bits):
        rows = pl.ds(pl.multiple_of(there[bits] * shard, shard), shard)
        return pltpu.make_async_remote_copy(
            src_ref=total_buf.at[which, rows], dst_ref=ff_out.at[which, :, columns(j_at)],
            send_sem=spread_send.at[which, bits - 1], recv_sem=spread_recv.at[which, bits - 1],
            device_id=chip[bits], device_id_type=MESH)

    def spread_keep(which):
        rows = pl.ds(pl.multiple_of(j_at * shard, shard), shard)
        return pltpu.make_async_copy(
            total_buf.at[which, rows], ff_out.at[which, :, columns(j_at)], spread_local.at[which])

    def line_done(which):
        for step in range(3, lines - 1):
            hop_step(which, step)
        own_load(which).wait()
        for sign, way in ways:

            @pl.when(place_of(sign) >= 1)
            def _():
                hop(which, sign, way, lines - 2).wait_recv()
                came = recv_buf[which, way, lines - 4].astype(f32)
                total_buf[which] = (total_buf[which].astype(f32) + came).astype(bf16)

        for bits in range(1, PLANE):
            spread(which, bits).start()
        spread_keep(which).start()

    for load in kv_loads:
        load.wait()
    for bits in range(1, PLANE):
        kv_copy(bits, 1).wait_recv()
    total = kv_other[...].astype(f32)
    for bits in range(1, PLANE):
        total = total + kv_plane[bits - 1, 1].astype(f32)
    kv_merged[...] = total.astype(bf16)
    kv_across = pltpu.make_async_remote_copy(
        src_ref=kv_merged, dst_ref=kv_line, send_sem=kv_line_send, recv_sem=kv_line_recv,
        device_id={"dp": line_partner(dp)}, device_id_type=MESH)
    kv_across.start()
    plane_start("q")
    line_done(2)
    for bits in range(1, PLANE):
        kv_copy(bits, 0).wait_recv()
    kv_across.wait_recv()
    total = kv_own[...].astype(f32) + kv_line[...].astype(f32)
    for bits in range(1, PLANE):
        total = total + kv_plane[bits - 1, 0].astype(f32)
    grads[:, q_width : q_width + 128] = turned_back(total[:, 0:128] * scale)
    grads[:, q_width + 128 :] = total[:, 128:256].astype(bf16)
    weight_part(part_kv, q_width, 256)
    plane_start("kv")

    def normed_grad(c):
        at = pl.ds(pl.multiple_of(c * half, half), half)
        return dot_nt(grads[at, :], first_in[...])

    far[...] = normed_grad(1 - core).astype(bf16)
    mate_copy = pltpu.make_async_remote_copy(
        src_ref=far, dst_ref=near, send_sem=mate_send, recv_sem=mate_recv, device_id=mate, device_id_type=MESH)
    mate_copy.start()
    mine = normed_grad(core)
    line_done(0)
    mate_copy.wait_recv()
    mine = mine + near[...].astype(f32)
    wide = x_in[...].astype(f32)
    norm = lax.rsqrt(jnp.mean(wide * wide, axis=1, keepdims=True) + EPS)
    z_own = wide * norm
    w = mine * gain_row_in[0:1, :]
    back = norm * (w - z_own * jnp.mean(w * z_own, axis=1, keepdims=True))
    input_grad_out[...] = (middle_grad_in[...] + back).astype(bf16)
    bias = jnp.sum(grads[...].astype(f32), axis=0, keepdims=True)
    small_own[...] = jnp.concatenate(
        [
            jnp.sum(mine * z_own, axis=0, keepdims=True),
            rows_in[...],
            jnp.concatenate([bias, jnp.zeros((1, width - q_width - 256), f32)], axis=1),
            jnp.zeros((5, width), f32),
        ],
        axis=0,
    )
    small_copy = pltpu.make_async_remote_copy(
        src_ref=small_own, dst_ref=small_mate, send_sem=small_mate_sem.at[0], recv_sem=small_mate_sem.at[1],
        device_id=mate, device_id_type=MESH)
    small_copy.start()
    plane_sum("q")
    plane_sum("kv")

    small_copy.wait_recv()
    gain_rows = lax.broadcasted_iota(jnp.int32, (8, width), 0) < 2
    small_plane[0] = small_own[...] + jnp.where(gain_rows, small_mate[...], 0.0)

    def small_plane_copy(bits):
        return pltpu.make_async_remote_copy(
            src_ref=small_plane.at[0], dst_ref=small_plane.at[bits],
            send_sem=small_plane_send.at[bits - 1], recv_sem=small_plane_recv.at[bits - 1],
            device_id=chip[bits], device_id_type=MESH)

    def small_line_copy(apart):
        return pltpu.make_async_remote_copy(
            src_ref=small_line.at[0], dst_ref=small_line.at[apart],
            send_sem=small_line_send.at[apart - 1], recv_sem=small_line_recv.at[apart - 1],
            device_id={"dp": lax.rem(z_at + apart, lines) * PLANE + j_at}, device_id_type=MESH)

    for bits in range(1, PLANE):
        small_plane_copy(bits).start()
    for bits in range(1, PLANE):
        small_plane_copy(bits).wait_recv()
    total = small_plane[0]
    for bits in range(1, PLANE):
        total = total + small_plane[bits]
    small_line[0] = total
    for apart in range(1, lines):
        small_line_copy(apart).start()
    line_sum("o")
    line_done(1)
    line_sum("q")
    line_sum("kv")
    for apart in range(1, lines):
        small_line_copy(apart).wait_recv()
    total = small_line[0]
    for apart in range(1, lines):
        total = total + small_line[apart]
    small_out[...] = total

    for which in order:
        for bits in range(1, PLANE):
            spread(which, bits).wait_recv()
            spread(which, bits).wait_send()
        spread_keep(which).wait()
        for sign, way in ways:
            for step in range(2, lines - 1):

                @pl.when(place_of(sign) <= step)
                def _():
                    hop(which, sign, way, step).wait_send()

    for bits in range(1, PLANE):
        small_plane_copy(bits).wait_send()
        for part in range(2):
            kv_copy(bits, part).wait_send()
        for name in ("q", "kv"):
            plane_copy(name, bits).wait_send()
    for apart in range(1, lines):
        small_line_copy(apart).wait_send()
        for name in groups:
            line_copy(name, apart).wait_send()
    kv_across.wait_send()
    mate_copy.wait_send()
    small_copy.wait_send()


def finish(dkv, dq, cosines, sines, normed, first, line_o, x, gain_rows, gain_row, middle_grad, ff_parts, up, down, lines, members, scale):
    bf16, f32 = jnp.bfloat16, jnp.float32
    half, width = x.shape
    local_tok = 2 * half
    q_width = dq.shape[1]
    slab_rows = width // lines
    shard = slab_rows // PLANE
    block = ff_parts.shape[-1]
    anywhere = pl.BlockSpec(memory_space=pl.ANY)
    inside = pl.BlockSpec(memory_space=pltpu.VMEM)
    dma = pltpu.SemaphoreType.DMA
    near = PLANE - 1
    vmem = lambda *shape: pltpu.VMEM(shape, bf16)
    wide = lambda *shape: pltpu.VMEM(shape, f32)
    pair = (local_tok, 256)
    return pl.pallas_call(
        functools.partial(back_kernel, lines=lines, members=members, scale=scale),
        out_shape=(
            jax.ShapeDtypeStruct((half, width), bf16),
            jax.ShapeDtypeStruct((shard, 2 * q_width + 256), f32),
            jax.ShapeDtypeStruct((8, width), f32),
            jax.ShapeDtypeStruct((3, shard, PLANE * block), bf16),
        ),
        in_specs=[anywhere] + [inside] * 10 + [anywhere] * 3,
        out_specs=(inside, inside, inside, anywhere),
        scratch_shapes=[
            vmem(*pair), vmem(*pair), vmem(near, 2, *pair), vmem(*pair), vmem(*pair),
            vmem(local_tok, q_width + 256), vmem(lines, PLANE, shard, q_width), vmem(lines, PLANE, shard, 256),
            vmem(near, lines, shard, q_width), vmem(near, lines, shard, 256),
            vmem(lines, shard, q_width), vmem(lines, shard, 256),
            vmem(lines - 1, shard, q_width), vmem(lines - 1, shard, 256), vmem(lines - 1, shard, q_width),
            vmem(half, width), vmem(half, width), wide(8, width), wide(8, width), wide(PLANE, 8, width), wide(lines, 8, width),
            vmem(3, 2, slab_rows, block), vmem(3, 2, lines - 3, slab_rows, block), vmem(3, 2, slab_rows, block), vmem(3, slab_rows, block),
            dma((2,)), dma((near, 2)), dma((near, 2)), dma, dma,
            dma((3, near)), dma((3, near)), dma((3, lines - 1)), dma((3, lines - 1)),
            dma, dma, dma((2,)), dma((near,)), dma((near,)), dma((lines - 1,)), dma((lines - 1,)),
            dma((3, 2)), dma((3,)), dma((3, 2)), dma((3, 2, lines - 3)), dma((3, 2, lines - 3)), dma((3,)), dma((3, near)), dma((3, near)),
        ],
        compiler_params=pltpu.CompilerParams(vmem_limit_bytes=62 << 20, collective_id=2, has_side_effects=True),
        name="back",
        cost_estimate=pl.CostEstimate(flops=6 * local_tok * width * (q_width + 256), bytes_accessed=40 << 20, transcendentals=0),
    )(dkv, dq, cosines, sines, normed, first, line_o, x, gain_rows, gain_row, middle_grad, ff_parts, up, down)


def swap(block, axis, count, bits):
    return lax.ppermute(block, axis, [(i, i ^ bits) for i in range(count)])


def rms_scale(values):
    return lax.rsqrt(jnp.mean(values * values, axis=1, keepdims=True) + EPS)


def norm_back(grad, values, gain):
    scale = rms_scale(values)
    z = values * scale
    w = grad * gain
    gain_grad = jnp.sum(grad * z, axis=0)
    return scale * (w - z * jnp.mean(w * z, axis=1, keepdims=True)), gain_grad


def rope_tables(positions):
    exponents = jnp.arange(64, dtype=jnp.float32) * (2.0 / 128)
    frequency = jnp.power(THETA, -exponents)
    angles = positions.astype(jnp.float32)[:, None] * frequency[None, :]
    cosines, sines = jnp.cos(angles), jnp.sin(angles)
    return (
        jnp.concatenate([cosines, cosines], axis=1),
        jnp.concatenate([-sines, sines], axis=1),
    )


def contract_rows(left, right):
    return lax.dot_general(
        left, right, (((0,), (0,)), ((), ())), preferred_element_type=jnp.float32
    )


def contract_cols(left, right):
    return lax.dot_general(
        left, right, (((1,), (1,)), ((), ())), preferred_element_type=jnp.float32
    )


def matmul(left, right):
    return jnp.dot(left, right, preferred_element_type=jnp.float32)


def attention_plan(segment_ids, parent_ids, dp_index, local_tok):
    members = TREE_TOK // local_tok
    first = dp_index // members * TREE_TOK
    slots = lax.dynamic_slice_in_dim(segment_ids, first, TREE_TOK)[::KB]
    numbers = jnp.arange(parent_ids.shape[0], dtype=jnp.int32)
    parents = jnp.sum(jnp.where(slots[:, None] == numbers[None, :], parent_ids[None, :], 0), axis=1)
    places = jnp.arange(slots.shape[0], dtype=jnp.int32)
    holder = jnp.sum(jnp.where(parents[:, None] == slots[None, :], places[None, :], 0), axis=1)
    starts = dp_index % members * local_tok + QB * jnp.arange(local_tok // QB, dtype=jnp.int32)
    slot = starts // KB
    chosen = slot[:, None] == places[None, :]
    pick = lambda table: jnp.sum(jnp.where(chosen, table[None, :], 0), axis=1)
    in_trunk = starts < TRUNK
    is_leaf = pick(parents) != slots[0]
    chunk = jnp.minimum(starts, TRUNK) // KC
    far = jnp.int32(1 << 20)
    block0 = jnp.where(in_trunk, 2 * chunk, jnp.where(is_leaf, pick(holder), TRUNK // KB))
    block1 = jnp.where(in_trunk, 2 * chunk + 1, slot)
    shift0 = jnp.where(in_trunk, block0 * KB - starts, jnp.where(is_leaf, -far, far))
    shift1 = block1 * KB - starts
    hot = jnp.where(~in_trunk[:, None] & (block0[:, None] == places[None, :]), 1.0, 0.0)
    return jnp.stack([shift0, shift1], axis=1).reshape(-1), hot.reshape(-1)


def on_device(
    dp_size,
    layer_input,
    out_cotangent,
    positions,
    segment_ids,
    parent_ids,
    attention_gain,
    query_weight,
    query_bias,
    key_weight,
    key_bias,
    value_weight,
    value_bias,
    output_weight,
    feedforward_gain,
    gate_weight,
    up_weight,
    down_weight,
):
    bf16, f32 = jnp.bfloat16, jnp.float32
    local_tok = positions.shape[0]
    half_tok, width = layer_input.shape
    shard = attention_gain.shape[0]
    heads, head_dim = query_bias.shape[0], 128
    per_head = query_bias.shape[1]
    q_width = heads * head_dim
    hidden = gate_weight.shape[1]
    lines = dp_size // PLANE
    members = TREE_TOK // local_tok
    dp_index = lax.axis_index("dp")
    core = lax.axis_index("tensor")
    scale = head_dim ** (-0.5)

    def line_route(sign, first, last):
        route = []
        for place in range(first, last + 1):
            z = place if sign == 1 else lines - 1 - place
            route += [(z * PLANE + j, (z + sign) * PLANE + j) for j in range(PLANE)]
        return route

    def by_core(mine):
        other = swap(mine, "tensor", 2, 1)
        first = jnp.where(core == 0, mine, other)
        second = jnp.where(core == 0, other, mine)
        return jnp.concatenate([first, second], axis=0)

    first_own = jnp.concatenate([query_weight, key_weight, value_weight], axis=1)
    biases = jnp.concatenate([query_bias, key_bias, value_bias], axis=0)
    bias_row = lax.dynamic_update_slice(
        jnp.zeros((heads + 2, head_dim), bf16), biases, (0, dp_index * per_head)
    ).reshape(1, -1)
    gains = lax.dynamic_update_slice(
        jnp.zeros((2, width), bf16), jnp.stack([attention_gain, feedforward_gain]), (0, dp_index * shard)
    )
    extra = jnp.concatenate(
        [gains, jnp.pad(bias_row, ((0, 0), (0, width - bias_row.shape[1]))), jnp.zeros((13, width), bf16)], axis=0
    )
    cosines, sines = rope_tables(positions)
    plan, hot = attention_plan(segment_ids, parent_ids, dp_index, local_tok)
    steps = lines - 3
    outs = front(
        gate_weight, up_weight, down_weight.T, first_own, output_weight.T, extra, layer_input, cosines, sines, lines, members
    )
    slab, ups, downs = outs[0], list(outs[1 : 1 + steps]), list(outs[1 + steps : 1 + 2 * steps])
    late_up, late_down, first_all, out_t, q_rot, tree, normed, rows = outs[1 + 2 * steps :]

    attended, lse, middle, normed_two, other, cot_came, *more = attend(
        plan, hot, q_rot, tree, out_t, layer_input, rows, out_cotangent, ups[-1], downs[-1], late_up, late_down,
        lines, members, scale,
    )

    normed_two_grad, y_own, y_other, ff_parts, up_first, down_first = feed_forward(
        normed_two, out_cotangent, cot_came, [slab] + ups + downs + [late_up, late_down] + more, lines, hidden
    )

    ff_parts = ff_parts.reshape(3, lines, width // lines, ff_parts.shape[-1])

    dq, dtree, middle_grad, gain_two_grad, line_o, layer_output, up_next, down_next = attend_back(
        plan, hot, q_rot, attended, lse, tree, other, out_t, normed_two_grad, middle, out_cotangent, rows, cosines, sines,
        y_own, y_other, ff_parts, up_first, down_first, lines, members, scale,
    )
    input_grad, sums, small, ff_sums = finish(
        dtree, dq, cosines, sines, normed, first_all, line_o, layer_input, gain_two_grad, rows,
        middle_grad, ff_parts, up_next, down_next, lines, members, scale,
    )
    ff_sums = ff_sums[:, :, :hidden].astype(f32)
    gains_out = lax.dynamic_slice(small[0:2], (0, dp_index * shard), (2, shard))
    bias_out = lax.dynamic_slice(
        small[2, : (heads + 2) * head_dim].reshape(heads + 2, head_dim), (0, dp_index * per_head), (heads + 2, per_head)
    )
    return (
        layer_output,
        input_grad,
        gains_out[0],
        sums[:, :q_width],
        bias_out[:heads],
        sums[:, q_width : q_width + 128],
        bias_out[heads : heads + 1],
        sums[:, q_width + 128 : q_width + 256],
        bias_out[heads + 1 :],
        sums[:, q_width + 256 :].T,
        gains_out[1],
        ff_sums[0],
        ff_sums[1],
        ff_sums[2].T,
    )


def solution(mesh):
    placed = (
        P(("dp", "tensor"), None),
        P(("dp", "tensor"), None),
        P("dp"),
        P(),
        P(),
        P("dp"),
        P("dp", "tensor"),
        P("tensor", "dp"),
        P("dp", "tensor"),
        P("tensor", "dp"),
        P("dp", "tensor"),
        P("tensor", "dp"),
        P("tensor", "dp"),
        P("dp"),
        P("dp", "tensor"),
        P("dp", "tensor"),
        P("tensor", "dp"),
    )
    return jax.shard_map(
        functools.partial(on_device, mesh.shape["dp"]),
        mesh=mesh,
        in_specs=placed,
        out_specs=(
            P(("dp", "tensor"), None),
            P(("dp", "tensor"), None),
            P("dp"),
            P("dp", "tensor"),
            P("tensor", "dp"),
            P("dp", "tensor"),
            P("tensor", "dp"),
            P("dp", "tensor"),
            P("tensor", "dp"),
            P("tensor", "dp"),
            P("dp"),
            P("dp", "tensor"),
            P("dp", "tensor"),
            P("tensor", "dp"),
        ),
        check_vma=False,
    )
```

```python
import functools

import jax
import jax.numpy as jnp
from jax import lax
from jax.experimental import pallas as pl
from jax.experimental.pallas import tpu as pltpu
from jax.sharding import PartitionSpec as P

EPS = 1e-06
THETA = 10000.0
TREE_TOK = 5120
TRUNK = 2048
PLANE = 4
NEG = -1e30
LATE = (2, 0)
QB=128; KC=512; KB=256
LOG2E=1.4426950408889634

MESH = pl.DeviceIdType.MESH


def dot_nt(a,b): return lax.dot_general(a,b,(((1,),(1,)),((),())),preferred_element_type=jnp.float32)
def dot_nn(a,b): return lax.dot_general(a,b,(((1,),(0,)),((),())),preferred_element_type=jnp.float32)

def plane_partner(dp, bits):
    one = dp + 1 - 2 * lax.rem(dp, 2)
    if bits == 1:
        return one
    two = 2 - 4 * lax.rem(dp // 2, 2)
    return (dp if bits == 2 else one) + two


def line_partner(dp):
    return dp + PLANE - 2 * PLANE * lax.rem(dp // PLANE, 2)


def greet(dp, core, lines):
    z_at = dp // PLANE
    barrier = pltpu.get_barrier_semaphore()
    for bits in range(1, PLANE):
        pl.semaphore_signal(barrier, inc=1, device_id={"dp": plane_partner(dp, bits)}, device_id_type=MESH)
    pl.semaphore_signal(barrier, inc=1, device_id={"tensor": 1 - core}, device_id_type=MESH)

    @pl.when(z_at > 0)
    def _():
        pl.semaphore_signal(barrier, inc=1, device_id={"dp": dp - PLANE}, device_id_type=MESH)

    @pl.when(z_at < lines - 1)
    def _():
        pl.semaphore_signal(barrier, inc=1, device_id={"dp": dp + PLANE}, device_id_type=MESH)

    beside = jnp.minimum(z_at, 1) + jnp.minimum(lines - 1 - z_at, 1)
    pl.semaphore_wait(barrier, PLANE + beside)


def second_block(start):
    return jnp.where(start < TRUNK, start // KC * (KC // KB) + 1, start // KB)


def masked_chunk(tree_ref, other_ref, blk, start):
    at = pl.ds(pl.multiple_of(second_block(start) * KB, KB), KB)
    k = jnp.concatenate([other_ref[blk, :, 0:128], tree_ref[at, 0:128]], axis=0)
    v = jnp.concatenate([other_ref[blk, :, 128:256], tree_ref[at, 128:256]], axis=0)
    return k, v


def attend_kernel(
    info, hot, q_ref, tree_ref, out_t, x_in, rows_in, cot_in, up_in, down_in, late_up, late_down,
    att_out, lse_out, middle_out, normed_out, other_ref, cot_out, mid_up, mid_down, last_up, last_down,
    far, near, pair_send, pair_recv, cot_send, cot_recv, half_send, half_recv, mid_send, mid_recv, last_send, last_recv,
    *, lines, members, scale,
):
    bf16, f32 = jnp.bfloat16, jnp.float32
    dp = lax.axis_index("dp")
    core = lax.axis_index("tensor")
    z_at = dp // PLANE
    half, width = x_in.shape
    local_tok, q_width = q_ref.shape
    heads = q_width // 128
    rows = heads * QB
    c2 = scale * LOG2E
    mate = {"tensor": 1 - core}
    chip = [None] + [{"dp": plane_partner(dp, bits)} for bits in range(1, PLANE)]
    ways = ((1, 0), (-1, 1))
    place_of = lambda sign: z_at if sign == 1 else lines - 1 - z_at

    def mid_hop(sign, way):
        return pltpu.make_async_remote_copy(
            src_ref=(up_in, down_in)[way].at[1], dst_ref=(mid_up, mid_down)[way],
            send_sem=mid_send.at[way], recv_sem=mid_recv.at[way],
            device_id={"dp": dp + sign * PLANE}, device_id_type=MESH)

    def last_hop(sign, way):
        return pltpu.make_async_remote_copy(
            src_ref=(late_up, late_down)[way].at[0], dst_ref=(last_up, last_down)[way],
            send_sem=last_send.at[way], recv_sem=last_recv.at[way],
            device_id={"dp": dp + sign * PLANE}, device_id_type=MESH)

    def cot_copy(bits):
        return pltpu.make_async_remote_copy(
            src_ref=cot_in, dst_ref=cot_out.at[bits - 1], send_sem=cot_send.at[bits - 1], recv_sem=cot_recv.at[bits - 1],
            device_id=chip[bits], device_id_type=MESH)

    def cot_half(bits):
        at = pl.ds((bits - 1) * (half // 2), half // 2)
        return pltpu.make_async_remote_copy(
            src_ref=cot_out.at[2 - bits, at], dst_ref=cot_out.at[2, at],
            send_sem=half_send.at[bits - 1], recv_sem=half_recv.at[bits - 1],
            device_id=chip[bits], device_id_type=MESH)

    greet(dp, core, lines)
    for sign, way in ways:
        place = place_of(sign)

        @pl.when((place >= lines - 3) & (place < lines - 1))
        def _():
            mid_hop(sign, way).start()

        @pl.when(place == lines - 2)
        def _():
            last_hop(sign, way).start()

    for bits in (1, 2):
        cot_copy(bits).start()

    def step(carry, s, v):
        m, l, acc = carry
        mt = s[:, :128]
        for j in range(1, KC // 128):
            mt = jnp.maximum(mt, s[:, j * 128 : (j + 1) * 128])
        mn = jnp.maximum(m, jnp.max(mt, axis=1, keepdims=True))
        p = jnp.exp2((s - mn) * c2)
        ps = p[:, :128]
        for j in range(1, KC // 128):
            ps = ps + p[:, j * 128 : (j + 1) * 128]
        a = jnp.exp2((m - mn) * c2)
        return mn, l * a + ps, acc * a + dot_nn(p.astype(bf16), v)

    @pl.loop(0, local_tok // QB)
    def _(blk):
        start = lax.rem(dp, members) * local_tok + blk * QB
        nfull = jnp.minimum(start, TRUNK) // KC
        mine = pl.ds(pl.multiple_of(blk * QB, QB), QB)
        slots = members * local_tok // KB
        at = pl.ds(pl.multiple_of(jnp.minimum(start, TRUNK - KC) // KC * KC, KC), KB)
        first = tree_ref[at, :].astype(f32) * jnp.where(start < TRUNK, 1.0, 0.0)
        for slot in range(TRUNK // KB, slots):
            first = first + hot[blk * slots + slot] * tree_ref[slot * KB : (slot + 1) * KB, :].astype(f32)
        other_ref[blk] = first.astype(bf16)
        q = jnp.concatenate([q_ref[mine, h * 128 : (h + 1) * 128] for h in range(heads)], axis=0)

        def body(c, carry):
            at = pl.ds(pl.multiple_of(c * KC, KC), KC)
            return step(carry, dot_nt(q, tree_ref[at, 0:128]), tree_ref[at, 128:256])

        init = (jnp.full((rows, 1), NEG, f32), jnp.zeros((rows, 128), f32), jnp.zeros((rows, 128), f32))
        k, v = masked_chunk(tree_ref, other_ref, blk, start)
        s = dot_nt(q, k)
        col = lax.broadcasted_iota(jnp.int32, (QB, KC), 1)
        row = lax.broadcasted_iota(jnp.int32, (QB, KC), 0)
        ok = col + jnp.where(col < KB, info[2 * blk], info[2 * blk + 1] - KB) <= row
        s = jnp.concatenate([jnp.where(ok, s[h * QB : (h + 1) * QB], NEG) for h in range(heads)], axis=0)
        m, l, acc = lax.fori_loop(0, nfull, body, step(init, s, v))
        lsum = jnp.sum(l, axis=1, keepdims=True)
        out = (acc / lsum).astype(bf16)
        for h in range(heads):
            att_out[mine, h * 128 : (h + 1) * 128] = out[h * QB : (h + 1) * QB]
        lse = jnp.broadcast_to(m * c2 + jnp.log2(lsum), (rows, 128)).T
        lse_out[blk] = lse[0:8, :]

    for bits in (1, 2):
        cot_copy(bits).wait_recv()
    for bits in (1, 2):
        cot_half(bits).start()

    def projected(c):
        at = pl.ds(pl.multiple_of(c * half, half), half)
        return dot_nt(att_out[at, :], out_t[...])

    far[...] = projected(1 - core).astype(bf16)
    pair = pltpu.make_async_remote_copy(
        src_ref=far, dst_ref=near, send_sem=pair_send, recv_sem=pair_recv, device_id=mate, device_id_type=MESH)
    pair.start()
    own = projected(core) + x_in[...].astype(f32)
    pair.wait_recv()
    middle = own + near[...].astype(f32)
    middle_out[...] = middle
    norm = lax.rsqrt(jnp.mean(middle * middle, axis=1, keepdims=True) + EPS)
    normed_out[...] = (middle * norm * rows_in[1:2, :]).astype(bf16)

    pair.wait_send()
    for bits in (1, 2):
        cot_half(bits).wait_recv()
        cot_copy(bits).wait_send()
        cot_half(bits).wait_send()
    for sign, way in ways:
        place = place_of(sign)

        @pl.when(place >= lines - 2)
        def _():
            mid_hop(sign, way).wait_recv()

        @pl.when((place >= lines - 3) & (place < lines - 1))
        def _():
            mid_hop(sign, way).wait_send()

        @pl.when(place == lines - 1)
        def _():
            last_hop(sign, way).wait_recv()

        @pl.when(place == lines - 2)
        def _():
            last_hop(sign, way).wait_send()


def attend(info, hot, q, tree, out_t, x, rows, cot, up, down, late_up, late_down, lines, members, scale):
    bf16, f32 = jnp.bfloat16, jnp.float32
    local_tok, q_width = q.shape
    half, width = x.shape
    anywhere = pl.BlockSpec(memory_space=pl.ANY)
    inside = pl.BlockSpec(memory_space=pltpu.VMEM)
    dma = pltpu.SemaphoreType.DMA
    slab = jax.ShapeDtypeStruct(up.shape[1:], bf16)
    return pl.pallas_call(
        functools.partial(attend_kernel, lines=lines, members=members, scale=scale),
        out_shape=(
            jax.ShapeDtypeStruct((local_tok, q_width), bf16),
            jax.ShapeDtypeStruct((local_tok // QB, 8, q_width // 128 * QB), f32),
            jax.ShapeDtypeStruct((half, width), f32),
            jax.ShapeDtypeStruct((half, width), bf16),
            jax.ShapeDtypeStruct((local_tok // QB, KB, 256), bf16),
            jax.ShapeDtypeStruct((PLANE - 1, half, width), bf16),
            slab, slab, slab, slab,
        ),
        in_specs=[pl.BlockSpec(memory_space=pltpu.SMEM)] * 2 + [inside] * 5 + [anywhere] * 5,
        out_specs=(inside,) * 5 + (anywhere,) * 5,
        scratch_shapes=[
            pltpu.VMEM((half, width), bf16), pltpu.VMEM((half, width), bf16),
            dma, dma, dma((2,)), dma((2,)), dma((2,)), dma((2,)), dma((2,)), dma((2,)), dma((2,)), dma((2,)),
        ],
        compiler_params=pltpu.CompilerParams(vmem_limit_bytes=56 << 20, collective_id=3, has_side_effects=True),
        name="attend",
        cost_estimate=pl.CostEstimate(
            flops=4 * local_tok * q_width * 2304, bytes_accessed=12 << 20, transcendentals=local_tok * q_width * 18
        ),
    )(info, hot, q, tree, out_t, x, rows, cot, up, down, late_up, late_down)


def attend_back_kernel(
    info, hot, q_ref, att_ref, lse_ref, tree_ref, other_ref, out_t, dx_in, middle_in, cot_in, gain_in, cos_in, sin_in,
    y_own, y_other, ff_in, carried_up, carried_down,
    dq_out, dtree_out, middle_grad_out, gain_out, line_out, layer_out, next_up, next_down,
    part_out, part_came, sum_ref, parent_ref, branch, att_grad, y_sum, y_tmp, y_came, own_buf, sum_buf,
    branch_send, branch_recv, y_load, y_send, y_recv, part_send, part_recv, load_sem, hop_send, hop_recv,
    *, lines, members, scale,
):
    bf16, f32 = jnp.bfloat16, jnp.float32
    dp = lax.axis_index("dp")
    core = lax.axis_index("tensor")
    z_at = dp // PLANE
    half, width = cot_in.shape
    local_tok, q_width = q_ref.shape
    heads = q_width // 128
    slab_rows = width // lines
    shard = slab_rows // PLANE
    rows = heads * QB
    c2 = scale * LOG2E
    mate = {"tensor": 1 - core}
    chip = [None] + [{"dp": plane_partner(dp, bits)} for bits in range(1, PLANE)]
    ways = ((1, 0), (-1, 1))
    place_of = lambda sign: z_at if sign == 1 else lines - 1 - z_at

    def own_slab(which, sign):
        return ff_in.at[which, lines - 1 if sign == 1 else 0]

    def own_load(which, sign):
        return pltpu.make_async_copy(own_slab(which, sign), own_buf.at[which], load_sem.at[which, 0])

    def carry_load(which, way):
        return pltpu.make_async_copy((carried_up, carried_down)[way].at[which], sum_buf.at[which], load_sem.at[which, 1])

    def hop(which, sign, way, first_place):
        slab = lines - 2 if sign == 1 else 1
        return pltpu.make_async_remote_copy(
            src_ref=ff_in.at[which, slab] if first_place else sum_buf.at[which],
            dst_ref=(next_up, next_down)[way].at[which],
            send_sem=hop_send.at[which, way], recv_sem=hop_recv.at[which, way],
            device_id={"dp": dp + sign * PLANE}, device_id_type=MESH)

    for sign, way in ways:

        @pl.when(place_of(sign) == 1)
        def _():
            for which in (2, 0, 1):
                own_load(which, sign).start()
                carry_load(which, way).start()

    def y_loads(k, act):
        act(pltpu.make_async_copy(y_own.at[k], y_sum.at[k], y_load.at[k, 0]))
        act(pltpu.make_async_copy(y_other.at[k], y_tmp.at[k], y_load.at[k, 1]))

    for k in range(PLANE):
        y_loads(k, lambda copy: copy.start())
    greet(dp, core, lines)
    for sign, way in ways:

        @pl.when(place_of(sign) == 0)
        def _():
            for which in (2, 0, 1):
                hop(which, sign, way, True).start()

        @pl.when(place_of(sign) == 1)
        def _():
            for which in (2, 0, 1):
                own_load(which, sign).wait()
                carry_load(which, way).wait()
                sum_buf[which] = (own_buf[which].astype(f32) + sum_buf[which].astype(f32)).astype(bf16)
                hop(which, sign, way, False).start()

    middle = middle_in[...]
    norm = lax.rsqrt(jnp.mean(middle * middle, axis=1, keepdims=True) + EPS)
    z_own = middle * norm
    gain_out[...] = jnp.sum(dx_in[...] * z_own, axis=0, keepdims=True)
    w = dx_in[...] * gain_in[1:2, :]
    middle_grad = cot_in[...].astype(f32) + norm * (w - z_own * jnp.mean(w * z_own, axis=1, keepdims=True))
    middle_grad_out[...] = middle_grad
    token_rows = pl.ds(pl.multiple_of(core * half, half), half)
    branch[token_rows, :] = middle_grad.astype(bf16)
    branch_copy = pltpu.make_async_remote_copy(
        src_ref=branch.at[token_rows], dst_ref=branch.at[token_rows], send_sem=branch_send, recv_sem=branch_recv,
        device_id=mate, device_id_type=MESH)
    branch_copy.start()

    quarter = lambda part: pl.ds(part * (half // 2), half // 2)

    def across_copy(bits):
        part = bits - 1
        return pltpu.make_async_remote_copy(
            src_ref=y_sum.at[3, quarter(part)], dst_ref=y_came.at[2, quarter(part)],
            send_sem=y_send.at[0, part], recv_sem=y_recv.at[0, part], device_id=chip[bits], device_id_type=MESH)

    def y_copy(bits, part):
        return pltpu.make_async_remote_copy(
            src_ref=y_sum.at[bits, quarter(part)], dst_ref=y_came.at[bits - 1, quarter(part)],
            send_sem=y_send.at[bits, part], recv_sem=y_recv.at[bits, part], device_id=chip[bits], device_id_type=MESH)

    for k in (3, 1, 2, 0):
        y_loads(k, lambda copy: copy.wait())
        y_sum[k] = (y_sum[k].astype(f32) + y_tmp[k].astype(f32)).astype(bf16)
        if k == 3:
            across_copy(1).start()
            across_copy(2).start()
        elif k:
            y_copy(k, k - 1).start()
    branch_copy.wait_recv()
    att_grad[...] = dot_nn(branch[...], out_t[...]).astype(bf16)
    for z in range(lines):
        tile = dot_nn(branch[:, z * slab_rows : (z + 1) * slab_rows].T, att_ref[...]).astype(bf16)
        for j in range(PLANE):
            part_out[z, j] = tile[j * shard : (j + 1) * shard]

    def part_copy(bits):
        there = lax.rem(plane_partner(dp, bits), PLANE)
        return pltpu.make_async_remote_copy(
            src_ref=part_out.at[:, there], dst_ref=part_came.at[bits - 1],
            send_sem=part_send.at[bits - 1], recv_sem=part_recv.at[bits - 1],
            device_id=chip[bits], device_id_type=MESH)

    for bits in (1, 2):
        across_copy(bits).wait_recv()
        at = quarter(bits - 1)
        y_sum[PLANE - 1 - bits, at] = (y_sum[PLANE - 1 - bits, at].astype(f32) + y_came[2, at].astype(f32)).astype(bf16)
        y_copy(PLANE - 1 - bits, bits - 1).start()
    for bits in range(1, PLANE):
        part_copy(bits).start()

    sum_ref[...] = jnp.zeros_like(sum_ref)
    cosines, sines = cos_in[...], sin_in[...]

    @pl.loop(0, local_tok // QB)
    def _(blk):
        start = lax.rem(dp, members) * local_tok + blk * QB
        nfull = jnp.minimum(start, TRUNK) // KC
        mine = pl.ds(pl.multiple_of(blk * QB, QB), QB)
        stacked = lambda ref: jnp.concatenate([ref[mine, h * 128 : (h + 1) * 128] for h in range(heads)], axis=0)
        q, do, o = stacked(q_ref), stacked(att_grad), stacked(att_ref)
        delta = jnp.sum((do.astype(f32) * o.astype(f32)).T, axis=0, keepdims=True)
        lse = lse_ref[blk][0:1, :]

        def tile(k, v, ok):
            p = jnp.exp2(dot_nt(k, q) * c2 - lse)
            if ok is not None:
                p = jnp.concatenate([jnp.where(ok, p[:, h * QB : (h + 1) * QB], 0.0) for h in range(heads)], axis=1)
            ds = (p * (dot_nt(v, do) - delta)).astype(bf16)
            dq = lax.dot_general(ds, k, (((0,), (0,)), ((), ())), preferred_element_type=f32)
            return dq, dot_nn(ds, q), dot_nn(p.astype(bf16), do)

        def body(c, acc):
            at = pl.ds(pl.multiple_of(c * KC, KC), KC)
            dq, dk, dv = tile(tree_ref[at, 0:128], tree_ref[at, 128:256], None)
            sum_ref[at, 0:128] += dk
            sum_ref[at, 128:256] += dv
            return acc + dq

        k, v = masked_chunk(tree_ref, other_ref, blk, start)
        col = lax.broadcasted_iota(jnp.int32, (KC, QB), 0)
        row = lax.broadcasted_iota(jnp.int32, (KC, QB), 1)
        ok = col + jnp.where(col < KB, info[2 * blk], info[2 * blk + 1] - KB) <= row
        dq, dk, dv = tile(k, v, ok)
        at = pl.ds(pl.multiple_of(second_block(start) * KB, KB), KB)
        sum_ref[at, 0:128] += dk[KB:]
        sum_ref[at, 128:256] += dv[KB:]
        parent_ref[blk, :, 0:128] = dk[:KB]
        parent_ref[blk, :, 128:256] = dv[:KB]

        @pl.when(start < TRUNK)
        def _():
            at = pl.ds(pl.multiple_of(start // KC * KC, KC), KB)
            sum_ref[at, 0:128] += dk[:KB]
            sum_ref[at, 128:256] += dv[:KB]

        dq = lax.fori_loop(0, nfull, body, dq) * scale
        place = pl.ds(pl.multiple_of(blk * QB, QB), QB)
        for h in range(heads):
            part = dq[h * QB : (h + 1) * QB]
            turned = part * cos_in[place, :] - pltpu.roll(part, 64, 1) * sin_in[place, :]
            dq_out[mine, h * 128 : (h + 1) * 128] = turned.astype(bf16)

    dtree_out[0:TRUNK, :] = sum_ref[0:TRUNK, :].astype(bf16)

    @pl.loop(TRUNK // KB, members * local_tok // KB)
    def _(slot):
        at = pl.ds(pl.multiple_of(slot * KB, KB), KB)
        total = sum_ref[at, :]
        for blk in range(local_tok // QB):
            total = total + hot[blk * (members * local_tok // KB) + slot] * parent_ref[blk]
        dtree_out[at, :] = total.astype(bf16)

    for bits in range(1, PLANE):
        part_copy(bits).wait_recv()
    for z in range(lines):
        total = part_out[z, lax.rem(dp, PLANE)].astype(f32)
        for bits in range(1, PLANE):
            total = total + part_came[bits - 1, z].astype(f32)
        line_out[z] = total.astype(bf16)
    for bits in (1, 2):
        for part in range(2):
            y_copy(bits, part).wait_recv()
    total = middle_in[...] + y_sum[0].astype(f32) + y_came[0].astype(f32) + y_came[1].astype(f32)
    layer_out[...] = total.astype(bf16)
    branch_copy.wait_send()
    for bits in range(1, PLANE):
        part_copy(bits).wait_send()
    for bits in (1, 2):
        across_copy(bits).wait_send()
        for part in range(2):
            y_copy(bits, part).wait_send()
    for sign, way in ways:

        @pl.when(place_of(sign) <= 1)
        def _():
            for which in range(3):
                hop(which, sign, way, False).wait_send()

        @pl.when((place_of(sign) >= 1) & (place_of(sign) <= 2))
        def _():
            for which in range(3):
                hop(which, sign, way, False).wait_recv()


def attend_back(info, hot, q, attended, lse, tree, other, out_t, dx, middle, cot, rows, cosines, sines, y_own, y_other, ff_parts, up, down, lines, members, scale):
    bf16, f32 = jnp.bfloat16, jnp.float32
    local_tok, q_width = q.shape
    half, width = cot.shape
    slab_rows = width // lines
    shard = slab_rows // PLANE
    block = up.shape[-1]
    anywhere = pl.BlockSpec(memory_space=pl.ANY)
    inside = pl.BlockSpec(memory_space=pltpu.VMEM)
    dma = pltpu.SemaphoreType.DMA
    slab = jax.ShapeDtypeStruct((3, slab_rows, block), bf16)
    return pl.pallas_call(
        functools.partial(attend_back_kernel, lines=lines, members=members, scale=scale),
        out_shape=(
            jax.ShapeDtypeStruct((local_tok, q_width), bf16),
            jax.ShapeDtypeStruct(tree.shape, bf16),
            jax.ShapeDtypeStruct((half, width), f32),
            jax.ShapeDtypeStruct((1, width), f32),
            jax.ShapeDtypeStruct((lines, shard, q_width), bf16),
            jax.ShapeDtypeStruct((half, width), bf16),
            slab, slab,
        ),
        in_specs=[pl.BlockSpec(memory_space=pltpu.SMEM)] * 2 + [inside] * 12 + [anywhere] * 5,
        out_specs=(inside,) * 6 + (anywhere,) * 2,
        scratch_shapes=[
            pltpu.VMEM((lines, PLANE, shard, q_width), bf16), pltpu.VMEM((PLANE - 1, lines, shard, q_width), bf16),
            pltpu.VMEM(tree.shape, f32), pltpu.VMEM((local_tok // QB, KB, 256), f32),
            pltpu.VMEM((local_tok, width), bf16), pltpu.VMEM((local_tok, q_width), bf16),
            pltpu.VMEM((PLANE, half, width), bf16), pltpu.VMEM((PLANE, half, width), bf16), pltpu.VMEM((PLANE - 1, half, width), bf16),
            pltpu.VMEM((3, slab_rows, block), bf16), pltpu.VMEM((3, slab_rows, block), bf16),
            dma, dma, dma((PLANE, 2)), dma((3, 2)), dma((3, 2)), dma((PLANE - 1,)), dma((PLANE - 1,)), dma((3, 2)), dma((3, 2)), dma((3, 2)),
        ],
        compiler_params=pltpu.CompilerParams(vmem_limit_bytes=62 << 20, collective_id=4, has_side_effects=True),
        name="attend_back",
        cost_estimate=pl.CostEstimate(
            flops=10 * local_tok * q_width * 2304, bytes_accessed=30 << 20, transcendentals=local_tok * q_width * 18
        ),
    )(info, hot, q, attended, lse, tree, other, out_t, dx, middle, cot, rows, cosines, sines, y_own, y_other, ff_parts, up, down)


class Gather:
    def __init__(self, own, whole, sems, dp, lines):
        self.own, self.whole, self.dp, self.lines = own, whole, dp, lines
        self.z_at = dp // PLANE
        self.local_sem, self.line_send, self.line_recv, self.plane_send, self.plane_recv = sems
        self.rows_per = own.shape[0]

    def rows(self, owner):
        return pl.ds(pl.multiple_of(owner * self.rows_per, self.rows_per), self.rows_per)

    def local(self):
        return pltpu.make_async_copy(self.own, self.whole.at[self.rows(self.dp)], self.local_sem)

    def place(self, sign):
        return self.z_at if sign == 1 else self.lines - 1 - self.z_at

    def line_copy(self, sign, step):
        owner = self.dp - sign * step * PLANE
        way = (1 - sign) // 2
        return pltpu.make_async_remote_copy(
            src_ref=self.own if step == 0 else self.whole.at[self.rows(owner)],
            dst_ref=self.whole.at[self.rows(owner)],
            send_sem=self.line_send.at[way, step], recv_sem=self.line_recv.at[way, step],
            device_id={"dp": self.dp + sign * PLANE}, device_id_type=MESH)

    def line_start(self, sign, step):
        place = self.place(sign)

        @pl.when((place >= step) & (place < self.lines - 1))
        def _():
            self.line_copy(sign, step).start()

    def line_wait_send(self, sign, step):
        place = self.place(sign)

        @pl.when((place >= step) & (place < self.lines - 1))
        def _():
            self.line_copy(sign, step).wait_send()

    def plane_copy(self, bits, owner, own=False):
        z = owner // PLANE
        return pltpu.make_async_remote_copy(
            src_ref=self.own if own else self.whole.at[self.rows(owner)],
            dst_ref=self.whole.at[self.rows(owner)],
            send_sem=self.plane_send.at[bits - 1, z], recv_sem=self.plane_recv.at[bits - 1, z],
            device_id={"dp": plane_partner(self.dp, bits)}, device_id_type=MESH)

    def plane_start_own(self):
        for bits in range(1, PLANE):
            self.plane_copy(bits, self.dp, True).start()

    def arrived(self, sign, step):
        place = self.place(sign)

        @pl.when(place >= step + 1)
        def _():
            owner = self.dp - sign * (step + 1) * PLANE
            pltpu.make_async_remote_copy(
                src_ref=self.own, dst_ref=self.whole.at[self.rows(owner)],
                send_sem=self.line_send.at[(1 - sign) // 2, step],
                recv_sem=self.line_recv.at[(1 - sign) // 2, step],
                device_id={"dp": self.dp - sign * PLANE}, device_id_type=MESH).wait_recv()
            if step + 1 < self.lines - 1:

                @pl.when(place < self.lines - 1)
                def _():
                    self.line_copy(sign, step + 1).start()

            for bits in range(1, PLANE):
                self.plane_copy(bits, owner).start()

    def plane_wait_recv(self):
        for bits in range(1, PLANE):
            for z in range(self.lines):
                owner = z * PLANE + lax.rem(plane_partner(self.dp, bits), PLANE)
                self.plane_copy(bits, owner).wait_recv()

    def finish(self):
        for sign in (1, -1):
            for step in range(self.lines - 1):
                self.line_wait_send(sign, step)
        for bits in range(1, PLANE):
            for z in range(self.lines):
                self.plane_copy(bits, z * PLANE + lax.rem(self.dp, PLANE)).wait_send()


def front_kernel(*refs, lines, members, steps):
    (
        gate_in, up_in, down_in, first_in, out_in, extra_in, x_in, cos_in, sin_in,
        own_out, *slab_outs,
    ) = refs[: 10 + 2 * steps]
    (
        late_up, late_down, first_out, out_t, q_out, tree_out, normed_out, rows_out,
        first_all, extra_all, x_all, normed, pair,
        first_local, first_ls, first_lr, first_ps, first_pr,
        extra_local, extra_ls, extra_lr, extra_ps, extra_pr,
        out_local, out_ls, out_lr, out_ps, out_pr,
        spread_local, spread_send, spread_recv, hop_send, hop_recv,
        x_local, x_send, x_recv, keep_sem, pair_local, pair_send, pair_recv, late_send, late_recv,
    ) = refs[10 + 2 * steps :]
    bf16, f32 = jnp.bfloat16, jnp.float32
    dp = lax.axis_index("dp")
    core = lax.axis_index("tensor")
    z_at = dp // PLANE
    j_at = lax.rem(dp, PLANE)
    half, width = x_in.shape
    shard = first_in.shape[0]
    local_tok = 2 * half
    slab_rows = PLANE * shard
    ups, downs = slab_outs[:steps], slab_outs[steps:]
    mate = {"tensor": 1 - core}

    first = Gather(first_in, first_all, (first_local, first_ls, first_lr, first_ps, first_pr), dp, lines)
    extra = Gather(extra_in, extra_all, (extra_local, extra_ls, extra_lr, extra_ps, extra_pr), dp, lines)
    outer = Gather(out_in, out_t, (out_local, out_ls, out_lr, out_ps, out_pr), dp, lines)

    token_rows = lambda c: pl.ds(pl.multiple_of(c * half, half), half)
    x_keep = pltpu.make_async_copy(x_in, x_all.at[token_rows(core)], x_local)
    x_copy = pltpu.make_async_remote_copy(
        src_ref=x_in, dst_ref=x_all.at[token_rows(core)], send_sem=x_send, recv_sem=x_recv,
        device_id=mate, device_id_type=MESH)
    shard_rows = lambda j: pl.ds(pl.multiple_of(j * shard, shard), shard)

    block = own_out.shape[-1]
    last = gate_in.shape[1] - (PLANE - 1) * block

    def by_width(owner, act):
        @pl.when(owner < PLANE - 1)
        def _():
            act(block)

        @pl.when(owner == PLANE - 1)
        def _():
            act(last)

    def piece(which, owner, size):
        at = pl.ds(pl.multiple_of(owner * block, 128), size)
        return (gate_in, up_in, down_in)[which].at[:, at], own_out.at[which, shard_rows(j_at), pl.ds(0, size)]

    def spread(which, bits, owner, size):
        src, dst = piece(which, owner, size)
        return pltpu.make_async_remote_copy(
            src_ref=src, dst_ref=dst,
            send_sem=spread_send.at[which, bits - 1], recv_sem=spread_recv.at[which, bits - 1],
            device_id={"dp": plane_partner(dp, bits)}, device_id_type=MESH)

    def spread_start(which):
        for bits in range(1, PLANE):
            owner = lax.rem(plane_partner(dp, bits), PLANE)
            by_width(owner, lambda size: spread(which, bits, owner, size).start())

    def spread_wait_send(which):
        for bits in range(1, PLANE):
            owner = lax.rem(plane_partner(dp, bits), PLANE)
            by_width(owner, lambda size: spread(which, bits, owner, size).wait_send())

    def spread_wait_recv(which):
        for bits in range(1, PLANE):
            by_width(j_at, lambda size: spread(which, bits, j_at, size).wait_recv())

    def spread_keep(which, act):
        def with_size(size):
            src, dst = piece(which, j_at, size)
            act(pltpu.make_async_copy(src, dst, spread_local.at[which]))

        by_width(j_at, with_size)

    def hop(which, sign, step):
        way = (1 - sign) // 2
        outs = ups if sign == 1 else downs
        return pltpu.make_async_remote_copy(
            src_ref=(own_out if step == 0 else outs[step - 1]).at[which], dst_ref=outs[step].at[which],
            send_sem=hop_send.at[which, way, step], recv_sem=hop_recv.at[which, way, step],
            device_id={"dp": dp + sign * PLANE}, device_id_type=MESH)

    def late_hop(index, sign):
        way = (1 - sign) // 2
        return pltpu.make_async_remote_copy(
            src_ref=(ups if sign == 1 else downs)[steps - 1].at[LATE[index]],
            dst_ref=(late_up if sign == 1 else late_down).at[index],
            send_sem=late_send.at[index, way], recv_sem=late_recv.at[index, way],
            device_id={"dp": dp + sign * PLANE}, device_id_type=MESH)

    for one in (first, extra, outer):
        one.local().start()
    x_keep.start()
    for which in range(3):
        spread_keep(which, lambda copy: copy.start())
    greet(dp, core, lines)
    x_copy.start()
    for sign in (1, -1):
        first.line_start(sign, 0)
        extra.line_start(sign, 0)
    spread_start(2)
    first.plane_start_own()
    extra.plane_start_own()
    for which in (0, 1):
        spread_start(which)

    x_keep.wait()
    x_copy.wait_recv()
    wide = x_all[...].astype(f32)
    scale = lax.rsqrt(jnp.mean(wide * wide, axis=1, keepdims=True) + EPS)

    def hop_start(which):
        spread_keep(which, lambda copy: copy.wait())
        spread_wait_recv(which)
        for sign in (1, -1):
            place = z_at if sign == 1 else lines - 1 - z_at

            @pl.when(place < lines - 1)
            def _():
                hop(which, sign, 0).start()

    for step in range(lines - 1):
        for sign in (1, -1):
            first.arrived(sign, step)
            extra.arrived(sign, step)
        if step == 0:
            hop_start(2)
    hop_start(0)
    hop_start(1)
    first.local().wait()
    extra.local().wait()
    for sign in (1, -1):
        outer.line_start(sign, 0)
    outer.plane_start_own()
    extra.plane_wait_recv()
    first.plane_wait_recv()
    keep = pltpu.make_async_copy(first_all, first_out, keep_sem)
    keep.start()
    small = extra_all[0:16, :].astype(f32)
    for owner in range(1, lines * PLANE):
        small = small + extra_all[16 * owner : 16 * (owner + 1), :].astype(f32)
    rows_out[...] = small
    normed[...] = (x_all[...].astype(f32) * scale * small[0:1, :]).astype(bf16)
    normed_out[...] = normed[...]
    columns = first_all.shape[1]
    q_width = columns - 256
    cosines, sines = cos_in[...], sin_in[...]

    def project(at, count):
        part = dot_nn(normed[...], first_all[:, at : at + count])
        return part + small[2:3, at : at + count]

    def turned(part):
        return (part * cosines + pltpu.roll(part, 64, 1) * sines).astype(bf16)

    both = project(q_width, 256)
    pair[:, 0:128] = turned(both[:, 0:128])
    pair[:, 128:256] = both[:, 128:256].astype(bf16)
    member = lax.rem(dp, members)
    tree_rows = lambda m: pl.ds(pl.multiple_of(m * local_tok, local_tok), local_tok)
    partner = lax.rem(line_partner(dp), members)
    pair_keep = pltpu.make_async_copy(pair, tree_out.at[tree_rows(member)], pair_local)
    pair_keep.start()

    def pair_copy(bits, forward=False):
        at = tree_rows(partner if forward else member)
        index = PLANE + bits - 1 if forward else bits
        return pltpu.make_async_remote_copy(
            src_ref=tree_out.at[at] if forward else pair, dst_ref=tree_out.at[at],
            send_sem=pair_send.at[index], recv_sem=pair_recv.at[index],
            device_id={"dp": plane_partner(dp, bits) if bits else line_partner(dp)}, device_id_type=MESH)

    for bits in range(PLANE):
        pair_copy(bits).start()
    for at in range(0, q_width, 256):
        part = project(at, 256)
        q_out[:, at : at + 128] = turned(part[:, 0:128])
        q_out[:, at + 128 : at + 256] = turned(part[:, 128:256])
    pltpu.make_async_remote_copy(
        src_ref=pair, dst_ref=tree_out.at[tree_rows(partner)], send_sem=pair_send.at[0],
        recv_sem=pair_recv.at[0], device_id={"dp": line_partner(dp)}, device_id_type=MESH).wait_recv()
    for bits in range(1, PLANE):
        pair_copy(bits, True).start()

    def pass_on(which):
        for step in range(steps):
            for sign in (1, -1):
                place = z_at if sign == 1 else lines - 1 - z_at

                @pl.when(place >= step + 1)
                def _():
                    hop(which, sign, step).wait_recv()
                    if step + 1 < steps:

                        @pl.when(place < lines - 1)
                        def _():
                            hop(which, sign, step + 1).start()

                    elif which in LATE:

                        @pl.when(place < lines - 1)
                        def _():
                            late_hop(LATE.index(which), sign).start()

    pass_on(2)
    for step in range(lines - 1):
        for sign in (1, -1):
            outer.arrived(sign, step)
    pass_on(0)
    pass_on(1)
    for bits in range(1, PLANE):
        pair_copy(bits).wait_recv()
        pair_copy(bits, True).wait_recv()
    outer.plane_wait_recv()
    for index in range(len(LATE)):
        for sign in (1, -1):
            place = z_at if sign == 1 else lines - 1 - z_at

            @pl.when(place >= lines - 2)
            def _():
                late_hop(index, sign).wait_recv()

            @pl.when((place >= lines - 3) & (place < lines - 1))
            def _():
                late_hop(index, sign).wait_send()

    for one in (first, extra, outer):
        one.finish()
    outer.local().wait()
    x_copy.wait_send()
    keep.wait()
    pair_keep.wait()
    for bits in range(PLANE):
        pair_copy(bits).wait_send()
        if bits:
            pair_copy(bits, True).wait_send()
    for which in range(3):
        spread_wait_send(which)
        for sign in (1, -1):
            for step in range(steps):
                place = z_at if sign == 1 else lines - 1 - z_at

                @pl.when((place >= step) & (place < lines - 1))
                def _():
                    hop(which, sign, step).wait_send()


def front(gate, up, down, first, out_t, extra, x, cosines, sines, lines, members):
    bf16, f32 = jnp.bfloat16, jnp.float32
    half, width = x.shape
    local_tok = 2 * half
    shard, columns = first.shape
    block = -(-gate.shape[1] // (PLANE * 128)) * 128
    q_width = out_t.shape[1]
    count = lines * PLANE
    steps = max(lines - 3, 1)
    anywhere = pl.BlockSpec(memory_space=pl.ANY)
    inside = pl.BlockSpec(memory_space=pltpu.VMEM)
    dma = pltpu.SemaphoreType.DMA
    slab = jax.ShapeDtypeStruct((3, PLANE * shard, block), bf16)
    gather_sems = [dma, dma((2, lines)), dma((2, lines)), dma((PLANE - 1, lines)), dma((PLANE - 1, lines))]
    return pl.pallas_call(
        functools.partial(front_kernel, lines=lines, members=members, steps=steps),
        out_shape=(slab,) * (1 + 2 * steps)
        + (jax.ShapeDtypeStruct((len(LATE), PLANE * shard, block), bf16),) * 2
        + (
            jax.ShapeDtypeStruct((width, columns), bf16),
            jax.ShapeDtypeStruct((width, q_width), bf16),
            jax.ShapeDtypeStruct((local_tok, q_width), bf16),
            jax.ShapeDtypeStruct((members * local_tok, 256), bf16),
            jax.ShapeDtypeStruct((local_tok, width), bf16),
            jax.ShapeDtypeStruct((16, width), f32),
        ),
        in_specs=[anywhere] * 7 + [inside] * 2,
        out_specs=(anywhere,) * (3 + 2 * steps) + (anywhere, anywhere, inside, anywhere, inside, inside),
        scratch_shapes=[
            pltpu.VMEM((width, columns), bf16), pltpu.VMEM((16 * count, width), bf16),
            pltpu.VMEM((local_tok, width), bf16), pltpu.VMEM((local_tok, width), bf16),
            pltpu.VMEM((local_tok, 256), bf16),
        ]
        + gather_sems * 3
        + [
            dma((3,)), dma((3, PLANE - 1)), dma((3, PLANE - 1)), dma((3, 2, steps)), dma((3, 2, steps)),
            dma, dma, dma, dma, dma, dma((2 * PLANE - 1,)), dma((2 * PLANE - 1,)),
            dma((len(LATE), 2)), dma((len(LATE), 2)),
        ],
        compiler_params=pltpu.CompilerParams(vmem_limit_bytes=56 << 20, collective_id=1, has_side_effects=True),
        name="front",
        cost_estimate=pl.CostEstimate(flops=2 * local_tok * width * columns, bytes_accessed=30 << 20, transcendentals=0),
    )(gate, up, down, first, out_t, extra, x, cosines, sines)


def ff_kernel(
    *refs, tile_h, tile_n, tile_m, lines, hidden,
):
    early = lines - 3
    x_in, cot_in, cot_came, slab = refs[:4]
    ups, downs = refs[4 : 4 + early], refs[4 + early : 4 + 2 * early]
    late_up, late_down, mid_up, mid_down, last_up, last_down = refs[4 + 2 * early : 10 + 2 * early]
    cots = [cot_in] + [cot_came.at[k] for k in range(PLANE - 1)]
    (
        dx_out, y_own, y_other, parts_out, carried_up, carried_down,
        x_all, cot_all, gate_w, up_w, down_w, prod, gate_g, up_g, far, near, back, y_stage, stage,
        x_send, x_recv, half_send, half_recv, fwd_send, fwd_recv, pair_send, pair_recv, dx_send, dx_recv,
        x_load, cot_load, cot_send, cot_recv, weight_sem, hop_send, hop_recv, y_keep, y_send, y_recv,
        stage_sem, first_send, first_recv,
    ) = refs[10 + 2 * early :]
    bf16 = jnp.bfloat16
    half = x_in.shape[0]
    width = x_in.shape[1]
    block = gate_w.shape[1]
    dp = lax.axis_index("dp")
    core = lax.axis_index("tensor")
    chip = [None] + [{"dp": plane_partner(dp, bits)} for bits in range(1, PLANE)]
    mate = {"tensor": 1 - core}
    rows = lambda k, r, n=1: pl.ds((2 * k + r) * half, n * half)

    z_at = dp // PLANE
    slab_rows = width // lines
    weights = (gate_w, up_w, down_w)
    ways = ((1, 0), (-1, 1))
    place_of = lambda sign: z_at if sign == 1 else lines - 1 - z_at
    place_rows = lambda z: pl.ds(pl.multiple_of(z * slab_rows, slab_rows), slab_rows)

    def second_to_last(which, way):
        if which == 1:
            return (mid_up, mid_down)[way]
        return (late_up, late_down)[way].at[LATE.index(which)]

    def weight_loads(which, act):
        for sign, way in ways:
            pieces = [piece.at[which] for piece in (ups, downs)[way]] + [second_to_last(which, way)]
            if which == 2:
                pieces.append((last_up, last_down)[way])
            for step, piece in enumerate(pieces):

                @pl.when(place_of(sign) >= step + 1)
                def _():
                    act(pltpu.make_async_copy(
                        piece, weights[which].at[place_rows(z_at - sign * (step + 1))],
                        weight_sem.at[which, 1 + way * (lines - 1) + step]))

        act(pltpu.make_async_copy(slab.at[which], weights[which].at[place_rows(z_at)], weight_sem.at[which, 0]))

    def last_hop(which, sign, way):
        origin = 0 if sign == 1 else lines - 1
        return pltpu.make_async_remote_copy(
            src_ref=second_to_last(which, way),
            dst_ref=weights[which].at[pl.ds(origin * slab_rows, slab_rows)],
            send_sem=hop_send.at[which, way], recv_sem=hop_recv.at[which, way],
            device_id={"dp": dp + sign * PLANE}, device_id_type=MESH)

    def weight_wait(which):
        weight_loads(which, lambda copy: copy.wait())
        for sign, way in ways if which < 2 else ():

            @pl.when(place_of(sign) == lines - 1)
            def _():
                last_hop(which, sign, way).wait_recv()

        last = hidden - (PLANE - 1) * block
        if last < block:

            @pl.when(lax.rem(dp, PLANE) == PLANE - 1)
            def _():
                weights[which][:, last:] = jnp.zeros((width, block - last), bf16)

    x_keep = pltpu.make_async_copy(x_in, x_all.at[rows(0, 0)], x_load)
    x_keep.start()

    def cot_keep(k):
        return pltpu.make_async_copy(cots[k], cot_all.at[rows(k, 0)], cot_load.at[k])

    def cot_copy(k):
        return pltpu.make_async_remote_copy(
            src_ref=cots[k], dst_ref=cot_all.at[rows(k, 1)], send_sem=cot_send.at[k], recv_sem=cot_recv.at[k],
            device_id=mate, device_id_type=MESH)

    for k in range(PLANE):
        cot_keep(k).start()
    for which in (2, 0, 1):
        weight_loads(which, lambda copy: copy.start())
    greet(dp, core, lines)
    for which in (0, 1):
        for sign, way in ways:

            @pl.when(place_of(sign) == lines - 2)
            def _():
                last_hop(which, sign, way).start()

    def x_copy(k):
        return pltpu.make_async_remote_copy(
            src_ref=x_in, dst_ref=x_all.at[rows(k, 0) if k else rows(0, 1)],
            send_sem=x_send.at[k], recv_sem=x_recv.at[k],
            device_id=chip[k] if k else mate, device_id_type=MESH)

    def x_half(k):
        at = lambda j: pl.ds(2 * j * half + (k - 1) * (half // 2), half // 2)
        return pltpu.make_async_remote_copy(
            src_ref=x_all.at[at(PLANE - 1 - k)], dst_ref=x_all.at[at(PLANE - 1)],
            send_sem=half_send.at[k - 1], recv_sem=half_recv.at[k - 1],
            device_id=chip[k], device_id_type=MESH)

    def x_forward(k):
        return pltpu.make_async_remote_copy(
            src_ref=x_all.at[rows(k, 0)], dst_ref=x_all.at[rows(k, 1)],
            send_sem=fwd_send.at[k - 1], recv_sem=fwd_recv.at[k - 1],
            device_id=mate, device_id_type=MESH)

    def pair_copy(k):
        return pltpu.make_async_remote_copy(
            src_ref=far.at[k], dst_ref=near.at[k],
            send_sem=pair_send.at[k], recv_sem=pair_recv.at[k],
            device_id=mate, device_id_type=MESH)

    def dx_copy(k):
        return pltpu.make_async_remote_copy(
            src_ref=near.at[k], dst_ref=back.at[k - 1],
            send_sem=dx_send.at[k - 1], recv_sem=dx_recv.at[k - 1],
            device_id=chip[k], device_id_type=MESH)

    x_copy(0).start()
    x_copy(1).start()
    x_copy(2).start()
    for k in range(PLANE):
        cot_copy(k).start()
    for k in range(PLANE):
        cot_keep(k).wait()
        cot_copy(k).wait_recv()
    weight_wait(2)

    starts = list(range(0, max(block - 1023, 0), tile_h)) or [0]
    if block - starts[-1] >= 2 * tile_h:
        starts.append(starts[-1] + tile_h)
    cuts = [pl.ds(at, end - at) for at, end in zip(starts, starts[1:] + [block])]

    @pl.loop(0, 2 * PLANE)
    def _(k):
        at = pl.ds(pl.multiple_of(k * half, half), half)
        for cols in cuts:
            up_g[at, cols] = dot_nn(cot_all[at, :], down_w[:, cols]).astype(bf16)

    def gate_part(k):
        @pl.loop(0, 2)
        def _(r):
            at = pl.ds(pl.multiple_of(2 * k * half + r * half, half), half)
            for cols in cuts:
                gate_g[at, cols] = dot_nn(x_all[at, :], gate_w[:, cols]).astype(bf16)

    def up_part(k):
        @pl.loop(0, 2)
        def _(r):
            at = pl.ds(pl.multiple_of(2 * k * half + r * half, half), half)
            for cols in cuts:
                up = dot_nn(x_all[at, :], up_w[:, cols])
                gate = gate_g[at, cols].astype(jnp.float32)
                pg = up_g[at, cols].astype(jnp.float32)
                sig = 0.5 * jnp.tanh(0.5 * gate) + 0.5
                silu = gate * sig
                prod[at, cols] = (silu * up).astype(bf16)
                up_g[at, cols] = (pg * silu).astype(bf16)
                gate_g[at, cols] = (pg * up * (sig + silu * (1.0 - sig))).astype(bf16)

    def dx_half(k, r):
        at = rows(k, r)

        part = dot_nt(gate_g[at, :], gate_w[...]) + dot_nt(up_g[at, :], up_w[...])
        if r:
            far[k] = part.astype(bf16)
        else:
            near[k] = (part + near[k].astype(jnp.float32)).astype(bf16)

    def dx_first(k):
        dx_half(k, 1)
        pair_copy(k).start()

    def dx_second(k):
        pair_copy(k).wait_recv()
        dx_half(k, 0)
        if k:
            dx_copy(k).start()

    def y_local(k):
        return pltpu.make_async_copy(y_stage.at[pl.ds(0, half)], y_own.at[k], y_keep)

    def y_copy(k):
        return pltpu.make_async_remote_copy(
            src_ref=y_stage.at[pl.ds(half, half)], dst_ref=y_other.at[k],
            send_sem=y_send.at[k], recv_sem=y_recv.at[k], device_id=mate, device_id_type=MESH)

    def y_part(k):
        if k:
            y_local(k - 1).wait()
            y_copy(k - 1).wait_send()

        @pl.loop(0, width // tile_n)
        def _(t):
            cols = pl.ds(pl.multiple_of(t * tile_n, tile_n), tile_n)
            y_stage[:, cols] = dot_nt(prod[rows(k, 0, 2), :], down_w[cols, :]).astype(bf16)

        y_local(k).start()
        y_copy(k).start()

    x_keep.wait()
    x_copy(0).wait_recv()
    weight_wait(0)
    gate_part(0)
    for k in (1, 2):
        x_copy(k).wait_recv()
        x_forward(k).start()
    for k in (1, 2):
        x_half(k).start()
    x_forward(1).wait_recv()
    gate_part(1)
    x_forward(2).wait_recv()
    gate_part(2)
    for k in (1, 2):
        x_half(k).wait_recv()
    x_forward(3).start()
    weight_wait(1)
    up_part(0)
    up_part(1)
    x_forward(3).wait_recv()
    gate_part(3)
    up_part(2)
    up_part(3)

    def first_hop(which, sign, way):
        at = pl.ds((lines - 1) * slab_rows if sign == 1 else 0, slab_rows)
        return pltpu.make_async_remote_copy(
            src_ref=parts_out.at[which, at], dst_ref=(carried_up, carried_down)[way].at[which],
            send_sem=first_send.at[which, way], recv_sem=first_recv.at[which, way],
            device_id={"dp": dp + sign * PLANE}, device_id_type=MESH)

    tiles = width // tile_m

    def stage_copy(which, m, slot):
        at = pl.ds(pl.multiple_of(m * tile_m, tile_m), tile_m)
        return pltpu.make_async_copy(stage.at[slot], parts_out.at[which, at], stage_sem.at[slot])

    def weight_grad(which, tokens, grad):
        @pl.loop(0, tiles)
        def _(m):
            at = pl.ds(pl.multiple_of(m * tile_m, tile_m), tile_m)
            tile = dot_nn(tokens[:, at].T, grad[...]).astype(bf16)
            slot = lax.rem(m, 2)

            @pl.when(m >= 2)
            def _():
                stage_copy(which, m - 2, slot).wait()

            stage[slot] = tile
            stage_copy(which, m, slot).start()

        for m in (tiles - 2, tiles - 1):
            stage_copy(which, m, m % 2).wait()
        for sign, way in ways:

            @pl.when(place_of(sign) == 0)
            def _():
                first_hop(which, sign, way).start()

    weight_grad(2, cot_all, prod)
    weight_grad(0, x_all, gate_g)
    dx_first(1)
    dx_first(2)
    dx_second(1)
    dx_first(3)
    dx_second(2)
    dx_first(0)
    dx_second(3)
    dx_second(0)
    weight_grad(1, x_all, up_g)
    for k in range(PLANE):
        y_part(k)

    for k in range(1, PLANE):
        dx_copy(k).wait_recv()
    total = near[0].astype(jnp.float32)
    for k in range(PLANE - 1):
        total = total + back[k].astype(jnp.float32)
    dx_out[...] = total

    for k in range(PLANE):
        if k < PLANE - 1:
            x_copy(k).wait_send()
        if k in (1, 2):
            x_half(k).wait_send()
        pair_copy(k).wait_send()
        if k:
            x_forward(k).wait_send()
            dx_copy(k).wait_send()
    y_local(PLANE - 1).wait()
    y_copy(PLANE - 1).wait_send()
    for k in range(PLANE):
        y_copy(k).wait_recv()
    for which in range(3):
        for sign, way in ways:
            if which < 2:

                @pl.when(place_of(sign) == lines - 2)
                def _():
                    last_hop(which, sign, way).wait_send()

            @pl.when(place_of(sign) == 0)
            def _():
                first_hop(which, sign, way).wait_send()

            @pl.when(place_of(sign) == 1)
            def _():
                first_hop(which, sign, way).wait_recv()

    for k in range(PLANE):
        cot_copy(k).wait_send()


def feed_forward(x, cot, cot_came, slabs, lines, hidden, tile_h=512, tile_n=768, tile_m=256):
    half, width = x.shape
    block = slabs[0].shape[-1]
    slab_rows = width // lines
    tokens = 2 * PLANE * half
    bf16 = jnp.bfloat16
    anywhere = pl.BlockSpec(memory_space=pl.ANY)
    dma = pltpu.SemaphoreType.DMA
    slab = jax.ShapeDtypeStruct((3, slab_rows, block), bf16)
    return pl.pallas_call(
        functools.partial(ff_kernel, tile_h=tile_h, tile_n=tile_n, tile_m=tile_m, lines=lines, hidden=hidden),
        out_shape=(
            jax.ShapeDtypeStruct((half, width), jnp.float32),
            jax.ShapeDtypeStruct((PLANE, half, width), bf16),
            jax.ShapeDtypeStruct((PLANE, half, width), bf16),
            jax.ShapeDtypeStruct((3, width, block), bf16),
            slab,
            slab,
        ),
        in_specs=[anywhere] * (3 + len(slabs)),
        out_specs=(pl.BlockSpec(memory_space=pltpu.VMEM),) + (anywhere,) * 5,
        scratch_shapes=[
            pltpu.VMEM((tokens, width), bf16), pltpu.VMEM((tokens, width), bf16),
            pltpu.VMEM((width, block), bf16), pltpu.VMEM((width, block), bf16), pltpu.VMEM((width, block), bf16),
            pltpu.VMEM((tokens, block), bf16), pltpu.VMEM((tokens, block), bf16), pltpu.VMEM((tokens, block), bf16),
            pltpu.VMEM((PLANE, half, width), bf16), pltpu.VMEM((PLANE, half, width), bf16), pltpu.VMEM((PLANE - 1, half, width), bf16),
            pltpu.VMEM((2 * half, width), bf16), pltpu.VMEM((2, tile_m, block), bf16),
            dma((PLANE - 1,)), dma((PLANE - 1,)), dma((2,)), dma((2,)), dma((PLANE - 1,)), dma((PLANE - 1,)), dma((PLANE,)), dma((PLANE,)),
            dma((PLANE - 1,)), dma((PLANE - 1,)), dma, dma((PLANE,)), dma((PLANE,)), dma((PLANE,)), dma((3, 2 * lines)), dma((3, 2)), dma((3, 2)), dma, dma((PLANE,)), dma((PLANE,)),
            dma((2,)), dma((3, 2)), dma((3, 2)),
        ],
        compiler_params=pltpu.CompilerParams(vmem_limit_bytes=62 << 20, collective_id=0, has_side_effects=True),
        name="feed_forward",
        cost_estimate=pl.CostEstimate(flops=18 * tokens * width * block, bytes_accessed=60 << 20, transcendentals=tokens * block),
    )(x, cot, cot_came, *slabs)


def back_kernel(
    dkv_in, dq_in, cos_in, sin_in, normed_in, first_in, line_o, x_in, rows_in, gain_row_in, middle_grad_in,
    ff_in, carried_up, carried_down,
    input_grad_out, sums_out, small_out, ff_out,
    kv_own, kv_other, kv_plane, kv_merged, kv_line, grads, part_q, part_kv,
    recv_q, recv_kv, line_q, line_kv, from_q, from_kv, from_o,
    far, near, small_own, small_mate, small_plane, small_line,
    own_buf, recv_buf, first_buf, total_buf,
    kv_local, kv_send, kv_recv, kv_line_send, kv_line_recv,
    plane_send, plane_recv, line_send, line_recv,
    mate_send, mate_recv, small_mate_sem, small_plane_send, small_plane_recv, small_line_send, small_line_recv,
    load_sem, own_sem, carry_sem, hop_send, hop_recv, spread_local, spread_send, spread_recv,
    *, lines, members, scale,
):
    bf16, f32 = jnp.bfloat16, jnp.float32
    dp = lax.axis_index("dp")
    core = lax.axis_index("tensor")
    z_at, j_at = dp // PLANE, lax.rem(dp, PLANE)
    half, width = x_in.shape
    local_tok = 2 * half
    slab_rows = width // lines
    shard = slab_rows // PLANE
    q_width = dq_in.shape[1]
    block = total_buf.shape[-1]
    mate = {"tensor": 1 - core}
    chip = [None] + [{"dp": plane_partner(dp, bits)} for bits in range(1, PLANE)]
    there = [j_at] + [lax.rem(plane_partner(dp, bits), PLANE) for bits in range(1, PLANE)]
    side = lax.rem(z_at, 2) * PLANE
    other_side = PLANE - side
    member = lax.rem(dp, members)
    del member
    ways = ((1, 0), (-1, 1))
    place_of = lambda sign: z_at if sign == 1 else lines - 1 - z_at
    tree_rows = lambda m: pl.ds(pl.multiple_of(m * local_tok, local_tok), local_tok)

    kv_loads = [
        pltpu.make_async_copy(dkv_in.at[tree_rows(side + j_at)], kv_own, kv_local.at[0]),
        pltpu.make_async_copy(dkv_in.at[tree_rows(other_side + j_at)], kv_other, kv_local.at[1]),
    ]
    for load in kv_loads:
        load.start()

    def slab_load(which, sign, way, step):
        target = lines - 1 - step + place_of(sign)
        slab = target if sign == 1 else lines - 1 - target
        return pltpu.make_async_copy(ff_in.at[which, slab], own_buf.at[which, way], load_sem.at[which, way])

    def own_load(which):
        return pltpu.make_async_copy(ff_in.at[which, z_at], total_buf.at[which], own_sem.at[which])

    def carry_load(which, sign, way):
        return pltpu.make_async_copy(
            (carried_up if sign == 1 else carried_down).at[which], first_buf.at[which, way], carry_sem.at[which, way])

    order = (2, 0, 1)
    for which in order:
        for sign, way in ways:
            carry_load(which, sign, way).start()

            @pl.when((place_of(sign) >= 1) & (place_of(sign) <= 2))
            def _():
                slab_load(which, sign, way, 2).start()

        own_load(which).start()

    barrier = pltpu.get_barrier_semaphore()
    for bits in range(1, PLANE):
        pl.semaphore_signal(barrier, inc=1, device_id=chip[bits], device_id_type=MESH)
    pl.semaphore_signal(barrier, inc=1, device_id=mate, device_id_type=MESH)
    for apart in range(1, lines):
        pl.semaphore_signal(
            barrier, inc=1, device_id={"dp": lax.rem(z_at + apart, lines) * PLANE + j_at}, device_id_type=MESH)
    pl.semaphore_wait(barrier, PLANE + lines - 1)

    def kv_copy(bits, part):
        at = tree_rows((side if part == 0 else other_side) + there[bits])
        return pltpu.make_async_remote_copy(
            src_ref=dkv_in.at[at], dst_ref=kv_plane.at[bits - 1, part],
            send_sem=kv_send.at[bits - 1, part], recv_sem=kv_recv.at[bits - 1, part],
            device_id=chip[bits], device_id_type=MESH)

    for part in (1, 0):
        for bits in range(1, PLANE):
            kv_copy(bits, part).start()

    def hop(which, sign, way, step, first_place=False):
        slab = lines - 1 - step if sign == 1 else step
        carried = first_buf.at[which, way] if step == 2 else recv_buf.at[which, way, step - 3]
        return pltpu.make_async_remote_copy(
            src_ref=ff_in.at[which, slab] if first_place else carried, dst_ref=recv_buf.at[which, way, step - 2],
            send_sem=hop_send.at[which, way, step - 2], recv_sem=hop_recv.at[which, way, step - 2],
            device_id={"dp": dp + sign * PLANE}, device_id_type=MESH)

    def hop_step(which, step):
        for sign, way in ways:
            place = place_of(sign)
            if step == 2:
                carry_load(which, sign, way).wait()

            @pl.when(place == 0)
            def _():
                hop(which, sign, way, step, True).start()

            @pl.when((place >= 1) & (place <= step))
            def _():
                if step > 2:
                    hop(which, sign, way, step - 1).wait_recv()
                slab_load(which, sign, way, step).wait()
                mine = own_buf[which, way].astype(f32)
                if step == 2:
                    first_buf[which, way] = (mine + first_buf[which, way].astype(f32)).astype(bf16)
                else:
                    recv_buf[which, way, step - 3] = (mine + recv_buf[which, way, step - 3].astype(f32)).astype(bf16)
                hop(which, sign, way, step).start()

            if step < lines - 2:

                @pl.when((place >= 1) & (place <= step + 1))
                def _():
                    slab_load(which, sign, way, step + 1).start()

    for which in order:
        hop_step(which, 2)

    groups = {
        "o": (0, None, None, line_o, from_o, q_width + 256, q_width),
        "q": (1, part_q, recv_q, line_q, from_q, 0, q_width),
        "kv": (2, part_kv, recv_kv, line_kv, from_kv, q_width, 256),
    }

    def plane_copy(name, bits):
        index, part, recv, *_ = groups[name]
        return pltpu.make_async_remote_copy(
            src_ref=part.at[:, there[bits]], dst_ref=recv.at[bits - 1],
            send_sem=plane_send.at[index, bits - 1], recv_sem=plane_recv.at[index, bits - 1],
            device_id=chip[bits], device_id_type=MESH)

    def line_copy(name, apart):
        index, _, _, line, came, *_ = groups[name]
        target = lax.rem(z_at + apart, lines)
        return pltpu.make_async_remote_copy(
            src_ref=line.at[target], dst_ref=came.at[apart - 1],
            send_sem=line_send.at[index, apart - 1], recv_sem=line_recv.at[index, apart - 1],
            device_id={"dp": target * PLANE + j_at}, device_id_type=MESH)

    def plane_start(name):
        for bits in range(1, PLANE):
            plane_copy(name, bits).start()

    def plane_sum(name):
        _, part, recv, line, *_ = groups[name]
        for bits in range(1, PLANE):
            plane_copy(name, bits).wait_recv()
        for z in range(lines):
            total = part[z, j_at].astype(f32)
            for bits in range(1, PLANE):
                total = total + recv[bits - 1, z].astype(f32)
            line[z] = total.astype(bf16)
        line_start(name)

    def line_start(name):
        for apart in range(1, lines):
            line_copy(name, apart).start()

    def line_sum(name):
        *_, line, came, at, size = groups[name]
        for apart in range(1, lines):
            line_copy(name, apart).wait_recv()
        total = line[z_at].astype(f32)
        for apart in range(1, lines):
            total = total + came[apart - 1].astype(f32)
        sums_out[:, at : at + size] = total

    line_start("o")
    cosines, sines = cos_in[...], sin_in[...]

    def turned_back(part):
        return (part * cosines - pltpu.roll(part, 64, 1) * sines).astype(bf16)

    grads[:, 0:q_width] = dq_in[...]

    def weight_part(part, at, size):
        for z in range(lines):
            turned = normed_in[:, z * slab_rows : (z + 1) * slab_rows].T
            tile = dot_nn(turned, grads[:, at : at + size]).astype(bf16)
            for j in range(PLANE):
                part[z, j] = tile[j * shard : (j + 1) * shard]

    weight_part(part_q, 0, q_width)

    columns = lambda j: pl.ds(pl.multiple_of(j * block, block), block)

    def spread(which, bits):
        rows = pl.ds(pl.multiple_of(there[bits] * shard, shard), shard)
        return pltpu.make_async_remote_copy(
            src_ref=total_buf.at[which, rows], dst_ref=ff_out.at[which, :, columns(j_at)],
            send_sem=spread_send.at[which, bits - 1], recv_sem=spread_recv.at[which, bits - 1],
            device_id=chip[bits], device_id_type=MESH)

    def spread_keep(which):
        rows = pl.ds(pl.multiple_of(j_at * shard, shard), shard)
        return pltpu.make_async_copy(
            total_buf.at[which, rows], ff_out.at[which, :, columns(j_at)], spread_local.at[which])

    def line_done(which):
        for step in range(3, lines - 1):
            hop_step(which, step)
        own_load(which).wait()
        for sign, way in ways:

            @pl.when(place_of(sign) >= 1)
            def _():
                hop(which, sign, way, lines - 2).wait_recv()
                came = recv_buf[which, way, lines - 4].astype(f32)
                total_buf[which] = (total_buf[which].astype(f32) + came).astype(bf16)

        for bits in range(1, PLANE):
            spread(which, bits).start()
        spread_keep(which).start()

    for load in kv_loads:
        load.wait()
    for bits in range(1, PLANE):
        kv_copy(bits, 1).wait_recv()
    total = kv_other[...].astype(f32)
    for bits in range(1, PLANE):
        total = total + kv_plane[bits - 1, 1].astype(f32)
    kv_merged[...] = total.astype(bf16)
    kv_across = pltpu.make_async_remote_copy(
        src_ref=kv_merged, dst_ref=kv_line, send_sem=kv_line_send, recv_sem=kv_line_recv,
        device_id={"dp": line_partner(dp)}, device_id_type=MESH)
    kv_across.start()
    plane_start("q")
    line_done(2)
    for bits in range(1, PLANE):
        kv_copy(bits, 0).wait_recv()
    kv_across.wait_recv()
    total = kv_own[...].astype(f32) + kv_line[...].astype(f32)
    for bits in range(1, PLANE):
        total = total + kv_plane[bits - 1, 0].astype(f32)
    grads[:, q_width : q_width + 128] = turned_back(total[:, 0:128] * scale)
    grads[:, q_width + 128 :] = total[:, 128:256].astype(bf16)
    weight_part(part_kv, q_width, 256)
    plane_start("kv")

    def normed_grad(c):
        at = pl.ds(pl.multiple_of(c * half, half), half)
        return dot_nt(grads[at, :], first_in[...])

    far[...] = normed_grad(1 - core).astype(bf16)
    mate_copy = pltpu.make_async_remote_copy(
        src_ref=far, dst_ref=near, send_sem=mate_send, recv_sem=mate_recv, device_id=mate, device_id_type=MESH)
    mate_copy.start()
    mine = normed_grad(core)
    line_done(0)
    mate_copy.wait_recv()
    mine = mine + near[...].astype(f32)
    wide = x_in[...].astype(f32)
    norm = lax.rsqrt(jnp.mean(wide * wide, axis=1, keepdims=True) + EPS)
    z_own = wide * norm
    w = mine * gain_row_in[0:1, :]
    back = norm * (w - z_own * jnp.mean(w * z_own, axis=1, keepdims=True))
    input_grad_out[...] = (middle_grad_in[...] + back).astype(bf16)
    bias = jnp.sum(grads[...].astype(f32), axis=0, keepdims=True)
    small_own[...] = jnp.concatenate(
        [
            jnp.sum(mine * z_own, axis=0, keepdims=True),
            rows_in[...],
            jnp.concatenate([bias, jnp.zeros((1, width - q_width - 256), f32)], axis=1),
            jnp.zeros((5, width), f32),
        ],
        axis=0,
    )
    small_copy = pltpu.make_async_remote_copy(
        src_ref=small_own, dst_ref=small_mate, send_sem=small_mate_sem.at[0], recv_sem=small_mate_sem.at[1],
        device_id=mate, device_id_type=MESH)
    small_copy.start()
    plane_sum("q")
    plane_sum("kv")

    small_copy.wait_recv()
    gain_rows = lax.broadcasted_iota(jnp.int32, (8, width), 0) < 2
    small_plane[0] = small_own[...] + jnp.where(gain_rows, small_mate[...], 0.0)

    def small_plane_copy(bits):
        return pltpu.make_async_remote_copy(
            src_ref=small_plane.at[0], dst_ref=small_plane.at[bits],
            send_sem=small_plane_send.at[bits - 1], recv_sem=small_plane_recv.at[bits - 1],
            device_id=chip[bits], device_id_type=MESH)

    def small_line_copy(apart):
        return pltpu.make_async_remote_copy(
            src_ref=small_line.at[0], dst_ref=small_line.at[apart],
            send_sem=small_line_send.at[apart - 1], recv_sem=small_line_recv.at[apart - 1],
            device_id={"dp": lax.rem(z_at + apart, lines) * PLANE + j_at}, device_id_type=MESH)

    for bits in range(1, PLANE):
        small_plane_copy(bits).start()
    for bits in range(1, PLANE):
        small_plane_copy(bits).wait_recv()
    total = small_plane[0]
    for bits in range(1, PLANE):
        total = total + small_plane[bits]
    small_line[0] = total
    for apart in range(1, lines):
        small_line_copy(apart).start()
    line_sum("o")
    line_done(1)
    line_sum("q")
    line_sum("kv")
    for apart in range(1, lines):
        small_line_copy(apart).wait_recv()
    total = small_line[0]
    for apart in range(1, lines):
        total = total + small_line[apart]
    small_out[...] = total

    for which in order:
        for bits in range(1, PLANE):
            spread(which, bits).wait_recv()
            spread(which, bits).wait_send()
        spread_keep(which).wait()
        for sign, way in ways:
            for step in range(2, lines - 1):

                @pl.when(place_of(sign) <= step)
                def _():
                    hop(which, sign, way, step).wait_send()

    for bits in range(1, PLANE):
        small_plane_copy(bits).wait_send()
        for part in range(2):
            kv_copy(bits, part).wait_send()
        for name in ("q", "kv"):
            plane_copy(name, bits).wait_send()
    for apart in range(1, lines):
        small_line_copy(apart).wait_send()
        for name in groups:
            line_copy(name, apart).wait_send()
    kv_across.wait_send()
    mate_copy.wait_send()
    small_copy.wait_send()


def finish(dkv, dq, cosines, sines, normed, first, line_o, x, gain_rows, gain_row, middle_grad, ff_parts, up, down, lines, members, scale):
    bf16, f32 = jnp.bfloat16, jnp.float32
    half, width = x.shape
    local_tok = 2 * half
    q_width = dq.shape[1]
    slab_rows = width // lines
    shard = slab_rows // PLANE
    block = ff_parts.shape[-1]
    anywhere = pl.BlockSpec(memory_space=pl.ANY)
    inside = pl.BlockSpec(memory_space=pltpu.VMEM)
    dma = pltpu.SemaphoreType.DMA
    near = PLANE - 1
    vmem = lambda *shape: pltpu.VMEM(shape, bf16)
    wide = lambda *shape: pltpu.VMEM(shape, f32)
    pair = (local_tok, 256)
    return pl.pallas_call(
        functools.partial(back_kernel, lines=lines, members=members, scale=scale),
        out_shape=(
            jax.ShapeDtypeStruct((half, width), bf16),
            jax.ShapeDtypeStruct((shard, 2 * q_width + 256), f32),
            jax.ShapeDtypeStruct((8, width), f32),
            jax.ShapeDtypeStruct((3, shard, PLANE * block), bf16),
        ),
        in_specs=[anywhere] + [inside] * 10 + [anywhere] * 3,
        out_specs=(inside, inside, inside, anywhere),
        scratch_shapes=[
            vmem(*pair), vmem(*pair), vmem(near, 2, *pair), vmem(*pair), vmem(*pair),
            vmem(local_tok, q_width + 256), vmem(lines, PLANE, shard, q_width), vmem(lines, PLANE, shard, 256),
            vmem(near, lines, shard, q_width), vmem(near, lines, shard, 256),
            vmem(lines, shard, q_width), vmem(lines, shard, 256),
            vmem(lines - 1, shard, q_width), vmem(lines - 1, shard, 256), vmem(lines - 1, shard, q_width),
            vmem(half, width), vmem(half, width), wide(8, width), wide(8, width), wide(PLANE, 8, width), wide(lines, 8, width),
            vmem(3, 2, slab_rows, block), vmem(3, 2, lines - 3, slab_rows, block), vmem(3, 2, slab_rows, block), vmem(3, slab_rows, block),
            dma((2,)), dma((near, 2)), dma((near, 2)), dma, dma,
            dma((3, near)), dma((3, near)), dma((3, lines - 1)), dma((3, lines - 1)),
            dma, dma, dma((2,)), dma((near,)), dma((near,)), dma((lines - 1,)), dma((lines - 1,)),
            dma((3, 2)), dma((3,)), dma((3, 2)), dma((3, 2, lines - 3)), dma((3, 2, lines - 3)), dma((3,)), dma((3, near)), dma((3, near)),
        ],
        compiler_params=pltpu.CompilerParams(vmem_limit_bytes=62 << 20, collective_id=2, has_side_effects=True),
        name="back",
        cost_estimate=pl.CostEstimate(flops=6 * local_tok * width * (q_width + 256), bytes_accessed=40 << 20, transcendentals=0),
    )(dkv, dq, cosines, sines, normed, first, line_o, x, gain_rows, gain_row, middle_grad, ff_parts, up, down)


def swap(block, axis, count, bits):
    return lax.ppermute(block, axis, [(i, i ^ bits) for i in range(count)])


def rms_scale(values):
    return lax.rsqrt(jnp.mean(values * values, axis=1, keepdims=True) + EPS)


def norm_back(grad, values, gain):
    scale = rms_scale(values)
    z = values * scale
    w = grad * gain
    gain_grad = jnp.sum(grad * z, axis=0)
    return scale * (w - z * jnp.mean(w * z, axis=1, keepdims=True)), gain_grad


def rope_tables(positions):
    exponents = jnp.arange(64, dtype=jnp.float32) * (2.0 / 128)
    frequency = jnp.power(THETA, -exponents)
    angles = positions.astype(jnp.float32)[:, None] * frequency[None, :]
    cosines, sines = jnp.cos(angles), jnp.sin(angles)
    return (
        jnp.concatenate([cosines, cosines], axis=1),
        jnp.concatenate([-sines, sines], axis=1),
    )


def contract_rows(left, right):
    return lax.dot_general(
        left, right, (((0,), (0,)), ((), ())), preferred_element_type=jnp.float32
    )


def contract_cols(left, right):
    return lax.dot_general(
        left, right, (((1,), (1,)), ((), ())), preferred_element_type=jnp.float32
    )


def matmul(left, right):
    return jnp.dot(left, right, preferred_element_type=jnp.float32)


def attention_plan(segment_ids, parent_ids, dp_index, local_tok):
    members = TREE_TOK // local_tok
    first = dp_index // members * TREE_TOK
    slots = lax.dynamic_slice_in_dim(segment_ids, first, TREE_TOK)[::KB]
    numbers = jnp.arange(parent_ids.shape[0], dtype=jnp.int32)
    parents = jnp.sum(jnp.where(slots[:, None] == numbers[None, :], parent_ids[None, :], 0), axis=1)
    places = jnp.arange(slots.shape[0], dtype=jnp.int32)
    holder = jnp.sum(jnp.where(parents[:, None] == slots[None, :], places[None, :], 0), axis=1)
    starts = dp_index % members * local_tok + QB * jnp.arange(local_tok // QB, dtype=jnp.int32)
    slot = starts // KB
    chosen = slot[:, None] == places[None, :]
    pick = lambda table: jnp.sum(jnp.where(chosen, table[None, :], 0), axis=1)
    in_trunk = starts < TRUNK
    is_leaf = pick(parents) != slots[0]
    chunk = jnp.minimum(starts, TRUNK) // KC
    far = jnp.int32(1 << 20)
    block0 = jnp.where(in_trunk, 2 * chunk, jnp.where(is_leaf, pick(holder), TRUNK // KB))
    block1 = jnp.where(in_trunk, 2 * chunk + 1, slot)
    shift0 = jnp.where(in_trunk, block0 * KB - starts, jnp.where(is_leaf, -far, far))
    shift1 = block1 * KB - starts
    hot = jnp.where(~in_trunk[:, None] & (block0[:, None] == places[None, :]), 1.0, 0.0)
    return jnp.stack([shift0, shift1], axis=1).reshape(-1), hot.reshape(-1)


def on_device(
    dp_size,
    layer_input,
    out_cotangent,
    positions,
    segment_ids,
    parent_ids,
    attention_gain,
    query_weight,
    query_bias,
    key_weight,
    key_bias,
    value_weight,
    value_bias,
    output_weight,
    feedforward_gain,
    gate_weight,
    up_weight,
    down_weight,
):
    bf16, f32 = jnp.bfloat16, jnp.float32
    local_tok = positions.shape[0]
    half_tok, width = layer_input.shape
    shard = attention_gain.shape[0]
    heads, head_dim = query_bias.shape[0], 128
    per_head = query_bias.shape[1]
    q_width = heads * head_dim
    hidden = gate_weight.shape[1]
    lines = dp_size // PLANE
    members = TREE_TOK // local_tok
    dp_index = lax.axis_index("dp")
    core = lax.axis_index("tensor")
    scale = head_dim ** (-0.5)

    def line_route(sign, first, last):
        route = []
        for place in range(first, last + 1):
            z = place if sign == 1 else lines - 1 - place
            route += [(z * PLANE + j, (z + sign) * PLANE + j) for j in range(PLANE)]
        return route

    def by_core(mine):
        other = swap(mine, "tensor", 2, 1)
        first = jnp.where(core == 0, mine, other)
        second = jnp.where(core == 0, other, mine)
        return jnp.concatenate([first, second], axis=0)

    first_own = jnp.concatenate([query_weight, key_weight, value_weight], axis=1)
    biases = jnp.concatenate([query_bias, key_bias, value_bias], axis=0)
    bias_row = lax.dynamic_update_slice(
        jnp.zeros((heads + 2, head_dim), bf16), biases, (0, dp_index * per_head)
    ).reshape(1, -1)
    gains = lax.dynamic_update_slice(
        jnp.zeros((2, width), bf16), jnp.stack([attention_gain, feedforward_gain]), (0, dp_index * shard)
    )
    extra = jnp.concatenate(
        [gains, jnp.pad(bias_row, ((0, 0), (0, width - bias_row.shape[1]))), jnp.zeros((13, width), bf16)], axis=0
    )
    cosines, sines = rope_tables(positions)
    plan, hot = attention_plan(segment_ids, parent_ids, dp_index, local_tok)
    steps = lines - 3
    outs = front(
        gate_weight, up_weight, down_weight.T, first_own, output_weight.T, extra, layer_input, cosines, sines, lines, members
    )
    slab, ups, downs = outs[0], list(outs[1 : 1 + steps]), list(outs[1 + steps : 1 + 2 * steps])
    late_up, late_down, first_all, out_t, q_rot, tree, normed, rows = outs[1 + 2 * steps :]

    attended, lse, middle, normed_two, other, cot_came, *more = attend(
        plan, hot, q_rot, tree, out_t, layer_input, rows, out_cotangent, ups[-1], downs[-1], late_up, late_down,
        lines, members, scale,
    )

    normed_two_grad, y_own, y_other, ff_parts, up_first, down_first = feed_forward(
        normed_two, out_cotangent, cot_came, [slab] + ups + downs + [late_up, late_down] + more, lines, hidden
    )

    ff_parts = ff_parts.reshape(3, lines, width // lines, ff_parts.shape[-1])

    dq, dtree, middle_grad, gain_two_grad, line_o, layer_output, up_next, down_next = attend_back(
        plan, hot, q_rot, attended, lse, tree, other, out_t, normed_two_grad, middle, out_cotangent, rows, cosines, sines,
        y_own, y_other, ff_parts, up_first, down_first, lines, members, scale,
    )
    input_grad, sums, small, ff_sums = finish(
        dtree, dq, cosines, sines, normed, first_all, line_o, layer_input, gain_two_grad, rows,
        middle_grad, ff_parts, up_next, down_next, lines, members, scale,
    )
    ff_sums = ff_sums[:, :, :hidden].astype(f32)
    gains_out = lax.dynamic_slice(small[0:2], (0, dp_index * shard), (2, shard))
    bias_out = lax.dynamic_slice(
        small[2, : (heads + 2) * head_dim].reshape(heads + 2, head_dim), (0, dp_index * per_head), (heads + 2, per_head)
    )
    return (
        layer_output,
        input_grad,
        gains_out[0],
        sums[:, :q_width],
        bias_out[:heads],
        sums[:, q_width : q_width + 128],
        bias_out[heads : heads + 1],
        sums[:, q_width + 128 : q_width + 256],
        bias_out[heads + 1 :],
        sums[:, q_width + 256 :].T,
        gains_out[1],
        ff_sums[0],
        ff_sums[1],
        ff_sums[2].T,
    )


def solution(mesh):
    placed = (
        P(("dp", "tensor"), None),
        P(("dp", "tensor"), None),
        P("dp"),
        P(),
        P(),
        P("dp"),
        P("dp", "tensor"),
        P("tensor", "dp"),
        P("dp", "tensor"),
        P("tensor", "dp"),
        P("dp", "tensor"),
        P("tensor", "dp"),
        P("tensor", "dp"),
        P("dp"),
        P("dp", "tensor"),
        P("dp", "tensor"),
        P("tensor", "dp"),
    )
    return jax.shard_map(
        functools.partial(on_device, mesh.shape["dp"]),
        mesh=mesh,
        in_specs=placed,
        out_specs=(
            P(("dp", "tensor"), None),
            P(("dp", "tensor"), None),
            P("dp"),
            P("dp", "tensor"),
            P("tensor", "dp"),
            P("dp", "tensor"),
            P("tensor", "dp"),
            P("dp", "tensor"),
            P("tensor", "dp"),
            P("tensor", "dp"),
            P("dp"),
            P("dp", "tensor"),
            P("dp", "tensor"),
            P("tensor", "dp"),
        ),
        check_vma=False,
    )
```
